32 devices in a mesh: frames: 4 (over y, x), heads: 8 (over z, core).
Axes of the slice: x: 2, y: 2, z: 4, core: 2. Of those that a mesh axis runs over, the one named last changes fastest.
Arguments:
- block_input: bfloat16 [16, 256, 1024], P('frames'), may hold values from -6 to 6
- action_ids: int32 [16], P('frames'), may hold values from 0 to 7
- segment_ids: int32 [16], replicated, may hold values from 0 to 2, as said below
- action_table: bfloat16 [8, 1024], replicated, may hold values from -3 to 3
- norm_gain: float32 [3, 1024], replicated, may hold values from 0.5 to 1.5
- norm_shift: float32 [3, 1024], replicated, may hold values from -2 to 2
- spatial_qkv: bfloat16 [1024, 3, 1024], P(None, None, 'heads'), may hold values from -0.1875 to 0.1875
- spatial_out: bfloat16 [1024, 1024], P('heads'), may hold values from -0.75 to 0.75
- temporal_qkv: bfloat16 [1024, 3, 1024], P(None, None, 'heads'), may hold values from -0.1875 to 0.1875
- temporal_out: bfloat16 [1024, 1024], P('heads'), may hold values from -0.5 to 0.5
- out_bias: float32 [3, 1024], replicated, may hold values from -2 to 2
- up_weight: bfloat16 [1024, 4096], P(None, 'heads'), may hold values from -0.1875 to 0.1875
- up_bias: float32 [4096], P('heads'), may hold values from -2 to 2
- down_weight: bfloat16 [4096, 1024], P('heads'), may hold values from -0.375 to 0.375
- cotangent: bfloat16 [16, 256, 1024], P('frames'), may hold values from -6 to 6
Outputs:
- block_output: bfloat16 [16, 256, 1024], P('frames', 'heads')
- input_grad: float32 [16, 256, 1024], P('frames', 'heads')
- table_grad: float32 [8, 1024], replicated
- gain_grad: float32 [3, 1024], replicated
- shift_grad: float32 [3, 1024], replicated
- spatial_qkv_grad: float32 [1024, 3, 1024], P(None, None, 'heads')
- spatial_out_grad: float32 [1024, 1024], P('heads')
- temporal_qkv_grad: float32 [1024, 3, 1024], P(None, None, 'heads')
- temporal_out_grad: float32 [1024, 1024], P('heads')
- bias_grad: float32 [3, 1024], replicated
- up_grad: float32 [1024, 4096], P(None, 'heads')
- up_bias_grad: float32 [4096], P('heads')
- down_grad: float32 [4096, 1024], P('heads')
The draws below stay inside these ranges and needn't reach their ends.
Inputs may be any that keep to these rules, and one draw needn't show every extreme that they name: `segment_ids`: clips are runs of consecutive frames whose numbers never fall; one clip starts within the first 4 frames and ends within the last 4 frames.
All inputs are finite; a program needn't handle non-finite values.
Results may differ from the reference program's by a relative error of at most 0.03.
Values may be sent and summed in bfloat16 or wider, within the bound.
A program may use at most 128 MiB of HBM per device.

```python
import jax
import jax.numpy as jnp
from jax import lax

D = 1024
H = 16
HD = 64
FF = 4096
ACTIONS = 8
PATCHES = 256
F_DEV = 4
FRAMES = 16


def draw_segment_ids(key, part):
    key = jax.random.fold_in(key, 11)
    first_key, last_key = jax.random.split(key)
    begin = jax.random.randint(first_key, (), 0, F_DEV)
    finish = jax.random.randint(last_key, (), FRAMES - F_DEV, FRAMES)
    frame_index = jnp.arange(FRAMES, dtype=jnp.int32)
    return (frame_index >= begin).astype(jnp.int32) + (frame_index > finish).astype(jnp.int32)


def touch_ends(array, own_key, smallest, high):
    longest = array.shape.index(max(array.shape))
    spots = []
    for shift in (0, 1):
        where = [jax.random.randint(jax.random.fold_in(own_key, axis), (), 0, length) for axis, length in enumerate(array.shape)]
        where[longest] = (where[longest] + shift) % array.shape[longest]
        spots.append(tuple(where))
    return array.at[spots[0]].set(smallest).at[spots[1]].set(high)


def shard_levels(rng, dims, cuts, least, high):
    def one(dim, blocks):
        steps = jax.random.uniform(jax.random.fold_in(jax.random.fold_in(rng, 6), dim), (blocks,), jnp.float32, least / len(cuts), high / len(cuts))
        return jnp.repeat(jnp.exp(steps), dims[dim] // blocks).reshape((-1,) + (1,) * (len(dims) - dim - 1))

    level = one(*cuts[0])
    for cut in cuts[1:]:
        level = level * one(*cut)
    return level


def noise(key, dims, width, limit, shards=(), kind=jnp.bfloat16):
    drawn = width * jax.random.normal(key, dims, jnp.float32)
    if shards:
        drawn = drawn * shard_levels(key, dims, shards, -0.22, 0.18)
    return jnp.clip(drawn, -limit, limit).astype(kind)


def setup_inputs(seed: int = 0) -> dict:
    key_list = jax.random.split(jax.random.key(seed), 16)
    block_input = noise(key_list[0], (FRAMES, PATCHES, D), 1.0, 6.0, ((0, 4),))
    action_ids = touch_ends(jax.random.randint(key_list[1], (FRAMES,), 0, ACTIONS), jax.random.fold_in(key_list[1], 1), 0, ACTIONS - 1).astype(jnp.int32)
    segment_ids = draw_segment_ids(jax.random.fold_in(key_list[15], 71), 0)
    action_table = noise(key_list[3], (ACTIONS, D), 0.5, 3.0)
    norm_gain = jnp.clip(1.0 + 0.1 * jax.random.normal(key_list[4], (3, D), jnp.float32), 0.5, 1.5)
    norm_shift = noise(key_list[5], (3, D), 0.3, 2.0, (), jnp.float32)
    spatial_qkv = noise(key_list[6], (D, 3, H * HD), D ** -0.5, 0.1875, ((2, 8),))
    spatial_out = noise(key_list[7], (H * HD, D), (max(1, H * HD // 16)) ** -0.5, 0.75, ((0, 8),))
    temporal_qkv = noise(key_list[8], (D, 3, H * HD), D ** -0.5, 0.1875, ((2, 8),))
    temporal_out = noise(key_list[9], (H * HD, D), (H * HD // 8) ** -0.5, 0.5, ((0, 8),))
    out_bias = noise(key_list[10], (3, D), 0.3, 2.0, (), jnp.float32)
    up_weight = noise(key_list[11], (D, FF), D ** -0.5, 0.1875, ((1, 8),))
    up_bias = noise(key_list[12], (FF,), 0.3, 2.0, ((0, 8),), jnp.float32)
    down_weight = noise(key_list[13], (FF, D), (FF // 16) ** -0.5, 0.375, ((0, 8),))
    cotangent = noise(key_list[14], (FRAMES, PATCHES, D), 1.0, 6.0, ((0, 4),))
    return dict(block_input=block_input, action_ids=action_ids, segment_ids=segment_ids, action_table=action_table, norm_gain=norm_gain, norm_shift=norm_shift, spatial_qkv=spatial_qkv, spatial_out=spatial_out, temporal_qkv=temporal_qkv, temporal_out=temporal_out, out_bias=out_bias, up_weight=up_weight, up_bias=up_bias, down_weight=down_weight, cotangent=cotangent)


HIGH = lax.Precision.HIGHEST

@jax.custom_vjp
def low(v):
    return lax.optimization_barrier(v.astype(jnp.bfloat16)).astype(jnp.float32)

@jax.custom_vjp
def low_back(v):
    return v

def low_keep(v):
    return (low(v), None)

def low_pass(kept, grad):
    return (grad,)

def back_keep(v):
    return (v, None)

def back_low(kept, grad):
    return (low(grad),)
low.defvjp(low_keep, low_pass)
low_back.defvjp(back_keep, back_low)

def layer_norm(value, gain, shift):
    centered = value - lax.optimization_barrier(jnp.mean(value, axis=-1, keepdims=True))
    spread = lax.optimization_barrier(jnp.mean(centered * centered, axis=-1, keepdims=True))
    return centered * lax.rsqrt(spread + 1e-05) * gain + shift

def spatial_frame(block):
    query, key, value = (block[0], block[1], block[2])
    scores = low_back(jnp.einsum('qhe,khe->hqk', query, key, precision=HIGH) * HD ** (-0.5))
    weights = low(jax.nn.softmax(scores, axis=-1))
    return jnp.einsum('hqk,khe->qhe', weights, value, precision=HIGH)

def block_forward(block_input, action_table, norm_gain, norm_shift, spatial_qkv, spatial_out, temporal_qkv, temporal_out, out_bias, up_weight, up_bias, down_weight, action_ids, segment_ids):
    state0 = block_input + action_table[action_ids][:, None, :]
    normed1 = low(layer_norm(state0, norm_gain[0], norm_shift[0]))
    s_proj = low_back(low(jnp.einsum('fsd,dch->fcsh', normed1, spatial_qkv, precision=HIGH)))
    s_proj = s_proj.reshape(FRAMES, 3, PATCHES, H, HD)
    s_mixed = low_back(low(lax.map(jax.checkpoint(spatial_frame), s_proj)))
    s_branch = jnp.einsum('fshe,hed->fsd', s_mixed, spatial_out.reshape(H, HD, D), precision=HIGH)
    state1 = state0 + low_back(s_branch) + out_bias[0]
    normed2 = low(layer_norm(state1, norm_gain[1], norm_shift[1]))
    t_proj = low_back(low(jnp.einsum('fsd,dch->csfh', normed2, temporal_qkv, precision=HIGH)))
    t_proj = t_proj.reshape(3, PATCHES, FRAMES, H, HD)
    scores = low_back(jnp.einsum('sqhe,skhe->shqk', t_proj[0], t_proj[1], precision=HIGH) * HD ** (-0.5))
    query_ids = lax.broadcasted_iota(jnp.int32, (FRAMES, FRAMES), 0)
    key_ids = lax.broadcasted_iota(jnp.int32, (FRAMES, FRAMES), 1)
    allowed = (key_ids <= query_ids) & (segment_ids[:, None] == segment_ids[None, :])
    scores = jnp.where(allowed, scores, -1000000000.0)
    weights = low(jax.nn.softmax(scores, axis=-1))
    t_mixed = low_back(low(jnp.einsum('shqk,skhe->sqhe', weights, t_proj[2], precision=HIGH)))
    t_branch = jnp.einsum('sfhe,hed->fsd', t_mixed, temporal_out.reshape(H, HD, D), precision=HIGH)
    state2 = state1 + low_back(t_branch) + out_bias[1]
    normed3 = low(layer_norm(state2, norm_gain[2], norm_shift[2]))
    pre = low_back(jnp.einsum('fsd,dk->fsk', normed3, up_weight, precision=HIGH) + up_bias)
    hidden = low(jax.nn.gelu(pre, approximate=True))
    f_branch = jnp.einsum('fsk,kd->fsd', hidden, down_weight, precision=HIGH)
    return state2 + low_back(f_branch) + out_bias[2]

def reference(block_input, action_ids, segment_ids, action_table, norm_gain, norm_shift, spatial_qkv, spatial_out, temporal_qkv, temporal_out, out_bias, up_weight, up_bias, down_weight, cotangent):

    def forward(a0, a1, a2, a3, a4, a5, a6, a7, a8, a9, a10, a11):
        return block_forward(a0, a1, a2, a3, a4, a5, a6, a7, a8, a9, a10, a11, action_ids, segment_ids)
    result, pullback = jax.vjp(forward, block_input.astype(jnp.float32), action_table.astype(jnp.float32), norm_gain.astype(jnp.float32), norm_shift.astype(jnp.float32), spatial_qkv.astype(jnp.float32), spatial_out.astype(jnp.float32), temporal_qkv.astype(jnp.float32), temporal_out.astype(jnp.float32), out_bias.astype(jnp.float32), up_weight.astype(jnp.float32), up_bias.astype(jnp.float32), down_weight.astype(jnp.float32))
    grads = pullback(cotangent.astype(jnp.float32))
    return (result.astype(jnp.bfloat16), grads[0], grads[1], grads[2], grads[3], grads[4], grads[5], grads[6], grads[7], grads[8], grads[9], grads[10], grads[11])
```

```python
import jax
import jax.numpy as jnp
import numpy as np
from jax import lax
from jax.experimental import pallas as pl
from jax.experimental.pallas import tpu as pltpu
from jax.sharding import PartitionSpec as P

HD = 64
SCALE = HD**-0.5
EPS = 1e-05
MASKED = -1000000000.0
F32 = jnp.float32
BF16 = jnp.bfloat16
MESH = pl.DeviceIdType.MESH
VMEM_LIMIT = 56 * 1024 * 1024
GELU_C = float(np.sqrt(2.0 / np.pi))
LAG = 2
LEAD = 3


def mm(a, b):
    return lax.dot_general(a, b, (((1,), (0,)), ((), ())), preferred_element_type=F32)


def mm_nt(a, b):
    return lax.dot_general(a, b, (((1,), (1,)), ((), ())), preferred_element_type=F32)


def mm_tn(a, b):
    return lax.dot_general(a, b, (((0,), (0,)), ((), ())), preferred_element_type=F32)


def norm_stats(value):
    centered = value - jnp.mean(value, axis=-1, keepdims=True)
    inv = lax.rsqrt(jnp.mean(centered * centered, axis=-1, keepdims=True) + EPS)
    return centered * inv, inv


def norm_back(value, grad, gain):
    normed, inv = norm_stats(value)
    e = grad * gain
    first = jnp.mean(e, axis=-1, keepdims=True)
    second = jnp.mean(e * normed, axis=-1, keepdims=True)
    gain_grad = jnp.sum(grad * normed, axis=0, keepdims=True)
    shift_grad = jnp.sum(grad, axis=0, keepdims=True)
    return (e - first - normed * second) * inv, gain_grad, shift_grad


def head_lanes(shape, head):
    lane = lax.broadcasted_iota(jnp.int32, shape, 1)
    return (lane >= head * HD) & (lane < (head + 1) * HD)


def softmax_of(q, k, mask):
    scores = mm_nt(q, k) * SCALE
    if mask is not None:
        scores = jnp.where(mask, scores, MASKED)
    raised = jnp.exp(scores - jnp.max(scores, axis=-1, keepdims=True))
    return raised / jnp.sum(raised, axis=-1, keepdims=True)


def attend(q, k, v, mask):
    heads = q.shape[1] // HD
    mixed = None
    for head in range(heads):
        lanes = head_lanes(q.shape, head)
        probs = softmax_of(jnp.where(lanes, q, jnp.zeros_like(q)), k, mask).astype(BF16)
        out = mm(probs, v)
        mixed = out if mixed is None else jnp.where(lanes, out, mixed)
    return mixed.astype(BF16)


def attend_back(q, k, v, mask, grad):
    heads = q.shape[1] // HD
    dq = dk = dv = None
    for head in range(heads):
        lanes = head_lanes(q.shape, head)
        qh = jnp.where(lanes, q, jnp.zeros_like(q))
        gh = jnp.where(lanes, grad, jnp.zeros_like(grad))
        probs = softmax_of(qh, k, mask)
        dvh = mm_tn(probs.astype(BF16), gh)
        dp = mm_nt(gh, v)
        ds = (probs * (dp - jnp.sum(dp * probs, axis=-1, keepdims=True))).astype(BF16)
        dqh = mm(ds, k) * SCALE
        dkh = mm_tn(ds, qh) * SCALE
        if head == 0:
            dq, dk, dv = dqh, dkh, dvh
        else:
            dq = jnp.where(lanes, dqh, dq)
            dk = dk + dkh
            dv = dv + dvh
    return dq.astype(BF16), dk.astype(BF16), dv.astype(BF16)


class Line:
    def __init__(self, sems, steps):
        self.frames = lax.axis_size("frames")
        self.heads = lax.axis_size("heads")
        self.chips = self.heads // 2
        self.f = lax.axis_index("frames")
        self.h = lax.axis_index("heads")
        self.z = self.h // 2
        self.c = self.h % 2
        self.steps = steps
        self.sems = sems

    def at(self, z):
        return (self.f, jnp.clip(z, 0, self.chips - 1) * 2 + self.c)

    def sibling(self):
        return (self.f, self.z * 2 + 1 - self.c)

    def barrier(self, over_frames, whole_line=False):
        sem = pltpu.get_barrier_semaphore()

        def greet(device):
            pl.semaphore_signal(sem, inc=1, device_id=device, device_id_type=MESH)

        greet(self.sibling())
        count = 1
        if over_frames:
            for k in range(1, self.frames):
                greet(((self.f + k) % self.frames, self.h))
            count += self.frames - 1
        if whole_line:
            for k in range(1, self.chips):
                greet(self.at((self.z + k) % self.chips))
            count += self.chips - 1
        else:

            @pl.when(self.z > 0)
            def _():
                greet(self.at(self.z - 1))

            @pl.when(self.z < self.chips - 1)
            def _():
                greet(self.at(self.z + 1))

            count = count + (self.z > 0).astype(jnp.int32)
            count = count + (self.z < self.chips - 1).astype(jnp.int32)
        pl.semaphore_wait(sem, count)

    def copy(self, src, dst, send, recv, device):
        return pltpu.make_async_remote_copy(
            src_ref=src,
            dst_ref=dst,
            send_sem=send,
            recv_sem=recv,
            device_id=device,
            device_id_type=MESH,
        )


class Gather:
    def __init__(self, line, buf, sems):
        self.line, self.buf = line, buf
        self.got, self.got_sib, self.sent_up, self.sent_down, self.sent_sib = sems

    def up(self, s, zb):
        ln = self.line
        ref = self.buf.at[s, zb, ln.c]
        return ln.copy(ref, ref, self.sent_up.at[s, zb], self.got.at[s, zb], ln.at(ln.z + 1))

    def down(self, s, zb):
        ln = self.line
        ref = self.buf.at[s, zb, ln.c]
        return ln.copy(ref, ref, self.sent_down.at[s, zb], self.got.at[s, zb], ln.at(ln.z - 1))

    def across(self, s, zb):
        ln = self.line
        ref = self.buf.at[s, zb, ln.c]
        return ln.copy(ref, ref, self.sent_sib.at[s, zb], self.got_sib.at[s, zb], ln.sibling())

    def wait_across(self, s, zb):
        ln = self.line
        ref = self.buf.at[s, zb, 1 - ln.c]
        ln.copy(
            ref, ref, self.sent_sib.at[s, zb], self.got_sib.at[s, zb], ln.sibling()
        ).wait_recv()

    def start(self, own):
        ln = self.line
        for s in range(ln.steps):
            self.buf[s, ln.z, ln.c] = own[s]

            @pl.when(ln.z < ln.chips - 1)
            def _():
                self.up(s, ln.z).start()

            @pl.when(ln.z > 0)
            def _():
                self.down(s, ln.z).start()

            self.across(s, ln.z).start()

    def arrive(self, distance, s):
        ln = self.line
        below, above = ln.z - distance, ln.z + distance

        @pl.when((distance > 0) & (below >= 0))
        def _():
            self.up(s, below).wait_recv()

            @pl.when(ln.z < ln.chips - 1)
            def _():
                self.up(s, below).start()

            self.across(s, below).start()

        @pl.when((distance > 0) & (above < ln.chips))
        def _():
            self.down(s, above).wait_recv()

            @pl.when(ln.z > 0)
            def _():
                self.down(s, above).start()

            self.across(s, above).start()

    def drain(self, s, zb):
        ln = self.line

        @pl.when((zb <= ln.z) & (ln.z < ln.chips - 1))
        def _():
            self.up(s, zb).wait_send()

        @pl.when((zb >= ln.z) & (ln.z > 0))
        def _():
            self.down(s, zb).wait_send()

        self.across(s, zb).wait_send()


class ChainSum:
    def __init__(self, line, bufs, sems):
        self.line = line
        self.part, self.sib, self.rise, self.fall, self.out = bufs
        self.sent_sib, self.got_sib, self.got_up, self.got_down, self.sent = sems

    def across(self, s, zb):
        ln = self.line
        return ln.copy(
            self.part.at[s, zb, 1 - ln.c],
            self.sib.at[s, zb],
            self.sent_sib.at[s, zb],
            self.got_sib.at[s, zb],
            ln.sibling(),
        )

    def up(self, s, o):
        ln = self.line
        return ln.copy(
            self.out.at[s, o],
            self.rise.at[s, o],
            self.sent.at[s, o],
            self.got_up.at[s, o],
            ln.at(ln.z + 1),
        )

    def down(self, s, o):
        ln = self.line
        return ln.copy(
            self.out.at[s, o],
            self.fall.at[s, o],
            self.sent.at[s, o],
            self.got_down.at[s, o],
            ln.at(ln.z - 1),
        )

    def mine(self, s, o):
        return self.part[s, o, self.line.c].astype(F32) + self.sib[s, o].astype(F32)

    def hop_up(self, s, o):
        ln = self.line
        self.across(s, o).wait_recv()

        @pl.when(ln.z == 0)
        def _():
            self.out[s, o] = self.mine(s, o).astype(BF16)

        @pl.when(ln.z > 0)
        def _():
            self.up(s, o).wait_recv()
            self.out[s, o] = (self.mine(s, o) + self.rise[s, o].astype(F32)).astype(BF16)

        self.up(s, o).start()

    def hop_down(self, s, o):
        ln = self.line
        self.across(s, o).wait_recv()

        @pl.when(ln.z == ln.chips - 1)
        def _():
            self.out[s, o] = self.mine(s, o).astype(BF16)

        @pl.when(ln.z < ln.chips - 1)
        def _():
            self.down(s, o).wait_recv()
            self.out[s, o] = (self.mine(s, o) + self.fall[s, o].astype(F32)).astype(BF16)

        self.down(s, o).start()

    def hops(self, t, near_first):
        ln = self.line
        last = ln.chips - 1
        for upward in (True, False):
            place = ln.z if upward else last - ln.z
            q = t - place * LAG
            turn = jnp.maximum(q, 0) // ln.steps
            s = jnp.maximum(q, 0) % ln.steps
            far = turn if near_first else last - turn
            far = jnp.clip(far, 0, last)
            ok = (q >= 0) & (turn < ln.chips) & (far > place)
            o = far if upward else last - far

            @pl.when(ok)
            def _():
                if upward:
                    self.hop_up(s, o)
                else:
                    self.hop_down(s, o)

    def finish(self, s, total):
        ln = self.line
        self.across(s, ln.z).wait_recv()
        total[s] = self.mine(s, ln.z)

        @pl.when(ln.z > 0)
        def _():
            self.up(s, ln.z).wait_recv()
            total[s] += self.rise[s, ln.z].astype(F32)

        @pl.when(ln.z < ln.chips - 1)
        def _():
            self.down(s, ln.z).wait_recv()
            total[s] += self.fall[s, ln.z].astype(F32)

    def drain(self, s, zb):
        ln = self.line
        self.across(s, zb).wait_send()

        @pl.when(zb != ln.z)
        def _():
            self.up(s, zb).wait_send()


def drain_all(line, things):
    def body(i, carry):
        for thing in things:
            thing.drain(i // line.chips, i % line.chips)
        return carry

    lax.fori_loop(0, line.steps * line.chips, body, 0)


class Swap:
    def __init__(self, line, bufs, sems):
        self.line = line
        self.src, self.dst = bufs
        self.sent, self.got = sems

    def copy(self, k):
        ln = self.line
        to = (ln.f + k) % ln.frames
        return ln.copy(
            self.src.at[to], self.dst.at[ln.f], self.sent.at[k], self.got.at[k], (to, ln.h)
        )

    def run(self, value):
        ln = self.line
        shape = self.src.shape
        self.src[...] = value.astype(self.src.dtype).reshape(shape)
        for k in range(1, ln.frames):
            self.copy(k).start()
        self.dst[ln.f] = self.src[ln.f]
        for k in range(1, ln.frames):
            self.copy(k).wait()
        return self.dst[...].reshape(shape[0] * shape[1], shape[2]).astype(BF16)


class FrameSum:
    def __init__(self, line, part, full, dim, reverse, recv_bufs, sems):
        self.line, self.part, self.full, self.dim = line, part, full, dim
        self.recv_bufs = recv_bufs
        self.sent, self.got, self.sent_back, self.got_back = sems
        bits = range(line.frames.bit_length() - 1)
        self.bits = list(reversed(bits)) if reverse else list(bits)
        self.spans = []
        start, size = 0, part.shape[dim]
        for bit in self.bits:
            size //= 2
            side = (line.f // (1 << bit)) % 2
            peer = (line.f + (1 - 2 * side) * (1 << bit), line.h)
            keep, give = start + side * size, start + (1 - side) * size
            self.spans.append((keep, give, size, peer))
            start = keep

    def view(self, ref, start, size):
        if self.dim == 0:
            return ref.at[pl.ds(pl.multiple_of(start, size), size)]
        return ref.at[:, pl.ds(pl.multiple_of(start, size), size)]

    def out(self, i):
        _, give, size, peer = self.spans[i]
        src = self.view(self.part, give, size)
        return self.line.copy(src, self.recv_bufs[i], self.sent.at[i], self.got.at[i], peer)

    def back(self, i):
        keep, _, size, peer = self.spans[i]
        ref = self.view(self.full, keep, size)
        return self.line.copy(ref, ref, self.sent_back.at[i], self.got_back.at[i], peer)

    def back_in(self, i):
        _, give, size, peer = self.spans[i]
        ref = self.view(self.full, give, size)
        return self.line.copy(ref, ref, self.sent_back.at[i], self.got_back.at[i], peer)

    def stages(self):
        return 2 * len(self.bits) + 1

    def stage(self, k):
        n = len(self.bits)
        if 1 <= k <= n:
            keep, _, size, _ = self.spans[k - 1]
            self.out(k - 1).wait()
            ref = self.view(self.part, keep, size)
            to = self.view(self.full, keep, size) if k == n else ref
            to[...] = (ref[...].astype(F32) + self.recv_bufs[k - 1][...].astype(F32)).astype(BF16)
        elif k > n:
            i = 2 * n - k
            self.back(i).wait_send()
            self.back_in(i).wait_recv()
        if k < n:
            self.out(k).start()
        elif k < 2 * n:
            self.back(2 * n - 1 - k).start()


def frame_sum_scratch(frames, shape, dim):
    bits = frames.bit_length() - 1
    scratch = []
    for i in range(bits):
        part = list(shape)
        part[dim] = shape[dim] >> (i + 1)
        scratch.append(pltpu.VMEM(tuple(part), BF16))
    return [pltpu.VMEM(shape, BF16)] + scratch + [pltpu.SemaphoreType.DMA((bits,))] * 4


def frame_sums(line, arrays, scratch):
    bits = line.frames.bit_length() - 1
    sums = []
    for full, dim, reverse in arrays:
        part, *mine = scratch[: bits + 5]
        scratch = scratch[bits + 5 :]
        sums.append(FrameSum(line, part, full, dim, reverse, mine[:bits], mine[bits:]))
    return sums


class Everyone:
    def __init__(self, line, bufs, sems):
        self.line = line
        self.src, self.dst_sib, self.dst_line, self.dst_frames = bufs
        self.sent, self.got = sems

    def run(self, value, frames_value):
        ln = self.line
        self.src[0] = value.astype(BF16)
        copy = ln.copy(self.src.at[0], self.dst_sib, self.sent.at[0], self.got.at[0], ln.sibling())
        copy.start()
        copy.wait()
        pair = self.src[0].astype(F32) + self.dst_sib[...].astype(F32)
        self.src[1] = pair.astype(BF16)
        copies = []
        for k in range(1, ln.chips):
            to = (ln.z + k) % ln.chips
            copies.append(
                ln.copy(
                    self.src.at[1],
                    self.dst_line.at[ln.z],
                    self.sent.at[k],
                    self.got.at[k],
                    ln.at(to),
                )
            )
            copies[-1].start()
        self.dst_line[ln.z] = self.src[1]
        for copy in copies:
            copy.wait()
        total = self.dst_line[0].astype(F32)
        for i in range(1, ln.chips):
            total = total + self.dst_line[i].astype(F32)
        self.src[2] = (total + frames_value).astype(BF16)
        copies = []
        for k in range(1, ln.frames):
            to = (ln.f + k) % ln.frames
            slot = ln.chips + k
            copies.append(
                ln.copy(
                    self.src.at[2],
                    self.dst_frames.at[ln.f],
                    self.sent.at[slot],
                    self.got.at[slot],
                    (to, ln.h),
                )
            )
            copies[-1].start()
        self.dst_frames[ln.f] = self.src[2]
        for copy in copies:
            copy.wait()
        total = self.dst_frames[0].astype(F32)
        for i in range(1, ln.frames):
            total = total + self.dst_frames[i].astype(F32)
        return total


def everyone_scratch(chips, frames, rows, width):
    one = (rows, width)
    return [
        pltpu.VMEM((3,) + one, BF16),
        pltpu.VMEM(one, BF16),
        pltpu.VMEM((chips,) + one, BF16),
        pltpu.VMEM((frames,) + one, BF16),
        pltpu.SemaphoreType.DMA((chips + frames,)),
        pltpu.SemaphoreType.DMA((chips + frames,)),
    ]


def gathered_sum(line, gather, sums, own, compute, total, beside, least):
    steps, chips = line.steps, line.chips
    gather.start(own)
    parts = steps * chips

    def body(t, carry):
        distance, s = t // steps, t % steps

        @pl.when(t < parts)
        def _():
            gather.arrive(distance, s)

        def side(upward, inner):
            u = jnp.maximum(t - 1, 0)
            away = u // steps
            zb = jnp.where(upward == 1, line.z + away, line.z - away)
            ok = (t >= 1) & (t <= parts) & (zb >= 0) & (zb < chips)
            ok = ok & ((away > 0) | (upward == 0))

            @pl.when(ok)
            def _():
                where = jnp.clip(zb, 0, chips - 1)
                gather.wait_across(u % steps, where)
                compute(u % steps, where)
                sums.across(u % steps, where).start()

            return inner

        lax.fori_loop(0, 2, side, 0)
        sums.hops(t - LEAD, True)
        beside(t)
        return carry

    lax.fori_loop(0, max(parts + LEAD + (chips - 1) * LAG, least), body, 0)
    for s in range(steps):
        sums.finish(s, total)


def computed_sum(line, sums, compute, total, beside=None):
    steps, chips = line.steps, line.chips

    def body(t, carry):
        @pl.when(t < steps)
        def _():
            compute(t)
            for zb in range(chips):
                sums.across(t, zb).start()

        sums.hops(t - 1, False)
        if beside is not None:
            beside(t)
        return carry

    lax.fori_loop(0, steps * chips + 1 + (chips - 1) * LAG, body, 0)
    for s in range(steps):
        sums.finish(s, total)


def sem_shapes(steps, chips, gather, swap_frames):
    grid = pltpu.SemaphoreType.DMA((steps, chips))
    shapes = [grid] * 5
    if gather:
        shapes += [grid] * 5
    if swap_frames:
        shapes += [pltpu.SemaphoreType.DMA((swap_frames,))] * 2
    return shapes


def sum_bufs(steps, chips, rows, width, streams=1):
    tail = (rows * streams, width)
    one = pltpu.VMEM((steps, chips) + tail, BF16)
    return [pltpu.VMEM((steps, chips, 2) + tail, BF16), one, one, one, one]


def swap_bufs(frames, rows, width):
    kind = BF16 if rows % 16 == 0 else F32
    return [pltpu.VMEM((frames, rows, width), kind)] * 2


def call(kernel, name, collective_id, outs, scratch, args, smem=(), left=()):
    specs = [
        pl.BlockSpec(
            memory_space=pltpu.SMEM if i in smem else pl.ANY if i in left else pltpu.VMEM
        )
        for i in range(len(args))
    ]
    return pl.pallas_call(
        kernel,
        name=name,
        out_shape=[jax.ShapeDtypeStruct(shape, kind) for shape, kind in outs],
        in_specs=specs,
        out_specs=[pl.BlockSpec(memory_space=pltpu.VMEM)] * len(outs),
        scratch_shapes=scratch,
        compiler_params=pltpu.CompilerParams(
            collective_id=collective_id, has_side_effects=True, vmem_limit_bytes=VMEM_LIMIT
        ),
    )(*args)


def spatial_forward(
    ids, x, table, gain, shift, bias, wqkv, wout, to_peers, to_parts,
    normed_out, qkv_out, mixed_out, state_out, next_out,
    part, sib, rise, fall, out, src, dst, total, state0, *sems,
):
    line = Line(sems, x.shape[0])
    sums = ChainSum(line, (part, sib, rise, fall, out), sems[:5])
    swap = Swap(line, (src, dst), sems[5:7])
    line.barrier(True)
    steps, patches, width = x.shape
    rows = patches // line.heads
    entries = table.shape[0]
    table_row = lax.broadcasted_iota(jnp.int32, (entries, width), 0)

    def compute(s):
        picked = jnp.where(table_row == ids[s], table[...].astype(F32), 0.0)
        added = jnp.sum(picked, axis=0, keepdims=True)
        whole = x[s].astype(F32) + added
        own = x[s, pl.ds(pl.multiple_of(line.h * rows, rows), rows)].astype(F32) + added
        state0[s] = own
        normed = (norm_stats(whole)[0] * gain[0:1, :] + shift[0:1, :]).astype(BF16)
        normed_out[s] = normed
        q = mm(normed, wqkv[0]).astype(BF16)
        k = mm(normed, wqkv[1]).astype(BF16)
        v = mm(normed, wqkv[2]).astype(BF16)
        qkv_out[0, s] = q
        qkv_out[1, s] = k
        qkv_out[2, s] = v
        mixed = attend(q, k, v, None)
        mixed_out[s] = mixed
        part[s] = mm(mixed, wout[...]).astype(BF16).reshape(part.shape[1:])

    computed_sum(line, sums, compute, total)
    tokens = steps * rows
    state = state0[...].reshape(tokens, width) + total[...].reshape(tokens, width)
    state = state + bias[0:1, :]
    state_out[...] = state
    normed = (norm_stats(state)[0] * gain[1:2, :] + shift[1:2, :]).astype(BF16)
    got = swap.run(mm(to_peers[...], normed).astype(BF16))
    next_out[...] = mm(to_parts[...], got).astype(BF16).reshape(next_out.shape)
    drain_all(line, (sums,))


def frame_mask(segments, rows):
    frames = segments.shape[0]
    shift = frames.bit_length() - 1

    def ids_along(axis, shape):
        index = lax.broadcasted_iota(jnp.int32, shape, axis)
        frame = index & (frames - 1)
        segment = jnp.zeros(shape, jnp.int32)
        for i in range(frames):
            segment = jnp.where(frame == i, segments[i], segment)
        return lax.shift_right_logical(index, shift), frame, segment

    place_q, frame_q, segment_q = ids_along(0, (rows, 1))
    place_k, frame_k, segment_k = ids_along(1, (1, rows))
    return (place_q == place_k) & (frame_k <= frame_q) & (segment_q == segment_k)


def temporal_forward(
    segments, own, wqkv, wout, gain, shift, bias, state1, from_parts, from_peers,
    normed_out, qkv_out, mixed_out, state_out, next_out,
    part, sib, rise, fall, out, src, dst, total, mask_ref, *sems,
):
    steps, chips, _, rows, width = normed_out.shape
    line = Line(sems, steps)
    sums = ChainSum(line, (part, sib, rise, fall, out), sems[:5])
    gather = Gather(line, normed_out, sems[5:10])
    swap = Swap(line, (src, dst), sems[10:12])
    line.barrier(True)
    mask_ref[...] = frame_mask(segments, 2 * rows).astype(F32)

    def compute(s, zb):
        a = normed_out[s, zb].reshape(2 * rows, width)
        q = mm(a, wqkv[0]).astype(BF16)
        k = mm(a, wqkv[1]).astype(BF16)
        v = mm(a, wqkv[2]).astype(BF16)
        qkv_out[0, s, zb] = q
        qkv_out[1, s, zb] = k
        qkv_out[2, s, zb] = v
        mixed = attend(q, k, v, mask_ref[...] > 0.0)
        mixed_out[s, zb] = mixed
        part[s, zb] = mm(mixed, wout[...]).astype(BF16).reshape(2, rows, width)

    gathered_sum(line, gather, sums, own, compute, total, lambda t: None, 0)
    tokens = steps * rows
    summed = total[...].reshape(tokens, width).astype(BF16)
    got = swap.run(mm(from_parts[...], summed).astype(BF16))
    state = state1[...] + mm(from_peers[...], got) + bias[1:2, :]
    state_out[...] = state
    normed = norm_stats(state)[0] * gain[2:3, :] + shift[2:3, :]
    next_out[...] = normed.astype(BF16).reshape(next_out.shape)
    drain_all(line, (gather, sums))


def mlp(
    own, up, up_bias, down, cotangent, gain, bias, state2, to_peers, to_parts,
    down_grad, up_grad, result_out, grad_out, next_out, small_out, bias_out,
    normed_out, act_out, dpre_out, part, sib, rise, fall, out, src, dst, total, *sems,
):
    steps, chips, _, rows, width = normed_out.shape
    line = Line(sems, steps)
    sums = ChainSum(line, (part, sib, rise, fall, out), sems[:5])
    gather = Gather(line, normed_out, sems[5:10])
    swap = Swap(line, (src, dst), sems[10:12])
    line.barrier(True)
    bias_out[...] = jnp.zeros_like(bias_out)

    def compute(s, zb):
        a = normed_out[s, zb].reshape(2 * rows, width)
        g = cotangent[s, pl.ds(pl.multiple_of(zb * 2 * rows, 2 * rows), 2 * rows)]
        pre = mm(a, up[...]) + up_bias[...]
        t = jnp.tanh(GELU_C * (pre + 0.044715 * (pre * pre * pre)))
        act = (0.5 * pre * (1.0 + t)).astype(BF16)
        act_out[s, zb] = act
        slope = 0.5 * (1.0 + t)
        slope = slope + 0.5 * pre * (1.0 - t * t) * (GELU_C * (1.0 + 0.134145 * (pre * pre)))
        dpre = (mm_nt(g, down[...]) * slope).astype(BF16)
        dpre_out[s, zb] = dpre
        bias_out[...] += jnp.sum(dpre.astype(F32), axis=0, keepdims=True)
        part[s, zb, :, pl.ds(0, rows)] = mm_nt(dpre, up[...]).astype(BF16).reshape(2, rows, width)
        part[s, zb, :, pl.ds(rows, rows)] = mm(act, down[...]).astype(BF16).reshape(2, rows, width)

    hidden = up.shape[1]
    all_tokens = steps * chips * 2 * rows
    n_down, n_up = hidden // 128, width // 256
    first = steps * chips + 1

    def beside(t):
        @pl.when((t >= first) & (t < first + n_down))
        def _():
            cols = pl.ds(pl.multiple_of((t - first) * 128, 128), 128)
            left = act_out[:, :, :, cols].reshape(all_tokens, 128)
            right = cotangent[...].reshape(all_tokens, width)
            down_grad[cols] = mm_tn(left, right).astype(BF16)

        @pl.when((t >= first + n_down) & (t < first + n_down + n_up))
        def _():
            cols = pl.ds(pl.multiple_of((t - first - n_down) * 256, 256), 256)
            left = normed_out[:, :, :, :, cols].reshape(all_tokens, 256)
            right = dpre_out[...].reshape(all_tokens, hidden)
            up_grad[cols] = mm_tn(left, right).astype(BF16)

    gathered_sum(
        line, gather, sums, own, compute, total, beside, first + n_down + n_up
    )
    tokens = steps * rows
    start = pl.multiple_of(line.h * rows, rows)
    state = state2[...]
    grad = cotangent[:, pl.ds(start, rows)].astype(F32).reshape(tokens, width)
    back, gain_grad, shift_grad = norm_back(
        state, total[:, pl.ds(0, rows)].reshape(tokens, width), gain[2:3, :]
    )
    dh = grad + back
    grad_out[...] = dh
    got = swap.run(mm(to_peers[...], dh.astype(BF16)).astype(BF16))
    next_out[...] = mm(to_parts[...], got).astype(BF16).reshape(next_out.shape)
    result = state + total[:, pl.ds(rows, rows)].reshape(tokens, width) + bias[2:3, :]
    result_out[...] = result.astype(BF16).reshape(result_out.shape)
    small_out[...] = jnp.concatenate(
        [
            gain_grad,
            shift_grad,
            jnp.sum(grad, axis=0, keepdims=True),
            jnp.sum(dh, axis=0, keepdims=True),
            jnp.zeros((4, width), F32),
        ],
        axis=0,
    )
    drain_all(line, (gather, sums))


def temporal_backward(
    segments, own, qkv, wqkv, wout, gain, state1, grad2, from_parts, from_peers,
    normed, mixed, down_part, up_part,
    qk_grad, v_grad, out_grad, down_grad, up_grad, grad_out, next_out, small_out,
    grad_gathered, dqkv_out, load_sems,
    part, sib, rise, fall, out, src, dst, total, mask_ref, *sems,
):
    steps, chips, _, rows, width = grad_gathered.shape
    line = Line(sems, steps)
    reduced = frame_sums(line, [(down_grad, 0, False), (up_grad, 0, True)], sems[12:])
    loads = [
        pltpu.make_async_copy(down_part, reduced[0].part, load_sems.at[0]),
        pltpu.make_async_copy(up_part, reduced[1].part, load_sems.at[1]),
    ]
    for load in loads:
        load.start()
    sums = ChainSum(line, (part, sib, rise, fall, out), sems[:5])
    gather = Gather(line, grad_gathered, sems[5:10])
    swap = Swap(line, (src, dst), sems[10:12])
    line.barrier(True)
    mask_ref[...] = frame_mask(segments, 2 * rows).astype(F32)

    def compute(s, zb):
        r = grad_gathered[s, zb].reshape(2 * rows, width)
        dm = mm_nt(r, wout[...]).astype(BF16)
        mask = mask_ref[...] > 0.0
        dq, dk, dv = attend_back(qkv[0, s, zb], qkv[1, s, zb], qkv[2, s, zb], mask, dm)
        dqkv_out[0, s, zb] = dq
        dqkv_out[1, s, zb] = dk
        dqkv_out[2, s, zb] = dv
        da = mm_nt(dq, wqkv[0]) + mm_nt(dk, wqkv[1]) + mm_nt(dv, wqkv[2])
        part[s, zb] = da.astype(BF16).reshape(2, rows, width)

    columns = wout.shape[0]
    all_tokens = steps * chips * 2 * rows
    first = steps * chips + 1
    n_cols = width // 256
    n_stages = reduced[0].stages()

    def beside(t):
        for k in range(n_stages - 1):

            @pl.when(t == (1, 9, 13, 17)[min(k, 3)] + 4 * max(k - 3, 0))
            def _():
                if k == 0:
                    for load in loads:
                        load.wait()
                for one in reduced:
                    one.stage(k)

        @pl.when(t == first)
        def _():
            left = mixed[...].reshape(all_tokens, columns)
            right = grad_gathered[...].reshape(all_tokens, width)
            out_grad[...] = mm_tn(left, right).astype(BF16)

        @pl.when((t > first) & (t <= first + n_cols))
        def _():
            qkv_grads(
                (t - first - 1) * 256, normed, dqkv_out, qk_grad, v_grad, all_tokens, columns
            )

    gathered_sum(line, gather, sums, own, compute, total, beside, first + n_cols + 1)
    tokens = steps * rows
    summed = total[...].reshape(tokens, width).astype(BF16)
    got = swap.run(mm(from_parts[...], summed).astype(BF16))
    back, gain_grad, shift_grad = norm_back(state1[...], mm(from_peers[...], got), gain[1:2, :])
    dh = grad2[...] + back
    grad_out[...] = dh
    next_out[...] = dh.astype(BF16).reshape(next_out.shape)
    small_out[...] = jnp.concatenate(
        [
            gain_grad,
            shift_grad,
            jnp.sum(dh, axis=0, keepdims=True),
            jnp.zeros((5, width), F32),
        ],
        axis=0,
    )
    for one in reduced:
        one.stage(n_stages - 1)
    drain_all(line, (gather, sums))


def qkv_grads(start, normed, dqkv, qk_grad, v_grad, all_tokens, columns):
    width = normed.shape[-1]
    cols = pl.ds(pl.multiple_of(start, 256), 256)
    lead = (slice(None),) * (len(normed.shape) - 1)
    left = normed[lead + (cols,)].reshape(all_tokens, 256)
    for i in range(3):
        grad = mm_tn(left, dqkv[i].reshape(all_tokens, columns)).astype(BF16)
        if i < 2:
            qk_grad[pl.ds(pl.multiple_of(i * width + start, 256), 256)] = grad
        else:
            v_grad[cols] = grad


def spatial_backward(
    ids, own, qkv, wqkv, wout, gain, x, table, grad1,
    normed, mixed, small2, small3, up_bias_part, t_qk_part, t_v_part, t_out_part,
    t_qk_grad, t_v_grad, t_out_grad, qk_grad, v_grad, out_grad, result_out, small_out,
    grad_gathered, dqkv_out, load_sems, every_src, every_sib, every_line, every_frames, every_sent,
    every_got,
    part, sib, rise, fall, out, total, dmixed, *sems,
):
    steps, chips, _, rows, width = grad_gathered.shape
    line = Line(sems, steps)
    reduced = frame_sums(
        line,
        [
            (t_qk_grad, 0, False), (t_v_grad, 0, True), (t_out_grad, 1, True),
            (qk_grad, 0, False), (v_grad, 0, True), (out_grad, 1, True),
        ],
        sems[10:],
    )
    earlier, later = reduced[:3], reduced[3:]
    loads = [
        pltpu.make_async_copy(t_qk_part, earlier[0].part, load_sems.at[0]),
        pltpu.make_async_copy(t_v_part, earlier[1].part, load_sems.at[1]),
        pltpu.make_async_copy(t_out_part, earlier[2].part, load_sems.at[2]),
    ]
    for load in loads:
        load.start()
    n_stages = earlier[0].stages()
    every = Everyone(line, (every_src, every_sib, every_line, every_frames), (every_sent, every_got))
    sums = ChainSum(line, (part, sib, rise, fall, out), sems[:5])
    gather = Gather(line, grad_gathered, sems[5:10])
    line.barrier(True, True)
    entries = table.shape[0]
    table_row = lax.broadcasted_iota(jnp.int32, (entries, width), 0)
    gather.start(own)
    parts = steps * chips

    def body(t, carry):
        @pl.when(t < parts)
        def _():
            gather.arrive(t // steps, t % steps)

        def side(upward, inner):
            u = jnp.maximum(t - 1, 0)
            away, s = u // steps, u % steps
            zb = jnp.where(upward == 1, line.z + away, line.z - away)
            ok = (t >= 1) & (zb >= 0) & (zb < chips) & ((away > 0) | (upward == 0))

            @pl.when(ok)
            def _():
                where = jnp.clip(zb, 0, chips - 1)
                gather.wait_across(s, where)
                r = grad_gathered[s, where].reshape(2 * rows, width)
                start = pl.multiple_of(where * 2 * rows, 2 * rows)
                dmixed[s, pl.ds(start, 2 * rows)] = mm_nt(r, wout[...]).astype(BF16)

            return inner

        lax.fori_loop(0, 2, side, 0)
        for k in range(n_stages):

            @pl.when(t == (1, 6, 9, 12, 16)[min(k, 4)] + 2 * max(k - 4, 0))
            def _():
                if k == 0:
                    for load in loads:
                        load.wait()
                for one in earlier:
                    one.stage(k)

        return carry

    lax.fori_loop(0, max(parts + 1, 17 + 2 * max(n_stages - 5, 0)), body, 0)
    columns = wout.shape[0]
    all_tokens = steps * chips * 2 * rows

    def compute(s):
        dq, dk, dv = attend_back(qkv[0, s], qkv[1, s], qkv[2, s], None, dmixed[s])
        dqkv_out[0, s] = dq
        dqkv_out[1, s] = dk
        dqkv_out[2, s] = dv
        da = mm_nt(dq, wqkv[0]) + mm_nt(dk, wqkv[1]) + mm_nt(dv, wqkv[2])
        part[s] = da.astype(BF16).reshape(part.shape[1:])

    def beside(t):
        @pl.when(t == steps)
        def _():
            left = mixed[...].reshape(all_tokens, columns)
            right = grad_gathered[...].reshape(all_tokens, width)
            later[2].part[...] = mm_tn(left, right).astype(BF16)

        @pl.when((t >= steps) & (t < steps + 2))
        def _():
            for i in range(width // 512):
                start = ((t - steps) * (width // 512) + i) * 256
                qkv_grads(
                    start, normed, dqkv_out, later[0].part, later[1].part, all_tokens, columns
                )

        for k in range(n_stages - 1):

            @pl.when(t == (steps + 1, steps + 5, steps + 7, steps + 9)[min(k, 3)] + 2 * max(k - 3, 0))
            def _():
                for one in later:
                    one.stage(k)

    computed_sum(line, sums, compute, total, beside)
    gain_grad = jnp.zeros((1, width), F32)
    shift_grad = jnp.zeros((1, width), F32)
    table_grad = jnp.zeros((entries, width), F32)
    for s in range(steps):
        picked = jnp.where(table_row == ids[s], table[...].astype(F32), 0.0)
        added = jnp.sum(picked, axis=0, keepdims=True)
        state = x[s, pl.ds(pl.multiple_of(line.h * rows, rows), rows)].astype(F32) + added
        back, one_gain, one_shift = norm_back(state, total[s], gain[0:1, :])
        grad = grad1[pl.ds(s * rows, rows)] + back
        result_out[s] = grad
        gain_grad += one_gain
        shift_grad += one_shift
        here = jnp.sum(grad, axis=0, keepdims=True)
        table_grad += jnp.where(table_row == ids[s], here, 0.0)
    rows_of = [
        gain_grad, small2[0:1], small3[0:1],
        shift_grad, small2[1:2], small3[1:2],
        small2[2:3], small3[3:4], small3[2:3],
        table_grad,
    ]
    filled = 9 + entries
    room = every_src.shape[1]
    value = jnp.concatenate(rows_of + [jnp.zeros((room - filled, width), F32)], axis=0)
    row = lax.broadcasted_iota(jnp.int32, (room, width), 0)
    frames_value = jnp.where(row == filled, up_bias_part[...], 0.0)
    small_out[...] = every.run(value, frames_value)
    for one in later:
        one.stage(n_stages - 1)
    drain_all(line, (gather, sums))


def orders(frames_local, frames, places, t_steps):
    tokens = frames_local * frames * places
    index = np.arange(tokens).reshape(frames_local, frames, places)
    first = index.transpose(1, 0, 2).reshape(-1)
    index = np.arange(tokens).reshape(frames * frames_local, t_steps, places // t_steps)
    second = index.transpose(1, 2, 0).reshape(-1)
    eye = np.eye(tokens, dtype=np.float32)
    to_peers, to_parts = eye[first], eye[second]
    return [jnp.asarray(m, BF16) for m in (to_peers, to_parts, to_parts.T, to_peers.T)]


def on_device(
    block_input,
    action_ids,
    segment_ids,
    action_table,
    norm_gain,
    norm_shift,
    spatial_qkv,
    spatial_out,
    temporal_qkv,
    temporal_out,
    out_bias,
    up_weight,
    up_bias,
    down_weight,
    cotangent,
):
    frames, heads = lax.axis_size("frames"), lax.axis_size("heads")
    chips = heads // 2
    steps, patches, width = block_input.shape
    rows = patches // heads
    tokens = steps * rows
    total_frames = segment_ids.shape[0]
    places = rows // frames
    t_steps = min(4, places)
    t_rows = tokens // t_steps
    columns = spatial_out.shape[0]
    hidden = up_weight.shape[1]
    s_qkv = spatial_qkv.transpose(1, 0, 2)
    t_qkv = temporal_qkv.transpose(1, 0, 2)
    to_peers, to_parts, from_parts, from_peers = orders(steps, frames, places, t_steps)
    swap = swap_bufs(frames, tokens // frames, width)
    owned = ((tokens, width), F32)
    s_blocks = (steps, rows, width)
    t_blocks = (t_steps, t_rows, width)
    t_mask = pltpu.VMEM((2 * t_rows, 2 * t_rows), F32)
    rest = 8, width

    normed1, s_proj, s_mixed, state1, own2 = call(
        spatial_forward,
        "spatial_forward",
        0,
        [
            ((steps, patches, width), BF16),
            ((3, steps, patches, columns), BF16),
            ((steps, patches, columns), BF16),
            owned,
            (t_blocks, BF16),
        ],
        sum_bufs(steps, chips, rows, width)
        + swap
        + [pltpu.VMEM(s_blocks, F32), pltpu.VMEM(s_blocks, F32)]
        + sem_shapes(steps, chips, False, frames),
        (
            action_ids, block_input, action_table, norm_gain, norm_shift, out_bias,
            s_qkv, spatial_out, to_peers, to_parts,
        ),
        smem=(0,),
    )
    t_all = (t_steps, chips, 2, t_rows, width)
    t_cols = (t_steps, chips, 2 * t_rows, columns)
    normed2, t_proj, t_mixed, state2, own3 = call(
        temporal_forward,
        "temporal_forward",
        1,
        [
            (t_all, BF16),
            ((3,) + t_cols, BF16),
            (t_cols, BF16),
            owned,
            (s_blocks, BF16),
        ],
        sum_bufs(t_steps, chips, t_rows, width)
        + swap
        + [pltpu.VMEM(t_blocks, F32), t_mask]
        + sem_shapes(t_steps, chips, True, frames),
        (
            segment_ids, own2, t_qkv, temporal_out, norm_gain, norm_shift, out_bias,
            state1, from_parts, from_peers,
        ),
        smem=(0,),
    )
    s_all = (steps, chips, 2, rows, width)
    f_cols = (steps, chips, 2 * rows, hidden)
    grads_mlp = [((hidden, width), BF16), ((width, hidden), BF16)]
    down_part, up_part, block_output, grad2, own4, small3, up_bias_part = call(
        mlp,
        "mlp",
        2,
        grads_mlp
        + [
            (s_blocks, BF16),
            owned,
            (t_blocks, BF16),
            (rest, F32),
            ((1, hidden), F32),
        ],
        [pltpu.VMEM(s_all, BF16), pltpu.VMEM(f_cols, BF16), pltpu.VMEM(f_cols, BF16)]
        + sum_bufs(steps, chips, rows, width, 2)
        + swap
        + [pltpu.VMEM((steps, 2 * rows, width), F32)]
        + sem_shapes(steps, chips, True, frames),
        (
            own3, up_weight, up_bias.reshape(1, hidden), down_weight, cotangent, norm_gain,
            out_bias, state2, to_peers, to_parts,
        ),
    )
    grads_attention = [
        ((2 * width, columns), BF16),
        ((width, columns), BF16),
        ((columns, width), BF16),
    ]
    dims_attention = (0, 0, 1)
    t_qk_part, t_v_part, t_out_part, g_down, g_up, grad1, own5, small2 = call(
        temporal_backward,
        "temporal_backward",
        3,
        grads_attention + grads_mlp + [owned, (s_blocks, BF16), (rest, F32)],
        [
            pltpu.VMEM(t_all, BF16),
            pltpu.VMEM((3,) + t_cols, BF16),
            pltpu.SemaphoreType.DMA((2,)),
        ]
        + sum_bufs(t_steps, chips, t_rows, width)
        + swap
        + [pltpu.VMEM(t_blocks, F32), t_mask]
        + sem_shapes(t_steps, chips, True, frames)
        + [x for shape, _ in grads_mlp for x in frame_sum_scratch(frames, shape, 0)],
        (
            segment_ids, own4, t_proj, t_qkv, temporal_out, norm_gain, state1, grad2,
            from_parts, from_peers, normed2, t_mixed, down_part, up_part,
        ),
        smem=(0,),
        left=(12, 13),
    )
    room = -(-(10 + action_table.shape[0]) // 16) * 16
    up_bias_row = jnp.pad(up_bias_part, ((0, 0), (0, width - hidden)))
    g_t_qk, g_t_v, g_t_out, g_s_qk, g_s_v, g_s_out, input_grad, small = call(
        spatial_backward,
        "spatial_backward",
        4,
        grads_attention * 2 + [(s_blocks, F32), ((room, width), F32)],
        [
            pltpu.VMEM(s_all, BF16),
            pltpu.VMEM((3, steps, patches, columns), BF16),
            pltpu.SemaphoreType.DMA((3,)),
        ]
        + everyone_scratch(chips, frames, room, width)
        + sum_bufs(steps, chips, rows, width)
        + [pltpu.VMEM(s_blocks, F32), pltpu.VMEM((steps, patches, columns), BF16)]
        + sem_shapes(steps, chips, True, 0)
        + [
            x
            for (shape, _), dim in zip(grads_attention * 2, dims_attention * 2)
            for x in frame_sum_scratch(frames, shape, dim)
        ],
        (
            action_ids, own5, s_proj, s_qkv, spatial_out, norm_gain, block_input, action_table,
            grad1, normed1, s_mixed, small2, small3, up_bias_row, t_qk_part, t_v_part, t_out_part,
        ),
        smem=(0,),
        left=(14, 15, 16),
    )

    def qkv_of(qk, v):
        whole = jnp.concatenate([qk, v], axis=0).reshape(3, width, columns)
        return whole.transpose(1, 0, 2).astype(F32)

    filled = 9 + action_table.shape[0]
    return (
        block_output,
        input_grad,
        small[9:filled],
        small[0:3],
        small[3:6],
        qkv_of(g_s_qk, g_s_v),
        g_s_out.astype(F32),
        qkv_of(g_t_qk, g_t_v),
        g_t_out.astype(F32),
        small[6:9],
        g_up.astype(F32),
        small[filled, :hidden],
        g_down.astype(F32),
    )


def solution(mesh):
    return jax.shard_map(
        on_device,
        mesh=mesh,
        in_specs=(
            P("frames", None, None),
            P("frames"),
            P(),
            P(),
            P(),
            P(),
            P(None, None, "heads"),
            P("heads", None),
            P(None, None, "heads"),
            P("heads", None),
            P(),
            P(None, "heads"),
            P("heads"),
            P("heads", None),
            P("frames", None, None),
        ),
        out_specs=(
            P("frames", "heads", None),
            P("frames", "heads", None),
            P(),
            P(),
            P(),
            P(None, None, "heads"),
            P("heads", None),
            P(None, None, "heads"),
            P("heads", None),
            P(),
            P(None, "heads"),
            P("heads"),
            P("heads", None),
        ),
        check_vma=False,
    )
```

```python
import jax
import jax.numpy as jnp
import numpy as np
from jax import lax
from jax.experimental import pallas as pl
from jax.experimental.pallas import tpu as pltpu
from jax.sharding import PartitionSpec as P

HD = 64
SCALE = HD**-0.5
EPS = 1e-05
MASKED = -1000000000.0
F32 = jnp.float32
BF16 = jnp.bfloat16
MESH = pl.DeviceIdType.MESH
VMEM_LIMIT = 56 * 1024 * 1024
GELU_C = float(np.sqrt(2.0 / np.pi))
LAG = 2
LEAD = 3


def mm(a, b):
    return lax.dot_general(a, b, (((1,), (0,)), ((), ())), preferred_element_type=F32)


def mm_nt(a, b):
    return lax.dot_general(a, b, (((1,), (1,)), ((), ())), preferred_element_type=F32)


def mm_tn(a, b):
    return lax.dot_general(a, b, (((0,), (0,)), ((), ())), preferred_element_type=F32)


def norm_stats(value):
    centered = value - jnp.mean(value, axis=-1, keepdims=True)
    inv = lax.rsqrt(jnp.mean(centered * centered, axis=-1, keepdims=True) + EPS)
    return centered * inv, inv


def norm_back(value, grad, gain):
    normed, inv = norm_stats(value)
    e = grad * gain
    first = jnp.mean(e, axis=-1, keepdims=True)
    second = jnp.mean(e * normed, axis=-1, keepdims=True)
    gain_grad = jnp.sum(grad * normed, axis=0, keepdims=True)
    shift_grad = jnp.sum(grad, axis=0, keepdims=True)
    return (e - first - normed * second) * inv, gain_grad, shift_grad


def head_lanes(shape, head):
    lane = lax.broadcasted_iota(jnp.int32, shape, 1)
    return (lane >= head * HD) & (lane < (head + 1) * HD)


def softmax_of(q, k, mask):
    scores = mm_nt(q, k) * SCALE
    if mask is not None:
        scores = jnp.where(mask, scores, MASKED)
    raised = jnp.exp(scores - jnp.max(scores, axis=-1, keepdims=True))
    return raised / jnp.sum(raised, axis=-1, keepdims=True)


def attend(q, k, v, mask):
    heads = q.shape[1] // HD
    mixed = None
    for head in range(heads):
        lanes = head_lanes(q.shape, head)
        probs = softmax_of(jnp.where(lanes, q, jnp.zeros_like(q)), k, mask).astype(BF16)
        out = mm(probs, v)
        mixed = out if mixed is None else jnp.where(lanes, out, mixed)
    return mixed.astype(BF16)


def attend_back(q, k, v, mask, grad):
    heads = q.shape[1] // HD
    dq = dk = dv = None
    for head in range(heads):
        lanes = head_lanes(q.shape, head)
        qh = jnp.where(lanes, q, jnp.zeros_like(q))
        gh = jnp.where(lanes, grad, jnp.zeros_like(grad))
        probs = softmax_of(qh, k, mask)
        dvh = mm_tn(probs.astype(BF16), gh)
        dp = mm_nt(gh, v)
        ds = (probs * (dp - jnp.sum(dp * probs, axis=-1, keepdims=True))).astype(BF16)
        dqh = mm(ds, k) * SCALE
        dkh = mm_tn(ds, qh) * SCALE
        if head == 0:
            dq, dk, dv = dqh, dkh, dvh
        else:
            dq = jnp.where(lanes, dqh, dq)
            dk = dk + dkh
            dv = dv + dvh
    return dq.astype(BF16), dk.astype(BF16), dv.astype(BF16)


class Line:
    def __init__(self, steps):
        self.frames = lax.axis_size("frames")
        self.heads = lax.axis_size("heads")
        self.chips = self.heads // 2
        self.f = lax.axis_index("frames")
        self.h = lax.axis_index("heads")
        self.z = self.h // 2
        self.c = self.h % 2
        self.steps = steps

    def at(self, z):
        return (self.f, jnp.clip(z, 0, self.chips - 1) * 2 + self.c)

    def sibling(self):
        return (self.f, self.z * 2 + 1 - self.c)

    def barrier(self, over_frames, whole_line=False):
        sem = pltpu.get_barrier_semaphore()

        def greet(device):
            pl.semaphore_signal(sem, inc=1, device_id=device, device_id_type=MESH)

        greet(self.sibling())
        count = 1
        if over_frames:
            for k in range(1, self.frames):
                greet(((self.f + k) % self.frames, self.h))
            count += self.frames - 1
        if whole_line:
            for k in range(1, self.chips):
                greet(self.at((self.z + k) % self.chips))
            count += self.chips - 1
        else:

            @pl.when(self.z > 0)
            def _():
                greet(self.at(self.z - 1))

            @pl.when(self.z < self.chips - 1)
            def _():
                greet(self.at(self.z + 1))

            count = count + (self.z > 0).astype(jnp.int32)
            count = count + (self.z < self.chips - 1).astype(jnp.int32)
        pl.semaphore_wait(sem, count)

    def copy(self, src, dst, send, recv, device):
        return pltpu.make_async_remote_copy(
            src_ref=src,
            dst_ref=dst,
            send_sem=send,
            recv_sem=recv,
            device_id=device,
            device_id_type=MESH,
        )


class Gather:
    def __init__(self, line, buf, sems):
        self.line, self.buf = line, buf
        self.got, self.got_sib, self.sent_up, self.sent_down, self.sent_sib = sems

    def up(self, s, zb):
        ln = self.line
        ref = self.buf.at[s, zb, ln.c]
        return ln.copy(ref, ref, self.sent_up.at[s, zb], self.got.at[s, zb], ln.at(ln.z + 1))

    def down(self, s, zb):
        ln = self.line
        ref = self.buf.at[s, zb, ln.c]
        return ln.copy(ref, ref, self.sent_down.at[s, zb], self.got.at[s, zb], ln.at(ln.z - 1))

    def across(self, s, zb):
        ln = self.line
        ref = self.buf.at[s, zb, ln.c]
        return ln.copy(ref, ref, self.sent_sib.at[s, zb], self.got_sib.at[s, zb], ln.sibling())

    def wait_across(self, s, zb):
        ln = self.line
        ref = self.buf.at[s, zb, 1 - ln.c]
        ln.copy(
            ref, ref, self.sent_sib.at[s, zb], self.got_sib.at[s, zb], ln.sibling()
        ).wait_recv()

    def send(self, s):
        ln = self.line

        @pl.when(ln.z < ln.chips - 1)
        def _():
            self.up(s, ln.z).start()

        @pl.when(ln.z > 0)
        def _():
            self.down(s, ln.z).start()

        self.across(s, ln.z).start()

    def start(self, own):
        ln = self.line
        for s in range(ln.steps):
            self.buf[s, ln.z, ln.c] = own[s]
            self.send(s)

    def arrive(self, distance, s):
        ln = self.line
        below, above = ln.z - distance, ln.z + distance

        @pl.when((distance > 0) & (below >= 0))
        def _():
            self.up(s, below).wait_recv()

            @pl.when(ln.z < ln.chips - 1)
            def _():
                self.up(s, below).start()

            self.across(s, below).start()

        @pl.when((distance > 0) & (above < ln.chips))
        def _():
            self.down(s, above).wait_recv()

            @pl.when(ln.z > 0)
            def _():
                self.down(s, above).start()

            self.across(s, above).start()

    def drain(self, s, zb):
        ln = self.line

        @pl.when((zb <= ln.z) & (ln.z < ln.chips - 1))
        def _():
            self.up(s, zb).wait_send()

        @pl.when((zb >= ln.z) & (ln.z > 0))
        def _():
            self.down(s, zb).wait_send()

        self.across(s, zb).wait_send()


class ChainSum:
    def __init__(self, line, bufs, sems):
        self.line = line
        self.part, self.sib, self.rise, self.fall, self.out = bufs
        self.sent_sib, self.got_sib, self.got_up, self.got_down, self.sent = sems

    def across(self, s, zb):
        ln = self.line
        return ln.copy(
            self.part.at[s, zb, 1 - ln.c],
            self.sib.at[s, zb],
            self.sent_sib.at[s, zb],
            self.got_sib.at[s, zb],
            ln.sibling(),
        )

    def up(self, s, o):
        ln = self.line
        return ln.copy(
            self.out.at[s, o],
            self.rise.at[s, o],
            self.sent.at[s, o],
            self.got_up.at[s, o],
            ln.at(ln.z + 1),
        )

    def down(self, s, o):
        ln = self.line
        return ln.copy(
            self.out.at[s, o],
            self.fall.at[s, o],
            self.sent.at[s, o],
            self.got_down.at[s, o],
            ln.at(ln.z - 1),
        )

    def mine(self, s, o):
        return self.part[s, o, self.line.c].astype(F32) + self.sib[s, o].astype(F32)

    def hop_up(self, s, o):
        ln = self.line
        self.across(s, o).wait_recv()

        @pl.when(ln.z == 0)
        def _():
            self.out[s, o] = self.mine(s, o).astype(BF16)

        @pl.when(ln.z > 0)
        def _():
            self.up(s, o).wait_recv()
            self.out[s, o] = (self.mine(s, o) + self.rise[s, o].astype(F32)).astype(BF16)

        self.up(s, o).start()

    def hop_down(self, s, o):
        ln = self.line
        self.across(s, o).wait_recv()

        @pl.when(ln.z == ln.chips - 1)
        def _():
            self.out[s, o] = self.mine(s, o).astype(BF16)

        @pl.when(ln.z < ln.chips - 1)
        def _():
            self.down(s, o).wait_recv()
            self.out[s, o] = (self.mine(s, o) + self.fall[s, o].astype(F32)).astype(BF16)

        self.down(s, o).start()

    def hops(self, t, part=None, fits=True):
        ln = self.line
        last = ln.chips - 1
        for upward in (True, False):
            place = ln.z if upward else last - ln.z
            q = t - place * LAG
            if part is None:
                turn = jnp.maximum(q, 0) // ln.steps
                s = jnp.maximum(q, 0) % ln.steps
            else:
                turn, s = jnp.maximum(q, 0), part
            far = jnp.clip(last - turn, 0, last)
            ok = (q >= 0) & (turn < last) & (far > place) & fits
            o = far if upward else last - far

            @pl.when(ok)
            def _():
                if upward:
                    self.hop_up(s, o)
                else:
                    self.hop_down(s, o)

    def finish(self, s, total):
        ln = self.line
        self.across(s, ln.z).wait_recv()
        total[...] = self.mine(s, ln.z)

        @pl.when(ln.z > 0)
        def _():
            self.up(s, ln.z).wait_recv()
            total[...] += self.rise[s, ln.z].astype(F32)

        @pl.when(ln.z < ln.chips - 1)
        def _():
            self.down(s, ln.z).wait_recv()
            total[...] += self.fall[s, ln.z].astype(F32)

    def drain(self, s, zb):
        ln = self.line
        self.across(s, zb).wait_send()

        @pl.when(zb != ln.z)
        def _():
            self.up(s, zb).wait_send()


def drain_all(line, things, parts):
    def body(i, carry):
        for thing in things:
            thing.drain(i // line.chips, i % line.chips)
        return carry

    lax.fori_loop(0, parts * line.chips, body, 0)


class Swap:
    def __init__(self, line, bufs, sems):
        self.line = line
        self.src, self.dst = bufs
        self.sent, self.got = sems

    def copy(self, k):
        ln = self.line
        to = (ln.f + k) % ln.frames
        return ln.copy(
            self.src.at[to], self.dst.at[ln.f], self.sent.at[k], self.got.at[k], (to, ln.h)
        )

    def start(self):
        ln = self.line
        for k in range(1, ln.frames):
            self.copy(k).start()
        self.dst[ln.f] = self.src[ln.f]

    def wait(self):
        for k in range(1, self.line.frames):
            self.copy(k).wait()

    def run(self, value):
        shape = self.src.shape
        self.src[...] = value.astype(self.src.dtype).reshape(shape)
        self.start()
        self.wait()
        return self.dst[...].reshape(shape[0] * shape[1], shape[2]).astype(BF16)


class FrameSum:
    def __init__(self, line, part, full, dim, reverse, recv_bufs, sems):
        self.line, self.part, self.full, self.dim = line, part, full, dim
        self.recv_bufs = recv_bufs
        self.sent, self.got, self.sent_back, self.got_back = sems
        bits = range(line.frames.bit_length() - 1)
        self.bits = list(reversed(bits)) if reverse else list(bits)
        self.spans = []
        start, size = 0, part.shape[dim]
        for bit in self.bits:
            size //= 2
            side = (line.f // (1 << bit)) % 2
            peer = (line.f + (1 - 2 * side) * (1 << bit), line.h)
            keep, give = start + side * size, start + (1 - side) * size
            self.spans.append((keep, give, size, peer))
            start = keep

    def view(self, ref, start, size):
        if self.dim == 0:
            return ref.at[pl.ds(pl.multiple_of(start, size), size)]
        return ref.at[:, pl.ds(pl.multiple_of(start, size), size)]

    def out(self, i):
        _, give, size, peer = self.spans[i]
        src = self.view(self.part, give, size)
        return self.line.copy(src, self.recv_bufs[i], self.sent.at[i], self.got.at[i], peer)

    def back(self, i):
        keep, _, size, peer = self.spans[i]
        ref = self.view(self.full, keep, size)
        return self.line.copy(ref, ref, self.sent_back.at[i], self.got_back.at[i], peer)

    def back_in(self, i):
        _, give, size, peer = self.spans[i]
        ref = self.view(self.full, give, size)
        return self.line.copy(ref, ref, self.sent_back.at[i], self.got_back.at[i], peer)

    def stages(self):
        return 2 * len(self.bits) + 1

    def stage(self, k):
        n = len(self.bits)
        if 1 <= k <= n:
            keep, _, size, _ = self.spans[k - 1]
            self.out(k - 1).wait()
            ref = self.view(self.part, keep, size)
            to = self.view(self.full, keep, size) if k == n else ref
            to[...] = (ref[...].astype(F32) + self.recv_bufs[k - 1][...].astype(F32)).astype(BF16)
        elif k > n:
            i = 2 * n - k
            self.back(i).wait_send()
            self.back_in(i).wait_recv()
        if k < n:
            self.out(k).start()
        elif k < 2 * n:
            self.back(2 * n - 1 - k).start()


def frame_sum_scratch(frames, shape, dim):
    bits = frames.bit_length() - 1
    scratch = []
    for i in range(bits):
        part = list(shape)
        part[dim] = shape[dim] >> (i + 1)
        scratch.append(pltpu.VMEM(tuple(part), BF16))
    return [pltpu.VMEM(shape, BF16)] + scratch + [pltpu.SemaphoreType.DMA((bits,))] * 4


def frame_sums(line, arrays, scratch):
    bits = line.frames.bit_length() - 1
    sums = []
    for full, dim, reverse in arrays:
        part, *mine = scratch[: bits + 5]
        scratch = scratch[bits + 5 :]
        sums.append(FrameSum(line, part, full, dim, reverse, mine[:bits], mine[bits:]))
    return sums


class Everyone:
    def __init__(self, line, bufs, sems):
        self.line = line
        self.src, self.dst_sib, self.dst_line, self.dst_frames = bufs
        self.sent, self.got = sems

    def run(self, value, frames_value):
        ln = self.line
        self.src[0] = value.astype(BF16)
        copy = ln.copy(self.src.at[0], self.dst_sib, self.sent.at[0], self.got.at[0], ln.sibling())
        copy.start()
        copy.wait()
        pair = self.src[0].astype(F32) + self.dst_sib[...].astype(F32)
        self.src[1] = pair.astype(BF16)
        copies = []
        for k in range(1, ln.chips):
            to = (ln.z + k) % ln.chips
            copies.append(
                ln.copy(
                    self.src.at[1],
                    self.dst_line.at[ln.z],
                    self.sent.at[k],
                    self.got.at[k],
                    ln.at(to),
                )
            )
            copies[-1].start()
        self.dst_line[ln.z] = self.src[1]
        for copy in copies:
            copy.wait()
        total = self.dst_line[0].astype(F32)
        for i in range(1, ln.chips):
            total = total + self.dst_line[i].astype(F32)
        self.src[2] = (total + frames_value).astype(BF16)
        copies = []
        for k in range(1, ln.frames):
            to = (ln.f + k) % ln.frames
            slot = ln.chips + k
            copies.append(
                ln.copy(
                    self.src.at[2],
                    self.dst_frames.at[ln.f],
                    self.sent.at[slot],
                    self.got.at[slot],
                    (to, ln.h),
                )
            )
            copies[-1].start()
        self.dst_frames[ln.f] = self.src[2]
        for copy in copies:
            copy.wait()
        total = self.dst_frames[0].astype(F32)
        for i in range(1, ln.frames):
            total = total + self.dst_frames[i].astype(F32)
        return total


def everyone_scratch(chips, frames, rows, width):
    one = (rows, width)
    return [
        pltpu.VMEM((3,) + one, BF16),
        pltpu.VMEM(one, BF16),
        pltpu.VMEM((chips,) + one, BF16),
        pltpu.VMEM((frames,) + one, BF16),
        pltpu.SemaphoreType.DMA((chips + frames,)),
        pltpu.SemaphoreType.DMA((chips + frames,)),
    ]


def pipeline(line, gather, sums, items, streams, compute, owner, total, beside):
    last = line.chips - 1
    at_compute = 2 * last + 1
    at_sum = at_compute + 1
    at_owner = at_sum + last * LAG
    every = -(-(at_owner + 2) // streams)

    def body(m, carry):
        for i in range(every):
            for behind in reversed(range(streams)):
                q = behind * every + i
                n = m - behind
                fits = (n >= 0) & (n < items)
                n = jnp.clip(n, 0, items - 1)
                if q == 0:

                    @pl.when(fits)
                    def _():
                        gather.send(n)

                if q % 2 == 0 and 1 <= q // 2 <= last:

                    @pl.when(fits)
                    def _():
                        gather.arrive(q // 2, n)

                if q == at_compute:

                    @pl.when(fits)
                    def _():
                        for zb in range(line.chips):
                            gather.wait_across(n, zb)
                        compute(n)
                        for zb in range(line.chips):
                            sums.across(n, zb).start()

                if at_sum <= q < at_owner:
                    sums.hops(q - at_sum, n, fits)
                if q == at_owner:

                    @pl.when(fits)
                    def _():
                        sums.finish(n, total)
                        owner(n)

            beside(m * every + i, i)
        return carry

    lax.fori_loop(0, items + streams - 1, body, 0)


def pipeline_steps(chips, items, streams):
    last = chips - 1
    at_compute = 2 * last + 1
    every = -(-(at_compute + 1 + last * LAG + 2) // streams)
    return every, lambda n: n + at_compute // every + 1, (items + streams - 1) * every


def computed_sum(line, sums, compute, totals, beside):
    steps, chips = line.steps, line.chips

    def body(t, carry):
        @pl.when(t < steps)
        def _():
            compute(t)
            for zb in range(chips):
                sums.across(t, zb).start()

        sums.hops(t - 1)
        beside(t)
        return carry

    lax.fori_loop(0, steps * chips + 1 + (chips - 1) * LAG, body, 0)
    for s in range(steps):
        sums.finish(s, totals.at[s])


def chain_sems(parts, chips):
    return [pltpu.SemaphoreType.DMA((parts, chips))] * 5


def swap_sems(frames):
    return [pltpu.SemaphoreType.DMA((frames,))] * 2


def sum_bufs(steps, chips, rows, width):
    tail = (rows, width)
    one = pltpu.VMEM((steps, chips) + tail, BF16)
    return [pltpu.VMEM((steps, chips, 2) + tail, BF16), one, one, one, one]


def swap_bufs(frames, part):
    kind = BF16 if part[-2] % 16 == 0 else F32
    return [pltpu.VMEM((frames,) + part, kind)] * 2


def call(kernel, name, collective_id, outs, scratch, args, smem=(), left=()):
    specs = [
        pl.BlockSpec(
            memory_space=pltpu.SMEM if i in smem else pl.ANY if i in left else pltpu.VMEM
        )
        for i in range(len(args))
    ]
    return pl.pallas_call(
        kernel,
        name=name,
        out_shape=[jax.ShapeDtypeStruct(shape, kind) for shape, kind in outs],
        in_specs=specs,
        out_specs=[pl.BlockSpec(memory_space=pltpu.VMEM)] * len(outs),
        scratch_shapes=scratch,
        compiler_params=pltpu.CompilerParams(
            collective_id=collective_id, has_side_effects=True, vmem_limit_bytes=VMEM_LIMIT
        ),
    )(*args)


def spatial_forward(
    ids, x, table, gain, shift, bias, wqkv, wout, cotangent, to_peers, to_parts,
    normed_out, qkv_out, mixed_out, state_out, cotangent_out,
    part, sib, rise, fall, out, src, dst, total, state0, g_src, g_dst, *sems,
):
    steps, patches, width = x.shape
    line = Line(steps)
    sums = ChainSum(line, (part, sib, rise, fall, out), sems[:5])
    swap = Swap(line, (src, dst), sems[5:7])
    g_swap = Swap(line, (g_src, g_dst), sems[7:9])
    line.barrier(True)
    rows = patches // line.heads
    tokens = steps * rows
    entries = table.shape[0]
    table_row = lax.broadcasted_iota(jnp.int32, (entries, width), 0)

    def to_peers_of(i, carry):
        block = cotangent[:, pl.ds(pl.multiple_of(i * rows, rows), rows)].reshape(tokens, width)
        moved = mm(to_peers[...], block).astype(BF16).astype(g_src.dtype)
        g_src[:, i] = moved.reshape(line.frames, tokens // line.frames, width)
        return carry

    lax.fori_loop(0, line.heads, to_peers_of, 0)
    g_swap.start()

    def compute(s):
        picked = jnp.where(table_row == ids[s], table[...].astype(F32), 0.0)
        added = jnp.sum(picked, axis=0, keepdims=True)
        whole = x[s].astype(F32) + added
        own = x[s, pl.ds(pl.multiple_of(line.h * rows, rows), rows)].astype(F32) + added
        state0[s] = own
        normed = (norm_stats(whole)[0] * gain[0:1, :] + shift[0:1, :]).astype(BF16)
        normed_out[s] = normed
        q = mm(normed, wqkv[0]).astype(BF16)
        k = mm(normed, wqkv[1]).astype(BF16)
        v = mm(normed, wqkv[2]).astype(BF16)
        qkv_out[0, s] = q
        qkv_out[1, s] = k
        qkv_out[2, s] = v
        mixed = attend(q, k, v, None)
        mixed_out[s] = mixed
        part[s] = mm(mixed, wout[...]).astype(BF16).reshape(part.shape[1:])

    computed_sum(line, sums, compute, total, lambda t: None)
    state = state0[...].reshape(tokens, width) + total[...].reshape(tokens, width)
    state = (state + bias[0:1, :]).astype(BF16)
    got = swap.run(mm(to_peers[...], state).astype(BF16))
    state_out[...] = mm(to_parts[...], got).astype(BF16).reshape(state_out.shape)
    g_swap.wait()

    def to_parts_of(i, carry):
        block = g_dst[:, i].reshape(tokens, width).astype(BF16)
        moved = mm(to_parts[...], block).astype(BF16)
        cotangent_out[:, i] = moved.reshape(state_out.shape)
        return carry

    lax.fori_loop(0, line.heads, to_parts_of, 0)
    drain_all(line, (sums,), steps)


def frame_mask(segments, rows):
    frames = segments.shape[0]
    shift = frames.bit_length() - 1

    def ids_along(axis, shape):
        index = lax.broadcasted_iota(jnp.int32, shape, axis)
        frame = index & (frames - 1)
        segment = jnp.zeros(shape, jnp.int32)
        for i in range(frames):
            segment = jnp.where(frame == i, segments[i], segment)
        return lax.shift_right_logical(index, shift), frame, segment

    place_q, frame_q, segment_q = ids_along(0, (rows, 1))
    place_k, frame_k, segment_k = ids_along(1, (1, rows))
    return (place_q == place_k) & (frame_k <= frame_q) & (segment_q == segment_k)


def middle(
    segments, state1, cotangent, wqkv, wout, up, up_bias, down, gain, shift, bias,
    from_parts, from_peers,
    down_grad, up_grad, qk_grad, v_grad, out_grad, y_part, result_out, next_out, small_out,
    bias_out,
    gathered, qkv, mixed_ref, act_ref, dpre_ref, dqkv, state2, grad2, grad1, mask_ref,
    part, sib, rise, fall, out, src, dst, total, *sems,
):
    items, chips, _, rows, width = gathered.shape
    streams = items // 3
    line = Line(items)
    sums = ChainSum(line, (part, sib, rise, fall, out), sems[:5])
    gather = Gather(line, gathered, sems[5:10])
    swap = Swap(line, (src, dst), sems[10:12])
    reduced = frame_sums(line, [(down_grad, 0, False), (up_grad, 0, True)], sems[12:])
    line.barrier(True)
    count = 2 * chips * rows
    columns, hidden = wout.shape[0], up.shape[1]
    mask_ref[...] = frame_mask(segments, count).astype(F32)
    bias_out[...] = jnp.zeros_like(bias_out)
    small_out[...] = jnp.zeros_like(small_out)

    def norm(value, i):
        return (norm_stats(value)[0] * gain[i : i + 1, :] + shift[i : i + 1, :]).astype(BF16)

    for s in range(streams):
        gathered[s, line.z, line.c] = norm(state1[s].astype(F32), 1)

    def compute_temporal(s, n):
        a = gathered[n].reshape(count, width)
        q = mm(a, wqkv[0]).astype(BF16)
        k = mm(a, wqkv[1]).astype(BF16)
        v = mm(a, wqkv[2]).astype(BF16)
        qkv[0, s] = q
        qkv[1, s] = k
        qkv[2, s] = v
        mixed = attend(q, k, v, mask_ref[...] > 0.0)
        mixed_ref[s] = mixed
        part[n] = mm(mixed, wout[...]).astype(BF16).reshape(chips, 2, rows, width)

    def compute_mlp(s, n):
        a = gathered[n].reshape(count, width)
        g = cotangent[s].reshape(count, width)
        pre = mm(a, up[...]) + up_bias[...]
        t = jnp.tanh(GELU_C * (pre + 0.044715 * (pre * pre * pre)))
        act = (0.5 * pre * (1.0 + t)).astype(BF16)
        act_ref[s] = act
        slope = 0.5 * (1.0 + t)
        slope = slope + 0.5 * pre * (1.0 - t * t) * (GELU_C * (1.0 + 0.134145 * (pre * pre)))
        dpre = (mm_nt(g, down[...]) * slope).astype(BF16)
        dpre_ref[s] = dpre
        bias_out[...] += jnp.sum(dpre.astype(F32), axis=0, keepdims=True)
        part[n] = mm_nt(dpre, up[...]).astype(BF16).reshape(chips, 2, rows, width)
        y_part[s] = mm(act, down[...]).astype(BF16).reshape(chips, 2, rows, width)

    def compute_back(s, n):
        r = gathered[n].reshape(count, width)
        dm = mm_nt(r, wout[...]).astype(BF16)
        dq, dk, dv = attend_back(qkv[0, s], qkv[1, s], qkv[2, s], mask_ref[...] > 0.0, dm)
        dqkv[0, s] = dq
        dqkv[1, s] = dk
        dqkv[2, s] = dv
        da = mm_nt(dq, wqkv[0]) + mm_nt(dk, wqkv[1]) + mm_nt(dv, wqkv[2])
        part[n] = da.astype(BF16).reshape(chips, 2, rows, width)

    def owner_temporal(s, n):
        state = state1[s].astype(F32) + total[...] + bias[1:2, :]
        state2[s] = state
        result_out[s] = state + bias[2:3, :]
        gathered[n + streams, line.z, line.c] = norm(state, 2)

    def row_sum(value):
        return jnp.sum(value, axis=0, keepdims=True)

    def owner_mlp(s, n):
        grad = cotangent[s, line.h].astype(F32)
        back, gain_grad, shift_grad = norm_back(state2[s], total[...], gain[2:3, :])
        dh = grad + back
        grad2[s] = dh
        gathered[n + streams, line.z, line.c] = dh.astype(BF16)
        small_out[0:1] += gain_grad
        small_out[1:2] += shift_grad
        small_out[2:3] += row_sum(grad)
        small_out[3:4] += row_sum(dh)

    def owner_back(s, n):
        back, gain_grad, shift_grad = norm_back(state1[s].astype(F32), total[...], gain[1:2, :])
        dh = grad2[s] + back
        grad1[s] = dh.astype(BF16)
        small_out[4:5] += gain_grad
        small_out[5:6] += shift_grad
        small_out[6:7] += row_sum(dh)

    def by_phase(bodies):
        def run(n):
            for i, one in enumerate(bodies):

                @pl.when(n // streams == i)
                def _():
                    one(n % streams, n)

        return run

    every, after, all_steps = pipeline_steps(chips, items, streams)
    mlp_turn, back_turn = after(2 * streams - 1), after(3 * streams - 1)
    n_stages = reduced[0].stages()
    begin = mlp_turn * every + every - 1
    moments = [begin, begin + 10, begin + 16] + [begin + 21 + 4 * i for i in range(n_stages)]
    moments = [t for t in moments[: n_stages - 1] if t < all_steps]
    all_tokens = streams * count

    def mlp_grads(which):
        def down_body(i, carry):
            cols = pl.ds(pl.multiple_of(i * 128, 128), 128)
            left = act_ref[:, :, cols].reshape(all_tokens, 128)
            right = cotangent[...].reshape(all_tokens, width)
            reduced[0].part[cols] = mm_tn(left, right).astype(BF16)
            return carry

        def up_body(i, carry):
            cols = pl.ds(pl.multiple_of(i * 256, 256), 256)
            left = gathered[streams : 2 * streams, :, :, :, cols].reshape(all_tokens, 256)
            right = dpre_ref[...].reshape(all_tokens, hidden)
            reduced[1].part[cols] = mm_tn(left, right).astype(BF16)
            return carry

        if which == 0:
            lax.fori_loop(0, hidden // 128, down_body, 0)
        else:
            lax.fori_loop(0, width // 256, up_body, 0)

    def attention_grads(which):
        if which == 0:
            left = mixed_ref[...].reshape(all_tokens, columns)
            right = gathered[2 * streams : 3 * streams].reshape(all_tokens, width)
            out_grad[...] = mm_tn(left, right).astype(BF16)
        else:

            def body(i, carry):
                start = i * 256
                cols = pl.ds(pl.multiple_of(start, 256), 256)
                left = gathered[0:streams, :, :, :, cols].reshape(all_tokens, 256)
                qkv_grads(start, left, dqkv, qk_grad, v_grad)
                return carry

            lax.fori_loop(0, width // 256, body, 0)

    def beside(t, i):
        for turn, grads in ((mlp_turn, mlp_grads), (back_turn, attention_grads)):
            for which, step in ((0, every // 2), (1, every - 1)):
                if i == step:

                    @pl.when(t == turn * every + step)
                    def _():
                        grads(which)

        for k, moment in enumerate(moments):
            if moment % every == i:

                @pl.when(t == moment)
                def _():
                    for one in reduced:
                        one.stage(k)

    def compute(n):
        by_phase((compute_temporal, compute_mlp, compute_back))(n)

    def owner(n):
        by_phase((owner_temporal, owner_mlp, owner_back))(n)

    pipeline(line, gather, sums, items, streams, compute, owner, total, beside)
    tokens = streams * rows
    own = grad1[...].reshape(tokens, width)
    got = swap.run(mm(from_parts[...], own).astype(BF16))
    next_out[...] = mm(from_peers[...], got).astype(BF16).reshape(next_out.shape)
    for k in range(len(moments), n_stages):
        for one in reduced:
            one.stage(k)
    drain_all(line, (gather, sums), items)


def qkv_grads(start, left, dqkv, qk_grad, v_grad):
    all_tokens, width = left.shape[0], v_grad.shape[0]
    for i in range(3):
        grad = mm_tn(left, dqkv[i].reshape(all_tokens, dqkv.shape[-1])).astype(BF16)
        if i < 2:
            qk_grad[pl.ds(pl.multiple_of(i * width + start, 256), 256)] = grad
        else:
            v_grad[pl.ds(pl.multiple_of(start, 256), 256)] = grad


def spatial_backward(
    ids, own, qkv, wqkv, wout, gain, x, table, normed, mixed, small2, up_bias_part, y_base,
    from_parts, from_peers, y_part, t_qk_part, t_v_part, t_out_part,
    t_qk_grad, t_v_grad, t_out_grad, qk_grad, v_grad, out_grad, y_out, result_out, small_out,
    grad_gathered, dqkv_out, load_sems, every_src, every_sib, every_line, every_frames, every_sent,
    every_got,
    part, sib, rise, fall, out, y_part_ref, y_sib, y_rise, y_fall, y_sums, src, dst, y_total, total,
    dmixed, *sems,
):
    steps, chips, _, rows, width = grad_gathered.shape
    line = Line(steps)
    sums = ChainSum(line, (part, sib, rise, fall, out), sems[:5])
    gather = Gather(line, grad_gathered, sems[5:10])
    y_line = Line(y_part_ref.shape[0])
    y_chain = ChainSum(y_line, (y_part_ref, y_sib, y_rise, y_fall, y_sums), sems[10:15])
    swap = Swap(line, (src, dst), sems[15:17])
    reduced = frame_sums(
        line,
        [
            (t_qk_grad, 0, False), (t_v_grad, 0, True), (t_out_grad, 1, True),
            (qk_grad, 0, False), (v_grad, 0, True), (out_grad, 1, True),
        ],
        sems[17:],
    )
    earlier, later = reduced[:3], reduced[3:]
    loads = [
        pltpu.make_async_copy(y_part, y_part_ref, load_sems.at[0]),
        pltpu.make_async_copy(t_qk_part, earlier[0].part, load_sems.at[1]),
        pltpu.make_async_copy(t_v_part, earlier[1].part, load_sems.at[2]),
        pltpu.make_async_copy(t_out_part, earlier[2].part, load_sems.at[3]),
    ]
    for load in loads:
        load.start()
    n_stages = earlier[0].stages()
    every = Everyone(line, (every_src, every_sib, every_line, every_frames), (every_sent, every_got))
    line.barrier(True, True)
    entries = table.shape[0]
    table_row = lax.broadcasted_iota(jnp.int32, (entries, width), 0)
    gather.start(own)
    loads[0].wait()

    def y_across(i, carry):
        y_chain.across(i // chips, i % chips).start()
        return carry

    lax.fori_loop(0, y_line.steps * chips, y_across, 0)
    parts = steps * chips

    def body(t, carry):
        for distance in range(1, chips):

            @pl.when(t // steps == distance)
            def _():
                gather.arrive(distance, t % steps)

        def side(upward, inner):
            u = jnp.maximum(t - 1, 0)
            away, s = u // steps, u % steps
            zb = jnp.where(upward == 1, line.z + away, line.z - away)
            ok = (t >= 1) & (t <= parts) & (zb >= 0) & (zb < chips)
            ok = ok & ((away > 0) | (upward == 0))

            @pl.when(ok)
            def _():
                where = jnp.clip(zb, 0, chips - 1)
                gather.wait_across(s, where)
                r = grad_gathered[s, where].reshape(2 * rows, width)
                start = pl.multiple_of(where * 2 * rows, 2 * rows)
                dmixed[s, pl.ds(start, 2 * rows)] = mm_nt(r, wout[...]).astype(BF16)

            return inner

        lax.fori_loop(0, 2, side, 0)
        y_chain.hops(t - 2)
        for k in range(n_stages):

            @pl.when(t == (1, 6, 9, 12, 16)[min(k, 4)] + 2 * max(k - 4, 0))
            def _():
                if k == 0:
                    for load in loads[1:]:
                        load.wait()
                for one in earlier:
                    one.stage(k)

        return carry

    y_bound = 2 + y_line.steps * (chips - 1) + (chips - 2) * LAG
    lax.fori_loop(0, max(parts + 1, 17 + 2 * max(n_stages - 5, 0), y_bound), body, 0)
    columns = wout.shape[0]
    all_tokens = parts * 2 * rows

    def compute(s):
        dq, dk, dv = attend_back(qkv[0, s], qkv[1, s], qkv[2, s], None, dmixed[s])
        dqkv_out[0, s] = dq
        dqkv_out[1, s] = dk
        dqkv_out[2, s] = dv
        da = mm_nt(dq, wqkv[0]) + mm_nt(dk, wqkv[1]) + mm_nt(dv, wqkv[2])
        part[s] = da.astype(BF16).reshape(part.shape[1:])

    def beside(t):
        @pl.when(t == steps)
        def _():
            left = mixed[...].reshape(all_tokens, columns)
            right = grad_gathered[...].reshape(all_tokens, width)
            later[2].part[...] = mm_tn(left, right).astype(BF16)

        @pl.when((t >= steps) & (t < steps + 2))
        def _():
            for i in range(width // 512):
                start = ((t - steps) * (width // 512) + i) * 256
                cols = pl.ds(pl.multiple_of(start, 256), 256)
                left = normed[:, :, cols].reshape(all_tokens, 256)
                qkv_grads(start, left, dqkv_out, later[0].part, later[1].part)

        for k in range(n_stages - 1):
            moment = steps + (1, 5, 7, 9)[min(k, 3)] + 2 * max(k - 3, 0)

            @pl.when(t == moment)
            def _():
                for one in later:
                    one.stage(k)

    computed_sum(line, sums, compute, total, beside)
    for s in range(y_line.steps):
        y_chain.finish(s, y_total.at[s])
    tokens = steps * rows
    result = (y_base[...] + y_total[...]).astype(BF16).reshape(tokens, width)
    swap.src[...] = mm(from_parts[...], result).astype(swap.src.dtype).reshape(swap.src.shape)
    swap.start()
    gain_grad = jnp.zeros((1, width), F32)
    shift_grad = jnp.zeros((1, width), F32)
    table_grad = jnp.zeros((entries, width), F32)
    for s in range(steps):
        picked = jnp.where(table_row == ids[s], table[...].astype(F32), 0.0)
        added = jnp.sum(picked, axis=0, keepdims=True)
        state = x[s, pl.ds(pl.multiple_of(line.h * rows, rows), rows)].astype(F32) + added
        back, one_gain, one_shift = norm_back(state, total[s], gain[0:1, :])
        grad = own[s].astype(F32) + back
        result_out[pl.ds(s * rows, rows)] = grad
        gain_grad += one_gain
        shift_grad += one_shift
        here = jnp.sum(grad, axis=0, keepdims=True)
        table_grad += jnp.where(table_row == ids[s], here, 0.0)
    rows_of = [
        gain_grad, small2[4:5], small2[0:1],
        shift_grad, small2[5:6], small2[1:2],
        small2[6:7], small2[3:4], small2[2:3],
        table_grad,
    ]
    filled = 9 + entries
    room = every_src.shape[1]
    value = jnp.concatenate(rows_of + [jnp.zeros((room - filled, width), F32)], axis=0)
    row = lax.broadcasted_iota(jnp.int32, (room, width), 0)
    frames_value = jnp.where(row == filled, up_bias_part[...], 0.0)
    small_out[...] = every.run(value, frames_value)
    swap.wait()
    got = swap.dst[...].reshape(tokens, width).astype(BF16)
    y_out[...] = mm(from_peers[...], got).astype(BF16)
    for one in later:
        one.stage(n_stages - 1)
    drain_all(line, (gather, sums), steps)
    drain_all(y_line, (y_chain,), y_line.steps)


def finish(
    t_qk, t_v, t_out, s_qk, s_v, s_out, up, down, y, grad, small,
    y_res, grad_res, table_res, gain_res, shift_res, s_qkv_res, s_out_res, t_qkv_res, t_out_res,
    bias_res, up_res, up_bias_res, down_res,
):
    for qk, v, res in ((t_qk, t_v, t_qkv_res), (s_qk, s_v, s_qkv_res)):
        res[0:2] = qk[...].astype(F32)
        res[2] = v[...].astype(F32)
    t_out_res[...] = t_out[...].astype(F32)
    s_out_res[...] = s_out[...].astype(F32)
    up_res[...] = up[...].astype(F32)
    down_res[...] = down[...].astype(F32)
    y_res[...] = y[...]
    grad_res[...] = grad[...]

    @pl.when(pl.program_id(0) == 0)
    def _():
        entries = table_res.shape[0]
        gain_res[...] = small[0:3]
        shift_res[...] = small[3:6]
        bias_res[...] = small[6:9]
        table_res[...] = small[9 : 9 + entries]
        up_bias_res[...] = small[9 + entries : 10 + entries, : up_bias_res.shape[1]]


def results(values, entries, hidden):
    grid = 8

    def blocks(shape, sliced=True):
        axis = len(shape) - 2
        block = list(shape)
        if sliced:
            block[axis] //= grid
        place = [0] * len(shape)

        def index(i):
            at = list(place)
            if sliced:
                at[axis] = i
            return tuple(at)

        return pl.BlockSpec(tuple(block), index)

    t_qk, t_v, t_out, _, _, _, g_up, g_down, y, grad, small = values
    width = g_up.shape[0]
    qkv = ((3,) + t_qk.shape[1:], F32, True)
    out = (t_out.shape, F32, True)
    few = ((3, width), F32, False)
    outs = [
        (y.shape, BF16, True), (grad.shape, F32, True), ((entries, width), F32, False), few, few,
        qkv, out, qkv, out, few,
        (g_up.shape, F32, True), ((1, hidden), F32, False), (g_down.shape, F32, True),
    ]
    return pl.pallas_call(
        finish,
        name="finish",
        grid=(grid,),
        out_shape=[jax.ShapeDtypeStruct(shape, kind) for shape, kind, _ in outs],
        in_specs=[blocks(v.shape, v is not small) for v in values],
        out_specs=[blocks(shape, sliced) for shape, _, sliced in outs],
    )(*values)


def orders(frames_local, frames, places, t_steps):
    tokens = frames_local * frames * places
    index = np.arange(tokens).reshape(frames_local, frames, places)
    first = index.transpose(1, 0, 2).reshape(-1)
    index = np.arange(tokens).reshape(frames * frames_local, t_steps, places // t_steps)
    second = index.transpose(1, 2, 0).reshape(-1)
    eye = np.eye(tokens, dtype=np.float32)
    to_peers, to_parts = eye[first], eye[second]
    return [jnp.asarray(m, BF16) for m in (to_peers, to_parts, to_parts.T, to_peers.T)]


def on_device(
    block_input,
    action_ids,
    segment_ids,
    action_table,
    norm_gain,
    norm_shift,
    spatial_qkv,
    spatial_out,
    temporal_qkv,
    temporal_out,
    out_bias,
    up_weight,
    up_bias,
    down_weight,
    cotangent,
):
    frames, heads = lax.axis_size("frames"), lax.axis_size("heads")
    chips = heads // 2
    steps, patches, width = block_input.shape
    rows = patches // heads
    tokens = steps * rows
    total_frames = segment_ids.shape[0]
    places = rows // frames
    t_steps = min(4, places)
    t_rows = tokens // t_steps
    columns = spatial_out.shape[0]
    hidden = up_weight.shape[1]
    s_qkv = spatial_qkv.transpose(1, 0, 2)
    t_qkv = temporal_qkv.transpose(1, 0, 2)
    to_peers, to_parts, from_parts, from_peers = orders(steps, frames, places, t_steps)
    swap = swap_bufs(frames, (tokens // frames, width))
    s_blocks = (steps, rows, width)
    t_blocks = (t_steps, t_rows, width)
    s_all = (steps, chips, 2, rows, width)
    count = heads * t_rows
    s_scratch = [pltpu.VMEM(s_blocks, F32)]
    t_scratch = [pltpu.VMEM(t_blocks, F32)]

    normed1, s_proj, s_mixed, state1, g_all = call(
        spatial_forward,
        "spatial_forward",
        0,
        [
            ((steps, patches, width), BF16),
            ((3, steps, patches, columns), BF16),
            ((steps, patches, columns), BF16),
            (t_blocks, BF16),
            ((t_steps, heads, t_rows, width), BF16),
        ],
        sum_bufs(steps, chips, rows, width)
        + swap
        + s_scratch * 2
        + swap_bufs(frames, (heads, tokens // frames, width))
        + chain_sems(steps, chips)
        + swap_sems(frames) * 2,
        (
            action_ids, block_input, action_table, norm_gain, norm_shift, out_bias,
            s_qkv, spatial_out, cotangent, to_peers, to_parts,
        ),
        smem=(0,),
    )
    items = 3 * t_steps
    grads_mlp = [((hidden, width), BF16), ((width, hidden), BF16)]
    grads_attention = [
        ((2 * width, columns), BF16),
        ((width, columns), BF16),
        ((columns, width), BF16),
    ]
    dims_attention = (0, 0, 1)
    t_cols = pltpu.VMEM((t_steps, count, columns), BF16)
    f_cols = pltpu.VMEM((t_steps, count, hidden), BF16)
    qkv_cols = pltpu.VMEM((3, t_steps, count, columns), BF16)
    (
        g_down, g_up, t_qk_part, t_v_part, t_out_part, y_part, y_base, own, small2, up_bias_part,
    ) = call(
        middle,
        "middle",
        1,
        grads_mlp
        + grads_attention
        + [
            ((t_steps, chips, 2, t_rows, width), BF16),
            (t_blocks, F32),
            (s_blocks, BF16),
            ((8, width), F32),
            ((1, hidden), F32),
        ],
        [
            pltpu.VMEM((items, chips, 2, t_rows, width), BF16),
            qkv_cols, t_cols, f_cols, f_cols, qkv_cols,
            pltpu.VMEM(t_blocks, F32), pltpu.VMEM(t_blocks, F32), pltpu.VMEM(t_blocks, BF16),
            pltpu.VMEM((count, count), F32),
        ]
        + sum_bufs(items, chips, t_rows, width)
        + swap
        + [pltpu.VMEM((t_rows, width), F32)]
        + chain_sems(items, chips) * 2
        + swap_sems(frames)
        + [x for shape, _ in grads_mlp for x in frame_sum_scratch(frames, shape, 0)],
        (
            segment_ids, state1, g_all, t_qkv, temporal_out, up_weight, up_bias.reshape(1, hidden),
            down_weight, norm_gain, norm_shift, out_bias, from_parts, from_peers,
        ),
        smem=(0,),
    )
    room = -(-(10 + action_table.shape[0]) // 16) * 16
    up_bias_row = jnp.pad(up_bias_part, ((0, 0), (0, width - hidden)))
    t_qk, t_v, t_out, s_qk, s_v, s_out, y, input_grad, small = call(
        spatial_backward,
        "spatial_backward",
        2,
        grads_attention * 2
        + [((tokens, width), BF16), ((tokens, width), F32), ((room, width), F32)],
        [
            pltpu.VMEM(s_all, BF16),
            pltpu.VMEM((3, steps, patches, columns), BF16),
            pltpu.SemaphoreType.DMA((4,)),
        ]
        + everyone_scratch(chips, frames, room, width)
        + sum_bufs(steps, chips, rows, width)
        + sum_bufs(t_steps, chips, t_rows, width)
        + swap
        + t_scratch
        + s_scratch
        + [pltpu.VMEM((steps, patches, columns), BF16)]
        + chain_sems(steps, chips) * 2
        + chain_sems(t_steps, chips)
        + swap_sems(frames)
        + [
            x
            for (shape, _), dim in zip(grads_attention * 2, dims_attention * 2)
            for x in frame_sum_scratch(frames, shape, dim)
        ],
        (
            action_ids, own, s_proj, s_qkv, spatial_out, norm_gain, block_input, action_table,
            normed1, s_mixed, small2, up_bias_row, y_base, from_parts, from_peers,
            y_part, t_qk_part, t_v_part, t_out_part,
        ),
        smem=(0,),
        left=(15, 16, 17, 18),
    )
    (
        block_output, input_grad, table_grad, gain_grad, shift_grad, s_qkv_grad, s_out_grad,
        t_qkv_grad, t_out_grad, bias_grad, up_grad, up_bias_grad, down_grad,
    ) = results(
        [
            t_qk.reshape(2, width, columns), t_v, t_out,
            s_qk.reshape(2, width, columns), s_v, s_out,
            g_up, g_down, y, input_grad, small,
        ],
        action_table.shape[0],
        hidden,
    )
    return (
        block_output.reshape(s_blocks),
        input_grad.reshape(s_blocks),
        table_grad,
        gain_grad,
        shift_grad,
        s_qkv_grad.transpose(1, 0, 2),
        s_out_grad,
        t_qkv_grad.transpose(1, 0, 2),
        t_out_grad,
        bias_grad,
        up_grad,
        up_bias_grad.reshape(hidden),
        down_grad,
    )


def solution(mesh):
    return jax.shard_map(
        on_device,
        mesh=mesh,
        in_specs=(
            P("frames", None, None),
            P("frames"),
            P(),
            P(),
            P(),
            P(),
            P(None, None, "heads"),
            P("heads", None),
            P(None, None, "heads"),
            P("heads", None),
            P(),
            P(None, "heads"),
            P("heads"),
            P("heads", None),
            P("frames", None, None),
        ),
        out_specs=(
            P("frames", "heads", None),
            P("frames", "heads", None),
            P(),
            P(),
            P(),
            P(None, None, "heads"),
            P("heads", None),
            P(None, None, "heads"),
            P("heads", None),
            P(),
            P(None, "heads"),
            P("heads"),
            P("heads", None),
        ),
        check_vma=False,
    )
```

```python
import jax
import jax.numpy as jnp
import numpy as np
from jax import lax
from jax.experimental import pallas as pl
from jax.experimental.pallas import tpu as pltpu
from jax.sharding import PartitionSpec as P

HD = 64
SCALE = HD**-0.5
EPS = 1e-05
MASKED = -1000000000.0
F32 = jnp.float32
BF16 = jnp.bfloat16
MESH = pl.DeviceIdType.MESH
VMEM_LIMIT = 62 * 1024 * 1024
GELU_C = float(np.sqrt(2.0 / np.pi))
LAG = 2
HOP = 3
SLACK = 2


def mm(a, b):
    return lax.dot_general(a, b, (((1,), (0,)), ((), ())), preferred_element_type=F32)


def mm_nt(a, b):
    return lax.dot_general(a, b, (((1,), (1,)), ((), ())), preferred_element_type=F32)


def mm_tn(a, b):
    return lax.dot_general(a, b, (((0,), (0,)), ((), ())), preferred_element_type=F32)


def norm_stats(value):
    centered = value - jnp.mean(value, axis=-1, keepdims=True)
    inv = lax.rsqrt(jnp.mean(centered * centered, axis=-1, keepdims=True) + EPS)
    return centered * inv, inv


def norm_back(value, grad, gain):
    normed, inv = norm_stats(value)
    e = grad * gain
    first = jnp.mean(e, axis=-1, keepdims=True)
    second = jnp.mean(e * normed, axis=-1, keepdims=True)
    gain_grad = jnp.sum(grad * normed, axis=0, keepdims=True)
    shift_grad = jnp.sum(grad, axis=0, keepdims=True)
    return (e - first - normed * second) * inv, gain_grad, shift_grad


def head_lanes(shape, head):
    lane = lax.broadcasted_iota(jnp.int32, shape, 1)
    return (lane >= head * HD) & (lane < (head + 1) * HD)


def softmax_of(q, k, mask):
    scores = mm_nt(q, k) * SCALE
    if mask is not None:
        scores = jnp.where(mask, scores, MASKED)
    raised = jnp.exp(scores - jnp.max(scores, axis=-1, keepdims=True))
    return raised / jnp.sum(raised, axis=-1, keepdims=True)


def attend(q, k, v, mask):
    heads = q.shape[1] // HD
    mixed = None
    for head in range(heads):
        lanes = head_lanes(q.shape, head)
        probs = softmax_of(jnp.where(lanes, q, jnp.zeros_like(q)), k, mask).astype(BF16)
        out = mm(probs, v)
        mixed = out if mixed is None else jnp.where(lanes, out, mixed)
    return mixed.astype(BF16)


def attend_back(q, k, v, mask, grad):
    heads = q.shape[1] // HD
    dq = dk = dv = None
    for head in range(heads):
        lanes = head_lanes(q.shape, head)
        qh = jnp.where(lanes, q, jnp.zeros_like(q))
        gh = jnp.where(lanes, grad, jnp.zeros_like(grad))
        probs = softmax_of(qh, k, mask)
        dvh = mm_tn(probs.astype(BF16), gh)
        dp = mm_nt(gh, v)
        ds = (probs * (dp - jnp.sum(dp * probs, axis=-1, keepdims=True))).astype(BF16)
        dqh = mm(ds, k) * SCALE
        dkh = mm_tn(ds, qh) * SCALE
        if head == 0:
            dq, dk, dv = dqh, dkh, dvh
        else:
            dq = jnp.where(lanes, dqh, dq)
            dk = dk + dkh
            dv = dv + dvh
    return dq.astype(BF16), dk.astype(BF16), dv.astype(BF16)


class Line:
    def __init__(self, steps):
        self.frames = lax.axis_size("frames")
        self.heads = lax.axis_size("heads")
        self.chips = self.heads // 2
        self.f = lax.axis_index("frames")
        self.h = lax.axis_index("heads")
        self.z = self.h // 2
        self.c = self.h % 2
        self.steps = steps

    def at(self, z):
        return (self.f, jnp.clip(z, 0, self.chips - 1) * 2 + self.c)

    def sibling(self):
        return (self.f, self.z * 2 + 1 - self.c)

    def barrier(self, over_frames, whole_line=False):
        sem = pltpu.get_barrier_semaphore()

        def greet(device):
            pl.semaphore_signal(sem, inc=1, device_id=device, device_id_type=MESH)

        greet(self.sibling())
        count = 1
        if over_frames:
            for k in range(1, self.frames):
                greet(((self.f + k) % self.frames, self.h))
            count += self.frames - 1
        if whole_line:
            for k in range(1, self.chips):
                greet(self.at((self.z + k) % self.chips))
            count += self.chips - 1
        else:

            @pl.when(self.z > 0)
            def _():
                greet(self.at(self.z - 1))

            @pl.when(self.z < self.chips - 1)
            def _():
                greet(self.at(self.z + 1))

            count = count + (self.z > 0).astype(jnp.int32)
            count = count + (self.z < self.chips - 1).astype(jnp.int32)
        pl.semaphore_wait(sem, count)

    def copy(self, src, dst, send, recv, device):
        return pltpu.make_async_remote_copy(
            src_ref=src,
            dst_ref=dst,
            send_sem=send,
            recv_sem=recv,
            device_id=device,
            device_id_type=MESH,
        )


class Gather:
    def __init__(self, line, buf, sems):
        self.line, self.buf = line, buf
        self.got, self.got_sib, self.sent_up, self.sent_down, self.sent_sib = sems

    def up(self, s, zb):
        ln = self.line
        ref = self.buf.at[s, zb, ln.c]
        return ln.copy(ref, ref, self.sent_up.at[s, zb], self.got.at[s, zb], ln.at(ln.z + 1))

    def down(self, s, zb):
        ln = self.line
        ref = self.buf.at[s, zb, ln.c]
        return ln.copy(ref, ref, self.sent_down.at[s, zb], self.got.at[s, zb], ln.at(ln.z - 1))

    def across(self, s, zb):
        ln = self.line
        ref = self.buf.at[s, zb, ln.c]
        return ln.copy(ref, ref, self.sent_sib.at[s, zb], self.got_sib.at[s, zb], ln.sibling())

    def wait_across(self, s, zb):
        ln = self.line
        ref = self.buf.at[s, zb, 1 - ln.c]
        ln.copy(
            ref, ref, self.sent_sib.at[s, zb], self.got_sib.at[s, zb], ln.sibling()
        ).wait_recv()

    def send(self, s):
        ln = self.line

        @pl.when(ln.z < ln.chips - 1)
        def _():
            self.up(s, ln.z).start()

        @pl.when(ln.z > 0)
        def _():
            self.down(s, ln.z).start()

        self.across(s, ln.z).start()

    def start(self, own):
        ln = self.line
        for s in range(ln.steps):
            self.buf[s, ln.z, ln.c] = own[s]
            self.send(s)

    def arrive(self, distance, s):
        ln = self.line
        below, above = ln.z - distance, ln.z + distance

        @pl.when((distance > 0) & (below >= 0))
        def _():
            self.up(s, below).wait_recv()

            @pl.when(ln.z < ln.chips - 1)
            def _():
                self.up(s, below).start()

            self.across(s, below).start()

        @pl.when((distance > 0) & (above < ln.chips))
        def _():
            self.down(s, above).wait_recv()

            @pl.when(ln.z > 0)
            def _():
                self.down(s, above).start()

            self.across(s, above).start()

    def drain(self, s, zb):
        ln = self.line

        @pl.when((zb <= ln.z) & (ln.z < ln.chips - 1))
        def _():
            self.up(s, zb).wait_send()

        @pl.when((zb >= ln.z) & (ln.z > 0))
        def _():
            self.down(s, zb).wait_send()

        self.across(s, zb).wait_send()


class ChainSum:
    def __init__(self, line, bufs, sems):
        self.line = line
        self.part, self.sib, self.rise, self.fall, self.out = bufs
        self.sent_sib, self.got_sib, self.got_up, self.got_down, self.sent = sems

    def across(self, s, zb):
        ln = self.line
        return ln.copy(
            self.part.at[s, zb, 1 - ln.c],
            self.sib.at[s, zb],
            self.sent_sib.at[s, zb],
            self.got_sib.at[s, zb],
            ln.sibling(),
        )

    def up(self, s, o):
        ln = self.line
        return ln.copy(
            self.out.at[s, o],
            self.rise.at[s, o],
            self.sent.at[s, o],
            self.got_up.at[s, o],
            ln.at(ln.z + 1),
        )

    def down(self, s, o):
        ln = self.line
        return ln.copy(
            self.out.at[s, o],
            self.fall.at[s, o],
            self.sent.at[s, o],
            self.got_down.at[s, o],
            ln.at(ln.z - 1),
        )

    def mine(self, s, o):
        return self.part[s, o, self.line.c].astype(F32) + self.sib[s, o].astype(F32)

    def hop_up(self, s, o):
        ln = self.line
        self.across(s, o).wait_recv()

        @pl.when(ln.z == 0)
        def _():
            self.out[s, o] = self.mine(s, o).astype(BF16)

        @pl.when(ln.z > 0)
        def _():
            self.up(s, o).wait_recv()
            self.out[s, o] = (self.mine(s, o) + self.rise[s, o].astype(F32)).astype(BF16)

        self.up(s, o).start()

    def hop_down(self, s, o):
        ln = self.line
        self.across(s, o).wait_recv()

        @pl.when(ln.z == ln.chips - 1)
        def _():
            self.out[s, o] = self.mine(s, o).astype(BF16)

        @pl.when(ln.z < ln.chips - 1)
        def _():
            self.down(s, o).wait_recv()
            self.out[s, o] = (self.mine(s, o) + self.fall[s, o].astype(F32)).astype(BF16)

        self.down(s, o).start()

    def hops(self, t, part=None, fits=True):
        ln = self.line
        last = ln.chips - 1
        for upward in (True, False):
            place = ln.z if upward else last - ln.z
            q = t - place * LAG
            if part is None:
                turn = jnp.maximum(q, 0) // ln.steps
                s = jnp.maximum(q, 0) % ln.steps
            else:
                turn, s = jnp.maximum(q, 0), part
            far = jnp.clip(last - turn, 0, last)
            ok = (q >= 0) & (turn < last) & (far > place) & fits
            o = far if upward else last - far

            @pl.when(ok)
            def _():
                if upward:
                    self.hop_up(s, o)
                else:
                    self.hop_down(s, o)

    def finish(self, s, total):
        ln = self.line
        self.across(s, ln.z).wait_recv()
        total[...] = self.mine(s, ln.z)

        @pl.when(ln.z > 0)
        def _():
            self.up(s, ln.z).wait_recv()
            total[...] += self.rise[s, ln.z].astype(F32)

        @pl.when(ln.z < ln.chips - 1)
        def _():
            self.down(s, ln.z).wait_recv()
            total[...] += self.fall[s, ln.z].astype(F32)

    def drain(self, s, zb):
        ln = self.line
        self.across(s, zb).wait_send()

        @pl.when(zb != ln.z)
        def _():
            self.up(s, zb).wait_send()


def drain_all(line, things, parts):
    def body(i, carry):
        for thing in things:
            thing.drain(i // line.chips, i % line.chips)
        return carry

    lax.fori_loop(0, parts * line.chips, body, 0)


class Swap:
    def __init__(self, line, src_at, dst, sems):
        self.line, self.src_at, self.dst = line, src_at, dst
        self.sent, self.got = sems

    def copy(self, part, k):
        ln = self.line
        to = (ln.f + k) % ln.frames
        return ln.copy(
            self.src_at(part, to),
            self.dst.at[part, ln.f],
            self.sent.at[part, k],
            self.got.at[part, k],
            (to, ln.h),
        )

    def start(self, part):
        ln = self.line
        for k in range(1, ln.frames):
            self.copy(part, k).start()
        self.dst[part, ln.f] = self.src_at(part, ln.f)[...]

    def wait(self, part):
        for k in range(1, self.line.frames):
            self.copy(part, k).wait()


class FrameSum:
    def __init__(self, line, part, full, dim, reverse, recv_bufs, sems):
        self.line, self.part, self.full, self.dim = line, part, full, dim
        self.recv_bufs = recv_bufs
        self.sent, self.got, self.sent_back, self.got_back = sems
        bits = range(line.frames.bit_length() - 1)
        self.bits = list(reversed(bits)) if reverse else list(bits)
        self.spans = []
        start, size = 0, part.shape[dim]
        for bit in self.bits:
            size //= 2
            side = (line.f // (1 << bit)) % 2
            peer = (line.f + (1 - 2 * side) * (1 << bit), line.h)
            keep, give = start + side * size, start + (1 - side) * size
            self.spans.append((keep, give, size, peer))
            start = keep

    def view(self, ref, start, size):
        if self.dim == 0:
            return ref.at[pl.ds(pl.multiple_of(start, size), size)]
        return ref.at[:, pl.ds(pl.multiple_of(start, size), size)]

    def out(self, i):
        _, give, size, peer = self.spans[i]
        src = self.view(self.part, give, size)
        return self.line.copy(src, self.recv_bufs[i], self.sent.at[i], self.got.at[i], peer)

    def back(self, i):
        keep, _, size, peer = self.spans[i]
        ref = self.view(self.full, keep, size)
        return self.line.copy(ref, ref, self.sent_back.at[i], self.got_back.at[i], peer)

    def back_in(self, i):
        _, give, size, peer = self.spans[i]
        ref = self.view(self.full, give, size)
        return self.line.copy(ref, ref, self.sent_back.at[i], self.got_back.at[i], peer)

    def stages(self):
        return 2 * len(self.bits) + 1

    def stage(self, k):
        n = len(self.bits)
        if 1 <= k <= n:
            keep, _, size, _ = self.spans[k - 1]
            self.out(k - 1).wait()
            ref = self.view(self.part, keep, size)
            to = self.view(self.full, keep, size) if k == n else ref
            to[...] = (ref[...].astype(F32) + self.recv_bufs[k - 1][...].astype(F32)).astype(BF16)
        elif k > n:
            i = 2 * n - k
            self.back(i).wait_send()
            self.back_in(i).wait_recv()
        if k < n:
            self.out(k).start()
        elif k < 2 * n:
            self.back(2 * n - 1 - k).start()


def frame_sum_scratch(frames, shape, dim):
    bits = frames.bit_length() - 1
    scratch = []
    for i in range(bits):
        part = list(shape)
        part[dim] = shape[dim] >> (i + 1)
        scratch.append(pltpu.VMEM(tuple(part), BF16))
    return [pltpu.VMEM(shape, BF16)] + scratch + [pltpu.SemaphoreType.DMA((bits,))] * 4


def frame_sums(line, arrays, scratch):
    bits = line.frames.bit_length() - 1
    sums = []
    for full, dim, reverse in arrays:
        part, *mine = scratch[: bits + 5]
        scratch = scratch[bits + 5 :]
        sums.append(FrameSum(line, part, full, dim, reverse, mine[:bits], mine[bits:]))
    return sums


class Everyone:
    def __init__(self, line, bufs, sems):
        self.line = line
        self.src, self.dst_sib, self.dst_line, self.dst_frames = bufs
        self.sent, self.got = sems

    def pair_copy(self):
        ln = self.line
        return ln.copy(
            self.src.at[0], self.dst_sib, self.sent.at[0], self.got.at[0], ln.sibling()
        )

    def line_copies(self):
        ln = self.line
        return [
            ln.copy(
                self.src.at[1],
                self.dst_line.at[ln.z],
                self.sent.at[k],
                self.got.at[k],
                ln.at((ln.z + k) % ln.chips),
            )
            for k in range(1, ln.chips)
        ]

    def frame_copies(self):
        ln = self.line
        return [
            ln.copy(
                self.src.at[2],
                self.dst_frames.at[ln.f],
                self.sent.at[ln.chips + k],
                self.got.at[ln.chips + k],
                ((ln.f + k) % ln.frames, ln.h),
            )
            for k in range(1, ln.frames)
        ]

    def over_pair(self, value):
        self.src[0] = value.astype(BF16)
        self.pair_copy().start()

    def over_line(self):
        self.pair_copy().wait()
        pair = self.src[0].astype(F32) + self.dst_sib[...].astype(F32)
        self.src[1] = pair.astype(BF16)
        copies = self.line_copies()
        for copy in copies:
            copy.start()
        self.dst_line[self.line.z] = self.src[1]

    def over_frames(self, frames_value):
        for copy in self.line_copies():
            copy.wait()
        total = self.dst_line[0].astype(F32)
        for i in range(1, self.line.chips):
            total = total + self.dst_line[i].astype(F32)
        self.src[2] = (total + frames_value).astype(BF16)
        for copy in self.frame_copies():
            copy.start()
        self.dst_frames[self.line.f] = self.src[2]

    def result(self):
        for copy in self.frame_copies():
            copy.wait()
        total = self.dst_frames[0].astype(F32)
        for i in range(1, self.line.frames):
            total = total + self.dst_frames[i].astype(F32)
        return total


class Timetable:
    def __init__(self, chips, streams):
        self.chips, self.streams = chips, streams
        self.every = chips
        while not self.place():
            self.every += 1

    def place(self):
        last, every = self.chips - 1, self.every
        self.arrive = [0]
        for _ in range(1, last):
            t = self.arrive[-1] + HOP
            while t % every in [a % every for a in self.arrive]:
                t += 1
            self.arrive.append(t)
        self.arrive.append(self.arrive[-1] + HOP)
        self.compute = self.arrive[-1] + 2
        self.hops = {}
        for p in range(last):
            taken = {a % every for a in self.arrive[: p + 1]}
            for far in range(last, p, -1):
                t = self.compute + 2
                if p:
                    t = max(t, self.hops[p - 1, far] + HOP)
                while t % every in taken:
                    t += 1
                taken.add(t % every)
                self.hops[p, far] = t
        self.owner = max(self.hops[far - 1, far] for far in range(1, self.chips)) + HOP
        self.turns = self.owner // every + 1
        return self.owner + SLACK <= self.streams * every

    def after(self, item):
        return item + self.compute // self.every + 1

    def steps(self, items):
        return (items + self.turns - 1) * self.every


def pipeline(line, times, gather, sums, phases, enter, compute, owner, total, beside):
    last, streams = line.chips - 1, times.streams
    items = phases * streams

    def body(m, carry):
        for i in range(times.every):
            for behind in reversed(range(times.turns)):
                q = behind * times.every + i
                n = m - behind
                fits = (n >= 0) & (n < items)
                gathers = fits & (n >= streams)
                n = jnp.clip(n, 0, items - 1)
                s = n % streams
                held = jnp.maximum(n - streams, 0)
                if q in times.arrive:
                    distance = times.arrive.index(q)

                    @pl.when(gathers)
                    def _():
                        if distance == 0:
                            enter(n)
                            gather.send(held)
                        else:
                            gather.arrive(distance, held)

                if q == times.compute:

                    @pl.when(gathers)
                    def _():
                        for zb in range(line.chips):
                            gather.wait_across(held, zb)
                            sums.drain(s, zb)

                    @pl.when(fits)
                    def _():
                        compute(n)
                        for zb in range(line.chips):
                            sums.across(s, zb).start()

                for (place, far), at in times.hops.items():
                    if at == q:

                        @pl.when(fits & (line.z == place))
                        def _():
                            sums.hop_up(s, far)

                        @pl.when(fits & (line.z == last - place))
                        def _():
                            sums.hop_down(s, last - far)

                if q == times.owner:

                    @pl.when(fits)
                    def _():
                        sums.finish(s, total)
                        owner(n)

            beside(m, i)
        return carry

    lax.fori_loop(0, items + times.turns - 1, body, 0)


def computed_sum(line, sums, compute, totals, beside):
    steps, chips = line.steps, line.chips

    def body(t, carry):
        @pl.when(t < steps)
        def _():
            compute(t)
            for zb in range(chips):
                sums.across(t, zb).start()

        sums.hops(t - 1)
        beside(t)
        return carry

    lax.fori_loop(0, steps * chips + 1 + (chips - 1) * LAG, body, 0)
    for s in range(steps):
        sums.finish(s, totals.at[s])


def frame_mask(segments, places, rows):
    frames = segments.shape[0]
    bits, place_bits = frames.bit_length() - 1, places.bit_length() - 1

    def ids_along(axis, shape):
        index = lax.broadcasted_iota(jnp.int32, shape, axis)
        frame = lax.shift_right_logical(index, place_bits) & (frames - 1)
        segment = jnp.zeros(shape, jnp.int32)
        for i in range(frames):
            segment = jnp.where(frame == i, segments[i], segment)
        block = lax.shift_right_logical(index, place_bits + bits)
        return block * places + (index & (places - 1)), frame, segment

    place_q, frame_q, segment_q = ids_along(0, (rows, 1))
    place_k, frame_k, segment_k = ids_along(1, (1, rows))
    return (place_q == place_k) & (frame_k <= frame_q) & (segment_q == segment_k)


def qkv_grads(start, left, dqkv, qk_grad, v_grad):
    all_tokens, width = left.shape[0], v_grad.shape[0]
    for i in range(3):
        grad = mm_tn(left, dqkv[i].reshape(all_tokens, dqkv.shape[-1])).astype(BF16)
        if i < 2:
            qk_grad[pl.ds(pl.multiple_of(i * width + start, 256), 256)] = grad
        else:
            v_grad[pl.ds(pl.multiple_of(start, 256), 256)] = grad


def row_sum(value):
    return jnp.sum(value, axis=0, keepdims=True)


def moved_exactly(order, value):
    out = None
    for _ in range(3):
        term = value.astype(BF16)
        value = value - term.astype(F32)
        out = mm(order, term) if out is None else out + mm(order, term)
    return out


class Refs:
    def __init__(self, names, refs):
        for name, ref in zip(names, refs, strict=True):
            setattr(self, name, ref)


def block(names, *refs):
    r = Refs(names, refs)
    steps, patches, width = r.x.shape
    streams, heads, rows, _ = r.g_all.shape
    line, t_line = Line(steps), Line(streams)
    chips, frames = line.chips, line.frames
    s_rows = patches // heads
    tokens = steps * s_rows
    columns, hidden = r.s_wout.shape[0], r.up.shape[1]
    entries = r.table.shape[0]
    count = heads * rows
    all_tokens = heads * tokens
    times = Timetable(chips, streams)
    sums = ChainSum(t_line, (r.part, r.sib, r.rise, r.fall, r.out), r.sum_sems)
    gather = Gather(t_line, r.gathered, r.gather_sems)
    last_part = getattr(r, "last_part", r.part)
    last_out = getattr(r, "last_out", r.out)
    last_sums = ChainSum(
        line, (last_part, r.last_sib, r.last_rise, r.last_fall, last_out), r.last_sems
    )
    shared = not hasattr(r, "g_src")

    def g_src_at(part, to):
        return r.gathered.at[3 * streams + to] if shared else r.g_src.at[part, to]

    g_swap = Swap(line, g_src_at, r.g_dst, r.g_sems)
    state_swap = Swap(line, lambda s, to: r.state_src.at[s, to], r.state_dst, r.state_sems)
    grad_swap = Swap(line, lambda s, to: r.grad_src.at[s, to], r.grad_dst, r.grad_sems)
    y_swap = Swap(line, lambda s, to: r.y_src.at[s, to], r.y_dst, r.y_sems)
    every = Everyone(line, (r.every_src, r.every_sib, r.every_line, r.every_frames), r.every_sems)
    reduced = frame_sums(
        line,
        [
            (r.down_grad, 0, False), (r.up_grad, 0, True),
            (r.t_qk, 0, False), (r.t_v, 0, True), (r.t_out, 1, True),
            (r.s_qk, 0, False), (r.s_v, 0, True), (r.s_out, 1, True),
        ],
        r.reduce,
    )
    mlp_sums, t_sums, s_sums = reduced[:2], reduced[2:5], reduced[5:]
    line.barrier(True, True)

    def g_out(i, carry):
        rows_of = pl.ds(pl.multiple_of(i * s_rows, s_rows), s_rows)
        moved = mm(r.to_peers[...], r.cotangent[:, rows_of].reshape(tokens, width))
        moved = moved.astype(BF16).astype(r.g_dst.dtype).reshape(frames, tokens // frames, width)
        if shared:
            r.gathered[3 * streams : 4 * streams, i // 2, i % 2] = moved
        else:
            r.g_src[0, :, i // 2, i % 2] = moved
        return carry

    lax.fori_loop(0, heads, g_out, 0)
    g_swap.start(0)

    def g_in(i):
        moved = r.g_dst[0, :, i // 2, i % 2].reshape(tokens, width).astype(BF16)
        r.g_all[:, i] = mm(r.to_parts[...], moved).astype(BF16).reshape(streams, rows, width)

    table_row = lax.broadcasted_iota(jnp.int32, (entries, width), 0)

    def added(s):
        return row_sum(jnp.where(table_row == r.ids[s], r.table[...].astype(F32), 0.0))

    def norm(value, i):
        scaled = norm_stats(value)[0] * r.gain[i : i + 1, :]
        return (scaled + r.shift[i : i + 1, :]).astype(BF16)

    def attention(s, carry):
        normed = norm(r.x[s].astype(F32) + added(s), 0)
        r.normed0[s] = normed
        q = mm(normed, r.s_wqkv[0]).astype(BF16)
        k = mm(normed, r.s_wqkv[1]).astype(BF16)
        v = mm(normed, r.s_wqkv[2]).astype(BF16)
        r.s_proj[0, s] = q
        r.s_proj[1, s] = k
        r.s_proj[2, s] = v
        r.s_cols[s] = attend(q, k, v, None)
        return carry

    lax.fori_loop(0, steps, attention, 0)

    def to_streams(i, carry):
        rows_of = pl.ds(pl.multiple_of(i * s_rows, s_rows), s_rows)
        moved = mm(r.to_streams[...], r.s_cols[:, rows_of].reshape(tokens, columns)).astype(BF16)
        r.s_mixed[:, i] = moved.reshape(streams, rows, columns)
        return carry

    lax.fori_loop(0, heads, to_streams, 0)
    own_rows = pl.ds(pl.multiple_of(line.h * s_rows, s_rows), s_rows)
    own = mm(r.to_streams[...], r.x[:, own_rows].reshape(tokens, width))
    row = lax.broadcasted_iota(jnp.int32, (tokens, 1), 0)
    frame = lax.shift_right_logical(row, (rows // (frames * steps)).bit_length() - 1) & (steps - 1)
    entry = jnp.zeros_like(row)
    for s in range(steps):
        entry = jnp.where(frame == s, r.ids[s], entry)
    picker = (entry == lax.broadcasted_iota(jnp.int32, (tokens, entries), 1)).astype(BF16)
    own = own + mm(picker, r.table[...])
    r.state0[...] = own.reshape(streams, rows, width)
    r.mask[...] = frame_mask(r.segments, rows // (frames * steps), count).astype(F32)
    r.up_bias_grad[...] = jnp.zeros_like(r.up_bias_grad)
    r.small[...] = jnp.zeros_like(r.small)

    def held(n):
        return n - streams

    def enter_temporal(s, n):
        state_swap.wait(s)
        state = r.state_dst[s].reshape(rows, width)
        r.state1[s] = state
        r.gathered[held(n), line.z, line.c] = norm(state, 1)

    def enter_spatial(s, n):
        grad_swap.wait(s)
        grad = r.grad_dst[s].reshape(rows, width)
        r.grad1[s] = grad
        r.gathered[held(n), line.z, line.c] = grad.astype(BF16)

    def compute_spatial(s, n):
        left = r.s_mixed[s].reshape(count, columns)
        r.part[s] = mm(left, r.s_wout[...]).astype(BF16).reshape(chips, 2, rows, width)

    def compute_temporal(s, n):
        a = r.gathered[held(n)].reshape(count, width)
        q = mm(a, r.t_wqkv[0]).astype(BF16)
        k = mm(a, r.t_wqkv[1]).astype(BF16)
        v = mm(a, r.t_wqkv[2]).astype(BF16)
        r.t_proj[0, s] = q
        r.t_proj[1, s] = k
        r.t_proj[2, s] = v
        mixed = attend(q, k, v, r.mask[...] > 0.0)
        r.t_mixed[s] = mixed
        r.part[s] = mm(mixed, r.t_wout[...]).astype(BF16).reshape(chips, 2, rows, width)

    def compute_mlp(s, n):
        a = r.gathered[held(n)].reshape(count, width)
        g = r.g_all[s].reshape(count, width)
        pre = mm(a, r.up[...]) + r.up_bias[...]
        t = jnp.tanh(GELU_C * (pre + 0.044715 * (pre * pre * pre)))
        act = (0.5 * pre * (1.0 + t)).astype(BF16)
        r.act[s] = act
        slope = 0.5 * (1.0 + t)
        slope = slope + 0.5 * pre * (1.0 - t * t) * (GELU_C * (1.0 + 0.134145 * (pre * pre)))
        dpre = (mm_nt(g, r.down[...]) * slope).astype(BF16)
        r.dpre[s] = dpre
        r.up_bias_grad[:, :hidden] += row_sum(dpre.astype(F32))
        r.part[s] = mm_nt(dpre, r.up[...]).astype(BF16).reshape(chips, 2, rows, width)

    def compute_back(s, n):
        grad = r.gathered[held(n)].reshape(count, width)
        dm = mm_nt(grad, r.t_wout[...]).astype(BF16)
        mask = r.mask[...] > 0.0
        dq, dk, dv = attend_back(r.t_proj[0, s], r.t_proj[1, s], r.t_proj[2, s], mask, dm)
        r.t_dproj[0, s] = dq
        r.t_dproj[1, s] = dk
        r.t_dproj[2, s] = dv
        da = mm_nt(dq, r.t_wqkv[0]) + mm_nt(dk, r.t_wqkv[1]) + mm_nt(dv, r.t_wqkv[2])
        r.part[s] = da.astype(BF16).reshape(chips, 2, rows, width)

    def compute_last(s, n):
        grad = r.gathered[held(n)].reshape(count, width)
        moved = mm_nt(grad, r.s_wout[...]).astype(BF16)
        r.s_dmixed[s] = moved.reshape(heads, rows, columns)
        y = mm(r.act[s], r.down[...])
        r.part[s] = y.astype(BF16).reshape(chips, 2, rows, width)

    def owner_spatial(s, n):
        state = r.state0[s] + r.total[...] + r.bias[0:1, :]
        r.state_src[s] = state.reshape(r.state_src.shape[1:])
        state_swap.start(s)

    def owner_temporal(s, n):
        state = r.state1[s] + r.total[...] + r.bias[1:2, :]
        r.state2[s] = state
        r.gathered[n, line.z, line.c] = norm(state, 2)

    def owner_mlp(s, n):
        grad = r.g_all[s, line.h].astype(F32)
        back, gain_grad, shift_grad = norm_back(r.state2[s], r.total[...], r.gain[2:3, :])
        dh = grad + back
        r.grad2[s] = dh
        r.gathered[n, line.z, line.c] = dh.astype(BF16)
        r.small[0:1] += gain_grad
        r.small[1:2] += shift_grad
        r.small[2:3] += row_sum(grad)
        r.small[3:4] += row_sum(dh)

    def owner_back(s, n):
        back, gain_grad, shift_grad = norm_back(r.state1[s], r.total[...], r.gain[1:2, :])
        dh = r.grad2[s] + back
        r.grad_src[s] = dh.reshape(r.grad_src.shape[1:])
        grad_swap.start(s)
        r.small[4:5] += gain_grad
        r.small[5:6] += shift_grad
        r.small[6:7] += row_sum(dh)

    def owner_last(s, n):
        r.y[s] = (r.state2[s] + r.total[...] + r.bias[2:3, :]).astype(BF16)

    def by_phase(bodies):
        def run(n):
            for i, one in enumerate(bodies):
                if one is not None:

                    @pl.when(n // streams == i)
                    def _():
                        one(n % streams, n)

        return run

    def down_chunk(i):
        cols = pl.ds(pl.multiple_of(i * 128, 128), 128)
        left = r.act[:, :, cols].reshape(all_tokens, 128)
        right = r.g_all[...].reshape(all_tokens, width)
        mlp_sums[0].part[cols] = mm_tn(left, right).astype(BF16)

    def up_chunk(i):
        cols = pl.ds(pl.multiple_of(i * 256, 256), 256)
        left = r.gathered[streams : 2 * streams, :, :, :, cols].reshape(all_tokens, 256)
        right = r.dpre[...].reshape(all_tokens, hidden)
        mlp_sums[1].part[cols] = mm_tn(left, right).astype(BF16)

    def t_out_chunk(i):
        left = r.t_mixed[...].reshape(all_tokens, columns)
        right = r.gathered[2 * streams : 3 * streams].reshape(all_tokens, width)
        t_sums[2].part[...] = mm_tn(left, right).astype(BF16)

    def t_qkv_chunk(i):
        start = i * 256
        cols = pl.ds(pl.multiple_of(start, 256), 256)
        left = r.gathered[0:streams, :, :, :, cols].reshape(all_tokens, 256)
        qkv_grads(start, left, r.t_dproj, t_sums[0].part, t_sums[1].part)

    def g_in_chunk(i):
        @pl.when(i == 0)
        def _():
            g_swap.wait(0)

        g_in(i)

    n_down, n_up = hidden // 128, width // 256
    turn_of = times.after
    mlp_turn, back_turn = turn_of(3 * streams - 1), turn_of(4 * streams - 1)
    chunks = (
        (streams + 1, 0, heads, g_in_chunk),
        (mlp_turn, 0, n_down, down_chunk),
        (mlp_turn, n_down, n_up, up_chunk),
        (back_turn, 0, 1, t_out_chunk),
        (back_turn, 1, width // 256, t_qkv_chunk),
    )
    slots = [i for i in range(times.every) if i % 2 == 1][:3]
    per_turn = 2 * len(slots)
    turns = 5 * streams + times.turns - 1
    stages = reduced[0].stages()
    bits = len(reduced[0].bits)

    def moments_of(begin, first):
        t, out = begin, []
        for k in range(stages):
            out.append(t)
            halvings = k if k < bits else max(2 * bits - 1 - k, 0)
            t += 2 + max(first >> halvings, 1)
        return out

    def begin_of(turn, number):
        return (turn + number // per_turn) * times.every + times.every - 1

    moments = (
        (mlp_sums, moments_of(begin_of(mlp_turn, n_down + n_up), 10)),
        (t_sums, moments_of(begin_of(back_turn, 1 + width // 256), 5)),
    )

    def beside(m, i):
        if i in slots:
            for turn, first, number, chunk in chunks:
                which = per_turn * (m - turn) + 2 * slots.index(i) - first
                here = jnp.clip(number - which, 0, 2)

                @pl.when((which > -2) & (which < number))
                def _():
                    def one(j, carry):
                        @pl.when(which + j >= 0)
                        def _():
                            chunk(which + j)

                        return carry

                    lax.fori_loop(0, here, one, 0)

        for sums_of, steps_of in moments:
            for k, moment in enumerate(steps_of):
                if moment % times.every == i and moment // times.every < turns:

                    @pl.when(m == moment // times.every)
                    def _():
                        for one in sums_of:
                            one.stage(k)

    enter = by_phase((None, enter_temporal, None, None, enter_spatial))
    compute = by_phase(
        (compute_spatial, compute_temporal, compute_mlp, compute_back, compute_last)
    )
    owner = by_phase((owner_spatial, owner_temporal, owner_mlp, owner_back, owner_last))
    pipeline(t_line, times, gather, sums, 5, enter, compute, owner, r.total, beside)
    drain_all(t_line, (sums,), streams)

    y = mm(r.from_parts[...], r.y[...].reshape(tokens, width)).astype(BF16)
    r.y_src[0] = y.astype(r.y_src.dtype).reshape(r.y_src.shape[1:])
    y_swap.start(0)

    def from_streams(i, carry):
        rows_of = pl.ds(pl.multiple_of(i * s_rows, s_rows), s_rows)
        moved = mm(r.from_streams[...], r.s_dmixed[:, i].reshape(tokens, columns)).astype(BF16)
        r.s_cols[:, rows_of] = moved.reshape(steps, s_rows, columns)
        return carry

    lax.fori_loop(0, heads, from_streams, 0)
    r.sums0[...] = jnp.zeros_like(r.sums0)

    def compute_spatial_back(s):
        dq, dk, dv = attend_back(r.s_proj[0, s], r.s_proj[1, s], r.s_proj[2, s], None, r.s_cols[s])
        r.s_dproj[0, s] = dq
        r.s_dproj[1, s] = dk
        r.s_dproj[2, s] = dv
        da = mm_nt(dq, r.s_wqkv[0]) + mm_nt(dk, r.s_wqkv[1]) + mm_nt(dv, r.s_wqkv[2])
        last_part[s] = da.astype(BF16).reshape(last_part.shape[1:])

    def small_part(s):
        state = r.x[s].astype(F32) + added(s)
        da = last_part[s].reshape(patches, width).astype(F32)
        back, gain_grad, shift_grad = norm_back(state, da, r.gain[0:1, :])
        r.sums0[0:1] += gain_grad
        r.sums0[1:2] += shift_grad
        r.sums0[8 : 8 + entries] += jnp.where(table_row == r.ids[s], row_sum(back), 0.0)

    room = r.every_src.shape[1]
    filled = 9 + entries

    def small_value(own_grad):
        for s in range(steps):
            here = row_sum(own_grad[s * s_rows : (s + 1) * s_rows])
            r.sums0[8 : 8 + entries] += jnp.where(table_row == r.ids[s], here, 0.0)
        rows_of = [
            r.sums0[0:1], r.small[4:5], r.small[0:1],
            r.sums0[1:2], r.small[5:6], r.small[1:2],
            r.small[6:7], r.small[3:4], r.small[2:3],
            r.sums0[8 : 8 + entries], jnp.zeros((room - filled, width), F32),
        ]
        return jnp.concatenate(rows_of, axis=0)

    s_moments = moments_of(steps + 1, 4)

    def beside_last(t):
        @pl.when(t == steps)
        def _():
            left = r.s_mixed[...].reshape(all_tokens, columns)
            right = r.gathered[3 * streams : 4 * streams].reshape(all_tokens, width)
            s_sums[2].part[...] = mm_tn(left, right).astype(BF16)

        @pl.when((t >= steps) & (t < steps + 2))
        def _():
            for i in range(width // 512):
                start = ((t - steps) * (width // 512) + i) * 256
                cols = pl.ds(pl.multiple_of(start, 256), 256)
                left = r.normed0[:, :, cols].reshape(all_tokens, 256)
                qkv_grads(start, left, r.s_dproj, s_sums[0].part, s_sums[1].part)

        for k in range(stages - 1):

            @pl.when(t == s_moments[k])
            def _():
                for one in s_sums:
                    one.stage(k)

        @pl.when((t >= steps + 2) & (t < 2 * steps + 2))
        def _():
            small_part(t - steps - 2)

        @pl.when(t == 2 * steps + 2)
        def _():
            grad = r.grad1[...].reshape(tokens, width)
            own_grad = moved_exactly(r.from_streams[...], grad)
            r.state0[...] = own_grad.reshape(r.state0.shape)
            every.over_pair(small_value(own_grad))

        @pl.when(t == 2 * steps + 4)
        def _():
            every.over_line()

        @pl.when(t == 2 * steps + 7)
        def _():
            row = lax.broadcasted_iota(jnp.int32, (room, width), 0)
            every.over_frames(jnp.where(row == filled, r.up_bias_grad[...], 0.0))

    computed_sum(line, last_sums, compute_spatial_back, r.last_total, beside_last)
    own_grad = r.state0[...].reshape(tokens, width)
    for s in range(steps):
        state = r.x[s, own_rows].astype(F32) + added(s)
        back, _, _ = norm_back(state, r.last_total[s], r.gain[0:1, :])
        r.grad_res[pl.ds(s * s_rows, s_rows)] = own_grad[s * s_rows : (s + 1) * s_rows] + back
    y_swap.wait(0)
    r.y_res[...] = mm(r.from_peers[...], r.y_dst[0].reshape(tokens, width).astype(BF16)).astype(BF16)
    r.small_res[...] = every.result()
    for sums_of, steps_of in moments:
        for k, moment in enumerate(steps_of):
            if moment // times.every >= turns:
                for one in sums_of:
                    one.stage(k)
    for k, moment in enumerate(s_moments):
        if k == stages - 1:
            for one in s_sums:
                one.stage(k)
    drain_all(line, (last_sums,), steps)
    drain_all(t_line, (gather,), 4 * streams)


def finish(
    t_qk, t_v, t_out, s_qk, s_v, s_out, up, down, y, grad, small,
    y_res, grad_res, table_res, gain_res, shift_res, s_qkv_res, s_out_res, t_qkv_res, t_out_res,
    bias_res, up_res, up_bias_res, down_res,
):
    for qk, v, res in ((t_qk, t_v, t_qkv_res), (s_qk, s_v, s_qkv_res)):
        res[0:2] = qk[...].astype(F32)
        res[2] = v[...].astype(F32)
    t_out_res[...] = t_out[...].astype(F32)
    s_out_res[...] = s_out[...].astype(F32)
    up_res[...] = up[...].astype(F32)
    down_res[...] = down[...].astype(F32)
    y_res[...] = y[...]
    grad_res[...] = grad[...]

    @pl.when(pl.program_id(0) == 0)
    def _():
        entries = table_res.shape[0]
        gain_res[...] = small[0:3]
        shift_res[...] = small[3:6]
        bias_res[...] = small[6:9]
        table_res[...] = small[9 : 9 + entries]
        up_bias_res[...] = small[9 + entries : 10 + entries, : up_bias_res.shape[1]]


def results(values, entries, hidden):
    grid = 8

    def blocks(shape, sliced=True):
        axis = len(shape) - 2
        block = list(shape)
        if sliced:
            block[axis] //= grid
        place = [0] * len(shape)

        def index(i):
            at = list(place)
            if sliced:
                at[axis] = i
            return tuple(at)

        return pl.BlockSpec(tuple(block), index)

    t_qk, t_v, t_out, _, _, _, g_up, g_down, y, grad, small = values
    width = g_up.shape[0]
    qkv = ((3,) + t_qk.shape[1:], F32, True)
    out = (t_out.shape, F32, True)
    few = ((3, width), F32, False)
    outs = [
        (y.shape, BF16, True), (grad.shape, F32, True), ((entries, width), F32, False), few, few,
        qkv, out, qkv, out, few,
        (g_up.shape, F32, True), ((1, hidden), F32, False), (g_down.shape, F32, True),
    ]
    return pl.pallas_call(
        finish,
        name="finish",
        grid=(grid,),
        out_shape=[jax.ShapeDtypeStruct(shape, kind) for shape, kind, _ in outs],
        in_specs=[blocks(v.shape, v is not small) for v in values],
        out_specs=[blocks(shape, sliced) for shape, _, sliced in outs],
    )(*values)


def orders(frames_local, frames, places, streams):
    tokens = frames_local * frames * places
    index = np.arange(tokens).reshape(frames_local, frames, streams, places // streams)
    to_streams = index.transpose(2, 1, 0, 3).reshape(-1)
    to_peers = index.transpose(1, 0, 2, 3).reshape(-1)
    index = np.arange(tokens).reshape(frames * frames_local, streams, places // streams)
    to_parts = index.transpose(1, 0, 2).reshape(-1)
    eye = np.eye(tokens, dtype=np.float32)
    there = [eye[order] for order in (to_streams, to_peers, to_parts)]
    back = [m.T for m in there]
    names = ("to_streams", "to_peers", "to_parts", "from_streams", "from_peers", "from_parts")
    return {name: jnp.asarray(m, BF16) for name, m in zip(names, there + back)}


def on_device(
    block_input,
    action_ids,
    segment_ids,
    action_table,
    norm_gain,
    norm_shift,
    spatial_qkv,
    spatial_out,
    temporal_qkv,
    temporal_out,
    out_bias,
    up_weight,
    up_bias,
    down_weight,
    cotangent,
):
    frames, heads = lax.axis_size("frames"), lax.axis_size("heads")
    chips = heads // 2
    steps, patches, width = block_input.shape
    rows = patches // heads
    tokens = steps * rows
    total_frames = segment_ids.shape[0]
    places = rows // frames
    streams = min(4, places)
    t_rows = tokens // streams
    columns = spatial_out.shape[0]
    hidden = up_weight.shape[1]
    entries = action_table.shape[0]
    count = heads * t_rows
    room = -(-(10 + entries) // 16) * 16
    args = dict(
        ids=action_ids,
        segments=segment_ids,
        x=block_input,
        cotangent=cotangent,
        table=action_table,
        gain=norm_gain,
        shift=norm_shift,
        bias=out_bias,
        s_wqkv=spatial_qkv.transpose(1, 0, 2),
        s_wout=spatial_out,
        t_wqkv=temporal_qkv.transpose(1, 0, 2),
        t_wout=temporal_out,
        up=up_weight,
        up_bias=up_bias.reshape(1, hidden),
        down=down_weight,
        **orders(steps, frames, places, streams),
    )
    qk, v, out = (2 * width, columns), (width, columns), (columns, width)
    down, up = (hidden, width), (width, hidden)
    outs = dict(
        t_qk=(qk, BF16),
        t_v=(v, BF16),
        t_out=(out, BF16),
        s_qk=(qk, BF16),
        s_v=(v, BF16),
        s_out=(out, BF16),
        up_grad=(up, BF16),
        down_grad=(down, BF16),
        y_res=((tokens, width), BF16),
        grad_res=((tokens, width), F32),
        small_res=((room, width), F32),
    )
    s_all = (steps, chips, 2, rows, width)
    t_all = (streams, chips, 2, t_rows, width)
    s_one, t_one = (steps, chips, rows, width), (streams, chips, t_rows, width)
    owned = (streams, t_rows, width)
    swapped = (streams, frames, t_rows // frames, width)
    whole = (1, frames, tokens // frames, width)
    g_part = (1, frames, chips, 2, tokens // frames, width)

    def kind_of(shape):
        return BF16 if shape[-2] % 16 == 0 else F32

    cols = dict(
        s_cols=(steps, patches, columns),
        s_proj=(3, steps, patches, columns),
        s_dproj=(3, steps, patches, columns),
        s_mixed=(streams, heads, t_rows, columns),
        s_dmixed=(streams, heads, t_rows, columns),
        t_proj=(3, streams, count, columns),
        t_dproj=(3, streams, count, columns),
        t_mixed=(streams, count, columns),
        act=(streams, count, hidden),
        dpre=(streams, count, hidden),
        normed0=(steps, patches, width),
        gathered=(4 * streams,) + t_all[1:],
        g_all=(streams, heads, t_rows, width),
        part=t_all,
        sib=t_one,
        rise=t_one,
        fall=t_one,
        out=t_one,
        **({} if s_all == t_all else dict(last_part=s_all, last_out=s_one)),
        last_sib=s_one,
        last_rise=s_one,
        last_fall=s_one,
        y=owned,
    )
    floats = dict(
        state0=owned,
        state1=owned,
        state2=owned,
        grad1=owned,
        grad2=owned,
        total=(t_rows, width),
        last_total=(steps, rows, width),
        mask=(count, count),
        small=(8, width),
        sums0=(8 + entries, width),
        up_bias_grad=(1, width),
        state_src=swapped,
        state_dst=swapped,
        grad_src=swapped,
        grad_dst=swapped,
    )
    scratch = {name: pltpu.VMEM(shape, BF16) for name, shape in cols.items()}
    scratch |= {name: pltpu.VMEM(shape, F32) for name, shape in floats.items()}
    moving = ("g_dst",) if g_part[1:] == t_all else ("g_src", "g_dst")
    scratch |= {name: pltpu.VMEM(g_part, kind_of(g_part)) for name in moving}
    scratch |= {name: pltpu.VMEM(whole, kind_of(whole)) for name in ("y_src", "y_dst")}
    every_shape = (room, width)
    scratch |= dict(
        every_src=pltpu.VMEM((3,) + every_shape, BF16),
        every_sib=pltpu.VMEM(every_shape, BF16),
        every_line=pltpu.VMEM((chips,) + every_shape, BF16),
        every_frames=pltpu.VMEM((frames,) + every_shape, BF16),
        every_sems=[pltpu.SemaphoreType.DMA((chips + frames,))] * 2,
        sum_sems=[pltpu.SemaphoreType.DMA((streams, chips))] * 5,
        last_sems=[pltpu.SemaphoreType.DMA((steps, chips))] * 5,
        gather_sems=[pltpu.SemaphoreType.DMA((4 * streams, chips))] * 5,
        state_sems=[pltpu.SemaphoreType.DMA((streams, frames))] * 2,
        grad_sems=[pltpu.SemaphoreType.DMA((streams, frames))] * 2,
        g_sems=[pltpu.SemaphoreType.DMA((1, frames))] * 2,
        y_sems=[pltpu.SemaphoreType.DMA((1, frames))] * 2,
        reduce=[
            x
            for shape, dim in (
                (down, 0), (up, 0), (qk, 0), (v, 0), (out, 1), (qk, 0), (v, 0), (out, 1)
            )
            for x in frame_sum_scratch(frames, shape, dim)
        ],
    )
    names = tuple(args) + tuple(outs) + tuple(scratch)
    parts = pl.pallas_call(
        lambda *refs: block(names, *refs),
        name="block",
        out_shape=[jax.ShapeDtypeStruct(shape, kind) for shape, kind in outs.values()],
        in_specs=[
            pl.BlockSpec(memory_space=pltpu.SMEM if name in ("ids", "segments") else pltpu.VMEM)
            for name in args
        ],
        out_specs=[pl.BlockSpec(memory_space=pltpu.VMEM)] * len(outs),
        scratch_shapes=list(scratch.values()),
        compiler_params=pltpu.CompilerParams(
            collective_id=0, has_side_effects=True, vmem_limit_bytes=VMEM_LIMIT
        ),
    )(*args.values())
    found = dict(zip(outs, parts))
    for name in ("t_qk", "s_qk"):
        found[name] = found[name].reshape(2, width, columns)
    (
        block_output, input_grad, table_grad, gain_grad, shift_grad, s_qkv_grad, s_out_grad,
        t_qkv_grad, t_out_grad, bias_grad, up_grad, up_bias_grad, down_grad,
    ) = results(list(found.values()), entries, hidden)
    s_blocks = (steps, rows, width)
    return (
        block_output.reshape(s_blocks),
        input_grad.reshape(s_blocks),
        table_grad,
        gain_grad,
        shift_grad,
        s_qkv_grad.transpose(1, 0, 2),
        s_out_grad,
        t_qkv_grad.transpose(1, 0, 2),
        t_out_grad,
        bias_grad,
        up_grad,
        up_bias_grad.reshape(hidden),
        down_grad,
    )


def solution(mesh):
    return jax.shard_map(
        on_device,
        mesh=mesh,
        in_specs=(
            P("frames", None, None),
            P("frames"),
            P(),
            P(),
            P(),
            P(),
            P(None, None, "heads"),
            P("heads", None),
            P(None, None, "heads"),
            P("heads", None),
            P(),
            P(None, "heads"),
            P("heads"),
            P("heads", None),
            P("frames", None, None),
        ),
        out_specs=(
            P("frames", "heads", None),
            P("frames", "heads", None),
            P(),
            P(),
            P(),
            P(None, None, "heads"),
            P("heads", None),
            P(None, None, "heads"),
            P("heads", None),
            P(),
            P(None, "heads"),
            P("heads"),
            P("heads", None),
        ),
        check_vma=False,
    )
```

```python
import jax
import jax.numpy as jnp
import numpy as np
from jax import lax
from jax.experimental import pallas as pl
from jax.experimental.pallas import tpu as pltpu
from jax.sharding import PartitionSpec as P

HD = 64
SCALE = HD**-0.5
EPS = 1e-05
MASKED = -1000000000.0
F32 = jnp.float32
BF16 = jnp.bfloat16
MESH = pl.DeviceIdType.MESH
VMEM_LIMIT = 62 * 1024 * 1024
GELU_C = float(np.sqrt(2.0 / np.pi))
LAG = 2
MLP_WAITS = (13, 8)
T_WAITS = (9, 6)
LAST_STAGES = (8, 11, 14)
LAST_SMALL = (9, 12, 15)
HOP_US, SIBLING_US, COMPUTE_US, LINK_US, OWNER_US = 3.4, 0.6, 0.6, 1.45, 0.4


def mm(a, b):
    return lax.dot_general(a, b, (((1,), (0,)), ((), ())), preferred_element_type=F32)


def mm_nt(a, b):
    return lax.dot_general(a, b, (((1,), (1,)), ((), ())), preferred_element_type=F32)


def mm_tn(a, b):
    return lax.dot_general(a, b, (((0,), (0,)), ((), ())), preferred_element_type=F32)


def norm_stats(value):
    centered = value - jnp.mean(value, axis=-1, keepdims=True)
    inv = lax.rsqrt(jnp.mean(centered * centered, axis=-1, keepdims=True) + EPS)
    return centered * inv, inv


def norm_back(value, grad, gain):
    normed, inv = norm_stats(value)
    e = grad * gain
    first = jnp.mean(e, axis=-1, keepdims=True)
    second = jnp.mean(e * normed, axis=-1, keepdims=True)
    gain_grad = jnp.sum(grad * normed, axis=0, keepdims=True)
    shift_grad = jnp.sum(grad, axis=0, keepdims=True)
    return (e - first - normed * second) * inv, gain_grad, shift_grad


def head_lanes(shape, head):
    lane = lax.broadcasted_iota(jnp.int32, shape, 1)
    return (lane >= head * HD) & (lane < (head + 1) * HD)


def softmax_of(q, k, mask):
    scores = mm_nt(q, k) * SCALE
    if mask is not None:
        scores = jnp.where(mask, scores, MASKED)
    raised = jnp.exp(scores - jnp.max(scores, axis=-1, keepdims=True))
    return raised / jnp.sum(raised, axis=-1, keepdims=True)


def attend(q, k, v, mask):
    heads = q.shape[1] // HD
    mixed = None
    for head in range(heads):
        lanes = head_lanes(q.shape, head)
        probs = softmax_of(jnp.where(lanes, q, jnp.zeros_like(q)), k, mask).astype(BF16)
        out = mm(probs, v)
        mixed = out if mixed is None else jnp.where(lanes, out, mixed)
    return mixed.astype(BF16)


def attend_back(q, k, v, mask, grad):
    heads = q.shape[1] // HD
    dq = dk = dv = None
    for head in range(heads):
        lanes = head_lanes(q.shape, head)
        qh = jnp.where(lanes, q, jnp.zeros_like(q))
        gh = jnp.where(lanes, grad, jnp.zeros_like(grad))
        probs = softmax_of(qh, k, mask)
        dvh = mm_tn(probs.astype(BF16), gh)
        dp = mm_nt(gh, v)
        ds = (probs * (dp - jnp.sum(dp * probs, axis=-1, keepdims=True))).astype(BF16)
        dqh = mm(ds, k) * SCALE
        dkh = mm_tn(ds, qh) * SCALE
        if head == 0:
            dq, dk, dv = dqh, dkh, dvh
        else:
            dq = jnp.where(lanes, dqh, dq)
            dk = dk + dkh
            dv = dv + dvh
    return dq.astype(BF16), dk.astype(BF16), dv.astype(BF16)


class Line:
    def __init__(self, steps):
        self.frames = lax.axis_size("frames")
        self.heads = lax.axis_size("heads")
        self.chips = self.heads // 2
        self.f = lax.axis_index("frames")
        self.h = lax.axis_index("heads")
        self.z = self.h // 2
        self.c = self.h % 2
        self.steps = steps

    def at(self, z):
        return (self.f, jnp.clip(z, 0, self.chips - 1) * 2 + self.c)

    def sibling(self):
        return (self.f, self.z * 2 + 1 - self.c)

    def barrier(self, over_frames, whole_line=False):
        sem = pltpu.get_barrier_semaphore()

        def greet(device):
            pl.semaphore_signal(sem, inc=1, device_id=device, device_id_type=MESH)

        greet(self.sibling())
        count = 1
        if over_frames:
            for k in range(1, self.frames):
                greet(((self.f + k) % self.frames, self.h))
            count += self.frames - 1
        if whole_line:
            for k in range(1, self.chips):
                greet(self.at((self.z + k) % self.chips))
            count += self.chips - 1
        else:

            @pl.when(self.z > 0)
            def _():
                greet(self.at(self.z - 1))

            @pl.when(self.z < self.chips - 1)
            def _():
                greet(self.at(self.z + 1))

            count = count + (self.z > 0).astype(jnp.int32)
            count = count + (self.z < self.chips - 1).astype(jnp.int32)
        pl.semaphore_wait(sem, count)

    def copy(self, src, dst, send, recv, device):
        return pltpu.make_async_remote_copy(
            src_ref=src,
            dst_ref=dst,
            send_sem=send,
            recv_sem=recv,
            device_id=device,
            device_id_type=MESH,
        )


class Gather:
    def __init__(self, line, buf, sems):
        self.line, self.buf = line, buf
        self.got, self.got_sib, self.sent_up, self.sent_down, self.sent_sib = sems

    def up(self, s, zb):
        ln = self.line
        ref = self.buf.at[s, zb, ln.c]
        return ln.copy(ref, ref, self.sent_up.at[s, zb], self.got.at[s, zb], ln.at(ln.z + 1))

    def down(self, s, zb):
        ln = self.line
        ref = self.buf.at[s, zb, ln.c]
        return ln.copy(ref, ref, self.sent_down.at[s, zb], self.got.at[s, zb], ln.at(ln.z - 1))

    def across(self, s, zb):
        ln = self.line
        ref = self.buf.at[s, zb, ln.c]
        return ln.copy(ref, ref, self.sent_sib.at[s, zb], self.got_sib.at[s, zb], ln.sibling())

    def wait_across(self, s, zb):
        ln = self.line
        ref = self.buf.at[s, zb, 1 - ln.c]
        ln.copy(
            ref, ref, self.sent_sib.at[s, zb], self.got_sib.at[s, zb], ln.sibling()
        ).wait_recv()

    def send(self, s):
        ln = self.line

        @pl.when(ln.z < ln.chips - 1)
        def _():
            self.up(s, ln.z).start()

        @pl.when(ln.z > 0)
        def _():
            self.down(s, ln.z).start()

        self.across(s, ln.z).start()

    def start(self, own):
        ln = self.line
        for s in range(ln.steps):
            self.buf[s, ln.z, ln.c] = own[s]
            self.send(s)

    def arrive(self, distance, s):
        ln = self.line
        below, above = ln.z - distance, ln.z + distance

        @pl.when((distance > 0) & (below >= 0))
        def _():
            self.up(s, below).wait_recv()

            @pl.when(ln.z < ln.chips - 1)
            def _():
                self.up(s, below).start()

            self.across(s, below).start()

        @pl.when((distance > 0) & (above < ln.chips))
        def _():
            self.down(s, above).wait_recv()

            @pl.when(ln.z > 0)
            def _():
                self.down(s, above).start()

            self.across(s, above).start()

    def drain(self, s, zb):
        ln = self.line

        @pl.when((zb <= ln.z) & (ln.z < ln.chips - 1))
        def _():
            self.up(s, zb).wait_send()

        @pl.when((zb >= ln.z) & (ln.z > 0))
        def _():
            self.down(s, zb).wait_send()

        self.across(s, zb).wait_send()


class ChainSum:
    def __init__(self, line, bufs, sems):
        self.line = line
        self.part, self.sib, self.rise, self.fall, self.out = bufs
        self.sent_sib, self.got_sib, self.got_up, self.got_down, self.sent = sems

    def across(self, s, zb):
        ln = self.line
        return ln.copy(
            self.part.at[s, zb, 1 - ln.c],
            self.sib.at[s, zb],
            self.sent_sib.at[s, zb],
            self.got_sib.at[s, zb],
            ln.sibling(),
        )

    def up(self, s, o):
        ln = self.line
        return ln.copy(
            self.out.at[s, o],
            self.rise.at[s, o],
            self.sent.at[s, o],
            self.got_up.at[s, o],
            ln.at(ln.z + 1),
        )

    def down(self, s, o):
        ln = self.line
        return ln.copy(
            self.out.at[s, o],
            self.fall.at[s, o],
            self.sent.at[s, o],
            self.got_down.at[s, o],
            ln.at(ln.z - 1),
        )

    def mine(self, s, o):
        return self.part[s, o, self.line.c].astype(F32) + self.sib[s, o].astype(F32)

    def hop_up(self, s, o):
        ln = self.line
        self.across(s, o).wait_recv()

        @pl.when(ln.z == 0)
        def _():
            self.out[s, o] = self.mine(s, o).astype(BF16)

        @pl.when(ln.z > 0)
        def _():
            self.up(s, o).wait_recv()
            self.out[s, o] = (self.mine(s, o) + self.rise[s, o].astype(F32)).astype(BF16)

        self.up(s, o).start()

    def hop_down(self, s, o):
        ln = self.line
        self.across(s, o).wait_recv()

        @pl.when(ln.z == ln.chips - 1)
        def _():
            self.out[s, o] = self.mine(s, o).astype(BF16)

        @pl.when(ln.z < ln.chips - 1)
        def _():
            self.down(s, o).wait_recv()
            self.out[s, o] = (self.mine(s, o) + self.fall[s, o].astype(F32)).astype(BF16)

        self.down(s, o).start()

    def hops(self, t, part=None, fits=True):
        ln = self.line
        last = ln.chips - 1
        for upward in (True, False):
            place = ln.z if upward else last - ln.z
            q = t - place * LAG
            if part is None:
                turn = jnp.maximum(q, 0) // ln.steps
                s = jnp.maximum(q, 0) % ln.steps
            else:
                turn, s = jnp.maximum(q, 0), part
            far = jnp.clip(last - turn, 0, last)
            ok = (q >= 0) & (turn < last) & (far > place) & fits
            o = far if upward else last - far

            @pl.when(ok)
            def _():
                if upward:
                    self.hop_up(s, o)
                else:
                    self.hop_down(s, o)

    def finish(self, s, total):
        ln = self.line
        self.across(s, ln.z).wait_recv()
        total[...] = self.mine(s, ln.z)

        @pl.when(ln.z > 0)
        def _():
            self.up(s, ln.z).wait_recv()
            total[...] += self.rise[s, ln.z].astype(F32)

        @pl.when(ln.z < ln.chips - 1)
        def _():
            self.down(s, ln.z).wait_recv()
            total[...] += self.fall[s, ln.z].astype(F32)

    def drain(self, s, zb):
        ln = self.line
        self.across(s, zb).wait_send()

        @pl.when(zb != ln.z)
        def _():
            self.up(s, zb).wait_send()


def drain_all(line, things, parts):
    def body(i, carry):
        for thing in things:
            thing.drain(i // line.chips, i % line.chips)
        return carry

    lax.fori_loop(0, parts * line.chips, body, 0)


class Swap:
    def __init__(self, line, src_at, dst, sems):
        self.line, self.src_at, self.dst = line, src_at, dst
        self.sent, self.got = sems

    def copy(self, part, k):
        ln = self.line
        to = (ln.f + k) % ln.frames
        return ln.copy(
            self.src_at(part, to),
            self.dst.at[part, ln.f],
            self.sent.at[part, k],
            self.got.at[part, k],
            (to, ln.h),
        )

    def start(self, part):
        ln = self.line
        for k in range(1, ln.frames):
            self.copy(part, k).start()
        self.dst[part, ln.f] = self.src_at(part, ln.f)[...]

    def wait(self, part):
        for k in range(1, self.line.frames):
            self.copy(part, k).wait()


class FrameSum:
    def __init__(self, line, part, full, dim, reverse, recv_bufs, sems):
        self.line, self.part, self.full, self.dim = line, part, full, dim
        self.recv_bufs = recv_bufs
        self.sent, self.got, self.sent_back, self.got_back = sems
        bits = range(line.frames.bit_length() - 1)
        self.bits = list(reversed(bits)) if reverse else list(bits)
        self.spans = []
        start, size = 0, part.shape[dim]
        for bit in self.bits:
            size //= 2
            side = (line.f // (1 << bit)) % 2
            peer = (line.f + (1 - 2 * side) * (1 << bit), line.h)
            keep, give = start + side * size, start + (1 - side) * size
            self.spans.append((keep, give, size, peer))
            start = keep

    def view(self, ref, start, size):
        if self.dim == 0:
            return ref.at[pl.ds(pl.multiple_of(start, size), size)]
        return ref.at[:, pl.ds(pl.multiple_of(start, size), size)]

    def out(self, i):
        _, give, size, peer = self.spans[i]
        src = self.view(self.part, give, size)
        return self.line.copy(src, self.recv_bufs[i], self.sent.at[i], self.got.at[i], peer)

    def back(self, i):
        keep, _, size, peer = self.spans[i]
        ref = self.view(self.full, keep, size)
        return self.line.copy(ref, ref, self.sent_back.at[i], self.got_back.at[i], peer)

    def back_in(self, i):
        _, give, size, peer = self.spans[i]
        ref = self.view(self.full, give, size)
        return self.line.copy(ref, ref, self.sent_back.at[i], self.got_back.at[i], peer)

    def stages(self):
        return 2 * len(self.bits) + 1

    def stage(self, k):
        n = len(self.bits)
        if 1 <= k <= n:
            keep, _, size, _ = self.spans[k - 1]
            self.out(k - 1).wait()
            ref = self.view(self.part, keep, size)
            to = self.view(self.full, keep, size) if k == n else ref
            to[...] = (ref[...].astype(F32) + self.recv_bufs[k - 1][...].astype(F32)).astype(BF16)
        elif k > n:
            i = 2 * n - k
            self.back(i).wait_send()
            self.back_in(i).wait_recv()
        if k < n:
            self.out(k).start()
        elif k < 2 * n:
            self.back(2 * n - 1 - k).start()


def frame_sum_scratch(frames, shape, dim):
    bits = frames.bit_length() - 1
    scratch = []
    for i in range(bits):
        part = list(shape)
        part[dim] = shape[dim] >> (i + 1)
        scratch.append(pltpu.VMEM(tuple(part), BF16))
    return [pltpu.VMEM(shape, BF16)] + scratch + [pltpu.SemaphoreType.DMA((bits,))] * 4


def frame_sums(line, arrays, scratch):
    bits = line.frames.bit_length() - 1
    sums = []
    for full, dim, reverse in arrays:
        part, *mine = scratch[: bits + 5]
        scratch = scratch[bits + 5 :]
        sums.append(FrameSum(line, part, full, dim, reverse, mine[:bits], mine[bits:]))
    return sums


class Everyone:
    def __init__(self, line, refs, sems):
        self.line = line
        self.src, self.dst_sib, self.dst_line, self.dst_frames, self.full = refs
        self.sent, self.got = sems
        self.share = self.src.shape[1] // line.chips

    def cols(self, z):
        return pl.ds(pl.multiple_of(z * self.share, self.share), self.share)

    def pair_copy(self):
        ln = self.line
        return ln.copy(self.src, self.dst_sib, self.sent.at[0], self.got.at[0], ln.sibling())

    def line_copies(self):
        ln, copies = self.line, []
        for k in range(1, ln.chips):
            to = (ln.z + k) % ln.chips
            src, dst = self.dst_sib.at[:, self.cols(to)], self.dst_line.at[ln.z]
            copies.append(ln.copy(src, dst, self.sent.at[k], self.got.at[k], ln.at(to)))
        return copies

    def frame_copies(self):
        ln, copies = self.line, []
        for k in range(1, ln.frames):
            to, i = ((ln.f + k) % ln.frames, ln.h), ln.chips + k
            src, dst = self.dst_line.at[ln.z], self.dst_frames.at[ln.f]
            copies.append(ln.copy(src, dst, self.sent.at[i], self.got.at[i], to))
        return copies

    def back_copies(self):
        ln, copies = self.line, []
        for k in range(1, ln.chips):
            to, i = ln.at((ln.z + k) % ln.chips), ln.chips + ln.frames + k
            ref = self.full.at[:, self.cols(ln.z)]
            copies.append(ln.copy(ref, ref, self.sent.at[i], self.got.at[i], to))
        return copies

    def over_pair(self, value):
        self.src[...] = value.astype(BF16)
        self.pair_copy().start()

    def over_line(self):
        self.pair_copy().wait()
        pair = self.src[...].astype(F32) + self.dst_sib[...].astype(F32)
        self.dst_sib[...] = pair.astype(BF16)
        for copy in self.line_copies():
            copy.start()

    def over_frames(self):
        ln = self.line
        for copy in self.line_copies():
            copy.wait()
        total = self.dst_sib[:, self.cols(ln.z)].astype(F32)
        for k in range(1, ln.chips):
            total = total + self.dst_line[(ln.z + k) % ln.chips].astype(F32)
        self.dst_line[ln.z] = total.astype(BF16)
        for copy in self.frame_copies():
            copy.start()
        self.dst_frames[ln.f] = self.dst_line[ln.z]

    def over_back(self):
        for copy in self.frame_copies():
            copy.wait()
        total = self.dst_frames[0].astype(F32)
        for i in range(1, self.line.frames):
            total = total + self.dst_frames[i].astype(F32)
        self.full[:, self.cols(self.line.z)] = total.astype(BF16)
        for copy in self.back_copies():
            copy.start()

    def result(self):
        for copy in self.back_copies():
            copy.wait()
        return self.full[...].astype(F32)


class Timetable:
    def __init__(self, chips, streams):
        last = chips - 1
        self.chips, self.streams = chips, streams
        steps = [(d * HOP_US, "arrive", d) for d in range(chips)]
        self.compute = last * HOP_US + SIBLING_US
        steps.append((self.compute, "compute", 0))
        first = self.compute + COMPUTE_US + SIBLING_US
        hops = {}
        for place in range(last):
            t = first
            for far in range(last, place, -1):
                if place:
                    t = max(t, hops[place - 1, far] + HOP_US)
                hops[place, far] = t
                steps.append((t, "hop", (place, far)))
                t += LINK_US
        owner = max(hops[far - 1, far] for far in range(1, chips)) + HOP_US
        steps.append((owner, "owner", 0))
        self.turn = max((owner + OWNER_US) / streams, chips * LINK_US)
        self.turns = int(owner / self.turn) + 1
        self.every = 6
        steps += [((i + 0.5) * self.turn / self.every, "beside", i) for i in range(self.every)]
        self.order = []
        for t, what, which in steps:
            behind = int(t / self.turn)
            self.order.append((t - behind * self.turn, -t, what, which, behind))
        self.order.sort(key=lambda step: step[:2])

    def after(self, item):
        return item + int(self.compute / self.turn) + 1


def pipeline(line, times, gather, sums, phases, enter, compute, owner, total, beside):
    last, streams = line.chips - 1, times.streams
    items = phases * streams

    def body(m, carry):
        for _, _, what, which, behind in times.order:
            n = m - behind
            fits = (n >= 0) & (n < items)
            gathers = fits & (n >= streams)
            n = jnp.clip(n, 0, items - 1)
            s = n % streams
            held = jnp.maximum(n - streams, 0)
            if what == "beside":
                beside(m, which)
            elif what == "arrive":

                @pl.when(gathers)
                def _():
                    if which == 0:
                        enter(n)
                        gather.send(held)
                    else:
                        gather.arrive(which, held)

            elif what == "compute":

                @pl.when(gathers)
                def _():
                    for zb in range(line.chips):
                        gather.wait_across(held, zb)
                        sums.drain(s, zb)

                @pl.when(fits)
                def _():
                    compute(n)
                    for zb in range(line.chips):
                        sums.across(s, zb).start()

            elif what == "hop":
                place, far = which

                @pl.when(fits & (line.z == place))
                def _():
                    sums.hop_up(s, far)

                @pl.when(fits & (line.z == last - place))
                def _():
                    sums.hop_down(s, last - far)

            else:

                @pl.when(fits)
                def _():
                    sums.finish(s, total)
                    owner(n)

        return carry

    lax.fori_loop(0, items + times.turns - 1, body, 0)


def frame_mask(segments, places, rows):
    frames = segments.shape[0]
    bits, place_bits = frames.bit_length() - 1, places.bit_length() - 1

    def ids_along(axis, shape):
        index = lax.broadcasted_iota(jnp.int32, shape, axis)
        frame = lax.shift_right_logical(index, place_bits) & (frames - 1)
        segment = jnp.zeros(shape, jnp.int32)
        for i in range(frames):
            segment = jnp.where(frame == i, segments[i], segment)
        block = lax.shift_right_logical(index, place_bits + bits)
        return block * places + (index & (places - 1)), frame, segment

    place_q, frame_q, segment_q = ids_along(0, (rows, 1))
    place_k, frame_k, segment_k = ids_along(1, (1, rows))
    return (place_q == place_k) & (frame_k <= frame_q) & (segment_q == segment_k)


def column_grads(start, left, right, out):
    rows = pl.ds(pl.multiple_of(start, 256), 256)
    out[rows] = mm_tn(left, right.reshape(left.shape[0], right.shape[-1])).astype(BF16)


def row_sum(value):
    return jnp.sum(value, axis=0, keepdims=True)


def moved_exactly(order, value):
    out = None
    for _ in range(3):
        term = value.astype(BF16)
        value = value - term.astype(F32)
        out = mm(order, term) if out is None else out + mm(order, term)
    return out


class Refs:
    def __init__(self, names, refs):
        for name, ref in zip(names, refs, strict=True):
            setattr(self, name, ref)


def block(names, *refs):
    r = Refs(names, refs)
    steps, patches, width = r.x.shape
    streams, rows, _ = r.y.shape
    heads = 2 * r.g_all.shape[1]
    line, t_line = Line(steps), Line(streams)
    chips, frames = line.chips, line.frames
    s_rows = patches // heads
    tokens = steps * s_rows
    columns, hidden = r.s_wout.shape[0], r.up.shape[1]
    entries = r.table.shape[0]
    count = heads * rows
    all_tokens = heads * tokens
    times = Timetable(chips, streams)
    sums = ChainSum(t_line, (r.part, r.sib, r.rise, r.fall, r.out), r.sum_sems)
    gather = Gather(t_line, r.gathered, r.gather_sems)
    last_part = getattr(r, "last_part", r.g_all)
    last_out = getattr(r, "last_out", r.out)
    last_sums = ChainSum(
        line, (last_part, r.last_sib, r.last_rise, r.last_fall, last_out), r.last_sems
    )
    shared = not hasattr(r, "g_src")

    def g_src_at(part, to):
        return r.gathered.at[3 * streams + to] if shared else r.g_src.at[part, to]

    g_swap = Swap(line, g_src_at, r.g_dst, r.g_sems)
    state_swap = Swap(line, lambda s, to: r.state_src.at[s, to], r.state_dst, r.state_sems)
    grad_swap = Swap(line, lambda s, to: r.grad_src.at[s, to], r.grad_dst, r.grad_sems)
    y_swap = Swap(line, lambda s, to: r.y_src.at[s, to], r.y_dst, r.y_sems)
    every = Everyone(
        line,
        (r.every_src, r.every_sib, r.every_line, r.every_frames, r.every_full),
        r.every_sems,
    )
    reduced = frame_sums(
        line,
        [
            (r.down_grad, 0, False), (r.up_grad, 0, True),
            (r.t_q, 0, False), (r.t_k, 0, True), (r.t_v, 0, False), (r.t_out, 1, True),
            (r.s_q, 0, False), (r.s_k, 0, True), (r.s_v, 0, False), (r.s_out, 1, True),
        ],
        r.reduce,
    )
    mlp_sums, t_sums, s_sums = reduced[:2], reduced[2:6], reduced[6:]
    bias_swap = Swap(line, lambda _, to: r.bias_src, r.bias_dst, r.bias_sems)
    line.barrier(True, True)

    def g_out(i, carry):
        rows_of = pl.ds(pl.multiple_of(i * s_rows, s_rows), s_rows)
        moved = mm(r.to_peers[...], r.cotangent[:, rows_of].reshape(tokens, width))
        moved = moved.astype(BF16).astype(r.g_dst.dtype).reshape(frames, tokens // frames, width)
        if shared:
            r.gathered[3 * streams : 4 * streams, i // 2, i % 2] = moved
        else:
            r.g_src[0, :, i // 2, i % 2] = moved
        return carry

    lax.fori_loop(0, heads, g_out, 0)
    g_swap.start(0)

    def g_in(i):
        moved = r.g_dst[0, :, i // 2, i % 2].reshape(tokens, width).astype(BF16)
        moved = mm(r.to_parts[...], moved).astype(BF16)
        r.g_all[:, i // 2, i % 2] = moved.reshape(streams, rows, width)

    table_row = lax.broadcasted_iota(jnp.int32, (entries, width), 0)

    def added(s):
        return row_sum(jnp.where(table_row == r.ids[s], r.table[...].astype(F32), 0.0))

    def norm(value, i):
        scaled = norm_stats(value)[0] * r.gain[i : i + 1, :]
        return (scaled + r.shift[i : i + 1, :]).astype(BF16)

    def attention(s, carry):
        normed = norm(r.x[s].astype(F32) + added(s), 0)
        r.normed0[s] = normed
        q = mm(normed, r.s_wqkv[0]).astype(BF16)
        k = mm(normed, r.s_wqkv[1]).astype(BF16)
        v = mm(normed, r.s_wqkv[2]).astype(BF16)
        r.s_proj[0, s] = q
        r.s_proj[1, s] = k
        r.s_proj[2, s] = v
        r.s_cols[s] = attend(q, k, v, None)
        return carry

    lax.fori_loop(0, steps, attention, 0)

    def to_streams(i, carry):
        rows_of = pl.ds(pl.multiple_of(i * s_rows, s_rows), s_rows)
        moved = mm(r.to_streams[...], r.s_cols[:, rows_of].reshape(tokens, columns)).astype(BF16)
        r.s_mixed[:, i] = moved.reshape(streams, rows, columns)
        return carry

    lax.fori_loop(0, heads, to_streams, 0)
    own_rows = pl.ds(pl.multiple_of(line.h * s_rows, s_rows), s_rows)
    own = mm(r.to_streams[...], r.x[:, own_rows].reshape(tokens, width))
    row = lax.broadcasted_iota(jnp.int32, (tokens, 1), 0)
    frame = lax.shift_right_logical(row, (rows // (frames * steps)).bit_length() - 1) & (steps - 1)
    entry = jnp.zeros_like(row)
    for s in range(steps):
        entry = jnp.where(frame == s, r.ids[s], entry)
    picker = (entry == lax.broadcasted_iota(jnp.int32, (tokens, entries), 1)).astype(BF16)
    own = own + mm(picker, r.table[...])
    r.state0[...] = own.reshape(streams, rows, width)
    r.mask[...] = frame_mask(r.segments, rows // (frames * steps), count).astype(F32)
    r.up_bias_grad[...] = jnp.zeros_like(r.up_bias_grad)
    r.small[...] = jnp.zeros_like(r.small)

    def held(n):
        return n - streams

    def enter_temporal(s, n):
        state_swap.wait(s)
        state = r.state_dst[s].reshape(rows, width)
        r.state1[s] = state
        r.gathered[held(n), line.z, line.c] = norm(state, 1)

    def enter_spatial(s, n):
        grad_swap.wait(s)
        grad = r.grad_dst[s].reshape(rows, width)
        r.grad1[s] = grad
        r.gathered[held(n), line.z, line.c] = grad.astype(BF16)

    def compute_spatial(s, n):
        left = r.s_mixed[s].reshape(count, columns)
        r.part[s] = mm(left, r.s_wout[...]).astype(BF16).reshape(chips, 2, rows, width)

    def compute_temporal(s, n):
        a = r.gathered[held(n)].reshape(count, width)
        q = mm(a, r.t_wqkv[0]).astype(BF16)
        k = mm(a, r.t_wqkv[1]).astype(BF16)
        v = mm(a, r.t_wqkv[2]).astype(BF16)
        r.t_proj[0, s] = q
        r.t_proj[1, s] = k
        r.t_proj[2, s] = v
        mixed = attend(q, k, v, r.mask[...] > 0.0)
        r.t_mixed[s] = mixed
        r.part[s] = mm(mixed, r.t_wout[...]).astype(BF16).reshape(chips, 2, rows, width)

    def compute_mlp(s, n):
        a = r.gathered[held(n)].reshape(count, width)
        g = r.g_all[s].reshape(count, width)
        pre = mm(a, r.up[...]) + r.up_bias[...]
        t = jnp.tanh(GELU_C * (pre + 0.044715 * (pre * pre * pre)))
        act = (0.5 * pre * (1.0 + t)).astype(BF16)
        r.act[s] = act
        slope = 0.5 * (1.0 + t)
        slope = slope + 0.5 * pre * (1.0 - t * t) * (GELU_C * (1.0 + 0.134145 * (pre * pre)))
        dpre = (mm_nt(g, r.down[...]) * slope).astype(BF16)
        r.dpre[s] = dpre
        r.up_bias_grad[:, :hidden] += row_sum(dpre.astype(F32))
        r.part[s] = mm_nt(dpre, r.up[...]).astype(BF16).reshape(chips, 2, rows, width)

    def compute_back(s, n):
        grad = r.gathered[held(n)].reshape(count, width)
        dm = mm_nt(grad, r.t_wout[...]).astype(BF16)
        mask = r.mask[...] > 0.0
        dq, dk, dv = attend_back(r.t_proj[0, s], r.t_proj[1, s], r.t_proj[2, s], mask, dm)
        r.t_dproj[0, s] = dq
        r.t_dproj[1, s] = dk
        r.t_dproj[2, s] = dv
        da = mm_nt(dq, r.t_wqkv[0]) + mm_nt(dk, r.t_wqkv[1]) + mm_nt(dv, r.t_wqkv[2])
        r.part[s] = da.astype(BF16).reshape(chips, 2, rows, width)

    def compute_last(s, n):
        grad = r.gathered[held(n)].reshape(count, width)
        moved = mm_nt(grad, r.s_wout[...]).astype(BF16)
        r.s_dmixed[s] = moved.reshape(heads, rows, columns)
        y = mm(r.act[s], r.down[...])
        r.part[s] = y.astype(BF16).reshape(chips, 2, rows, width)

    def owner_spatial(s, n):
        state = r.state0[s] + r.total[...] + r.bias[0:1, :]
        r.state_src[s] = state.reshape(r.state_src.shape[1:])
        state_swap.start(s)

    def owner_temporal(s, n):
        state = r.state1[s] + r.total[...] + r.bias[1:2, :]
        r.state2[s] = state
        r.gathered[n, line.z, line.c] = norm(state, 2)

    def owner_mlp(s, n):
        grad = r.g_all[s, line.z, line.c].astype(F32)
        back, gain_grad, shift_grad = norm_back(r.state2[s], r.total[...], r.gain[2:3, :])
        dh = grad + back
        r.grad2[s] = dh
        r.gathered[n, line.z, line.c] = dh.astype(BF16)
        r.small[0:1] += gain_grad
        r.small[1:2] += shift_grad
        r.small[2:3] += row_sum(grad)
        r.small[3:4] += row_sum(dh)

    def owner_back(s, n):
        back, gain_grad, shift_grad = norm_back(r.state1[s], r.total[...], r.gain[1:2, :])
        dh = r.grad2[s] + back
        r.grad_src[s] = dh.reshape(r.grad_src.shape[1:])
        grad_swap.start(s)
        r.small[4:5] += gain_grad
        r.small[5:6] += shift_grad
        r.small[6:7] += row_sum(dh)

    def owner_last(s, n):
        r.y[s] = (r.state2[s] + r.total[...] + r.bias[2:3, :]).astype(BF16)

    def by_phase(bodies):
        def run(n):
            for i, one in enumerate(bodies):
                if one is not None:

                    @pl.when(n // streams == i)
                    def _():
                        one(n % streams, n)

        return run

    def down_chunk(i):
        cols = pl.ds(pl.multiple_of(i * 128, 128), 128)
        left = r.act[:, :, cols].reshape(all_tokens, 128)
        right = r.g_all[...].reshape(all_tokens, width)
        mlp_sums[0].part[cols] = mm_tn(left, right).astype(BF16)

    def up_chunk(i):
        cols = pl.ds(pl.multiple_of(i * 256, 256), 256)
        left = r.gathered[streams : 2 * streams, :, :, :, cols].reshape(all_tokens, 256)
        right = r.dpre[...].reshape(all_tokens, hidden)
        mlp_sums[1].part[cols] = mm_tn(left, right).astype(BF16)

    def t_out_chunk(i):
        left = r.t_mixed[...].reshape(all_tokens, columns)
        right = r.gathered[2 * streams : 3 * streams].reshape(all_tokens, width)
        t_sums[3].part[...] = mm_tn(left, right).astype(BF16)

    def t_qkv_chunk(i):
        start = i * 256
        cols = pl.ds(pl.multiple_of(start, 256), 256)
        left = r.gathered[0:streams, :, :, :, cols].reshape(all_tokens, 256)
        for j in range(3):
            column_grads(start, left, r.t_dproj[j], t_sums[j].part)

    def s_cols_chunk(_):
        def from_streams(i, carry):
            rows_of = pl.ds(pl.multiple_of(i * s_rows, s_rows), s_rows)
            moved = mm(r.from_streams[...], r.s_dmixed[:, i].reshape(tokens, columns)).astype(BF16)
            r.s_cols[:, rows_of] = moved.reshape(steps, s_rows, columns)
            return carry

        lax.fori_loop(0, heads, from_streams, 0)

    def s_back_chunk(s):
        dq, dk, dv = attend_back(r.s_proj[0, s], r.s_proj[1, s], r.s_proj[2, s], None, r.s_cols[s])
        r.s_dproj[0, s] = dq
        r.s_dproj[1, s] = dk
        r.s_dproj[2, s] = dv
        da = mm_nt(dq, r.s_wqkv[0]) + mm_nt(dk, r.s_wqkv[1]) + mm_nt(dv, r.s_wqkv[2])
        last_part[s] = da.astype(BF16).reshape(last_part.shape[1:])
        for zb in range(chips):
            last_sums.across(s, zb).start()

    def s_out_chunk(_):
        left = r.s_mixed[...].reshape(all_tokens, columns)
        right = r.gathered[3 * streams : 4 * streams].reshape(all_tokens, width)
        s_sums[3].part[...] = mm_tn(left, right).astype(BF16)

    def bias_chunk(_):
        r.bias_src[...] = jnp.broadcast_to(r.up_bias_grad[...], r.bias_src.shape)
        bias_swap.start(0)

    def g_in_chunk(i):
        @pl.when(i == 0)
        def _():
            g_swap.wait(0)

        g_in(i)

    n_down, n_up = hidden // 128, width // 256
    turn_of = times.after
    mlp_turn, back_turn = turn_of(3 * streams - 1), turn_of(4 * streams - 1)
    last_turn = turn_of(5 * streams - 1)
    chunks = (
        (streams + 1, 0, heads, g_in_chunk),
        (mlp_turn, 0, n_down, down_chunk),
        (mlp_turn, n_down, n_up, up_chunk),
        (mlp_turn, n_down + n_up, 1, bias_chunk),
        (back_turn, 0, 1, t_out_chunk),
        (back_turn, 1, width // 256, t_qkv_chunk),
        (last_turn, 0, 1, s_cols_chunk),
        (last_turn, 1, steps, s_back_chunk),
        (last_turn, 1 + steps, 1, s_out_chunk),
    )
    slots = [i for i in range(times.every) if i % 2 == 1][:3]
    per_turn = 2 * len(slots)
    turns = 5 * streams + times.turns - 1
    stages = reduced[0].stages()
    bits = len(reduced[0].bits)

    def begin_of(turn, number):
        return (turn + number // per_turn) * times.every + times.every - 1

    def moments_of(begin, waits):
        out = [begin]
        for k in range(1, stages):
            half = k if k <= bits else 2 * bits + 1 - k
            out.append(out[-1] + waits[min(half, len(waits)) - 1])
        return out

    moments = (
        (mlp_sums, moments_of(begin_of(mlp_turn, n_down + n_up), MLP_WAITS)),
        (t_sums, moments_of(begin_of(back_turn, 1 + width // 256), T_WAITS)),
    )
    late = [
        (k, sums_of)
        for sums_of, steps_of in moments
        for k, moment in enumerate(steps_of)
        if moment // times.every >= turns
    ]

    def beside(m, i):
        if i in slots:
            for turn, first, number, chunk in chunks:
                which = per_turn * (m - turn) + 2 * slots.index(i) - first
                here = jnp.clip(number - which, 0, 2)

                @pl.when((which > -2) & (which < number))
                def _():
                    def one(j, carry):
                        @pl.when(which + j >= 0)
                        def _():
                            chunk(which + j)

                        return carry

                    lax.fori_loop(0, here, one, 0)

        for sums_of, steps_of in moments:
            for k, moment in enumerate(steps_of):
                if moment % times.every == i and moment // times.every < turns:

                    @pl.when(m == moment // times.every)
                    def _():
                        for one in sums_of:
                            one.stage(k)

    enter = by_phase((None, enter_temporal, None, None, enter_spatial))
    compute = by_phase(
        (compute_spatial, compute_temporal, compute_mlp, compute_back, compute_last)
    )
    owner = by_phase((owner_spatial, owner_temporal, owner_mlp, owner_back, owner_last))
    pipeline(t_line, times, gather, sums, 5, enter, compute, owner, r.total, beside)
    drain_all(t_line, (sums,), streams)

    y = mm(r.from_parts[...], r.y[...].reshape(tokens, width)).astype(BF16)
    r.y_src[0] = y.astype(r.y_src.dtype).reshape(r.y_src.shape[1:])
    y_swap.start(0)

    r.sums0[...] = jnp.zeros_like(r.sums0)

    def small_part(s):
        state = r.x[s].astype(F32) + added(s)
        da = last_part[s].reshape(patches, width).astype(F32)
        back, gain_grad, shift_grad = norm_back(state, da, r.gain[0:1, :])
        r.sums0[0:1] += gain_grad
        r.sums0[1:2] += shift_grad
        r.sums0[8 : 8 + entries] += jnp.where(table_row == r.ids[s], row_sum(back), 0.0)

    room = r.every_src.shape[0]
    filled = 9 + entries

    def small_value(own_grad):
        for s in range(steps):
            here = row_sum(own_grad[s * s_rows : (s + 1) * s_rows])
            r.sums0[8 : 8 + entries] += jnp.where(table_row == r.ids[s], here, 0.0)
        rows_of = [
            r.sums0[0:1], r.small[4:5], r.small[0:1],
            r.sums0[1:2], r.small[5:6], r.small[1:2],
            r.small[6:7], r.small[3:4], r.small[2:3],
            r.sums0[8 : 8 + entries], jnp.zeros((room - filled, width), F32),
        ]
        return jnp.concatenate(rows_of, axis=0)

    def body(t, carry):
        last_sums.hops(t)
        for j in range(3):

            @pl.when(t == j)
            def _():
                for i in range(width // 256):
                    left = r.normed0[:, :, i * 256 : (i + 1) * 256].reshape(all_tokens, 256)
                    column_grads(i * 256, left, r.s_dproj[j], s_sums[j].part)
                s_sums[j].stage(0)
                if j == 0:
                    s_sums[3].stage(0)
                    for k, sums_of in late:
                        for one in sums_of:
                            one.stage(k)

        @pl.when((t >= 3) & (t < 3 + steps))
        def _():
            small_part(t - 3)

        for k in range(1, stages - 1):

            @pl.when(t == LAST_STAGES[min(k, 3) - 1] + 4 * max(k - 3, 0))
            def _():
                for one in s_sums:
                    one.stage(k)

        @pl.when(t == 3 + steps)
        def _():
            grad = r.grad1[...].reshape(tokens, width)
            own_grad = moved_exactly(r.from_streams[...], grad)
            r.state0[...] = own_grad.reshape(r.state0.shape)
            every.over_pair(small_value(own_grad))

        for moment, step in zip(LAST_SMALL, (every.over_line, every.over_frames, every.over_back)):

            @pl.when(t == moment)
            def _():
                step()

        return carry

    bound = steps * (chips - 1) + (chips - 2) * LAG
    bound = max(bound, LAST_SMALL[-1] + 1, LAST_STAGES[2] + 4 * max(stages - 5, 0) + 1)
    lax.fori_loop(0, bound, body, 0)
    for s in range(steps):
        last_sums.finish(s, r.last_total.at[s])
    own_grad = r.state0[...].reshape(tokens, width)
    for s in range(steps):
        state = r.x[s, own_rows].astype(F32) + added(s)
        back, _, _ = norm_back(state, r.last_total[s], r.gain[0:1, :])
        r.grad_res[pl.ds(s * s_rows, s_rows)] = own_grad[s * s_rows : (s + 1) * s_rows] + back
    y_swap.wait(0)
    r.y_res[...] = mm(r.from_peers[...], r.y_dst[0].reshape(tokens, width).astype(BF16)).astype(BF16)
    r.small_res[...] = every.result()
    bias_swap.wait(0)
    up_bias = r.bias_dst[0, 0]
    for i in range(1, frames):
        up_bias = up_bias + r.bias_dst[0, i]
    r.up_bias_res[...] = up_bias
    for one in s_sums:
        one.stage(stages - 1)
    drain_all(line, (last_sums,), steps)
    drain_all(t_line, (gather,), 4 * streams)


def finish(
    t_q, t_k, t_v, t_out, s_q, s_k, s_v, s_out, up, down, y, grad, small, up_bias,
    y_res, grad_res, table_res, gain_res, shift_res, s_qkv_res, s_out_res, t_qkv_res, t_out_res,
    bias_res, up_res, up_bias_res, down_res,
):
    for parts, res in (((t_q, t_k, t_v), t_qkv_res), ((s_q, s_k, s_v), s_qkv_res)):
        for i, part in enumerate(parts):
            res[i] = part[...].astype(F32)
    t_out_res[...] = t_out[...].astype(F32)
    s_out_res[...] = s_out[...].astype(F32)
    up_res[...] = up[...].astype(F32)
    down_res[...] = down[...].astype(F32)
    y_res[...] = y[...]
    grad_res[...] = grad[...]

    @pl.when(pl.program_id(0) == 0)
    def _():
        gain_res[...] = small[0:3]
        shift_res[...] = small[3:6]
        bias_res[...] = small[6:9]
        table_res[...] = small[9 : 9 + table_res.shape[0]]
        up_bias_res[...] = up_bias[0:1, : up_bias_res.shape[1]]


def results(values, entries, hidden):
    grid = 4

    def blocks(shape, sliced=True):
        axis = len(shape) - 2
        block = list(shape)
        if sliced:
            block[axis] //= grid
        place = [0] * len(shape)

        def index(i):
            at = list(place)
            if sliced:
                at[axis] = i
            return tuple(at)

        return pl.BlockSpec(tuple(block), index)

    t_q, _, _, t_out, _, _, _, _, g_up, g_down, y, grad, small, up_bias = values
    width = g_up.shape[0]
    qkv = ((3,) + t_q.shape, F32, True)
    out = (t_out.shape, F32, True)
    few = ((3, width), F32, False)
    outs = [
        (y.shape, BF16, True), (grad.shape, F32, True), ((entries, width), F32, False), few, few,
        qkv, out, qkv, out, few,
        (g_up.shape, F32, True), ((1, hidden), F32, False), (g_down.shape, F32, True),
    ]
    return pl.pallas_call(
        finish,
        name="finish",
        grid=(grid,),
        out_shape=[jax.ShapeDtypeStruct(shape, kind) for shape, kind, _ in outs],
        in_specs=[blocks(v.shape, v is not small and v is not up_bias) for v in values],
        out_specs=[blocks(shape, sliced) for shape, _, sliced in outs],
    )(*values)


def orders(frames_local, frames, places, streams):
    tokens = frames_local * frames * places
    index = np.arange(tokens).reshape(frames_local, frames, streams, places // streams)
    to_streams = index.transpose(2, 1, 0, 3).reshape(-1)
    to_peers = index.transpose(1, 0, 2, 3).reshape(-1)
    index = np.arange(tokens).reshape(frames * frames_local, streams, places // streams)
    to_parts = index.transpose(1, 0, 2).reshape(-1)
    eye = np.eye(tokens, dtype=np.float32)
    there = [eye[order] for order in (to_streams, to_peers, to_parts)]
    back = [m.T for m in there]
    names = ("to_streams", "to_peers", "to_parts", "from_streams", "from_peers", "from_parts")
    return {name: jnp.asarray(m, BF16) for name, m in zip(names, there + back)}


def on_device(
    block_input,
    action_ids,
    segment_ids,
    action_table,
    norm_gain,
    norm_shift,
    spatial_qkv,
    spatial_out,
    temporal_qkv,
    temporal_out,
    out_bias,
    up_weight,
    up_bias,
    down_weight,
    cotangent,
):
    frames, heads = lax.axis_size("frames"), lax.axis_size("heads")
    chips = heads // 2
    steps, patches, width = block_input.shape
    rows = patches // heads
    tokens = steps * rows
    total_frames = segment_ids.shape[0]
    places = rows // frames
    streams = min(4, places)
    t_rows = tokens // streams
    columns = spatial_out.shape[0]
    hidden = up_weight.shape[1]
    entries = action_table.shape[0]
    count = heads * t_rows
    room = -(-(10 + entries) // 16) * 16
    args = dict(
        ids=action_ids,
        segments=segment_ids,
        x=block_input,
        cotangent=cotangent,
        table=action_table,
        gain=norm_gain,
        shift=norm_shift,
        bias=out_bias,
        s_wqkv=spatial_qkv.transpose(1, 0, 2),
        s_wout=spatial_out,
        t_wqkv=temporal_qkv.transpose(1, 0, 2),
        t_wout=temporal_out,
        up=up_weight,
        up_bias=up_bias.reshape(1, hidden),
        down=down_weight,
        **orders(steps, frames, places, streams),
    )
    qkv, out = (width, columns), (columns, width)
    down, up = (hidden, width), (width, hidden)
    outs = dict(
        t_q=(qkv, BF16),
        t_k=(qkv, BF16),
        t_v=(qkv, BF16),
        t_out=(out, BF16),
        s_q=(qkv, BF16),
        s_k=(qkv, BF16),
        s_v=(qkv, BF16),
        s_out=(out, BF16),
        up_grad=(up, BF16),
        down_grad=(down, BF16),
        y_res=((tokens, width), BF16),
        grad_res=((tokens, width), F32),
        small_res=((room, width), F32),
        up_bias_res=((8, width), F32),
    )
    s_all = (steps, chips, 2, rows, width)
    t_all = (streams, chips, 2, t_rows, width)
    s_one, t_one = (steps, chips, rows, width), (streams, chips, t_rows, width)
    owned = (streams, t_rows, width)
    swapped = (streams, frames, t_rows // frames, width)
    whole = (1, frames, tokens // frames, width)
    g_part = (1, frames, chips, 2, tokens // frames, width)

    def kind_of(shape):
        return BF16 if shape[-2] % 16 == 0 else F32

    cols = dict(
        s_cols=(steps, patches, columns),
        s_proj=(3, steps, patches, columns),
        s_dproj=(3, steps, patches, columns),
        s_mixed=(streams, heads, t_rows, columns),
        s_dmixed=(streams, heads, t_rows, columns),
        t_proj=(3, streams, count, columns),
        t_dproj=(3, streams, count, columns),
        t_mixed=(streams, count, columns),
        act=(streams, count, hidden),
        dpre=(streams, count, hidden),
        normed0=(steps, patches, width),
        gathered=(4 * streams,) + t_all[1:],
        g_all=t_all,
        part=t_all,
        sib=t_one,
        rise=t_one,
        fall=t_one,
        out=t_one,
        **({} if s_all == t_all else dict(last_part=s_all, last_out=s_one)),
        last_sib=s_one,
        last_rise=s_one,
        last_fall=s_one,
        y=owned,
    )
    floats = dict(
        state0=owned,
        state1=owned,
        state2=owned,
        grad1=owned,
        grad2=owned,
        total=(t_rows, width),
        last_total=(steps, rows, width),
        mask=(count, count),
        small=(8, width),
        sums0=(8 + entries, width),
        up_bias_grad=(1, width),
        state_src=swapped,
        state_dst=swapped,
        grad_src=swapped,
        grad_dst=swapped,
    )
    scratch = {name: pltpu.VMEM(shape, BF16) for name, shape in cols.items()}
    scratch |= {name: pltpu.VMEM(shape, F32) for name, shape in floats.items()}
    moving = ("g_dst",) if g_part[1:] == t_all else ("g_src", "g_dst")
    scratch |= {name: pltpu.VMEM(g_part, kind_of(g_part)) for name in moving}
    scratch |= {name: pltpu.VMEM(whole, kind_of(whole)) for name in ("y_src", "y_dst")}
    every_shape = (room, width)
    scratch |= dict(
        every_src=pltpu.VMEM(every_shape, BF16),
        every_sib=pltpu.VMEM(every_shape, BF16),
        every_line=pltpu.VMEM((chips, room, width // chips), BF16),
        every_frames=pltpu.VMEM((frames, room, width // chips), BF16),
        every_full=pltpu.VMEM(every_shape, BF16),
        every_sems=[pltpu.SemaphoreType.DMA((2 * chips + frames,))] * 2,
        bias_src=pltpu.VMEM((8, width), F32),
        bias_dst=pltpu.VMEM((1, frames, 8, width), F32),
        bias_sems=[pltpu.SemaphoreType.DMA((1, frames))] * 2,
        sum_sems=[pltpu.SemaphoreType.DMA((streams, chips))] * 5,
        last_sems=[pltpu.SemaphoreType.DMA((steps, chips))] * 5,
        gather_sems=[pltpu.SemaphoreType.DMA((4 * streams, chips))] * 5,
        state_sems=[pltpu.SemaphoreType.DMA((streams, frames))] * 2,
        grad_sems=[pltpu.SemaphoreType.DMA((streams, frames))] * 2,
        g_sems=[pltpu.SemaphoreType.DMA((1, frames))] * 2,
        y_sems=[pltpu.SemaphoreType.DMA((1, frames))] * 2,
        reduce=[
            x
            for shape, dim in ((down, 0), (up, 0)) + 2 * (((qkv, 0),) * 3 + ((out, 1),))
            for x in frame_sum_scratch(frames, shape, dim)
        ],
    )
    names = tuple(args) + tuple(outs) + tuple(scratch)
    parts = pl.pallas_call(
        lambda *refs: block(names, *refs),
        name="block",
        out_shape=[jax.ShapeDtypeStruct(shape, kind) for shape, kind in outs.values()],
        in_specs=[
            pl.BlockSpec(memory_space=pltpu.SMEM if name in ("ids", "segments") else pltpu.VMEM)
            for name in args
        ],
        out_specs=[pl.BlockSpec(memory_space=pltpu.VMEM)] * len(outs),
        scratch_shapes=list(scratch.values()),
        compiler_params=pltpu.CompilerParams(
            collective_id=0, has_side_effects=True, vmem_limit_bytes=VMEM_LIMIT
        ),
    )(*args.values())
    found = dict(zip(outs, parts))
    (
        block_output, input_grad, table_grad, gain_grad, shift_grad, s_qkv_grad, s_out_grad,
        t_qkv_grad, t_out_grad, bias_grad, up_grad, up_bias_grad, down_grad,
    ) = results(list(found.values()), entries, hidden)
    s_blocks = (steps, rows, width)
    return (
        block_output.reshape(s_blocks),
        input_grad.reshape(s_blocks),
        table_grad,
        gain_grad,
        shift_grad,
        s_qkv_grad.transpose(1, 0, 2),
        s_out_grad,
        t_qkv_grad.transpose(1, 0, 2),
        t_out_grad,
        bias_grad,
        up_grad,
        up_bias_grad.reshape(hidden),
        down_grad,
    )


def solution(mesh):
    return jax.shard_map(
        on_device,
        mesh=mesh,
        in_specs=(
            P("frames", None, None),
            P("frames"),
            P(),
            P(),
            P(),
            P(),
            P(None, None, "heads"),
            P("heads", None),
            P(None, None, "heads"),
            P("heads", None),
            P(),
            P(None, "heads"),
            P("heads"),
            P("heads", None),
            P("frames", None, None),
        ),
        out_specs=(
            P("frames", "heads", None),
            P("frames", "heads", None),
            P(),
            P(),
            P(),
            P(None, None, "heads"),
            P("heads", None),
            P(None, None, "heads"),
            P("heads", None),
            P(),
            P(None, "heads"),
            P("heads"),
            P("heads", None),
        ),
        check_vma=False,
    )
```

```python
import jax
import jax.numpy as jnp
import numpy as np
from jax import lax
from jax.experimental import pallas as pl
from jax.experimental.pallas import tpu as pltpu
from jax.sharding import PartitionSpec as P

HD = 64
SCALE = HD**-0.5
EPS = 1e-05
MASKED = -1000000000.0
F32 = jnp.float32
BF16 = jnp.bfloat16
MESH = pl.DeviceIdType.MESH
MLP_RESULTS = ("down_grad", "up_grad")
T_RESULTS = ("t_q", "t_k", "t_v", "t_out")
S_RESULTS = ("s_q", "s_k", "s_v", "s_out")
VMEM_LIMIT = 62 * 1024 * 1024
GELU_C = float(np.sqrt(2.0 / np.pi))
LAG = 2
MLP_WAITS = (13, 8)
T_WAITS = (9, 6)
LAST_STAGES = (8, 11, 14)
LAST_SMALL = (9, 12, 15)
HOP_US, SIBLING_US, COMPUTE_US, LINK_US, OWNER_US, SWAP_US = 3.4, 1.0, 1.6, 1.45, 0.6, 4.0


def mm(a, b):
    return lax.dot_general(a, b, (((1,), (0,)), ((), ())), preferred_element_type=F32)


def mm_nt(a, b):
    return lax.dot_general(a, b, (((1,), (1,)), ((), ())), preferred_element_type=F32)


def mm_tn(a, b):
    return lax.dot_general(a, b, (((0,), (0,)), ((), ())), preferred_element_type=F32)


def norm_stats(value):
    centered = value - jnp.mean(value, axis=-1, keepdims=True)
    inv = lax.rsqrt(jnp.mean(centered * centered, axis=-1, keepdims=True) + EPS)
    return centered * inv, inv


def norm_back(value, grad, gain):
    normed, inv = norm_stats(value)
    e = grad * gain
    first = jnp.mean(e, axis=-1, keepdims=True)
    second = jnp.mean(e * normed, axis=-1, keepdims=True)
    gain_grad = jnp.sum(grad * normed, axis=0, keepdims=True)
    shift_grad = jnp.sum(grad, axis=0, keepdims=True)
    return (e - first - normed * second) * inv, gain_grad, shift_grad


def head_lanes(shape, head):
    lane = lax.broadcasted_iota(jnp.int32, shape, 1)
    return (lane >= head * HD) & (lane < (head + 1) * HD)


def softmax_of(q, k, mask):
    scores = mm_nt(q, k) * SCALE
    if mask is not None:
        scores = jnp.where(mask, scores, MASKED)
    raised = jnp.exp(scores - jnp.max(scores, axis=-1, keepdims=True))
    return raised / jnp.sum(raised, axis=-1, keepdims=True)


def attend(q, k, v, mask):
    heads = q.shape[1] // HD
    mixed = None
    for head in range(heads):
        lanes = head_lanes(q.shape, head)
        probs = softmax_of(jnp.where(lanes, q, jnp.zeros_like(q)), k, mask).astype(BF16)
        out = mm(probs, v)
        mixed = out if mixed is None else jnp.where(lanes, out, mixed)
    return mixed.astype(BF16)


def attend_back(q, k, v, mask, grad):
    heads = q.shape[1] // HD
    dq = dk = dv = None
    for head in range(heads):
        lanes = head_lanes(q.shape, head)
        qh = jnp.where(lanes, q, jnp.zeros_like(q))
        gh = jnp.where(lanes, grad, jnp.zeros_like(grad))
        probs = softmax_of(qh, k, mask)
        dvh = mm_tn(probs.astype(BF16), gh)
        dp = mm_nt(gh, v)
        ds = (probs * (dp - jnp.sum(dp * probs, axis=-1, keepdims=True))).astype(BF16)
        dqh = mm(ds, k) * SCALE
        dkh = mm_tn(ds, qh) * SCALE
        if head == 0:
            dq, dk, dv = dqh, dkh, dvh
        else:
            dq = jnp.where(lanes, dqh, dq)
            dk = dk + dkh
            dv = dv + dvh
    return dq.astype(BF16), dk.astype(BF16), dv.astype(BF16)


class Line:
    def __init__(self, steps):
        self.frames = lax.axis_size("frames")
        self.heads = lax.axis_size("heads")
        self.chips = self.heads // 2
        self.f = lax.axis_index("frames")
        self.h = lax.axis_index("heads")
        self.z = self.h // 2
        self.c = self.h % 2
        self.steps = steps

    def at(self, z):
        return (self.f, jnp.clip(z, 0, self.chips - 1) * 2 + self.c)

    def sibling(self):
        return (self.f, self.z * 2 + 1 - self.c)

    def barrier(self, over_frames, whole_line=False):
        sem = pltpu.get_barrier_semaphore()

        def greet(device):
            pl.semaphore_signal(sem, inc=1, device_id=device, device_id_type=MESH)

        greet(self.sibling())
        count = 1
        if over_frames:
            for k in range(1, self.frames):
                greet(((self.f + k) % self.frames, self.h))
            count += self.frames - 1
        if whole_line:
            for k in range(1, self.chips):
                greet(self.at((self.z + k) % self.chips))
            count += self.chips - 1
        else:

            @pl.when(self.z > 0)
            def _():
                greet(self.at(self.z - 1))

            @pl.when(self.z < self.chips - 1)
            def _():
                greet(self.at(self.z + 1))

            count = count + (self.z > 0).astype(jnp.int32)
            count = count + (self.z < self.chips - 1).astype(jnp.int32)
        pl.semaphore_wait(sem, count)

    def copy(self, src, dst, send, recv, device):
        return pltpu.make_async_remote_copy(
            src_ref=src,
            dst_ref=dst,
            send_sem=send,
            recv_sem=recv,
            device_id=device,
            device_id_type=MESH,
        )


class Gather:
    def __init__(self, line, buf, sems):
        self.line, self.buf = line, buf
        self.got, self.got_sib, self.sent_up, self.sent_down, self.sent_sib = sems

    def up(self, s, zb):
        ln = self.line
        ref = self.buf.at[s, zb, ln.c]
        return ln.copy(ref, ref, self.sent_up.at[s, zb], self.got.at[s, zb], ln.at(ln.z + 1))

    def down(self, s, zb):
        ln = self.line
        ref = self.buf.at[s, zb, ln.c]
        return ln.copy(ref, ref, self.sent_down.at[s, zb], self.got.at[s, zb], ln.at(ln.z - 1))

    def across(self, s, zb):
        ln = self.line
        ref = self.buf.at[s, zb, ln.c]
        return ln.copy(ref, ref, self.sent_sib.at[s, zb], self.got_sib.at[s, zb], ln.sibling())

    def wait_across(self, s, zb):
        ln = self.line
        ref = self.buf.at[s, zb, 1 - ln.c]
        ln.copy(
            ref, ref, self.sent_sib.at[s, zb], self.got_sib.at[s, zb], ln.sibling()
        ).wait_recv()

    def send(self, s):
        ln = self.line

        @pl.when(ln.z < ln.chips - 1)
        def _():
            self.up(s, ln.z).start()

        @pl.when(ln.z > 0)
        def _():
            self.down(s, ln.z).start()

        self.across(s, ln.z).start()

    def start(self, own):
        ln = self.line
        for s in range(ln.steps):
            self.buf[s, ln.z, ln.c] = own[s]
            self.send(s)

    def arrive(self, distance, s):
        ln = self.line
        below, above = ln.z - distance, ln.z + distance

        @pl.when((distance > 0) & (below >= 0))
        def _():
            self.up(s, below).wait_recv()

            @pl.when(ln.z < ln.chips - 1)
            def _():
                self.up(s, below).start()

            self.across(s, below).start()

        @pl.when((distance > 0) & (above < ln.chips))
        def _():
            self.down(s, above).wait_recv()

            @pl.when(ln.z > 0)
            def _():
                self.down(s, above).start()

            self.across(s, above).start()

    def drain(self, s, zb):
        ln = self.line

        @pl.when((zb <= ln.z) & (ln.z < ln.chips - 1))
        def _():
            self.up(s, zb).wait_send()

        @pl.when((zb >= ln.z) & (ln.z > 0))
        def _():
            self.down(s, zb).wait_send()

        self.across(s, zb).wait_send()


class ChainSum:
    def __init__(self, line, bufs, sems):
        self.line = line
        self.part, self.sib, self.rise, self.fall, self.out = bufs
        self.sent_sib, self.got_sib, self.got_up, self.got_down, self.sent = sems

    def across(self, s, zb):
        ln = self.line
        return ln.copy(
            self.part.at[s, zb, 1 - ln.c],
            self.sib.at[s, zb],
            self.sent_sib.at[s, zb],
            self.got_sib.at[s, zb],
            ln.sibling(),
        )

    def up(self, s, o):
        ln = self.line
        return ln.copy(
            self.out.at[s, o],
            self.rise.at[s, o],
            self.sent.at[s, o],
            self.got_up.at[s, o],
            ln.at(ln.z + 1),
        )

    def down(self, s, o):
        ln = self.line
        return ln.copy(
            self.out.at[s, o],
            self.fall.at[s, o],
            self.sent.at[s, o],
            self.got_down.at[s, o],
            ln.at(ln.z - 1),
        )

    def mine(self, s, o):
        return self.part[s, o, self.line.c].astype(F32) + self.sib[s, o].astype(F32)

    def hop_up(self, s, o):
        ln = self.line
        self.across(s, o).wait_recv()

        @pl.when(ln.z == 0)
        def _():
            self.out[s, o] = self.mine(s, o).astype(BF16)

        @pl.when(ln.z > 0)
        def _():
            self.up(s, o).wait_recv()
            self.out[s, o] = (self.mine(s, o) + self.rise[s, o].astype(F32)).astype(BF16)

        self.up(s, o).start()

    def hop_down(self, s, o):
        ln = self.line
        self.across(s, o).wait_recv()

        @pl.when(ln.z == ln.chips - 1)
        def _():
            self.out[s, o] = self.mine(s, o).astype(BF16)

        @pl.when(ln.z < ln.chips - 1)
        def _():
            self.down(s, o).wait_recv()
            self.out[s, o] = (self.mine(s, o) + self.fall[s, o].astype(F32)).astype(BF16)

        self.down(s, o).start()

    def hops(self, t, part=None, fits=True):
        ln = self.line
        last = ln.chips - 1
        for upward in (True, False):
            place = ln.z if upward else last - ln.z
            q = t - place * LAG
            if part is None:
                turn = jnp.maximum(q, 0) // ln.steps
                s = jnp.maximum(q, 0) % ln.steps
            else:
                turn, s = jnp.maximum(q, 0), part
            far = jnp.clip(last - turn, 0, last)
            ok = (q >= 0) & (turn < last) & (far > place) & fits
            o = far if upward else last - far

            @pl.when(ok)
            def _():
                if upward:
                    self.hop_up(s, o)
                else:
                    self.hop_down(s, o)

    def finish(self, s, total):
        ln = self.line
        self.across(s, ln.z).wait_recv()
        total[...] = self.mine(s, ln.z)

        @pl.when(ln.z > 0)
        def _():
            self.up(s, ln.z).wait_recv()
            total[...] += self.rise[s, ln.z].astype(F32)

        @pl.when(ln.z < ln.chips - 1)
        def _():
            self.down(s, ln.z).wait_recv()
            total[...] += self.fall[s, ln.z].astype(F32)

    def drain(self, s, zb):
        ln = self.line
        self.across(s, zb).wait_send()

        @pl.when(zb != ln.z)
        def _():
            self.up(s, zb).wait_send()


def drain_all(line, things, parts):
    def body(i, carry):
        for thing in things:
            thing.drain(i // line.chips, i % line.chips)
        return carry

    lax.fori_loop(0, parts * line.chips, body, 0)


class Swap:
    def __init__(self, line, src_at, dst, sems):
        self.line, self.src_at, self.dst = line, src_at, dst
        self.sent, self.got = sems

    def copy(self, part, k):
        ln = self.line
        to = (ln.f + k) % ln.frames
        return ln.copy(
            self.src_at(part, to),
            self.dst.at[part, ln.f],
            self.sent.at[part, k],
            self.got.at[part, k],
            (to, ln.h),
        )

    def start(self, part):
        ln = self.line
        for k in range(1, ln.frames):
            self.copy(part, k).start()
        self.dst[part, ln.f] = self.src_at(part, ln.f)[...]

    def wait(self, part):
        for k in range(1, self.line.frames):
            self.copy(part, k).wait()


class FrameSum:
    def __init__(self, line, part, full, dim, reverse, recv_bufs, sems):
        self.line, self.part, self.full, self.dim = line, part, full, dim
        self.recv_bufs = recv_bufs
        self.sent, self.got, self.sent_back, self.got_back = sems
        bits = range(line.frames.bit_length() - 1)
        self.bits = list(reversed(bits)) if reverse else list(bits)
        self.spans = []
        start, size = 0, part.shape[dim]
        for bit in self.bits:
            size //= 2
            side = (line.f // (1 << bit)) % 2
            peer = (line.f + (1 - 2 * side) * (1 << bit), line.h)
            keep, give = start + side * size, start + (1 - side) * size
            self.spans.append((keep, give, size, peer))
            start = keep

    def view(self, ref, start, size):
        if self.dim == 0:
            return ref.at[pl.ds(pl.multiple_of(start, size), size)]
        return ref.at[:, pl.ds(pl.multiple_of(start, size), size)]

    def out(self, i):
        _, give, size, peer = self.spans[i]
        src = self.view(self.part, give, size)
        return self.line.copy(src, self.recv_bufs[i], self.sent.at[i], self.got.at[i], peer)

    def back(self, i):
        keep, _, size, peer = self.spans[i]
        ref = self.view(self.full, keep, size)
        return self.line.copy(ref, ref, self.sent_back.at[i], self.got_back.at[i], peer)

    def back_in(self, i):
        _, give, size, peer = self.spans[i]
        ref = self.view(self.full, give, size)
        return self.line.copy(ref, ref, self.sent_back.at[i], self.got_back.at[i], peer)

    def stages(self):
        return 2 * len(self.bits) + 1

    def stage(self, k):
        n = len(self.bits)
        if 1 <= k <= n:
            keep, _, size, _ = self.spans[k - 1]
            self.out(k - 1).wait()
            ref = self.view(self.part, keep, size)
            to = self.view(self.full, keep, size) if k == n else ref
            to[...] = (ref[...].astype(F32) + self.recv_bufs[k - 1][...].astype(F32)).astype(BF16)
        elif k > n:
            i = 2 * n - k
            self.back(i).wait_send()
            self.back_in(i).wait_recv()
        if k < n:
            self.out(k).start()
        elif k < 2 * n:
            self.back(2 * n - 1 - k).start()


def frame_sum_scratch(frames, shape, dim):
    bits = frames.bit_length() - 1
    scratch = []
    for i in range(bits):
        part = list(shape)
        part[dim] = shape[dim] >> (i + 1)
        scratch.append(pltpu.VMEM(tuple(part), BF16))
    return [pltpu.VMEM(shape, BF16)] + scratch + [pltpu.SemaphoreType.DMA((bits,))] * 4


def frame_sums(line, arrays, scratch):
    bits = line.frames.bit_length() - 1
    sums = []
    for full, dim, reverse in arrays:
        part, *mine = scratch[: bits + 5]
        scratch = scratch[bits + 5 :]
        sums.append(FrameSum(line, part, full, dim, reverse, mine[:bits], mine[bits:]))
    return sums


class Everyone:
    def __init__(self, line, refs, sems):
        self.line = line
        self.src, self.dst_sib, self.dst_line, self.dst_frames, self.full = refs
        self.sent, self.got = sems
        self.share = self.src.shape[1] // line.chips

    def cols(self, z):
        return pl.ds(pl.multiple_of(z * self.share, self.share), self.share)

    def pair_copy(self):
        ln = self.line
        return ln.copy(self.src, self.dst_sib, self.sent.at[0], self.got.at[0], ln.sibling())

    def line_copies(self):
        ln, copies = self.line, []
        for k in range(1, ln.chips):
            to = (ln.z + k) % ln.chips
            src, dst = self.dst_sib.at[:, self.cols(to)], self.dst_line.at[ln.z]
            copies.append(ln.copy(src, dst, self.sent.at[k], self.got.at[k], ln.at(to)))
        return copies

    def frame_copies(self):
        ln, copies = self.line, []
        for k in range(1, ln.frames):
            to, i = ((ln.f + k) % ln.frames, ln.h), ln.chips + k
            src, dst = self.dst_line.at[ln.z], self.dst_frames.at[ln.f]
            copies.append(ln.copy(src, dst, self.sent.at[i], self.got.at[i], to))
        return copies

    def back_copies(self):
        ln, copies = self.line, []
        for k in range(1, ln.chips):
            to, i = ln.at((ln.z + k) % ln.chips), ln.chips + ln.frames + k
            ref = self.full.at[:, self.cols(ln.z)]
            copies.append(ln.copy(ref, ref, self.sent.at[i], self.got.at[i], to))
        return copies

    def over_pair(self, value):
        self.src[...] = value.astype(BF16)
        self.pair_copy().start()

    def over_line(self):
        self.pair_copy().wait()
        pair = self.src[...].astype(F32) + self.dst_sib[...].astype(F32)
        self.dst_sib[...] = pair.astype(BF16)
        for copy in self.line_copies():
            copy.start()

    def over_frames(self):
        ln = self.line
        for copy in self.line_copies():
            copy.wait()
        total = self.dst_sib[:, self.cols(ln.z)].astype(F32)
        for k in range(1, ln.chips):
            total = total + self.dst_line[(ln.z + k) % ln.chips].astype(F32)
        self.dst_line[ln.z] = total.astype(BF16)
        for copy in self.frame_copies():
            copy.start()
        self.dst_frames[ln.f] = self.dst_line[ln.z]

    def over_back(self):
        for copy in self.frame_copies():
            copy.wait()
        total = self.dst_frames[0].astype(F32)
        for i in range(1, self.line.frames):
            total = total + self.dst_frames[i].astype(F32)
        self.full[:, self.cols(self.line.z)] = total.astype(BF16)
        for copy in self.back_copies():
            copy.start()

    def result(self):
        for copy in self.back_copies():
            copy.wait()
        return self.full[...].astype(F32)


class Timetable:
    PHASES = 5

    def __init__(self, chips, streams):
        self.chips, self.streams = chips, streams
        last = chips - 1
        arrivals = [(d * HOP_US, "arrive", d) for d in range(chips)]
        gathered = last * HOP_US + SIBLING_US
        first = self.sum_steps(0.0)
        middle = self.sum_steps(gathered)
        self.turn = max((middle[-1][0] + OWNER_US) / streams, chips * LINK_US)
        period = self.turn * streams
        second = max(HOP_US, SIBLING_US + COMPUTE_US + SIBLING_US)
        y = self.sum_steps(second - COMPUTE_US - SIBLING_US)
        leads = [0.0, first[-1][0] + OWNER_US + SWAP_US - period]
        leads.append(leads[1] + max(middle[-1][0] + OWNER_US + SWAP_US - period, 0.0))
        groups = (
            (0, 0, leads[0], first),
            (1, 3, leads[1], arrivals + middle),
            (4, 4, leads[2], arrivals + [(gathered, "gathered", 0)] + y),
        )
        self.every = 6
        self.order = []
        for i in range(self.every):
            at = (i + 0.5) * self.turn / self.every
            self.order.append((at, 0.0, "beside", i, 0, 0, 0))
        self.computed = {}
        self.turns = 0
        for low, high, lead, steps in groups:
            for t, what, which in steps:
                t += lead
                behind = int(np.floor(t / self.turn))
                at = t - behind * self.turn
                self.order.append((at, -t, what, which, behind, low, high))
                if what == ("gathered" if low == 4 else "compute"):
                    self.computed |= {phase: behind for phase in range(low, high + 1)}
                self.turns = max(self.turns, (high + 1) * streams + behind)
        self.order.sort(key=lambda step: step[:2])

    def sum_steps(self, compute):
        last = self.chips - 1
        steps = [(compute, "compute", 0)]
        start = compute + COMPUTE_US + SIBLING_US
        hops = {}
        for place in range(last):
            t = start
            for far in range(last, place, -1):
                if place:
                    t = max(t, hops[place - 1, far] + HOP_US)
                hops[place, far] = t
                steps.append((t, "hop", (place, far)))
                t += LINK_US
        owner = max(hops[far - 1, far] for far in range(1, self.chips)) + HOP_US
        return steps + [(owner, "owner", 0)]

    def after(self, item):
        return item + self.computed[item // self.streams] + 1


def pipeline(line, times, turns, gather, sums, enter, compute, gathered, owner, total, beside):
    last, streams = line.chips - 1, times.streams

    def body(m, carry):
        for _, _, what, which, behind, low, high in times.order:
            if what == "beside":
                beside(m, which)
                continue
            n = m - behind
            fits = (n >= low * streams) & (n < (high + 1) * streams)
            n = jnp.clip(n, low * streams, (high + 1) * streams - 1)
            s = n % streams
            held = n - streams
            if what == "hop":
                place, far = which

                @pl.when(fits & (line.z == place))
                def _():
                    sums.hop_up(s, far)

                @pl.when(fits & (line.z == last - place))
                def _():
                    sums.hop_down(s, last - far)

                continue

            @pl.when(fits)
            def _():
                if what == "arrive":
                    if which == 0:
                        enter(n)
                        gather.send(held)
                    else:
                        gather.arrive(which, held)
                elif what == "compute":
                    if low == 4:
                        gather.wait_across(held, line.z)
                    for zb in range(line.chips):
                        if 1 <= low <= 3:
                            gather.wait_across(held, zb)
                        if low:
                            sums.drain(s, zb)
                    compute(n, low, high)
                    for zb in range(line.chips):
                        sums.across(s, zb).start()
                elif what == "gathered":
                    for zb in range(line.chips):

                        @pl.when(line.z != zb)
                        def _():
                            gather.wait_across(held, zb)

                    gathered(n)
                else:
                    sums.finish(s, total)
                    owner(n, low, high)

        return carry

    lax.fori_loop(0, turns, body, 0)


def frame_mask(segments, places, rows):
    frames = segments.shape[0]
    bits, place_bits = frames.bit_length() - 1, places.bit_length() - 1

    def ids_along(axis, shape):
        index = lax.broadcasted_iota(jnp.int32, shape, axis)
        frame = lax.shift_right_logical(index, place_bits) & (frames - 1)
        segment = jnp.zeros(shape, jnp.int32)
        for i in range(frames):
            segment = jnp.where(frame == i, segments[i], segment)
        block = lax.shift_right_logical(index, place_bits + bits)
        return block * places + (index & (places - 1)), frame, segment

    place_q, frame_q, segment_q = ids_along(0, (rows, 1))
    place_k, frame_k, segment_k = ids_along(1, (1, rows))
    return (place_q == place_k) & (frame_k <= frame_q) & (segment_q == segment_k)


def column_grads(start, left, right, out):
    rows = pl.ds(pl.multiple_of(start, 256), 256)
    out[rows] = mm_tn(left, right.reshape(left.shape[0], right.shape[-1])).astype(BF16)


def row_sum(value):
    return jnp.sum(value, axis=0, keepdims=True)


def moved_exactly(order, value):
    out = None
    for _ in range(3):
        term = value.astype(BF16)
        value = value - term.astype(F32)
        out = mm(order, term) if out is None else out + mm(order, term)
    return out


class Refs:
    def __init__(self, names, refs):
        for name, ref in zip(names, refs, strict=True):
            setattr(self, name, ref)


def block(fetched, results, names, *refs):
    ends = len(fetched), len(fetched) + len(results)
    r = Refs(names, refs[ends[1] :])
    r.fetched = dict(zip(fetched, refs))
    r.stored = dict(zip(results, refs[ends[0] :]))
    r.ids, r.segments = r.fetched.pop("ids"), r.fetched.pop("segments")
    steps, patches, width = r.x.shape
    streams, rows, _ = r.y.shape
    heads = 2 * r.g_all.shape[1]
    line, t_line = Line(steps), Line(streams)
    chips, frames = line.chips, line.frames
    s_rows = patches // heads
    tokens = steps * s_rows
    columns, hidden = r.s_wout.shape[0], r.up.shape[1]
    entries = r.table.shape[0]
    count = heads * rows
    all_tokens = heads * tokens
    times = Timetable(chips, streams)
    sums = ChainSum(t_line, (r.part, r.sib, r.rise, r.fall, r.out), r.sum_sems)
    gather = Gather(t_line, r.gathered, r.gather_sems)
    last_part = getattr(r, "last_part", r.g_all)
    last_out = getattr(r, "last_out", r.out)
    last_sums = ChainSum(
        line, (last_part, r.last_sib, r.last_rise, r.last_fall, last_out), r.last_sems
    )
    shared = not hasattr(r, "g_src")

    def g_src_at(part, to):
        return r.gathered.at[3 * streams + to] if shared else r.g_src.at[part, to]

    g_swap = Swap(line, g_src_at, r.g_dst, r.g_sems)
    state_swap = Swap(line, lambda s, to: r.state_src.at[s, to], r.state_dst, r.state_sems)
    grad_swap = Swap(line, lambda s, to: r.grad_src.at[s, to], r.grad_dst, r.grad_sems)
    y_swap = Swap(line, lambda s, to: r.y_src.at[s, to], r.y_dst, r.y_sems)
    every = Everyone(
        line,
        (r.every_src, r.every_sib, r.every_line, r.every_frames, r.every_full),
        r.every_sems,
    )
    reduced = frame_sums(
        line,
        [
            (r.down_grad, 0, False), (r.up_grad, 0, True),
            (r.t_q, 0, False), (r.t_k, 0, True), (r.t_v, 0, False), (r.t_out, 1, True),
            (r.s_q, 0, False), (r.s_k, 0, True), (r.s_v, 0, False), (r.s_out, 1, True),
        ],
        r.reduce,
    )
    mlp_sums, t_sums, s_sums = reduced[:2], reduced[2:6], reduced[6:]
    bias_swap = Swap(line, lambda _, to: r.bias_src, r.bias_dst, r.bias_sems)
    fetches = [
        pltpu.make_async_copy(r.fetched[name], getattr(r, name), r.fetch_sems.at[i])
        for i, name in enumerate(r.fetched)
    ]
    for fetch in fetches:
        fetch.start()
    line.barrier(True, True)
    for fetch in fetches:
        fetch.wait()
    stored = []

    def store(name):
        i = list(r.stored).index(name)
        stored.append(
            pltpu.make_async_copy(getattr(r, name), r.stored[name], r.store_sems.at[i])
        )
        stored[-1].start()

    def g_out(i, carry):
        rows_of = pl.ds(pl.multiple_of(i * s_rows, s_rows), s_rows)
        moved = mm(r.to_peers[...], r.cotangent[:, rows_of].reshape(tokens, width))
        moved = moved.astype(BF16).astype(r.g_dst.dtype).reshape(frames, tokens // frames, width)
        if shared:
            r.gathered[3 * streams : 4 * streams, i // 2, i % 2] = moved
        else:
            r.g_src[0, :, i // 2, i % 2] = moved
        return carry

    lax.fori_loop(0, heads, g_out, 0)
    g_swap.start(0)

    def g_in(i):
        moved = r.g_dst[0, :, i // 2, i % 2].reshape(tokens, width).astype(BF16)
        moved = mm(r.to_parts[...], moved).astype(BF16)
        r.g_all[:, i // 2, i % 2] = moved.reshape(streams, rows, width)

    table_row = lax.broadcasted_iota(jnp.int32, (entries, width), 0)

    def added(s):
        return row_sum(jnp.where(table_row == r.ids[s], r.table[...].astype(F32), 0.0))

    def norm(value, i):
        scaled = norm_stats(value)[0] * r.gain[i : i + 1, :]
        return (scaled + r.shift[i : i + 1, :]).astype(BF16)

    def attention(s, carry):
        normed = norm(r.x[s].astype(F32) + added(s), 0)
        r.normed0[s] = normed
        q = mm(normed, r.s_wqkv[0]).astype(BF16)
        k = mm(normed, r.s_wqkv[1]).astype(BF16)
        v = mm(normed, r.s_wqkv[2]).astype(BF16)
        r.s_proj[0, s] = q
        r.s_proj[1, s] = k
        r.s_proj[2, s] = v
        r.s_cols[s] = attend(q, k, v, None)
        return carry

    lax.fori_loop(0, steps, attention, 0)

    def to_streams(i, carry):
        rows_of = pl.ds(pl.multiple_of(i * s_rows, s_rows), s_rows)
        moved = mm(r.to_streams[...], r.s_cols[:, rows_of].reshape(tokens, columns)).astype(BF16)
        r.s_mixed[:, i] = moved.reshape(streams, rows, columns)
        return carry

    lax.fori_loop(0, heads, to_streams, 0)
    own_rows = pl.ds(pl.multiple_of(line.h * s_rows, s_rows), s_rows)
    own = mm(r.to_streams[...], r.x[:, own_rows].reshape(tokens, width))
    row = lax.broadcasted_iota(jnp.int32, (tokens, 1), 0)
    frame = lax.shift_right_logical(row, (rows // (frames * steps)).bit_length() - 1) & (steps - 1)
    entry = jnp.zeros_like(row)
    for s in range(steps):
        entry = jnp.where(frame == s, r.ids[s], entry)
    picker = (entry == lax.broadcasted_iota(jnp.int32, (tokens, entries), 1)).astype(BF16)
    own = own + mm(picker, r.table[...])
    r.state0[...] = own.reshape(streams, rows, width)
    r.mask[...] = frame_mask(r.segments, rows // (frames * steps), count).astype(F32)
    r.up_bias_grad[...] = jnp.zeros_like(r.up_bias_grad)
    r.small[...] = jnp.zeros_like(r.small)

    def held(n):
        return n - streams

    def enter_temporal(s, n):
        state_swap.wait(s)
        state = r.state_dst[s].reshape(rows, width)
        r.state1[s] = state
        r.gathered[held(n), line.z, line.c] = norm(state, 1)

    def enter_spatial(s, n):
        grad_swap.wait(s)
        grad = r.grad_dst[s].reshape(rows, width)
        r.grad1[s] = grad
        r.gathered[held(n), line.z, line.c] = grad.astype(BF16)

    def compute_spatial(s, n):
        left = r.s_mixed[s].reshape(count, columns)
        r.part[s] = mm(left, r.s_wout[...]).astype(BF16).reshape(chips, 2, rows, width)

    def compute_temporal(s, n):
        a = r.gathered[held(n)].reshape(count, width)
        q = mm(a, r.t_wqkv[0]).astype(BF16)
        k = mm(a, r.t_wqkv[1]).astype(BF16)
        v = mm(a, r.t_wqkv[2]).astype(BF16)
        r.t_proj[0, s] = q
        r.t_proj[1, s] = k
        r.t_proj[2, s] = v
        mixed = attend(q, k, v, r.mask[...] > 0.0)
        r.t_mixed[s] = mixed
        r.part[s] = mm(mixed, r.t_wout[...]).astype(BF16).reshape(chips, 2, rows, width)

    def compute_mlp(s, n):
        a = r.gathered[held(n)].reshape(count, width)
        g = r.g_all[s].reshape(count, width)
        pre = mm(a, r.up[...]) + r.up_bias[...]
        t = jnp.tanh(GELU_C * (pre + 0.044715 * (pre * pre * pre)))
        act = (0.5 * pre * (1.0 + t)).astype(BF16)
        r.act[s] = act
        slope = 0.5 * (1.0 + t)
        slope = slope + 0.5 * pre * (1.0 - t * t) * (GELU_C * (1.0 + 0.134145 * (pre * pre)))
        dpre = (mm_nt(g, r.down[...]) * slope).astype(BF16)
        r.dpre[s] = dpre
        r.up_bias_grad[:, :hidden] += row_sum(dpre.astype(F32))
        r.part[s] = mm_nt(dpre, r.up[...]).astype(BF16).reshape(chips, 2, rows, width)

    def compute_back(s, n):
        grad = r.gathered[held(n)].reshape(count, width)
        dm = mm_nt(grad, r.t_wout[...]).astype(BF16)
        mask = r.mask[...] > 0.0
        dq, dk, dv = attend_back(r.t_proj[0, s], r.t_proj[1, s], r.t_proj[2, s], mask, dm)
        r.t_dproj[0, s] = dq
        r.t_dproj[1, s] = dk
        r.t_dproj[2, s] = dv
        da = mm_nt(dq, r.t_wqkv[0]) + mm_nt(dk, r.t_wqkv[1]) + mm_nt(dv, r.t_wqkv[2])
        r.part[s] = da.astype(BF16).reshape(chips, 2, rows, width)

    def gathered_last(n):
        grad = r.gathered[held(n)].reshape(count, width)
        moved = mm_nt(grad, r.s_wout[...]).astype(BF16)
        r.s_dmixed[n % streams] = moved.reshape(heads, rows, columns)

    def compute_last(s, n):
        y = mm(r.act[s], r.down[...])
        r.part[s] = y.astype(BF16).reshape(chips, 2, rows, width)

    def owner_spatial(s, n):
        state = r.state0[s] + r.total[...] + r.bias[0:1, :]
        r.state_src[s] = state.reshape(r.state_src.shape[1:])
        state_swap.start(s)

    def owner_temporal(s, n):
        state = r.state1[s] + r.total[...] + r.bias[1:2, :]
        r.state2[s] = state
        r.gathered[n, line.z, line.c] = norm(state, 2)

    def owner_mlp(s, n):
        grad = r.g_all[s, line.z, line.c].astype(F32)
        back, gain_grad, shift_grad = norm_back(r.state2[s], r.total[...], r.gain[2:3, :])
        dh = grad + back
        r.grad2[s] = dh
        r.gathered[n, line.z, line.c] = dh.astype(BF16)
        r.small[0:1] += gain_grad
        r.small[1:2] += shift_grad
        r.small[2:3] += row_sum(grad)
        r.small[3:4] += row_sum(dh)

    def owner_back(s, n):
        back, gain_grad, shift_grad = norm_back(r.state1[s], r.total[...], r.gain[1:2, :])
        dh = r.grad2[s] + back
        r.grad_src[s] = dh.reshape(r.grad_src.shape[1:])
        grad_swap.start(s)
        r.small[4:5] += gain_grad
        r.small[5:6] += shift_grad
        r.small[6:7] += row_sum(dh)

    def owner_last(s, n):
        r.y[s] = (r.state2[s] + r.total[...] + r.bias[2:3, :]).astype(BF16)

    def by_phase(bodies):
        def run(n, low=0, high=4):
            for i, one in enumerate(bodies):
                if one is not None and low <= i <= high:

                    @pl.when(n // streams == i)
                    def _():
                        one(n % streams, n)

        return run

    def down_chunk(i):
        cols = pl.ds(pl.multiple_of(i * 128, 128), 128)
        left = r.act[:, :, cols].reshape(all_tokens, 128)
        right = r.g_all[...].reshape(all_tokens, width)
        mlp_sums[0].part[cols] = mm_tn(left, right).astype(BF16)

    def up_chunk(i):
        cols = pl.ds(pl.multiple_of(i * 256, 256), 256)
        left = r.gathered[streams : 2 * streams, :, :, :, cols].reshape(all_tokens, 256)
        right = r.dpre[...].reshape(all_tokens, hidden)
        mlp_sums[1].part[cols] = mm_tn(left, right).astype(BF16)

    def t_out_chunk(i):
        left = r.t_mixed[...].reshape(all_tokens, columns)
        right = r.gathered[2 * streams : 3 * streams].reshape(all_tokens, width)
        t_sums[3].part[...] = mm_tn(left, right).astype(BF16)

    def t_qkv_chunk(i):
        start = i * 256
        cols = pl.ds(pl.multiple_of(start, 256), 256)
        left = r.gathered[0:streams, :, :, :, cols].reshape(all_tokens, 256)
        for j in range(3):
            column_grads(start, left, r.t_dproj[j], t_sums[j].part)

    def s_cols_chunk(_):
        def from_streams(i, carry):
            rows_of = pl.ds(pl.multiple_of(i * s_rows, s_rows), s_rows)
            moved = mm(r.from_streams[...], r.s_dmixed[:, i].reshape(tokens, columns)).astype(BF16)
            r.s_cols[:, rows_of] = moved.reshape(steps, s_rows, columns)
            return carry

        lax.fori_loop(0, heads, from_streams, 0)

    def s_back_chunk(s):
        dq, dk, dv = attend_back(r.s_proj[0, s], r.s_proj[1, s], r.s_proj[2, s], None, r.s_cols[s])
        r.s_dproj[0, s] = dq
        r.s_dproj[1, s] = dk
        r.s_dproj[2, s] = dv
        da = mm_nt(dq, r.s_wqkv[0]) + mm_nt(dk, r.s_wqkv[1]) + mm_nt(dv, r.s_wqkv[2])
        last_part[s] = da.astype(BF16).reshape(last_part.shape[1:])
        for zb in range(chips):
            last_sums.across(s, zb).start()

    def s_out_chunk(_):
        left = r.s_mixed[...].reshape(all_tokens, columns)
        right = r.gathered[3 * streams : 4 * streams].reshape(all_tokens, width)
        s_sums[3].part[...] = mm_tn(left, right).astype(BF16)

    def bias_chunk(_):
        r.bias_src[...] = jnp.broadcast_to(r.up_bias_grad[...], r.bias_src.shape)
        bias_swap.start(0)

    def g_in_chunk(i):
        @pl.when(i == 0)
        def _():
            g_swap.wait(0)

        g_in(i)

    n_down, n_up = hidden // 128, width // 256
    turn_of = times.after
    mlp_turn, back_turn = turn_of(3 * streams - 1), turn_of(4 * streams - 1)
    last_turn = turn_of(5 * streams - 1)
    chunks = (
        (streams + 1, 0, heads, g_in_chunk),
        (mlp_turn, 0, n_down, down_chunk),
        (mlp_turn, n_down, n_up, up_chunk),
        (mlp_turn, n_down + n_up, 1, bias_chunk),
        (back_turn, 0, 1, t_out_chunk),
        (back_turn, 1, width // 256, t_qkv_chunk),
        (last_turn, 0, 1, s_cols_chunk),
        (last_turn, 1, steps, s_back_chunk),
        (last_turn, 1 + steps, 1, s_out_chunk),
    )
    slots = [i for i in range(times.every) if i % 2 == 1][:3]
    per_turn = 2 * len(slots)
    turns = max(times.turns, last_turn + -(-(steps + 2) // per_turn))
    stages = reduced[0].stages()
    bits = len(reduced[0].bits)

    def begin_of(turn, number):
        return (turn + number // per_turn) * times.every + times.every - 1

    def moments_of(begin, waits):
        out = [begin]
        for k in range(1, stages):
            half = k if k <= bits else 2 * bits + 1 - k
            out.append(out[-1] + waits[min(half, len(waits)) - 1])
        return out

    moments = (
        (mlp_sums, moments_of(begin_of(mlp_turn, n_down + n_up), MLP_WAITS)),
        (t_sums, moments_of(begin_of(back_turn, 1 + width // 256), T_WAITS)),
    )
    late = [
        (k, sums_of)
        for sums_of, steps_of in moments
        for k, moment in enumerate(steps_of)
        if moment // times.every >= turns
    ]

    def beside(m, i):
        if i in slots:
            for turn, first, number, chunk in chunks:
                which = per_turn * (m - turn) + 2 * slots.index(i) - first
                here = jnp.clip(number - which, 0, 2)

                @pl.when((which > -2) & (which < number))
                def _():
                    def one(j, carry):
                        @pl.when(which + j >= 0)
                        def _():
                            chunk(which + j)

                        return carry

                    lax.fori_loop(0, here, one, 0)

        for sums_of, steps_of in moments:
            for k, moment in enumerate(steps_of):
                if moment % times.every == i and moment // times.every < turns:

                    @pl.when(m == moment // times.every)
                    def _():
                        for one in sums_of:
                            one.stage(k)

    enter = by_phase((None, enter_temporal, None, None, enter_spatial))
    compute = by_phase(
        (compute_spatial, compute_temporal, compute_mlp, compute_back, compute_last)
    )
    owner = by_phase((owner_spatial, owner_temporal, owner_mlp, owner_back, owner_last))
    pipeline(
        t_line, times, turns, gather, sums, enter, compute, gathered_last, owner, r.total, beside
    )
    drain_all(t_line, (sums,), streams)
    for sums_of, group in ((mlp_sums, MLP_RESULTS), (t_sums, T_RESULTS)):
        if (stages - 1, sums_of) not in late:
            for name in group:
                store(name)

    y = mm(r.from_parts[...], r.y[...].reshape(tokens, width)).astype(BF16)
    r.y_src[0] = y.astype(r.y_src.dtype).reshape(r.y_src.shape[1:])
    y_swap.start(0)

    r.sums0[...] = jnp.zeros_like(r.sums0)

    def small_part(s):
        state = r.x[s].astype(F32) + added(s)
        da = last_part[s].reshape(patches, width).astype(F32)
        back, gain_grad, shift_grad = norm_back(state, da, r.gain[0:1, :])
        r.sums0[0:1] += gain_grad
        r.sums0[1:2] += shift_grad
        r.sums0[8 : 8 + entries] += jnp.where(table_row == r.ids[s], row_sum(back), 0.0)

    room = r.every_src.shape[0]
    filled = 9 + entries

    def small_value(own_grad):
        for s in range(steps):
            here = row_sum(own_grad[s * s_rows : (s + 1) * s_rows])
            r.sums0[8 : 8 + entries] += jnp.where(table_row == r.ids[s], here, 0.0)
        rows_of = [
            r.sums0[0:1], r.small[4:5], r.small[0:1],
            r.sums0[1:2], r.small[5:6], r.small[1:2],
            r.small[6:7], r.small[3:4], r.small[2:3],
            r.sums0[8 : 8 + entries], jnp.zeros((room - filled, width), F32),
        ]
        return jnp.concatenate(rows_of, axis=0)

    def body(t, carry):
        last_sums.hops(t)
        for j in range(3):

            @pl.when(t == j)
            def _():
                for i in range(width // 256):
                    left = r.normed0[:, :, i * 256 : (i + 1) * 256].reshape(all_tokens, 256)
                    column_grads(i * 256, left, r.s_dproj[j], s_sums[j].part)
                s_sums[j].stage(0)
                if j == 0:
                    s_sums[3].stage(0)
                    for k, sums_of in late:
                        for one in sums_of:
                            one.stage(k)

        @pl.when((t >= 3) & (t < 3 + steps))
        def _():
            small_part(t - 3)

        for k in range(1, stages - 1):

            @pl.when(t == LAST_STAGES[min(k, 3) - 1] + 4 * max(k - 3, 0))
            def _():
                for one in s_sums:
                    one.stage(k)

        @pl.when(t == 3 + steps)
        def _():
            grad = r.grad1[...].reshape(tokens, width)
            own_grad = moved_exactly(r.from_streams[...], grad)
            r.state0[...] = own_grad.reshape(r.state0.shape)
            every.over_pair(small_value(own_grad))

        for moment, step in zip(LAST_SMALL, (every.over_line, every.over_frames, every.over_back)):

            @pl.when(t == moment)
            def _():
                step()

        return carry

    bound = steps * (chips - 1) + (chips - 2) * LAG
    bound = max(bound, LAST_SMALL[-1] + 1, LAST_STAGES[2] + 4 * max(stages - 5, 0) + 1)
    lax.fori_loop(0, bound, body, 0)
    for s in range(steps):
        last_sums.finish(s, r.last_total.at[s])
    own_grad = r.state0[...].reshape(tokens, width)
    for s in range(steps):
        state = r.x[s, own_rows].astype(F32) + added(s)
        back, _, _ = norm_back(state, r.last_total[s], r.gain[0:1, :])
        r.grad_res[pl.ds(s * s_rows, s_rows)] = own_grad[s * s_rows : (s + 1) * s_rows] + back
    y_swap.wait(0)
    r.y_res[...] = mm(r.from_peers[...], r.y_dst[0].reshape(tokens, width).astype(BF16)).astype(BF16)
    r.small_res[...] = every.result()
    bias_swap.wait(0)
    up_bias = r.bias_dst[0, 0]
    for i in range(1, frames):
        up_bias = up_bias + r.bias_dst[0, i]
    r.up_bias_res[...] = up_bias
    for name in ("grad_res", "y_res", "small_res", "up_bias_res"):
        store(name)
    for one in s_sums:
        one.stage(stages - 1)
    for sums_of, group in ((mlp_sums, MLP_RESULTS), (t_sums, T_RESULTS)):
        if (stages - 1, sums_of) in late:
            for name in group:
                store(name)
    for name in S_RESULTS:
        store(name)
    drain_all(line, (last_sums,), steps)
    drain_all(t_line, (gather,), 4 * streams)
    for one in stored:
        one.wait()


def finish(names, parts, *refs):
    sources = dict(zip(names, refs))
    results = dict(zip(parts, refs[len(names) :]))
    held = refs[len(names) + len(parts) :]
    sems_in, sems_out = held[-2:]
    local = dict(zip(names, held))
    made = dict(zip(parts, held[len(names) :]))
    loads = {
        name: pltpu.make_async_copy(sources[name], local[name], sems_in.at[i])
        for i, name in enumerate(names)
    }
    for load in loads.values():
        load.start()
    loaded, stores = set(), []
    for i, (name, given) in enumerate(parts.items()):
        for j, (source, low, high, columns) in enumerate(given):
            if source not in loaded:
                loads[source].wait()
                loaded.add(source)
            value = local[source][low:high, :columns].astype(made[name].dtype)
            if len(given) > 1:
                made[name][j] = value
            else:
                made[name][...] = value
        stores.append(pltpu.make_async_copy(made[name], results[name], sems_out.at[i]))
        stores[-1].start()
    for store in stores:
        store.wait()


def results(found, entries):
    width, hidden = found["up_grad"].shape

    def whole(name):
        rows, columns = found[name].shape
        return [(name, 0, rows, columns)]

    parts = {
        "down": whole("down_grad"),
        "up": whole("up_grad"),
        "t_qkv": whole("t_q") + whole("t_k") + whole("t_v"),
        "t_out": whole("t_out"),
        "grad": whole("grad_res"),
        "y": whole("y_res"),
        "gain": [("small_res", 0, 3, width)],
        "shift": [("small_res", 3, 6, width)],
        "bias": [("small_res", 6, 9, width)],
        "table": [("small_res", 9, 9 + entries, width)],
        "up_bias": [("up_bias_res", 0, 1, hidden)],
        "s_out": whole("s_out"),
        "s_qkv": whole("s_q") + whole("s_k") + whole("s_v"),
    }
    shapes = []
    for name, given in parts.items():
        _, low, high, columns = given[0]
        lead = (len(given),) if len(given) > 1 else ()
        kind = BF16 if name == "y" else F32
        shapes.append(jax.ShapeDtypeStruct(lead + (high - low, columns), kind))
    names = tuple(found)
    made = pl.pallas_call(
        lambda *refs: finish(names, parts, *refs),
        name="finish",
        out_shape=shapes,
        in_specs=[pl.BlockSpec(memory_space=pltpu.HBM)] * len(names),
        out_specs=[pl.BlockSpec(memory_space=pltpu.HBM)] * len(shapes),
        scratch_shapes=[pltpu.VMEM(v.shape, v.dtype) for v in found.values()]
        + [pltpu.VMEM(v.shape, v.dtype) for v in shapes]
        + [pltpu.SemaphoreType.DMA((len(names),)), pltpu.SemaphoreType.DMA((len(shapes),))],
        compiler_params=pltpu.CompilerParams(vmem_limit_bytes=VMEM_LIMIT),
    )(*found.values())
    return dict(zip(parts, made))


def orders(frames_local, frames, places, streams):
    tokens = frames_local * frames * places
    index = np.arange(tokens).reshape(frames_local, frames, streams, places // streams)
    to_streams = index.transpose(2, 1, 0, 3).reshape(-1)
    to_peers = index.transpose(1, 0, 2, 3).reshape(-1)
    index = np.arange(tokens).reshape(frames * frames_local, streams, places // streams)
    to_parts = index.transpose(1, 0, 2).reshape(-1)
    eye = np.eye(tokens, dtype=np.float32)
    there = [eye[order] for order in (to_streams, to_peers, to_parts)]
    back = [m.T for m in there]
    names = ("to_streams", "to_peers", "to_parts", "from_streams", "from_peers", "from_parts")
    return {name: jnp.asarray(m, BF16) for name, m in zip(names, there + back)}


def on_device(
    block_input,
    action_ids,
    segment_ids,
    action_table,
    norm_gain,
    norm_shift,
    spatial_qkv,
    spatial_out,
    temporal_qkv,
    temporal_out,
    out_bias,
    up_weight,
    up_bias,
    down_weight,
    cotangent,
):
    frames, heads = lax.axis_size("frames"), lax.axis_size("heads")
    chips = heads // 2
    steps, patches, width = block_input.shape
    rows = patches // heads
    tokens = steps * rows
    total_frames = segment_ids.shape[0]
    places = rows // frames
    streams = min(4, places)
    t_rows = tokens // streams
    columns = spatial_out.shape[0]
    hidden = up_weight.shape[1]
    entries = action_table.shape[0]
    count = heads * t_rows
    room = -(-(10 + entries) // 16) * 16
    args = dict(
        ids=action_ids,
        segments=segment_ids,
        x=block_input,
        cotangent=cotangent,
        table=action_table,
        gain=norm_gain,
        shift=norm_shift,
        bias=out_bias,
        s_wqkv=spatial_qkv.transpose(1, 0, 2),
        s_wout=spatial_out,
        t_wqkv=temporal_qkv.transpose(1, 0, 2),
        t_wout=temporal_out,
        up=up_weight,
        up_bias=up_bias.reshape(1, hidden),
        down=down_weight,
        **orders(steps, frames, places, streams),
    )
    qkv, out = (width, columns), (columns, width)
    down, up = (hidden, width), (width, hidden)
    outs = dict(
        t_q=(qkv, BF16),
        t_k=(qkv, BF16),
        t_v=(qkv, BF16),
        t_out=(out, BF16),
        s_q=(qkv, BF16),
        s_k=(qkv, BF16),
        s_v=(qkv, BF16),
        s_out=(out, BF16),
        up_grad=(up, BF16),
        down_grad=(down, BF16),
        y_res=((tokens, width), BF16),
        grad_res=((tokens, width), F32),
        small_res=((room, width), F32),
        up_bias_res=((8, width), F32),
    )
    s_all = (steps, chips, 2, rows, width)
    t_all = (streams, chips, 2, t_rows, width)
    s_one, t_one = (steps, chips, rows, width), (streams, chips, t_rows, width)
    owned = (streams, t_rows, width)
    swapped = (streams, frames, t_rows // frames, width)
    whole = (1, frames, tokens // frames, width)
    g_part = (1, frames, chips, 2, tokens // frames, width)

    def kind_of(shape):
        return BF16 if shape[-2] % 16 == 0 else F32

    cols = dict(
        s_cols=(steps, patches, columns),
        s_proj=(3, steps, patches, columns),
        s_dproj=(3, steps, patches, columns),
        s_mixed=(streams, heads, t_rows, columns),
        s_dmixed=(streams, heads, t_rows, columns),
        t_proj=(3, streams, count, columns),
        t_dproj=(3, streams, count, columns),
        t_mixed=(streams, count, columns),
        act=(streams, count, hidden),
        dpre=(streams, count, hidden),
        normed0=(steps, patches, width),
        gathered=(4 * streams,) + t_all[1:],
        g_all=t_all,
        part=t_all,
        sib=t_one,
        rise=t_one,
        fall=t_one,
        out=t_one,
        **({} if s_all == t_all else dict(last_part=s_all, last_out=s_one)),
        last_sib=s_one,
        last_rise=s_one,
        last_fall=s_one,
        y=owned,
    )
    floats = dict(
        state0=owned,
        state1=owned,
        state2=owned,
        grad1=owned,
        grad2=owned,
        total=(t_rows, width),
        last_total=(steps, rows, width),
        mask=(count, count),
        small=(8, width),
        sums0=(8 + entries, width),
        up_bias_grad=(1, width),
        state_src=swapped,
        state_dst=swapped,
        grad_src=swapped,
        grad_dst=swapped,
    )
    scratch = {name: pltpu.VMEM(shape, BF16) for name, shape in cols.items()}
    scratch |= {name: pltpu.VMEM(shape, F32) for name, shape in floats.items()}
    moving = ("g_dst",) if g_part[1:] == t_all else ("g_src", "g_dst")
    scratch |= {name: pltpu.VMEM(g_part, kind_of(g_part)) for name in moving}
    scratch |= {name: pltpu.VMEM(whole, kind_of(whole)) for name in ("y_src", "y_dst")}
    every_shape = (room, width)
    scratch |= dict(
        every_src=pltpu.VMEM(every_shape, BF16),
        every_sib=pltpu.VMEM(every_shape, BF16),
        every_line=pltpu.VMEM((chips, room, width // chips), BF16),
        every_frames=pltpu.VMEM((frames, room, width // chips), BF16),
        every_full=pltpu.VMEM(every_shape, BF16),
        every_sems=[pltpu.SemaphoreType.DMA((2 * chips + frames,))] * 2,
        bias_src=pltpu.VMEM((8, width), F32),
        bias_dst=pltpu.VMEM((1, frames, 8, width), F32),
        bias_sems=[pltpu.SemaphoreType.DMA((1, frames))] * 2,
        sum_sems=[pltpu.SemaphoreType.DMA((streams, chips))] * 5,
        last_sems=[pltpu.SemaphoreType.DMA((steps, chips))] * 5,
        gather_sems=[pltpu.SemaphoreType.DMA((4 * streams, chips))] * 5,
        state_sems=[pltpu.SemaphoreType.DMA((streams, frames))] * 2,
        grad_sems=[pltpu.SemaphoreType.DMA((streams, frames))] * 2,
        g_sems=[pltpu.SemaphoreType.DMA((1, frames))] * 2,
        y_sems=[pltpu.SemaphoreType.DMA((1, frames))] * 2,
        reduce=[
            x
            for shape, dim in ((down, 0), (up, 0)) + 2 * (((qkv, 0),) * 3 + ((out, 1),))
            for x in frame_sum_scratch(frames, shape, dim)
        ],
    )
    held = {k: v for k, v in args.items() if k not in ("ids", "segments")}
    scratch |= {name: pltpu.VMEM(v.shape, v.dtype) for name, v in held.items()}
    scratch |= {name: pltpu.VMEM(shape, kind) for name, (shape, kind) in outs.items()}
    scratch["fetch_sems"] = pltpu.SemaphoreType.DMA((len(held),))
    scratch["store_sems"] = pltpu.SemaphoreType.DMA((len(outs),))
    fetched, results_of, names = tuple(args), tuple(outs), tuple(scratch)
    parts = pl.pallas_call(
        lambda *refs: block(fetched, results_of, names, *refs),
        name="block",
        out_shape=[jax.ShapeDtypeStruct(shape, kind) for shape, kind in outs.values()],
        in_specs=[
            pl.BlockSpec(memory_space=pltpu.HBM if name in held else pltpu.SMEM)
            for name in args
        ],
        out_specs=[pl.BlockSpec(memory_space=pltpu.HBM)] * len(outs),
        scratch_shapes=list(scratch.values()),
        compiler_params=pltpu.CompilerParams(
            collective_id=0, has_side_effects=True, vmem_limit_bytes=VMEM_LIMIT
        ),
    )(*args.values())
    made = results(dict(zip(outs, parts)), entries)
    s_blocks = (steps, rows, width)
    return (
        made["y"].reshape(s_blocks),
        made["grad"].reshape(s_blocks),
        made["table"],
        made["gain"],
        made["shift"],
        made["s_qkv"].transpose(1, 0, 2),
        made["s_out"],
        made["t_qkv"].transpose(1, 0, 2),
        made["t_out"],
        made["bias"],
        made["up"],
        made["up_bias"].reshape(hidden),
        made["down"],
    )


def solution(mesh):
    return jax.shard_map(
        on_device,
        mesh=mesh,
        in_specs=(
            P("frames", None, None),
            P("frames"),
            P(),
            P(),
            P(),
            P(),
            P(None, None, "heads"),
            P("heads", None),
            P(None, None, "heads"),
            P("heads", None),
            P(),
            P(None, "heads"),
            P("heads"),
            P("heads", None),
            P("frames", None, None),
        ),
        out_specs=(
            P("frames", "heads", None),
            P("frames", "heads", None),
            P(),
            P(),
            P(),
            P(None, None, "heads"),
            P("heads", None),
            P(None, None, "heads"),
            P("heads", None),
            P(),
            P(None, "heads"),
            P("heads"),
            P("heads", None),
        ),
        check_vma=False,
    )
```

```python
import jax
import jax.numpy as jnp
import numpy as np
from jax import lax
from jax.experimental import pallas as pl
from jax.experimental.pallas import tpu as pltpu
from jax.sharding import PartitionSpec as P

HD = 64
SCALE = HD**-0.5
EPS = 1e-05
MASKED = -1000000000.0
F32 = jnp.float32
BF16 = jnp.bfloat16
MESH = pl.DeviceIdType.MESH
MLP_RESULTS = ("down_grad", "up_grad")
T_RESULTS = ("t_q", "t_k", "t_v", "t_out")
S_RESULTS = ("s_q", "s_k", "s_v", "s_out")
VMEM_LIMIT = 62 * 1024 * 1024
GELU_C = float(np.sqrt(2.0 / np.pi))
LAG = 2
SLOT_US, STEP_US, FRAME_US, MLP_US, ATTENTION_US, LAST_FRAME_US = 1.15, 1.45, 4.5, 5.8, 2.9, 3.6
CHUNK_US, WHOLE_US = 1.45, 100.0
ADJUST = {}
LAST_GRADS = 3
LAST_SMALL = (5, 6, 9, 12)
HOP_US, SIBLING_US, COMPUTE_US, LINK_US, OWNER_US, SWAP_US = 3.4, 1.0, 2.0, 1.45, 1.0, 4.0


def mm(a, b):
    return lax.dot_general(a, b, (((1,), (0,)), ((), ())), preferred_element_type=F32)


def mm_nt(a, b):
    return lax.dot_general(a, b, (((1,), (1,)), ((), ())), preferred_element_type=F32)


def mm_tn(a, b):
    return lax.dot_general(a, b, (((0,), (0,)), ((), ())), preferred_element_type=F32)


def norm_stats(value):
    centered = value - jnp.mean(value, axis=-1, keepdims=True)
    inv = lax.rsqrt(jnp.mean(centered * centered, axis=-1, keepdims=True) + EPS)
    return centered * inv, inv


def norm_back(value, grad, gain):
    normed, inv = norm_stats(value)
    e = grad * gain
    first = jnp.mean(e, axis=-1, keepdims=True)
    second = jnp.mean(e * normed, axis=-1, keepdims=True)
    gain_grad = jnp.sum(grad * normed, axis=0, keepdims=True)
    shift_grad = jnp.sum(grad, axis=0, keepdims=True)
    return (e - first - normed * second) * inv, gain_grad, shift_grad


def head_lanes(shape, head):
    lane = lax.broadcasted_iota(jnp.int32, shape, 1)
    return (lane >= head * HD) & (lane < (head + 1) * HD)


def softmax_of(q, k, mask):
    scores = mm_nt(q, k) * SCALE
    if mask is not None:
        scores = jnp.where(mask, scores, MASKED)
    raised = jnp.exp(scores - jnp.max(scores, axis=-1, keepdims=True))
    return raised / jnp.sum(raised, axis=-1, keepdims=True)


def attend(q, k, v, mask):
    heads = q.shape[1] // HD
    mixed = None
    for head in range(heads):
        lanes = head_lanes(q.shape, head)
        probs = softmax_of(jnp.where(lanes, q, jnp.zeros_like(q)), k, mask).astype(BF16)
        out = mm(probs, v)
        mixed = out if mixed is None else jnp.where(lanes, out, mixed)
    return mixed.astype(BF16)


def attend_back(q, k, v, mask, grad):
    heads = q.shape[1] // HD
    dq = dk = dv = None
    for head in range(heads):
        lanes = head_lanes(q.shape, head)
        qh = jnp.where(lanes, q, jnp.zeros_like(q))
        gh = jnp.where(lanes, grad, jnp.zeros_like(grad))
        probs = softmax_of(qh, k, mask)
        dvh = mm_tn(probs.astype(BF16), gh)
        dp = mm_nt(gh, v)
        ds = (probs * (dp - jnp.sum(dp * probs, axis=-1, keepdims=True))).astype(BF16)
        dqh = mm(ds, k) * SCALE
        dkh = mm_tn(ds, qh) * SCALE
        if head == 0:
            dq, dk, dv = dqh, dkh, dvh
        else:
            dq = jnp.where(lanes, dqh, dq)
            dk = dk + dkh
            dv = dv + dvh
    return dq.astype(BF16), dk.astype(BF16), dv.astype(BF16)


class Line:
    def __init__(self, steps):
        self.frames = lax.axis_size("frames")
        self.heads = lax.axis_size("heads")
        self.chips = self.heads // 2
        self.f = lax.axis_index("frames")
        self.h = lax.axis_index("heads")
        self.z = self.h // 2
        self.c = self.h % 2
        self.steps = steps

    def at(self, z):
        return (self.f, jnp.clip(z, 0, self.chips - 1) * 2 + self.c)

    def sibling(self):
        return (self.f, self.z * 2 + 1 - self.c)

    def barrier(self, over_frames, whole_line=False):
        sem = pltpu.get_barrier_semaphore()

        def greet(device):
            pl.semaphore_signal(sem, inc=1, device_id=device, device_id_type=MESH)

        greet(self.sibling())
        count = 1
        if over_frames:
            for k in range(1, self.frames):
                greet(((self.f + k) % self.frames, self.h))
            count += self.frames - 1
        if whole_line:
            for k in range(1, self.chips):
                greet(self.at((self.z + k) % self.chips))
            count += self.chips - 1
        else:

            @pl.when(self.z > 0)
            def _():
                greet(self.at(self.z - 1))

            @pl.when(self.z < self.chips - 1)
            def _():
                greet(self.at(self.z + 1))

            count = count + (self.z > 0).astype(jnp.int32)
            count = count + (self.z < self.chips - 1).astype(jnp.int32)
        pl.semaphore_wait(sem, count)

    def copy(self, src, dst, send, recv, device):
        return pltpu.make_async_remote_copy(
            src_ref=src,
            dst_ref=dst,
            send_sem=send,
            recv_sem=recv,
            device_id=device,
            device_id_type=MESH,
        )


class Gather:
    def __init__(self, line, buf, sems):
        self.line, self.buf = line, buf
        self.got, self.got_sib, self.sent_up, self.sent_down, self.sent_sib = sems

    def up(self, s, zb):
        ln = self.line
        ref = self.buf.at[s, zb, ln.c]
        return ln.copy(ref, ref, self.sent_up.at[s, zb], self.got.at[s, zb], ln.at(ln.z + 1))

    def down(self, s, zb):
        ln = self.line
        ref = self.buf.at[s, zb, ln.c]
        return ln.copy(ref, ref, self.sent_down.at[s, zb], self.got.at[s, zb], ln.at(ln.z - 1))

    def across(self, s, zb):
        ln = self.line
        ref = self.buf.at[s, zb, ln.c]
        return ln.copy(ref, ref, self.sent_sib.at[s, zb], self.got_sib.at[s, zb], ln.sibling())

    def wait_across(self, s, zb):
        ln = self.line
        ref = self.buf.at[s, zb, 1 - ln.c]
        ln.copy(
            ref, ref, self.sent_sib.at[s, zb], self.got_sib.at[s, zb], ln.sibling()
        ).wait_recv()

    def send(self, s):
        ln = self.line

        @pl.when(ln.z < ln.chips - 1)
        def _():
            self.up(s, ln.z).start()

        @pl.when(ln.z > 0)
        def _():
            self.down(s, ln.z).start()

        self.across(s, ln.z).start()

    def start(self, own):
        ln = self.line
        for s in range(ln.steps):
            self.buf[s, ln.z, ln.c] = own[s]
            self.send(s)

    def arrive(self, distance, s):
        ln = self.line
        below, above = ln.z - distance, ln.z + distance

        @pl.when((distance > 0) & (below >= 0))
        def _():
            self.up(s, below).wait_recv()

            @pl.when(ln.z < ln.chips - 1)
            def _():
                self.up(s, below).start()

            self.across(s, below).start()

        @pl.when((distance > 0) & (above < ln.chips))
        def _():
            self.down(s, above).wait_recv()

            @pl.when(ln.z > 0)
            def _():
                self.down(s, above).start()

            self.across(s, above).start()

    def drain(self, s, zb):
        ln = self.line

        @pl.when((zb <= ln.z) & (ln.z < ln.chips - 1))
        def _():
            self.up(s, zb).wait_send()

        @pl.when((zb >= ln.z) & (ln.z > 0))
        def _():
            self.down(s, zb).wait_send()

        self.across(s, zb).wait_send()


class ChainSum:
    def __init__(self, line, bufs, sems):
        self.line = line
        self.part, self.sib, self.rise, self.fall, self.out = bufs
        self.sent_sib, self.got_sib, self.got_up, self.got_down, self.sent = sems

    def across(self, s, zb):
        ln = self.line
        return ln.copy(
            self.part.at[s, zb, 1 - ln.c],
            self.sib.at[s, zb],
            self.sent_sib.at[s, zb],
            self.got_sib.at[s, zb],
            ln.sibling(),
        )

    def up(self, s, o):
        ln = self.line
        return ln.copy(
            self.out.at[s, o],
            self.rise.at[s, o],
            self.sent.at[s, o],
            self.got_up.at[s, o],
            ln.at(ln.z + 1),
        )

    def down(self, s, o):
        ln = self.line
        return ln.copy(
            self.out.at[s, o],
            self.fall.at[s, o],
            self.sent.at[s, o],
            self.got_down.at[s, o],
            ln.at(ln.z - 1),
        )

    def mine(self, s, o):
        return self.part[s, o, self.line.c].astype(F32) + self.sib[s, o].astype(F32)

    def hop_up(self, s, o):
        ln = self.line
        self.across(s, o).wait_recv()

        @pl.when(ln.z == 0)
        def _():
            self.out[s, o] = self.mine(s, o).astype(BF16)

        @pl.when(ln.z > 0)
        def _():
            self.up(s, o).wait_recv()
            self.out[s, o] = (self.mine(s, o) + self.rise[s, o].astype(F32)).astype(BF16)

        self.up(s, o).start()

    def hop_down(self, s, o):
        ln = self.line
        self.across(s, o).wait_recv()

        @pl.when(ln.z == ln.chips - 1)
        def _():
            self.out[s, o] = self.mine(s, o).astype(BF16)

        @pl.when(ln.z < ln.chips - 1)
        def _():
            self.down(s, o).wait_recv()
            self.out[s, o] = (self.mine(s, o) + self.fall[s, o].astype(F32)).astype(BF16)

        self.down(s, o).start()

    def hops(self, t, part=None, fits=True):
        ln = self.line
        last = ln.chips - 1
        for upward in (True, False):
            place = ln.z if upward else last - ln.z
            q = t - place * LAG
            if part is None:
                turn = jnp.maximum(q, 0) // ln.steps
                s = jnp.maximum(q, 0) % ln.steps
            else:
                turn, s = jnp.maximum(q, 0), part
            far = jnp.clip(last - turn, 0, last)
            ok = (q >= 0) & (turn < last) & (far > place) & fits
            o = far if upward else last - far

            @pl.when(ok)
            def _():
                if upward:
                    self.hop_up(s, o)
                else:
                    self.hop_down(s, o)

    def finish(self, s, total):
        ln = self.line
        self.across(s, ln.z).wait_recv()
        total[...] = self.mine(s, ln.z)

        @pl.when(ln.z > 0)
        def _():
            self.up(s, ln.z).wait_recv()
            total[...] += self.rise[s, ln.z].astype(F32)

        @pl.when(ln.z < ln.chips - 1)
        def _():
            self.down(s, ln.z).wait_recv()
            total[...] += self.fall[s, ln.z].astype(F32)

    def drain(self, s, zb):
        ln = self.line
        self.across(s, zb).wait_send()

        @pl.when(zb != ln.z)
        def _():
            self.up(s, zb).wait_send()


def drain_all(line, things, parts):
    def body(i, carry):
        for thing in things:
            thing.drain(i // line.chips, i % line.chips)
        return carry

    lax.fori_loop(0, parts * line.chips, body, 0)


class Swap:
    def __init__(self, line, src_at, dst, sems):
        self.line, self.src_at, self.dst = line, src_at, dst
        self.sent, self.got = sems

    def copy(self, part, k):
        ln = self.line
        to = (ln.f + k) % ln.frames
        return ln.copy(
            self.src_at(part, to),
            self.dst.at[part, ln.f],
            self.sent.at[part, k],
            self.got.at[part, k],
            (to, ln.h),
        )

    def start(self, part):
        ln = self.line
        for k in range(1, ln.frames):
            self.copy(part, k).start()
        self.dst[part, ln.f] = self.src_at(part, ln.f)[...]

    def wait(self, part):
        for k in range(1, self.line.frames):
            self.copy(part, k).wait()


class FrameSum:
    def __init__(self, line, part, full, dim, reverse, recv_bufs, sems):
        self.line, self.part, self.full, self.dim = line, part, full, dim
        self.recv_bufs = recv_bufs
        self.sent, self.got, self.sent_back, self.got_back = sems
        bits = range(line.frames.bit_length() - 1)
        self.bits = list(reversed(bits)) if reverse else list(bits)
        self.spans = []
        start, size = 0, part.shape[dim]
        for bit in self.bits:
            size //= 2
            side = (line.f // (1 << bit)) % 2
            peer = (line.f + (1 - 2 * side) * (1 << bit), line.h)
            keep, give = start + side * size, start + (1 - side) * size
            self.spans.append((keep, give, size, peer))
            start = keep

    def view(self, ref, start, size, step):
        if self.dim == 0:
            return ref.at[pl.ds(pl.multiple_of(start, step), size)]
        return ref.at[:, pl.ds(pl.multiple_of(start, step), size)]

    def out(self, i, chunk=0, chunks=1):
        _, give, size, peer = self.spans[i]
        step = size // chunks
        src = self.view(self.part, give + chunk * step, step, step)
        dst = self.view(self.recv_bufs[i], chunk * step, step, step)
        return self.line.copy(src, dst, self.sent.at[i], self.got.at[i], peer)

    def back(self, i, chunk=0, chunks=1):
        keep, _, size, peer = self.spans[i]
        step = size // chunks
        ref = self.view(self.full, keep + chunk * step, step, step)
        return self.line.copy(ref, ref, self.sent_back.at[i], self.got_back.at[i], peer)

    def back_in(self, i):
        _, give, size, peer = self.spans[i]
        ref = self.view(self.full, give, size, size)
        return self.line.copy(ref, ref, self.sent_back.at[i], self.got_back.at[i], peer)

    def send(self, k, chunk=0, chunks=1):
        n = len(self.bits)
        if k < n:
            self.out(k, chunk, chunks).start()
        else:
            self.back(2 * n - 1 - k, chunk, chunks).start()

    def end(self, k):
        n = len(self.bits)
        if k < n:
            keep, _, size, _ = self.spans[k]
            self.out(k).wait()
            ref = self.view(self.part, keep, size, size)
            to = self.view(self.full, keep, size, size) if k == n - 1 else ref
            to[...] = (ref[...].astype(F32) + self.recv_bufs[k][...].astype(F32)).astype(BF16)
        else:
            i = 2 * n - 1 - k
            self.back(i).wait_send()
            self.back_in(i).wait_recv()


def frame_sum_scratch(frames, shape, dim, pieces):
    bits = frames.bit_length() - 1
    scratch = [pltpu.VMEM(shape, BF16)]
    for _ in range(pieces):
        for i in range(bits):
            part = list(shape)
            part[dim] = (shape[dim] // pieces) >> (i + 1)
            scratch.append(pltpu.VMEM(tuple(part), BF16))
        scratch += [pltpu.SemaphoreType.DMA((bits,))] * 4
    return scratch


def frame_sums(line, arrays, scratch):
    bits = line.frames.bit_length() - 1
    out = []
    for full, dim, reverse, pieces in arrays:
        part, scratch = scratch[0], scratch[1:]
        sums = []
        for i in range(pieces):
            mine, scratch = scratch[: bits + 4], scratch[bits + 4 :]
            size = full.shape[dim] // pieces
            at = (slice(None),) * dim + (pl.ds(i * size, size),)
            views = (part.at[at], full.at[at]) if pieces > 1 else (part, full)
            sums.append(FrameSum(line, *views, dim, reverse, mine[:bits], mine[bits:]))
        out.append((part, sums))
    return out


def stage_times(sums, begins, first, bits, free, latency, chunk_us):
    ready = list(begins)
    plan = []
    for k in range(2 * bits):
        for i, group in enumerate(sums):
            length = first / 2 ** (k if k < bits else 2 * bits - 1 - k)
            chunks = 1 << max(int(np.log2(length / chunk_us) + 0.5), 0)
            start = max(free, ready[i])
            for j in range(chunks):
                plan.append((start + j * length / chunks, len(plan), ("send", group, k, j, chunks)))
            free = start + length
            ready[i] = free + latency
            plan.append((ready[i], len(plan), ("end", group, k, 0, 0)))
    return plan, free


def run_step(step):
    what, group, k, chunk, chunks = step
    for one in group:
        if what == "send":
            one.send(k, chunk, chunks)
        else:
            one.end(k)


class Everyone:
    def __init__(self, line, refs, sems):
        self.line = line
        self.src, self.dst_sib, self.dst_line, self.dst_frames, self.full = refs
        self.sent, self.got = sems
        self.share = self.src.shape[1] // line.chips

    def cols(self, z):
        return pl.ds(pl.multiple_of(z * self.share, self.share), self.share)

    def pair_copy(self):
        ln = self.line
        return ln.copy(self.src, self.dst_sib, self.sent.at[0], self.got.at[0], ln.sibling())

    def line_copies(self):
        ln, copies = self.line, []
        for k in range(1, ln.chips):
            to = (ln.z + k) % ln.chips
            src, dst = self.dst_sib.at[:, self.cols(to)], self.dst_line.at[ln.z]
            copies.append(ln.copy(src, dst, self.sent.at[k], self.got.at[k], ln.at(to)))
        return copies

    def frame_copies(self):
        ln, copies = self.line, []
        for k in range(1, ln.frames):
            to, i = ((ln.f + k) % ln.frames, ln.h), ln.chips + k
            src, dst = self.dst_line.at[ln.z], self.dst_frames.at[ln.f]
            copies.append(ln.copy(src, dst, self.sent.at[i], self.got.at[i], to))
        return copies

    def back_copies(self):
        ln, copies = self.line, []
        for k in range(1, ln.chips):
            to, i = ln.at((ln.z + k) % ln.chips), ln.chips + ln.frames + k
            ref = self.full.at[:, self.cols(ln.z)]
            copies.append(ln.copy(ref, ref, self.sent.at[i], self.got.at[i], to))
        return copies

    def over_pair(self, value):
        self.src[...] = value.astype(BF16)
        self.pair_copy().start()

    def over_line(self):
        self.pair_copy().wait()
        pair = self.src[...].astype(F32) + self.dst_sib[...].astype(F32)
        self.dst_sib[...] = pair.astype(BF16)
        for copy in self.line_copies():
            copy.start()

    def over_frames(self):
        ln = self.line
        for copy in self.line_copies():
            copy.wait()
        total = self.dst_sib[:, self.cols(ln.z)].astype(F32)
        for k in range(1, ln.chips):
            total = total + self.dst_line[(ln.z + k) % ln.chips].astype(F32)
        self.dst_line[ln.z] = total.astype(BF16)
        for copy in self.frame_copies():
            copy.start()
        self.dst_frames[ln.f] = self.dst_line[ln.z]

    def over_back(self):
        for copy in self.frame_copies():
            copy.wait()
        total = self.dst_frames[0].astype(F32)
        for i in range(1, self.line.frames):
            total = total + self.dst_frames[i].astype(F32)
        self.full[:, self.cols(self.line.z)] = total.astype(BF16)
        for copy in self.back_copies():
            copy.start()

    def result(self):
        for copy in self.back_copies():
            copy.wait()
        return self.full[...].astype(F32)


class Timetable:
    PHASES = 5

    def __init__(self, chips, streams):
        self.chips, self.streams = chips, streams
        last = chips - 1
        arrivals = [(d * HOP_US, "arrive", d) for d in range(chips)]
        gathered = last * HOP_US + SIBLING_US
        first = self.sum_steps(0.0)
        middle = self.sum_steps(gathered)
        self.turn = max((middle[-1][0] + OWNER_US) / streams, chips * LINK_US)
        period = self.turn * streams
        second = max(HOP_US, SIBLING_US + COMPUTE_US + SIBLING_US)
        y = self.sum_steps(second - COMPUTE_US - SIBLING_US)
        leads = [0.0, first[-1][0] + OWNER_US + SWAP_US - period]
        leads.append(leads[1] + max(middle[-1][0] + OWNER_US + SWAP_US - period, 0.0))
        groups = (
            (0, 0, leads[0], first),
            (1, 3, leads[1], arrivals + middle),
            (4, 4, leads[2], arrivals + [(gathered, "gathered", 0)] + y),
        )
        self.every = 6
        self.order = []
        for i in range(self.every):
            at = (i + 0.5) * self.turn / self.every
            self.order.append((at, 0.0, "beside", i, 0, 0, 0))
        self.computed = {}
        self.turns = 0
        for low, high, lead, steps in groups:
            for t, what, which in steps:
                t += lead + ADJUST.get((low, what, which), 0.0)
                behind = int(np.floor(t / self.turn))
                at = t - behind * self.turn
                self.order.append((at, -t, what, which, behind, low, high))
                if what == ("gathered" if low == 4 else "compute"):
                    self.computed |= {phase: behind for phase in range(low, high + 1)}
                self.turns = max(self.turns, (high + 1) * streams + behind)
        self.order.sort(key=lambda step: step[:2])

    def sum_steps(self, compute):
        last = self.chips - 1
        steps = [(compute, "compute", 0)]
        start = compute + COMPUTE_US + SIBLING_US
        hops = {}
        for place in range(last):
            t = start
            for far in range(last, place, -1):
                if place:
                    t = max(t, hops[place - 1, far] + HOP_US)
                hops[place, far] = t
                steps.append((t, "hop", (place, far)))
                t += LINK_US
        owner = max(hops[far - 1, far] for far in range(1, self.chips)) + HOP_US
        return steps + [(owner, "owner", 0)]

    def y_owner(self, item):
        t = [t for t in self.order if t[2] == "owner" and t[5] == 4][0]
        return (item + t[4]) * self.every + int(t[0] / self.turn * self.every + 0.5)

    def after(self, item):
        return item + self.computed[item // self.streams] + 1


def pipeline(line, times, turns, gather, sums, enter, compute, gathered, owner, total, beside):
    last, streams = line.chips - 1, times.streams

    def body(m, carry):
        for _, _, what, which, behind, low, high in times.order:
            if what == "beside":
                beside(m, which)
                continue
            n = m - behind
            fits = (n >= low * streams) & (n < (high + 1) * streams)
            n = jnp.clip(n, low * streams, (high + 1) * streams - 1)
            s = n % streams
            held = n - streams
            if what == "hop":
                place, far = which

                @pl.when(fits & (line.z == place))
                def _():
                    sums.hop_up(s, far)

                @pl.when(fits & (line.z == last - place))
                def _():
                    sums.hop_down(s, last - far)

                continue

            @pl.when(fits)
            def _():
                if what == "arrive":
                    if which == 0:
                        enter(n)
                        gather.send(held)
                    else:
                        gather.arrive(which, held)
                elif what == "compute":
                    if low == 4:
                        gather.wait_across(held, line.z)
                    for zb in range(line.chips):
                        if 1 <= low <= 3:
                            gather.wait_across(held, zb)
                        if low:
                            sums.drain(s, zb)
                    compute(n, low, high)
                    for zb in range(line.chips):
                        sums.across(s, zb).start()
                elif what == "gathered":
                    for zb in range(line.chips):

                        @pl.when(line.z != zb)
                        def _():
                            gather.wait_across(held, zb)

                    gathered(n)
                else:
                    sums.finish(s, total)
                    owner(n, low, high)

        return carry

    lax.fori_loop(0, turns, body, 0)


def frame_mask(segments, places, rows):
    frames = segments.shape[0]
    bits, place_bits = frames.bit_length() - 1, places.bit_length() - 1

    def ids_along(axis, shape):
        index = lax.broadcasted_iota(jnp.int32, shape, axis)
        frame = lax.shift_right_logical(index, place_bits) & (frames - 1)
        segment = jnp.zeros(shape, jnp.int32)
        for i in range(frames):
            segment = jnp.where(frame == i, segments[i], segment)
        block = lax.shift_right_logical(index, place_bits + bits)
        return block * places + (index & (places - 1)), frame, segment

    place_q, frame_q, segment_q = ids_along(0, (rows, 1))
    place_k, frame_k, segment_k = ids_along(1, (1, rows))
    return (place_q == place_k) & (frame_k <= frame_q) & (segment_q == segment_k)


def column_grads(start, left, right, out):
    rows = pl.ds(pl.multiple_of(start, 256), 256)
    out[rows] = mm_tn(left, right.reshape(left.shape[0], right.shape[-1])).astype(BF16)


def row_sum(value):
    return jnp.sum(value, axis=0, keepdims=True)


def moved_exactly(order, value):
    out = None
    for _ in range(3):
        term = value.astype(BF16)
        value = value - term.astype(F32)
        out = mm(order, term) if out is None else out + mm(order, term)
    return out


class Refs:
    def __init__(self, names, refs):
        for name, ref in zip(names, refs, strict=True):
            setattr(self, name, ref)


def block(fetched, results, names, *refs):
    ends = len(fetched), len(fetched) + len(results)
    r = Refs(names, refs[ends[1] :])
    r.fetched = dict(zip(fetched, refs))
    r.stored = dict(zip(results, refs[ends[0] :]))
    r.ids, r.segments = r.fetched.pop("ids"), r.fetched.pop("segments")
    steps, patches, width = r.x.shape
    streams, rows, _ = r.y.shape
    heads = 2 * r.g_all.shape[1]
    line, t_line = Line(steps), Line(streams)
    chips, frames = line.chips, line.frames
    s_rows = patches // heads
    tokens = steps * s_rows
    columns, hidden = r.s_wout.shape[0], r.up.shape[1]
    entries = r.table.shape[0]
    count = heads * rows
    all_tokens = heads * tokens
    times = Timetable(chips, streams)
    sums = ChainSum(t_line, (r.part, r.sib, r.rise, r.fall, r.out), r.sum_sems)
    gather = Gather(t_line, r.gathered, r.gather_sems)
    last_part = getattr(r, "last_part", r.g_all)
    last_out = getattr(r, "last_out", r.out)
    last_total = getattr(r, "last_total", r.grad2)
    last_sums = ChainSum(
        line, (last_part, r.last_sib, r.last_rise, r.last_fall, last_out), r.last_sems
    )
    shared = not hasattr(r, "g_src")

    def g_src_at(part, to):
        return r.gathered.at[3 * streams + to] if shared else r.g_src.at[part, to]

    g_swap = Swap(line, g_src_at, r.g_dst, r.g_sems)
    state_swap = Swap(line, lambda s, to: r.state_src.at[s, to], r.state_dst, r.state_sems)
    grad_swap = Swap(line, lambda s, to: r.grad_src.at[s, to], r.grad_dst, r.grad_sems)
    y_swap = Swap(line, lambda s, to: r.y_src.at[s, to], r.y_dst, r.y_sems)
    every = Everyone(
        line,
        (r.every_src, r.every_sib, r.every_line, r.every_frames, r.every_full),
        r.every_sems,
    )
    (
        (down_part, down_sums), (up_part, up_sums),
        (t_q_part, t_q_sums), (t_k_part, t_k_sums), (t_v_part, t_v_sums), (t_out_part, t_out_sums),
        (s_q_part, s_q_sums), (s_k_part, s_k_sums), (s_v_part, s_v_sums), (s_out_part, s_out_sums),
    ) = frame_sums(
        line,
        [
            (r.down_grad, 0, False, 2), (r.up_grad, 0, True, 2),
            (r.t_q, 0, False, 1), (r.t_k, 0, True, 1), (r.t_v, 0, False, 1), (r.t_out, 1, True, 1),
            (r.s_q, 0, False, 1), (r.s_k, 0, True, 1), (r.s_v, 0, False, 1), (r.s_out, 1, True, 1),
        ],
        r.reduce,
    )
    t_parts = t_q_part, t_k_part, t_v_part
    s_parts = s_q_part, s_k_part, s_v_part
    mlp_sums = list(zip(down_sums, up_sums))
    t_sums = [t_q_sums + t_k_sums, t_v_sums + t_out_sums]
    s_sums = [s_q_sums + s_k_sums, s_v_sums]
    bits = len(down_sums[0].bits)
    bias_swap = Swap(line, lambda _, to: r.bias_src, r.bias_dst, r.bias_sems)
    fetches = [
        pltpu.make_async_copy(r.fetched[name], getattr(r, name), r.fetch_sems.at[i])
        for i, name in enumerate(r.fetched)
    ]
    for fetch in fetches:
        fetch.start()
    line.barrier(True, True)
    for fetch in fetches:
        fetch.wait()
    stored = []

    def store(name):
        i = list(r.stored).index(name)
        stored.append(
            pltpu.make_async_copy(getattr(r, name), r.stored[name], r.store_sems.at[i])
        )
        stored[-1].start()

    def g_out(i, carry):
        rows_of = pl.ds(pl.multiple_of(i * s_rows, s_rows), s_rows)
        moved = mm(r.to_peers[...], r.cotangent[:, rows_of].reshape(tokens, width))
        moved = moved.astype(BF16).astype(r.g_dst.dtype).reshape(frames, tokens // frames, width)
        if shared:
            r.gathered[3 * streams : 4 * streams, i // 2, i % 2] = moved
        else:
            r.g_src[0, :, i // 2, i % 2] = moved
        return carry

    lax.fori_loop(0, heads, g_out, 0)
    g_swap.start(0)

    def g_in(i):
        moved = r.g_dst[0, :, i // 2, i % 2].reshape(tokens, width).astype(BF16)
        moved = mm(r.to_parts[...], moved).astype(BF16)
        r.g_all[:, i // 2, i % 2] = moved.reshape(streams, rows, width)

    table_row = lax.broadcasted_iota(jnp.int32, (entries, width), 0)

    def added(s):
        return row_sum(jnp.where(table_row == r.ids[s], r.table[...].astype(F32), 0.0))

    def norm(value, i):
        scaled = norm_stats(value)[0] * r.gain[i : i + 1, :]
        return (scaled + r.shift[i : i + 1, :]).astype(BF16)

    def attention(s, carry):
        normed = norm(r.x[s].astype(F32) + added(s), 0)
        r.normed0[s] = normed
        q = mm(normed, r.s_wqkv[0]).astype(BF16)
        k = mm(normed, r.s_wqkv[1]).astype(BF16)
        v = mm(normed, r.s_wqkv[2]).astype(BF16)
        r.s_proj[0, s] = q
        r.s_proj[1, s] = k
        r.s_proj[2, s] = v
        r.s_cols[s] = attend(q, k, v, None)
        return carry

    lax.fori_loop(0, steps, attention, 0)

    def to_streams(i, carry):
        rows_of = pl.ds(pl.multiple_of(i * s_rows, s_rows), s_rows)
        moved = mm(r.to_streams[...], r.s_cols[:, rows_of].reshape(tokens, columns)).astype(BF16)
        r.s_mixed[:, i] = moved.reshape(streams, rows, columns)
        return carry

    lax.fori_loop(0, heads, to_streams, 0)
    own_rows = pl.ds(pl.multiple_of(line.h * s_rows, s_rows), s_rows)
    own = mm(r.to_streams[...], r.x[:, own_rows].reshape(tokens, width))
    row = lax.broadcasted_iota(jnp.int32, (tokens, 1), 0)
    frame = lax.shift_right_logical(row, (rows // (frames * steps)).bit_length() - 1) & (steps - 1)
    entry = jnp.zeros_like(row)
    for s in range(steps):
        entry = jnp.where(frame == s, r.ids[s], entry)
    picker = (entry == lax.broadcasted_iota(jnp.int32, (tokens, entries), 1)).astype(BF16)
    own = own + mm(picker, r.table[...])
    r.state0[...] = own.reshape(streams, rows, width)
    r.mask[...] = frame_mask(r.segments, rows // (frames * steps), count).astype(F32)
    r.up_bias_grad[...] = jnp.zeros_like(r.up_bias_grad)
    r.small[...] = jnp.zeros_like(r.small)

    def held(n):
        return n - streams

    def enter_temporal(s, n):
        state_swap.wait(s)
        state = r.state_dst[s].reshape(rows, width)
        r.state1[s] = state
        r.gathered[held(n), line.z, line.c] = norm(state, 1)

    def enter_spatial(s, n):
        grad_swap.wait(s)
        grad = r.grad_dst[s].reshape(rows, width)
        r.grad1[s] = grad
        r.gathered[held(n), line.z, line.c] = grad.astype(BF16)

    def compute_spatial(s, n):
        left = r.s_mixed[s].reshape(count, columns)
        r.part[s] = mm(left, r.s_wout[...]).astype(BF16).reshape(chips, 2, rows, width)

    def compute_temporal(s, n):
        a = r.gathered[held(n)].reshape(count, width)
        q = mm(a, r.t_wqkv[0]).astype(BF16)
        k = mm(a, r.t_wqkv[1]).astype(BF16)
        v = mm(a, r.t_wqkv[2]).astype(BF16)
        r.t_proj[0, s] = q
        r.t_proj[1, s] = k
        r.t_proj[2, s] = v
        mixed = attend(q, k, v, r.mask[...] > 0.0)
        r.t_mixed[s] = mixed
        r.part[s] = mm(mixed, r.t_wout[...]).astype(BF16).reshape(chips, 2, rows, width)

    def compute_mlp(s, n):
        a = r.gathered[held(n)].reshape(count, width)
        g = r.g_all[s].reshape(count, width)
        pre = mm(a, r.up[...]) + r.up_bias[...]
        t = jnp.tanh(GELU_C * (pre + 0.044715 * (pre * pre * pre)))
        act = (0.5 * pre * (1.0 + t)).astype(BF16)
        r.act[s] = act
        slope = 0.5 * (1.0 + t)
        slope = slope + 0.5 * pre * (1.0 - t * t) * (GELU_C * (1.0 + 0.134145 * (pre * pre)))
        dpre = (mm_nt(g, r.down[...]) * slope).astype(BF16)
        r.dpre[s] = dpre
        r.up_bias_grad[:, :hidden] += row_sum(dpre.astype(F32))
        r.part[s] = mm_nt(dpre, r.up[...]).astype(BF16).reshape(chips, 2, rows, width)

    def compute_back(s, n):
        grad = r.gathered[held(n)].reshape(count, width)
        dm = mm_nt(grad, r.t_wout[...]).astype(BF16)
        mask = r.mask[...] > 0.0
        dq, dk, dv = attend_back(r.t_proj[0, s], r.t_proj[1, s], r.t_proj[2, s], mask, dm)
        r.t_dproj[0, s] = dq
        r.t_dproj[1, s] = dk
        r.t_dproj[2, s] = dv
        da = mm_nt(dq, r.t_wqkv[0]) + mm_nt(dk, r.t_wqkv[1]) + mm_nt(dv, r.t_wqkv[2])
        r.part[s] = da.astype(BF16).reshape(chips, 2, rows, width)

    def gathered_last(n):
        grad = r.gathered[held(n)].reshape(count, width)
        moved = mm_nt(grad, r.s_wout[...]).astype(BF16)
        r.s_dmixed[n % streams] = moved.reshape(heads, rows, columns)

    def compute_last(s, n):
        y = mm(r.act[s], r.down[...])
        r.part[s] = y.astype(BF16).reshape(chips, 2, rows, width)

    def owner_spatial(s, n):
        state = r.state0[s] + r.total[...] + r.bias[0:1, :]
        r.state_src[s] = state.reshape(r.state_src.shape[1:])
        state_swap.start(s)

    def owner_temporal(s, n):
        state = r.state1[s] + r.total[...] + r.bias[1:2, :]
        r.state2[s] = state
        r.gathered[n, line.z, line.c] = norm(state, 2)

    def owner_mlp(s, n):
        grad = r.g_all[s, line.z, line.c].astype(F32)
        back, gain_grad, shift_grad = norm_back(r.state2[s], r.total[...], r.gain[2:3, :])
        dh = grad + back
        r.grad2[s] = dh
        r.gathered[n, line.z, line.c] = dh.astype(BF16)
        r.small[0:1] += gain_grad
        r.small[1:2] += shift_grad
        r.small[2:3] += row_sum(grad)
        r.small[3:4] += row_sum(dh)

    def owner_back(s, n):
        back, gain_grad, shift_grad = norm_back(r.state1[s], r.total[...], r.gain[1:2, :])
        dh = r.grad2[s] + back
        r.grad_src[s] = dh.reshape(r.grad_src.shape[1:])
        grad_swap.start(s)
        r.small[4:5] += gain_grad
        r.small[5:6] += shift_grad
        r.small[6:7] += row_sum(dh)

    def owner_last(s, n):
        r.y[s] = (r.state2[s] + r.total[...] + r.bias[2:3, :]).astype(BF16)

    def by_phase(bodies):
        def run(n, low=0, high=4):
            for i, one in enumerate(bodies):
                if one is not None and low <= i <= high:

                    @pl.when(n // streams == i)
                    def _():
                        one(n % streams, n)

        return run

    def down_chunk(i):
        cols = pl.ds(pl.multiple_of(i * 128, 128), 128)
        left = r.act[:, :, cols].reshape(all_tokens, 128)
        right = r.g_all[...].reshape(all_tokens, width)
        down_part[cols] = mm_tn(left, right).astype(BF16)

    def up_chunk(i):
        cols = pl.ds(pl.multiple_of(i * 256, 256), 256)
        left = r.gathered[streams : 2 * streams, :, :, :, cols].reshape(all_tokens, 256)
        right = r.dpre[...].reshape(all_tokens, hidden)
        up_part[cols] = mm_tn(left, right).astype(BF16)

    def t_out_chunk(i):
        left = r.t_mixed[...].reshape(all_tokens, columns)
        right = r.gathered[2 * streams : 3 * streams].reshape(all_tokens, width)
        t_out_part[...] = mm_tn(left, right).astype(BF16)

    def t_qkv_chunk(i):
        start = i * 256
        cols = pl.ds(pl.multiple_of(start, 256), 256)
        left = r.gathered[0:streams, :, :, :, cols].reshape(all_tokens, 256)
        for j in range(3):
            column_grads(start, left, r.t_dproj[j], t_parts[j])

    def s_cols_chunk(_):
        def from_streams(i, carry):
            rows_of = pl.ds(pl.multiple_of(i * s_rows, s_rows), s_rows)
            moved = mm(r.from_streams[...], r.s_dmixed[:, i].reshape(tokens, columns)).astype(BF16)
            r.s_cols[:, rows_of] = moved.reshape(steps, s_rows, columns)
            return carry

        lax.fori_loop(0, heads, from_streams, 0)

    def s_back_chunk(s):
        dq, dk, dv = attend_back(r.s_proj[0, s], r.s_proj[1, s], r.s_proj[2, s], None, r.s_cols[s])
        r.s_dproj[0, s] = dq
        r.s_dproj[1, s] = dk
        r.s_dproj[2, s] = dv
        da = mm_nt(dq, r.s_wqkv[0]) + mm_nt(dk, r.s_wqkv[1]) + mm_nt(dv, r.s_wqkv[2])
        last_part[s] = da.astype(BF16).reshape(last_part.shape[1:])
        for zb in range(chips):
            last_sums.across(s, zb).start()
        if early:

            @pl.when(s == 1)
            def _():
                drain_all(t_line, (sums,), streams)

            @pl.when(s > 0)
            def _():
                last_sums.hops(s - 1)

    def s_out_chunk(_):
        left = r.s_mixed[...].reshape(all_tokens, columns)
        right = r.gathered[3 * streams : 4 * streams].reshape(all_tokens, width)
        s_out_part[...] = mm_tn(left, right).astype(BF16)
        s_out_sums[0].send(0)

    def bias_chunk(_):
        r.bias_src[...] = jnp.broadcast_to(r.up_bias_grad[...], r.bias_src.shape)
        bias_swap.start(0)

    def g_in_chunk(i):
        @pl.when(i == 0)
        def _():
            g_swap.wait(0)

        g_in(i)

    n_down, n_up = hidden // 128, width // 256
    turn_of = times.after
    mlp_turn, back_turn = turn_of(3 * streams - 1), turn_of(4 * streams - 1)
    last_turn = turn_of(5 * streams - 1)
    chunks = (
        (streams + 1, 0, heads, g_in_chunk),
        (mlp_turn, 0, n_down, down_chunk),
        (mlp_turn, n_down, n_up, up_chunk),
        (mlp_turn, n_down + n_up, 1, bias_chunk),
        (back_turn, 0, 1, t_out_chunk),
        (back_turn, 1, width // 256, t_qkv_chunk),
        (last_turn, 0, 1, s_out_chunk),
        (last_turn, 1, 1, s_cols_chunk),
        (last_turn, 2, steps, s_back_chunk),
    )
    slots = [i for i in range(times.every) if i % 2 == 1][:3]
    per_slot = 3
    per_turn = per_slot * len(slots)
    turns = max(times.turns, last_turn + -(-(steps + 2) // per_turn))
    early = times.y_owner(5 * streams - 1) < last_turn * times.every + slots[1]

    def begin_of(turn, number):
        return (turn + number // per_turn) * times.every + times.every - 1

    begin = begin_of(mlp_turn, n_down + n_up) * SLOT_US
    plan, free = stage_times(mlp_sums, [begin] * 2, MLP_US, bits, 0.0, FRAME_US, CHUNK_US)
    begin = begin_of(back_turn, 1 + width // 256) * SLOT_US
    plan += stage_times(t_sums, [begin] * 2, ATTENTION_US, bits, free, FRAME_US, WHOLE_US)[0]
    plan = [(t, i, step) for i, (t, _, step) in enumerate(plan)]
    plan.sort(key=lambda entry: entry[:2])
    end = turns * times.every * SLOT_US
    late = [entry for entry in plan if entry[0] >= end]

    def beside(m, i):
        if i in slots:
            for turn, first, number, chunk in chunks:
                which = per_turn * (m - turn) + per_slot * slots.index(i) - first
                here = jnp.clip(number - which, 0, per_slot)

                @pl.when((which > -per_slot) & (which < number))
                def _():
                    def one(j, carry):
                        @pl.when(which + j >= 0)
                        def _():
                            chunk(which + j)

                        return carry

                    lax.fori_loop(0, here, one, 0)

        for t, _, step in plan:
            moment = int(t / SLOT_US)
            if t < end and moment % times.every == i:

                @pl.when(m == moment // times.every)
                def _():
                    run_step(step)

    enter = by_phase((None, enter_temporal, None, None, enter_spatial))
    compute = by_phase(
        (compute_spatial, compute_temporal, compute_mlp, compute_back, compute_last)
    )
    owner = by_phase((owner_spatial, owner_temporal, owner_mlp, owner_back, owner_last))
    pipeline(
        t_line, times, turns, gather, sums, enter, compute, gathered_last, owner, r.total, beside
    )
    if not early:
        drain_all(t_line, (sums,), streams)

    y = mm(r.from_parts[...], r.y[...].reshape(tokens, width)).astype(BF16)
    r.y_src[0] = y.astype(r.y_src.dtype).reshape(r.y_src.shape[1:])
    y_swap.start(0)

    r.sums0[...] = jnp.zeros_like(r.sums0)

    def small_part(s):
        state = r.x[s].astype(F32) + added(s)
        da = last_part[s].reshape(patches, width).astype(F32)
        back, gain_grad, shift_grad = norm_back(state, da, r.gain[0:1, :])
        r.sums0[0:1] += gain_grad
        r.sums0[1:2] += shift_grad
        r.sums0[8 : 8 + entries] += jnp.where(table_row == r.ids[s], row_sum(back), 0.0)

    room = r.every_src.shape[0]
    filled = 9 + entries

    def small_value(own_grad):
        for s in range(steps):
            here = row_sum(own_grad[s * s_rows : (s + 1) * s_rows])
            r.sums0[8 : 8 + entries] += jnp.where(table_row == r.ids[s], here, 0.0)
        rows_of = [
            r.sums0[0:1], r.small[4:5], r.small[0:1],
            r.sums0[1:2], r.small[5:6], r.small[1:2],
            r.small[6:7], r.small[3:4], r.small[2:3],
            r.sums0[8 : 8 + entries], jnp.zeros((room - filled, width), F32),
        ]
        return jnp.concatenate(rows_of, axis=0)

    first = steps - 1 if early else 0
    begin = LAST_GRADS * STEP_US + 2.5
    last_plan = [(max(int((t - end) / STEP_US), 0) + first + 1, i, step) for t, i, step in late]
    begins = [begin] * len(s_sums) + [begin - 4.0]
    s_plan, _ = stage_times(
        s_sums + [s_out_sums], begins, ATTENTION_US, bits, 0.0, LAST_FRAME_US, WHOLE_US
    )
    last_plan += [
        (int(np.ceil(t / STEP_US)), len(plan) + i, step)
        for t, i, step in s_plan
        if step[0] == "end" or step[2] > 0
    ]
    last_plan.sort(key=lambda entry: entry[:2])
    bound = steps * (chips - 1) + (chips - 2) * LAG + 1
    bound = max(bound, LAST_SMALL[-1] + 1)

    def body(t, carry):
        last_sums.hops(t)

        @pl.when(t == LAST_GRADS)
        def _():
            for j in range(3):
                for i in range(width // 256):
                    left = r.normed0[:, :, i * 256 : (i + 1) * 256].reshape(all_tokens, 256)
                    column_grads(i * 256, left, r.s_dproj[j], s_parts[j])
            for one in s_q_sums + s_k_sums + s_v_sums:
                one.send(0)

        @pl.when((t > LAST_GRADS) & (t <= LAST_GRADS + steps // 2))
        def _():
            def one(i, carry):
                small_part((t - LAST_GRADS - 1) * 2 + i)
                return carry

            lax.fori_loop(0, 2, one, 0)

        @pl.when(t == LAST_SMALL[0])
        def _():
            grad = r.grad1[...].reshape(tokens, width)
            own_grad = moved_exactly(r.from_streams[...], grad)
            r.state0[...] = own_grad.reshape(r.state0.shape)
            every.over_pair(small_value(own_grad))

        steps_of = (every.over_line, every.over_frames, every.over_back)
        for moment, step in zip(LAST_SMALL[1:], steps_of):

            @pl.when(t == moment)
            def _():
                step()

        for moment, _, step in last_plan:
            if moment < bound:

                @pl.when(t == max(moment, first))
                def _():
                    run_step(step)

        return carry

    lax.fori_loop(first, bound, body, 0)
    for s in range(steps):
        last_sums.finish(s, last_total.at[s])
    own_grad = r.state0[...].reshape(tokens, width)
    for s in range(steps):
        state = r.x[s, own_rows].astype(F32) + added(s)
        back, _, _ = norm_back(state, last_total[s], r.gain[0:1, :])
        r.grad_res[pl.ds(s * s_rows, s_rows)] = own_grad[s * s_rows : (s + 1) * s_rows] + back
    y_swap.wait(0)
    r.y_res[...] = mm(r.from_peers[...], r.y_dst[0].reshape(tokens, width).astype(BF16)).astype(BF16)
    r.small_res[...] = every.result()
    bias_swap.wait(0)
    up_bias = r.bias_dst[0, 0]
    for i in range(1, frames):
        up_bias = up_bias + r.bias_dst[0, i]
    r.up_bias_res[...] = up_bias
    for name in ("grad_res", "y_res", "small_res", "up_bias_res") + MLP_RESULTS:
        store(name)
    for moment, _, step in last_plan:
        if moment >= bound:
            run_step(step)
    for name in T_RESULTS + S_RESULTS:
        store(name)
    drain_all(line, (last_sums,), steps)
    drain_all(t_line, (gather,), 4 * streams)
    for one in stored:
        one.wait()


def finish(names, parts, *refs):
    sources = dict(zip(names, refs))
    results = dict(zip(parts, refs[len(names) :]))
    held = refs[len(names) + len(parts) :]
    sems_in, sems_out = held[-2:]
    local = dict(zip(names, held))
    made = dict(zip(parts, held[len(names) :]))
    loads = {
        name: pltpu.make_async_copy(sources[name], local[name], sems_in.at[i])
        for i, name in enumerate(names)
    }
    for load in loads.values():
        load.start()
    loaded, stores = set(), []
    for i, (name, given) in enumerate(parts.items()):
        for j, (source, low, high, columns) in enumerate(given):
            if source not in loaded:
                loads[source].wait()
                loaded.add(source)
            value = local[source][low:high, :columns].astype(made[name].dtype)
            if len(given) > 1:
                made[name][j] = value
            else:
                made[name][...] = value
        stores.append(pltpu.make_async_copy(made[name], results[name], sems_out.at[i]))
        stores[-1].start()
    for store in stores:
        store.wait()


def results(found, entries):
    width, hidden = found["up_grad"].shape

    def whole(name):
        rows, columns = found[name].shape
        return [(name, 0, rows, columns)]

    parts = {
        "down": whole("down_grad"),
        "up": whole("up_grad"),
        "t_qkv": whole("t_q") + whole("t_k") + whole("t_v"),
        "t_out": whole("t_out"),
        "grad": whole("grad_res"),
        "y": whole("y_res"),
        "gain": [("small_res", 0, 3, width)],
        "shift": [("small_res", 3, 6, width)],
        "bias": [("small_res", 6, 9, width)],
        "table": [("small_res", 9, 9 + entries, width)],
        "up_bias": [("up_bias_res", 0, 1, hidden)],
        "s_out": whole("s_out"),
        "s_qkv": whole("s_q") + whole("s_k") + whole("s_v"),
    }
    shapes = []
    for name, given in parts.items():
        _, low, high, columns = given[0]
        lead = (len(given),) if len(given) > 1 else ()
        kind = BF16 if name == "y" else F32
        shapes.append(jax.ShapeDtypeStruct(lead + (high - low, columns), kind))
    names = tuple(found)
    made = pl.pallas_call(
        lambda *refs: finish(names, parts, *refs),
        name="finish",
        out_shape=shapes,
        in_specs=[pl.BlockSpec(memory_space=pltpu.HBM)] * len(names),
        out_specs=[pl.BlockSpec(memory_space=pltpu.HBM)] * len(shapes),
        scratch_shapes=[pltpu.VMEM(v.shape, v.dtype) for v in found.values()]
        + [pltpu.VMEM(v.shape, v.dtype) for v in shapes]
        + [pltpu.SemaphoreType.DMA((len(names),)), pltpu.SemaphoreType.DMA((len(shapes),))],
        compiler_params=pltpu.CompilerParams(vmem_limit_bytes=VMEM_LIMIT),
    )(*found.values())
    return dict(zip(parts, made))


def orders(frames_local, frames, places, streams):
    tokens = frames_local * frames * places
    index = np.arange(tokens).reshape(frames_local, frames, streams, places // streams)
    to_streams = index.transpose(2, 1, 0, 3).reshape(-1)
    to_peers = index.transpose(1, 0, 2, 3).reshape(-1)
    index = np.arange(tokens).reshape(frames * frames_local, streams, places // streams)
    to_parts = index.transpose(1, 0, 2).reshape(-1)
    eye = np.eye(tokens, dtype=np.float32)
    there = [eye[order] for order in (to_streams, to_peers, to_parts)]
    back = [m.T for m in there]
    names = ("to_streams", "to_peers", "to_parts", "from_streams", "from_peers", "from_parts")
    return {name: jnp.asarray(m, BF16) for name, m in zip(names, there + back)}


def on_device(
    block_input,
    action_ids,
    segment_ids,
    action_table,
    norm_gain,
    norm_shift,
    spatial_qkv,
    spatial_out,
    temporal_qkv,
    temporal_out,
    out_bias,
    up_weight,
    up_bias,
    down_weight,
    cotangent,
):
    frames, heads = lax.axis_size("frames"), lax.axis_size("heads")
    chips = heads // 2
    steps, patches, width = block_input.shape
    rows = patches // heads
    tokens = steps * rows
    total_frames = segment_ids.shape[0]
    places = rows // frames
    streams = min(4, places)
    t_rows = tokens // streams
    columns = spatial_out.shape[0]
    hidden = up_weight.shape[1]
    entries = action_table.shape[0]
    count = heads * t_rows
    room = -(-(10 + entries) // 16) * 16
    args = dict(
        ids=action_ids,
        segments=segment_ids,
        x=block_input,
        cotangent=cotangent,
        table=action_table,
        gain=norm_gain,
        shift=norm_shift,
        bias=out_bias,
        s_wqkv=spatial_qkv.transpose(1, 0, 2),
        s_wout=spatial_out,
        t_wqkv=temporal_qkv.transpose(1, 0, 2),
        t_wout=temporal_out,
        up=up_weight,
        up_bias=up_bias.reshape(1, hidden),
        down=down_weight,
        **orders(steps, frames, places, streams),
    )
    qkv, out = (width, columns), (columns, width)
    down, up = (hidden, width), (width, hidden)
    outs = dict(
        t_q=(qkv, BF16),
        t_k=(qkv, BF16),
        t_v=(qkv, BF16),
        t_out=(out, BF16),
        s_q=(qkv, BF16),
        s_k=(qkv, BF16),
        s_v=(qkv, BF16),
        s_out=(out, BF16),
        up_grad=(up, BF16),
        down_grad=(down, BF16),
        y_res=((tokens, width), BF16),
        grad_res=((tokens, width), F32),
        small_res=((room, width), F32),
        up_bias_res=((8, width), F32),
    )
    s_all = (steps, chips, 2, rows, width)
    t_all = (streams, chips, 2, t_rows, width)
    s_one, t_one = (steps, chips, rows, width), (streams, chips, t_rows, width)
    owned = (streams, t_rows, width)
    swapped = (streams, frames, t_rows // frames, width)
    whole = (1, frames, tokens // frames, width)
    g_part = (1, frames, chips, 2, tokens // frames, width)

    def kind_of(shape):
        return BF16 if shape[-2] % 16 == 0 else F32

    cols = dict(
        s_cols=(steps, patches, columns),
        s_proj=(3, steps, patches, columns),
        s_dproj=(3, steps, patches, columns),
        s_mixed=(streams, heads, t_rows, columns),
        s_dmixed=(streams, heads, t_rows, columns),
        t_proj=(3, streams, count, columns),
        t_dproj=(3, streams, count, columns),
        t_mixed=(streams, count, columns),
        act=(streams, count, hidden),
        dpre=(streams, count, hidden),
        normed0=(steps, patches, width),
        gathered=(4 * streams,) + t_all[1:],
        g_all=t_all,
        part=t_all,
        sib=t_one,
        rise=t_one,
        fall=t_one,
        out=t_one,
        **({} if s_all == t_all else dict(last_part=s_all, last_out=s_one)),
        last_sib=s_one,
        last_rise=s_one,
        last_fall=s_one,
        y=owned,
    )
    floats = dict(
        state0=owned,
        state1=owned,
        state2=owned,
        grad1=owned,
        grad2=owned,
        total=(t_rows, width),
        **({} if (steps, rows) == (streams, t_rows) else dict(last_total=(steps, rows, width))),
        mask=(count, count),
        small=(8, width),
        sums0=(8 + entries, width),
        up_bias_grad=(1, width),
        state_src=swapped,
        state_dst=swapped,
        grad_src=swapped,
        grad_dst=swapped,
    )
    scratch = {name: pltpu.VMEM(shape, BF16) for name, shape in cols.items()}
    scratch |= {name: pltpu.VMEM(shape, F32) for name, shape in floats.items()}
    moving = ("g_dst",) if g_part[1:] == t_all else ("g_src", "g_dst")
    scratch |= {name: pltpu.VMEM(g_part, kind_of(g_part)) for name in moving}
    scratch |= {name: pltpu.VMEM(whole, kind_of(whole)) for name in ("y_src", "y_dst")}
    every_shape = (room, width)
    scratch |= dict(
        every_src=pltpu.VMEM(every_shape, BF16),
        every_sib=pltpu.VMEM(every_shape, BF16),
        every_line=pltpu.VMEM((chips, room, width // chips), BF16),
        every_frames=pltpu.VMEM((frames, room, width // chips), BF16),
        every_full=pltpu.VMEM(every_shape, BF16),
        every_sems=[pltpu.SemaphoreType.DMA((2 * chips + frames,))] * 2,
        bias_src=pltpu.VMEM((8, width), F32),
        bias_dst=pltpu.VMEM((1, frames, 8, width), F32),
        bias_sems=[pltpu.SemaphoreType.DMA((1, frames))] * 2,
        sum_sems=[pltpu.SemaphoreType.DMA((streams, chips))] * 5,
        last_sems=[pltpu.SemaphoreType.DMA((steps, chips))] * 5,
        gather_sems=[pltpu.SemaphoreType.DMA((4 * streams, chips))] * 5,
        state_sems=[pltpu.SemaphoreType.DMA((streams, frames))] * 2,
        grad_sems=[pltpu.SemaphoreType.DMA((streams, frames))] * 2,
        g_sems=[pltpu.SemaphoreType.DMA((1, frames))] * 2,
        y_sems=[pltpu.SemaphoreType.DMA((1, frames))] * 2,
        reduce=[
            x
            for shape, dim, pieces in ((down, 0, 2), (up, 0, 2))
            + 2 * (((qkv, 0, 1),) * 3 + ((out, 1, 1),))
            for x in frame_sum_scratch(frames, shape, dim, pieces)
        ],
    )
    held = {k: v for k, v in args.items() if k not in ("ids", "segments")}
    scratch |= {name: pltpu.VMEM(v.shape, v.dtype) for name, v in held.items()}
    scratch |= {name: pltpu.VMEM(shape, kind) for name, (shape, kind) in outs.items()}
    scratch["fetch_sems"] = pltpu.SemaphoreType.DMA((len(held),))
    scratch["store_sems"] = pltpu.SemaphoreType.DMA((len(outs),))
    fetched, results_of, names = tuple(args), tuple(outs), tuple(scratch)
    parts = pl.pallas_call(
        lambda *refs: block(fetched, results_of, names, *refs),
        name="block",
        out_shape=[jax.ShapeDtypeStruct(shape, kind) for shape, kind in outs.values()],
        in_specs=[
            pl.BlockSpec(memory_space=pltpu.HBM if name in held else pltpu.SMEM)
            for name in args
        ],
        out_specs=[pl.BlockSpec(memory_space=pltpu.HBM)] * len(outs),
        scratch_shapes=list(scratch.values()),
        compiler_params=pltpu.CompilerParams(
            collective_id=0, has_side_effects=True, vmem_limit_bytes=VMEM_LIMIT
        ),
    )(*args.values())
    made = results(dict(zip(outs, parts)), entries)
    s_blocks = (steps, rows, width)
    return (
        made["y"].reshape(s_blocks),
        made["grad"].reshape(s_blocks),
        made["table"],
        made["gain"],
        made["shift"],
        made["s_qkv"].transpose(1, 0, 2),
        made["s_out"],
        made["t_qkv"].transpose(1, 0, 2),
        made["t_out"],
        made["bias"],
        made["up"],
        made["up_bias"].reshape(hidden),
        made["down"],
    )


def solution(mesh):
    return jax.shard_map(
        on_device,
        mesh=mesh,
        in_specs=(
            P("frames", None, None),
            P("frames"),
            P(),
            P(),
            P(),
            P(),
            P(None, None, "heads"),
            P("heads", None),
            P(None, None, "heads"),
            P("heads", None),
            P(),
            P(None, "heads"),
            P("heads"),
            P("heads", None),
            P("frames", None, None),
        ),
        out_specs=(
            P("frames", "heads", None),
            P("frames", "heads", None),
            P(),
            P(),
            P(),
            P(None, None, "heads"),
            P("heads", None),
            P(None, None, "heads"),
            P("heads", None),
            P(),
            P(None, "heads"),
            P("heads"),
            P("heads", None),
        ),
        check_vma=False,
    )
```

```python
import jax
import jax.numpy as jnp
import numpy as np
from jax import lax
from jax.experimental import pallas as pl
from jax.experimental.pallas import tpu as pltpu
from jax.sharding import PartitionSpec as P

HD = 64
SCALE = HD**-0.5
EPS = 1e-05
MASKED = -1000000000.0
F32 = jnp.float32
BF16 = jnp.bfloat16
MESH = pl.DeviceIdType.MESH
MLP_RESULTS = ("down_grad", "up_grad")
T_RESULTS = ("t_q", "t_k", "t_v", "t_out")
S_RESULTS = ("s_q", "s_k", "s_v", "s_out")
VMEM_LIMIT = 62 * 1024 * 1024
GELU_C = float(np.sqrt(2.0 / np.pi))
LAG = 2
SLOT_US, STEP_US, FRAME_US, MLP_US, ATTENTION_US, LAST_FRAME_US = 1.15, 1.45, 4.5, 5.8, 2.9, 3.6
CHUNK_US, WHOLE_US = 1.45, 100.0
ADJUST = {(1, 'hop', (0, 3)): -1.2, (4, 'owner', 0): 0.3}
LAST_GRADS = 3
LAST_SMALL = (5, 6, 9, 12)
HOP_US, SIBLING_US, COMPUTE_US, LINK_US, OWNER_US, SWAP_US = 3.4, 1.0, 2.0, 1.45, 1.0, 4.0


def mm(a, b):
    return lax.dot_general(a, b, (((1,), (0,)), ((), ())), preferred_element_type=F32)


def mm_nt(a, b):
    return lax.dot_general(a, b, (((1,), (1,)), ((), ())), preferred_element_type=F32)


def mm_tn(a, b):
    return lax.dot_general(a, b, (((0,), (0,)), ((), ())), preferred_element_type=F32)


def norm_stats(value):
    centered = value - jnp.mean(value, axis=-1, keepdims=True)
    inv = lax.rsqrt(jnp.mean(centered * centered, axis=-1, keepdims=True) + EPS)
    return centered * inv, inv


def norm_back(value, grad, gain):
    normed, inv = norm_stats(value)
    e = grad * gain
    first = jnp.mean(e, axis=-1, keepdims=True)
    second = jnp.mean(e * normed, axis=-1, keepdims=True)
    gain_grad = jnp.sum(grad * normed, axis=0, keepdims=True)
    shift_grad = jnp.sum(grad, axis=0, keepdims=True)
    return (e - first - normed * second) * inv, gain_grad, shift_grad


def head_lanes(shape, head):
    lane = lax.broadcasted_iota(jnp.int32, shape, 1)
    return (lane >= head * HD) & (lane < (head + 1) * HD)


def softmax_of(q, k, mask):
    scores = mm_nt(q, k) * SCALE
    if mask is not None:
        scores = jnp.where(mask, scores, MASKED)
    raised = jnp.exp(scores - jnp.max(scores, axis=-1, keepdims=True))
    return raised / jnp.sum(raised, axis=-1, keepdims=True)


def attend(q, k, v, mask):
    heads = q.shape[1] // HD
    mixed = None
    for head in range(heads):
        lanes = head_lanes(q.shape, head)
        probs = softmax_of(jnp.where(lanes, q, jnp.zeros_like(q)), k, mask).astype(BF16)
        out = mm(probs, v)
        mixed = out if mixed is None else jnp.where(lanes, out, mixed)
    return mixed.astype(BF16)


def attend_back(q, k, v, mask, grad):
    heads = q.shape[1] // HD
    dq = dk = dv = None
    for head in range(heads):
        lanes = head_lanes(q.shape, head)
        qh = jnp.where(lanes, q, jnp.zeros_like(q))
        gh = jnp.where(lanes, grad, jnp.zeros_like(grad))
        probs = softmax_of(qh, k, mask)
        dvh = mm_tn(probs.astype(BF16), gh)
        dp = mm_nt(gh, v)
        ds = (probs * (dp - jnp.sum(dp * probs, axis=-1, keepdims=True))).astype(BF16)
        dqh = mm(ds, k) * SCALE
        dkh = mm_tn(ds, qh) * SCALE
        if head == 0:
            dq, dk, dv = dqh, dkh, dvh
        else:
            dq = jnp.where(lanes, dqh, dq)
            dk = dk + dkh
            dv = dv + dvh
    return dq.astype(BF16), dk.astype(BF16), dv.astype(BF16)


class Line:
    def __init__(self, steps):
        self.frames = lax.axis_size("frames")
        self.heads = lax.axis_size("heads")
        self.chips = self.heads // 2
        self.f = lax.axis_index("frames")
        self.h = lax.axis_index("heads")
        self.z = self.h // 2
        self.c = self.h % 2
        self.steps = steps

    def at(self, z):
        return (self.f, jnp.clip(z, 0, self.chips - 1) * 2 + self.c)

    def sibling(self):
        return (self.f, self.z * 2 + 1 - self.c)

    def barrier(self, over_frames, whole_line=False):
        sem = pltpu.get_barrier_semaphore()

        def greet(device):
            pl.semaphore_signal(sem, inc=1, device_id=device, device_id_type=MESH)

        greet(self.sibling())
        count = 1
        if over_frames:
            for k in range(1, self.frames):
                greet(((self.f + k) % self.frames, self.h))
            count += self.frames - 1
        if whole_line:
            for k in range(1, self.chips):
                greet(self.at((self.z + k) % self.chips))
            count += self.chips - 1
        else:

            @pl.when(self.z > 0)
            def _():
                greet(self.at(self.z - 1))

            @pl.when(self.z < self.chips - 1)
            def _():
                greet(self.at(self.z + 1))

            count = count + (self.z > 0).astype(jnp.int32)
            count = count + (self.z < self.chips - 1).astype(jnp.int32)
        pl.semaphore_wait(sem, count)

    def copy(self, src, dst, send, recv, device):
        return pltpu.make_async_remote_copy(
            src_ref=src,
            dst_ref=dst,
            send_sem=send,
            recv_sem=recv,
            device_id=device,
            device_id_type=MESH,
        )


class Gather:
    def __init__(self, line, buf, sems):
        self.line, self.buf = line, buf
        self.got, self.got_sib, self.sent_up, self.sent_down, self.sent_sib = sems

    def up(self, s, zb):
        ln = self.line
        ref = self.buf.at[s, zb, ln.c]
        return ln.copy(ref, ref, self.sent_up.at[s, zb], self.got.at[s, zb], ln.at(ln.z + 1))

    def down(self, s, zb):
        ln = self.line
        ref = self.buf.at[s, zb, ln.c]
        return ln.copy(ref, ref, self.sent_down.at[s, zb], self.got.at[s, zb], ln.at(ln.z - 1))

    def across(self, s, zb):
        ln = self.line
        ref = self.buf.at[s, zb, ln.c]
        return ln.copy(ref, ref, self.sent_sib.at[s, zb], self.got_sib.at[s, zb], ln.sibling())

    def wait_across(self, s, zb):
        ln = self.line
        ref = self.buf.at[s, zb, 1 - ln.c]
        ln.copy(
            ref, ref, self.sent_sib.at[s, zb], self.got_sib.at[s, zb], ln.sibling()
        ).wait_recv()

    def send(self, s):
        ln = self.line

        @pl.when(ln.z < ln.chips - 1)
        def _():
            self.up(s, ln.z).start()

        @pl.when(ln.z > 0)
        def _():
            self.down(s, ln.z).start()

        self.across(s, ln.z).start()

    def start(self, own):
        ln = self.line
        for s in range(ln.steps):
            self.buf[s, ln.z, ln.c] = own[s]
            self.send(s)

    def arrive(self, distance, s):
        ln = self.line
        below, above = ln.z - distance, ln.z + distance

        @pl.when((distance > 0) & (below >= 0))
        def _():
            self.up(s, below).wait_recv()

            @pl.when(ln.z < ln.chips - 1)
            def _():
                self.up(s, below).start()

            self.across(s, below).start()

        @pl.when((distance > 0) & (above < ln.chips))
        def _():
            self.down(s, above).wait_recv()

            @pl.when(ln.z > 0)
            def _():
                self.down(s, above).start()

            self.across(s, above).start()

    def drain(self, s, zb):
        ln = self.line

        @pl.when((zb <= ln.z) & (ln.z < ln.chips - 1))
        def _():
            self.up(s, zb).wait_send()

        @pl.when((zb >= ln.z) & (ln.z > 0))
        def _():
            self.down(s, zb).wait_send()

        self.across(s, zb).wait_send()


class ChainSum:
    def __init__(self, line, bufs, sems):
        self.line = line
        self.part, self.sib, self.rise, self.fall, self.out = bufs
        self.sent_sib, self.got_sib, self.got_up, self.got_down, self.sent = sems

    def across(self, s, zb):
        ln = self.line
        return ln.copy(
            self.part.at[s, zb, 1 - ln.c],
            self.sib.at[s, zb],
            self.sent_sib.at[s, zb],
            self.got_sib.at[s, zb],
            ln.sibling(),
        )

    def up(self, s, o):
        ln = self.line
        return ln.copy(
            self.out.at[s, o],
            self.rise.at[s, o],
            self.sent.at[s, o],
            self.got_up.at[s, o],
            ln.at(ln.z + 1),
        )

    def down(self, s, o):
        ln = self.line
        return ln.copy(
            self.out.at[s, o],
            self.fall.at[s, o],
            self.sent.at[s, o],
            self.got_down.at[s, o],
            ln.at(ln.z - 1),
        )

    def mine(self, s, o):
        return self.part[s, o, self.line.c].astype(F32) + self.sib[s, o].astype(F32)

    def hop_up(self, s, o):
        ln = self.line
        self.across(s, o).wait_recv()

        @pl.when(ln.z == 0)
        def _():
            self.out[s, o] = self.mine(s, o).astype(BF16)

        @pl.when(ln.z > 0)
        def _():
            self.up(s, o).wait_recv()
            self.out[s, o] = (self.mine(s, o) + self.rise[s, o].astype(F32)).astype(BF16)

        self.up(s, o).start()

    def hop_down(self, s, o):
        ln = self.line
        self.across(s, o).wait_recv()

        @pl.when(ln.z == ln.chips - 1)
        def _():
            self.out[s, o] = self.mine(s, o).astype(BF16)

        @pl.when(ln.z < ln.chips - 1)
        def _():
            self.down(s, o).wait_recv()
            self.out[s, o] = (self.mine(s, o) + self.fall[s, o].astype(F32)).astype(BF16)

        self.down(s, o).start()

    def hops(self, t, part=None, fits=True):
        ln = self.line
        last = ln.chips - 1
        for upward in (True, False):
            place = ln.z if upward else last - ln.z
            q = t - place * LAG
            if part is None:
                turn = jnp.maximum(q, 0) // ln.steps
                s = jnp.maximum(q, 0) % ln.steps
            else:
                turn, s = jnp.maximum(q, 0), part
            far = jnp.clip(last - turn, 0, last)
            ok = (q >= 0) & (turn < last) & (far > place) & fits
            o = far if upward else last - far

            @pl.when(ok)
            def _():
                if upward:
                    self.hop_up(s, o)
                else:
                    self.hop_down(s, o)

    def finish(self, s, total):
        ln = self.line
        self.across(s, ln.z).wait_recv()
        total[...] = self.mine(s, ln.z)

        @pl.when(ln.z > 0)
        def _():
            self.up(s, ln.z).wait_recv()
            total[...] += self.rise[s, ln.z].astype(F32)

        @pl.when(ln.z < ln.chips - 1)
        def _():
            self.down(s, ln.z).wait_recv()
            total[...] += self.fall[s, ln.z].astype(F32)

    def drain(self, s, zb):
        ln = self.line
        self.across(s, zb).wait_send()

        @pl.when(zb != ln.z)
        def _():
            self.up(s, zb).wait_send()


def drain_all(line, things, parts):
    def body(i, carry):
        for thing in things:
            thing.drain(i // line.chips, i % line.chips)
        return carry

    lax.fori_loop(0, parts * line.chips, body, 0)


class Swap:
    def __init__(self, line, src_at, dst, sems):
        self.line, self.src_at, self.dst = line, src_at, dst
        self.sent, self.got = sems

    def copy(self, part, k):
        ln = self.line
        to = (ln.f + k) % ln.frames
        return ln.copy(
            self.src_at(part, to),
            self.dst.at[part, ln.f],
            self.sent.at[part, k],
            self.got.at[part, k],
            (to, ln.h),
        )

    def start(self, part):
        ln = self.line
        for k in range(1, ln.frames):
            self.copy(part, k).start()
        self.dst[part, ln.f] = self.src_at(part, ln.f)[...]

    def wait(self, part):
        for k in range(1, self.line.frames):
            self.copy(part, k).wait()


class FrameSum:
    def __init__(self, line, part, full, dim, reverse, recv_bufs, sems):
        self.line, self.part, self.full, self.dim = line, part, full, dim
        self.recv_bufs = recv_bufs
        self.sent, self.got, self.sent_back, self.got_back = sems
        bits = range(line.frames.bit_length() - 1)
        self.bits = list(reversed(bits)) if reverse else list(bits)
        self.spans = []
        start, size = 0, part.shape[dim]
        for bit in self.bits:
            size //= 2
            side = (line.f // (1 << bit)) % 2
            peer = (line.f + (1 - 2 * side) * (1 << bit), line.h)
            keep, give = start + side * size, start + (1 - side) * size
            self.spans.append((keep, give, size, peer))
            start = keep

    def view(self, ref, start, size, step):
        if self.dim == 0:
            return ref.at[pl.ds(pl.multiple_of(start, step), size)]
        return ref.at[:, pl.ds(pl.multiple_of(start, step), size)]

    def out(self, i, chunk=0, chunks=1):
        _, give, size, peer = self.spans[i]
        step = size // chunks
        src = self.view(self.part, give + chunk * step, step, step)
        dst = self.view(self.recv_bufs[i], chunk * step, step, step)
        return self.line.copy(src, dst, self.sent.at[i], self.got.at[i], peer)

    def back(self, i, chunk=0, chunks=1):
        keep, _, size, peer = self.spans[i]
        step = size // chunks
        ref = self.view(self.full, keep + chunk * step, step, step)
        return self.line.copy(ref, ref, self.sent_back.at[i], self.got_back.at[i], peer)

    def back_in(self, i):
        _, give, size, peer = self.spans[i]
        ref = self.view(self.full, give, size, size)
        return self.line.copy(ref, ref, self.sent_back.at[i], self.got_back.at[i], peer)

    def send(self, k, chunk=0, chunks=1):
        n = len(self.bits)
        if k < n:
            self.out(k, chunk, chunks).start()
        else:
            self.back(2 * n - 1 - k, chunk, chunks).start()

    def end(self, k):
        n = len(self.bits)
        if k < n:
            keep, _, size, _ = self.spans[k]
            self.out(k).wait()
            ref = self.view(self.part, keep, size, size)
            to = self.view(self.full, keep, size, size) if k == n - 1 else ref
            to[...] = (ref[...].astype(F32) + self.recv_bufs[k][...].astype(F32)).astype(BF16)
        else:
            i = 2 * n - 1 - k
            self.back(i).wait_send()
            self.back_in(i).wait_recv()


def frame_sum_scratch(frames, shape, dim, pieces):
    bits = frames.bit_length() - 1
    scratch = [pltpu.VMEM(shape, BF16)]
    for _ in range(pieces):
        for i in range(bits):
            part = list(shape)
            part[dim] = (shape[dim] // pieces) >> (i + 1)
            scratch.append(pltpu.VMEM(tuple(part), BF16))
        scratch += [pltpu.SemaphoreType.DMA((bits,))] * 4
    return scratch


def frame_sums(line, arrays, scratch):
    bits = line.frames.bit_length() - 1
    out = []
    for full, dim, reverse, pieces in arrays:
        part, scratch = scratch[0], scratch[1:]
        sums = []
        for i in range(pieces):
            mine, scratch = scratch[: bits + 4], scratch[bits + 4 :]
            size = full.shape[dim] // pieces
            at = (slice(None),) * dim + (pl.ds(i * size, size),)
            views = (part.at[at], full.at[at]) if pieces > 1 else (part, full)
            sums.append(FrameSum(line, *views, dim, reverse, mine[:bits], mine[bits:]))
        out.append((part, sums))
    return out


def stage_times(sums, begins, first, bits, free, latency, chunk_us):
    ready = list(begins)
    plan = []
    for k in range(2 * bits):
        for i, group in enumerate(sums):
            length = first / 2 ** (k if k < bits else 2 * bits - 1 - k)
            chunks = 1 << max(int(np.log2(length / chunk_us) + 0.5), 0)
            start = max(free, ready[i])
            for j in range(chunks):
                plan.append((start + j * length / chunks, len(plan), ("send", group, k, j, chunks)))
            free = start + length
            ready[i] = free + latency
            plan.append((ready[i], len(plan), ("end", group, k, 0, 0)))
    return plan, free


def run_step(step):
    what, group, k, chunk, chunks = step
    for one in group:
        if what == "send":
            one.send(k, chunk, chunks)
        else:
            one.end(k)


class Everyone:
    def __init__(self, line, refs, sems):
        self.line = line
        self.src, self.dst_sib, self.dst_line, self.dst_frames, self.full = refs
        self.sent, self.got = sems
        self.share = self.src.shape[1] // line.chips

    def cols(self, z):
        return pl.ds(pl.multiple_of(z * self.share, self.share), self.share)

    def pair_copy(self):
        ln = self.line
        return ln.copy(self.src, self.dst_sib, self.sent.at[0], self.got.at[0], ln.sibling())

    def line_copies(self):
        ln, copies = self.line, []
        for k in range(1, ln.chips):
            to = (ln.z + k) % ln.chips
            src, dst = self.dst_sib.at[:, self.cols(to)], self.dst_line.at[ln.z]
            copies.append(ln.copy(src, dst, self.sent.at[k], self.got.at[k], ln.at(to)))
        return copies

    def frame_copies(self):
        ln, copies = self.line, []
        for k in range(1, ln.frames):
            to, i = ((ln.f + k) % ln.frames, ln.h), ln.chips + k
            src, dst = self.dst_line.at[ln.z], self.dst_frames.at[ln.f]
            copies.append(ln.copy(src, dst, self.sent.at[i], self.got.at[i], to))
        return copies

    def back_copies(self):
        ln, copies = self.line, []
        for k in range(1, ln.chips):
            to, i = ln.at((ln.z + k) % ln.chips), ln.chips + ln.frames + k
            ref = self.full.at[:, self.cols(ln.z)]
            copies.append(ln.copy(ref, ref, self.sent.at[i], self.got.at[i], to))
        return copies

    def over_pair(self, value):
        self.src[...] = value.astype(BF16)
        self.pair_copy().start()

    def over_line(self):
        self.pair_copy().wait()
        pair = self.src[...].astype(F32) + self.dst_sib[...].astype(F32)
        self.dst_sib[...] = pair.astype(BF16)
        for copy in self.line_copies():
            copy.start()

    def over_frames(self):
        ln = self.line
        for copy in self.line_copies():
            copy.wait()
        total = self.dst_sib[:, self.cols(ln.z)].astype(F32)
        for k in range(1, ln.chips):
            total = total + self.dst_line[(ln.z + k) % ln.chips].astype(F32)
        self.dst_line[ln.z] = total.astype(BF16)
        for copy in self.frame_copies():
            copy.start()
        self.dst_frames[ln.f] = self.dst_line[ln.z]

    def over_back(self):
        for copy in self.frame_copies():
            copy.wait()
        total = self.dst_frames[0].astype(F32)
        for i in range(1, self.line.frames):
            total = total + self.dst_frames[i].astype(F32)
        self.full[:, self.cols(self.line.z)] = total.astype(BF16)
        for copy in self.back_copies():
            copy.start()

    def result(self):
        for copy in self.back_copies():
            copy.wait()
        return self.full[...].astype(F32)


class Timetable:
    PHASES = 5

    def __init__(self, chips, streams):
        self.chips, self.streams = chips, streams
        last = chips - 1
        arrivals = [(d * HOP_US, "arrive", d) for d in range(chips)]
        gathered = last * HOP_US + SIBLING_US
        first = self.sum_steps(0.0)
        middle = self.sum_steps(gathered)
        self.turn = max((middle[-1][0] + OWNER_US) / streams, chips * LINK_US)
        period = self.turn * streams
        second = max(HOP_US, SIBLING_US + COMPUTE_US + SIBLING_US)
        y = self.sum_steps(second - COMPUTE_US - SIBLING_US)
        leads = [0.0, first[-1][0] + OWNER_US + SWAP_US - period]
        leads.append(leads[1] + max(middle[-1][0] + OWNER_US + SWAP_US - period, 0.0))
        groups = (
            (0, 0, leads[0], first),
            (1, 3, leads[1], arrivals + middle),
            (4, 4, leads[2], arrivals + [(gathered, "gathered", 0)] + y),
        )
        self.every = 6
        self.order = []
        for i in range(self.every):
            at = (i + 0.5) * self.turn / self.every
            self.order.append((at, 0.0, "beside", i, 0, 0, 0))
        self.computed = {}
        self.turns = 0
        for low, high, lead, steps in groups:
            for t, what, which in steps:
                t += lead + ADJUST.get((low, what, which), 0.0)
                behind = int(np.floor(t / self.turn))
                at = t - behind * self.turn
                self.order.append((at, -t, what, which, behind, low, high))
                if what == ("gathered" if low == 4 else "compute"):
                    self.computed |= {phase: behind for phase in range(low, high + 1)}
                self.turns = max(self.turns, (high + 1) * streams + behind)
        self.order.sort(key=lambda step: step[:2])

    def sum_steps(self, compute):
        last = self.chips - 1
        steps = [(compute, "compute", 0)]
        start = compute + COMPUTE_US + SIBLING_US
        hops = {}
        for place in range(last):
            t = start
            for far in range(last, place, -1):
                if place:
                    t = max(t, hops[place - 1, far] + HOP_US)
                hops[place, far] = t
                steps.append((t, "hop", (place, far)))
                t += LINK_US
        owner = max(hops[far - 1, far] for far in range(1, self.chips)) + HOP_US
        return steps + [(owner, "owner", 0)]

    def y_owner(self, item):
        t = [t for t in self.order if t[2] == "owner" and t[5] == 4][0]
        return (item + t[4]) * self.every + int(t[0] / self.turn * self.every + 0.5)

    def after(self, item):
        return item + self.computed[item // self.streams] + 1


def pipeline(line, times, turns, gather, sums, enter, compute, gathered, owner, total, beside):
    last, streams = line.chips - 1, times.streams

    def body(m, carry):
        for _, _, what, which, behind, low, high in times.order:
            if what == "beside":
                beside(m, which)
                continue
            n = m - behind
            fits = (n >= low * streams) & (n < (high + 1) * streams)
            n = jnp.clip(n, low * streams, (high + 1) * streams - 1)
            s = n % streams
            held = n - streams
            if what == "hop":
                place, far = which

                @pl.when(fits & (line.z == place))
                def _():
                    sums.hop_up(s, far)

                @pl.when(fits & (line.z == last - place))
                def _():
                    sums.hop_down(s, last - far)

                continue

            @pl.when(fits)
            def _():
                if what == "arrive":
                    if which == 0:
                        enter(n)
                        gather.send(held)
                    else:
                        gather.arrive(which, held)
                elif what == "compute":
                    if low == 4:
                        gather.wait_across(held, line.z)
                    for zb in range(line.chips):
                        if 1 <= low <= 3:
                            gather.wait_across(held, zb)
                        if low:
                            sums.drain(s, zb)
                    compute(n, low, high)
                    for zb in range(line.chips):
                        sums.across(s, zb).start()
                elif what == "gathered":
                    for zb in range(line.chips):

                        @pl.when(line.z != zb)
                        def _():
                            gather.wait_across(held, zb)

                    gathered(n)
                else:
                    sums.finish(s, total)
                    owner(n, low, high)

        return carry

    lax.fori_loop(0, turns, body, 0)


def frame_mask(segments, places, rows):
    frames = segments.shape[0]
    bits, place_bits = frames.bit_length() - 1, places.bit_length() - 1

    def ids_along(axis, shape):
        index = lax.broadcasted_iota(jnp.int32, shape, axis)
        frame = lax.shift_right_logical(index, place_bits) & (frames - 1)
        segment = jnp.zeros(shape, jnp.int32)
        for i in range(frames):
            segment = jnp.where(frame == i, segments[i], segment)
        block = lax.shift_right_logical(index, place_bits + bits)
        return block * places + (index & (places - 1)), frame, segment

    place_q, frame_q, segment_q = ids_along(0, (rows, 1))
    place_k, frame_k, segment_k = ids_along(1, (1, rows))
    return (place_q == place_k) & (frame_k <= frame_q) & (segment_q == segment_k)


def column_grads(start, left, right, out):
    rows = pl.ds(pl.multiple_of(start, 256), 256)
    out[rows] = mm_tn(left, right.reshape(left.shape[0], right.shape[-1])).astype(BF16)


def row_sum(value):
    return jnp.sum(value, axis=0, keepdims=True)


def moved_exactly(order, value):
    out = None
    for _ in range(3):
        term = value.astype(BF16)
        value = value - term.astype(F32)
        out = mm(order, term) if out is None else out + mm(order, term)
    return out


class Refs:
    def __init__(self, names, refs):
        for name, ref in zip(names, refs, strict=True):
            setattr(self, name, ref)


def block(fetched, results, names, *refs):
    ends = len(fetched), len(fetched) + len(results)
    r = Refs(names, refs[ends[1] :])
    r.fetched = dict(zip(fetched, refs))
    r.stored = dict(zip(results, refs[ends[0] :]))
    r.ids, r.segments = r.fetched.pop("ids"), r.fetched.pop("segments")
    steps, patches, width = r.x.shape
    streams, rows, _ = r.y.shape
    heads = 2 * r.g_all.shape[1]
    line, t_line = Line(steps), Line(streams)
    chips, frames = line.chips, line.frames
    s_rows = patches // heads
    tokens = steps * s_rows
    columns, hidden = r.s_wout.shape[0], r.up.shape[1]
    entries = r.table.shape[0]
    count = heads * rows
    all_tokens = heads * tokens
    times = Timetable(chips, streams)
    sums = ChainSum(t_line, (r.part, r.sib, r.rise, r.fall, r.out), r.sum_sems)
    gather = Gather(t_line, r.gathered, r.gather_sems)
    last_part = getattr(r, "last_part", r.g_all)
    last_out = getattr(r, "last_out", r.out)
    last_total = getattr(r, "last_total", r.grad2)
    last_sums = ChainSum(
        line, (last_part, r.last_sib, r.last_rise, r.last_fall, last_out), r.last_sems
    )
    shared = not hasattr(r, "g_src")

    def g_src_at(part, to):
        return r.gathered.at[3 * streams + to, part] if shared else r.g_src.at[0, to, part]

    g_swap = Swap(line, g_src_at, r.g_dst, r.g_sems)
    state_swap = Swap(line, lambda s, to: r.state_src.at[s, to], r.state_dst, r.state_sems)
    grad_swap = Swap(line, lambda s, to: r.grad_src.at[s, to], r.grad_dst, r.grad_sems)
    y_swap = Swap(line, lambda s, to: r.y_src.at[s, to], r.y_dst, r.y_sems)
    every = Everyone(
        line,
        (r.every_src, r.every_sib, r.every_line, r.every_frames, r.every_full),
        r.every_sems,
    )
    (
        (down_part, down_sums), (up_part, up_sums),
        (t_q_part, t_q_sums), (t_k_part, t_k_sums), (t_v_part, t_v_sums), (t_out_part, t_out_sums),
        (s_q_part, s_q_sums), (s_k_part, s_k_sums), (s_v_part, s_v_sums), (s_out_part, s_out_sums),
    ) = frame_sums(
        line,
        [
            (r.down_grad, 0, False, 2), (r.up_grad, 0, True, 2),
            (r.t_q, 0, False, 1), (r.t_k, 0, True, 1), (r.t_v, 0, False, 1), (r.t_out, 1, True, 1),
            (r.s_q, 0, False, 1), (r.s_k, 0, True, 1), (r.s_v, 0, False, 1), (r.s_out, 1, True, 1),
        ],
        r.reduce,
    )
    t_parts = t_q_part, t_k_part, t_v_part
    s_parts = s_q_part, s_k_part, s_v_part
    mlp_sums = list(zip(down_sums, up_sums))
    t_sums = [t_q_sums + t_k_sums, t_v_sums + t_out_sums]
    s_sums = [s_q_sums + s_k_sums, s_v_sums]
    bits = len(down_sums[0].bits)
    bias_swap = Swap(line, lambda _, to: r.bias_src, r.bias_dst, r.bias_sems)
    fetches = [
        pltpu.make_async_copy(r.fetched[name], getattr(r, name), r.fetch_sems.at[i])
        for i, name in enumerate(r.fetched)
    ]
    for fetch in fetches:
        fetch.start()
    line.barrier(True, True)
    for fetch in fetches:
        fetch.wait()
    stored = []

    def store(name):
        i = list(r.stored).index(name)
        stored.append(
            pltpu.make_async_copy(getattr(r, name), r.stored[name], r.store_sems.at[i])
        )
        stored[-1].start()

    def g_out(i, carry):
        rows_of = pl.ds(pl.multiple_of(i * s_rows, s_rows), s_rows)
        moved = mm(r.to_peers[...], r.cotangent[:, rows_of].reshape(tokens, width))
        moved = moved.astype(BF16).astype(r.g_dst.dtype).reshape(frames, tokens // frames, width)
        if shared:
            r.gathered[3 * streams : 4 * streams, i // 2, i % 2] = moved
        else:
            r.g_src[0, :, i // 2, i % 2] = moved
        return carry

    lax.fori_loop(0, heads, g_out, 0)
    for part in range(chips - 1):
        g_swap.start(part)

    def g_in(i):
        moved = r.g_dst[i // 2, :, i % 2].reshape(tokens, width).astype(BF16)
        moved = mm(r.to_parts[...], moved).astype(BF16)
        r.g_all[:, i // 2, i % 2] = moved.reshape(streams, rows, width)

    table_row = lax.broadcasted_iota(jnp.int32, (entries, width), 0)

    def added(s):
        return row_sum(jnp.where(table_row == r.ids[s], r.table[...].astype(F32), 0.0))

    def norm(value, i):
        scaled = norm_stats(value)[0] * r.gain[i : i + 1, :]
        return (scaled + r.shift[i : i + 1, :]).astype(BF16)

    def attention(s, carry):
        normed = norm(r.x[s].astype(F32) + added(s), 0)
        r.normed0[s] = normed
        q = mm(normed, r.s_wqkv[0]).astype(BF16)
        k = mm(normed, r.s_wqkv[1]).astype(BF16)
        v = mm(normed, r.s_wqkv[2]).astype(BF16)
        r.s_proj[0, s] = q
        r.s_proj[1, s] = k
        r.s_proj[2, s] = v
        r.s_cols[s] = attend(q, k, v, None)
        return carry

    lax.fori_loop(0, steps, attention, 0)

    def to_streams(i, carry):
        rows_of = pl.ds(pl.multiple_of(i * s_rows, s_rows), s_rows)
        moved = mm(r.to_streams[...], r.s_cols[:, rows_of].reshape(tokens, columns)).astype(BF16)
        r.s_mixed[:, i] = moved.reshape(streams, rows, columns)
        return carry

    lax.fori_loop(0, heads, to_streams, 0)
    own_rows = pl.ds(pl.multiple_of(line.h * s_rows, s_rows), s_rows)
    own = mm(r.to_streams[...], r.x[:, own_rows].reshape(tokens, width))
    row = lax.broadcasted_iota(jnp.int32, (tokens, 1), 0)
    frame = lax.shift_right_logical(row, (rows // (frames * steps)).bit_length() - 1) & (steps - 1)
    entry = jnp.zeros_like(row)
    for s in range(steps):
        entry = jnp.where(frame == s, r.ids[s], entry)
    picker = (entry == lax.broadcasted_iota(jnp.int32, (tokens, entries), 1)).astype(BF16)
    own = own + mm(picker, r.table[...])
    r.state0[...] = own.reshape(streams, rows, width)
    r.mask[...] = frame_mask(r.segments, rows // (frames * steps), count).astype(F32)
    r.up_bias_grad[...] = jnp.zeros_like(r.up_bias_grad)
    r.small[...] = jnp.zeros_like(r.small)

    def held(n):
        return n - streams

    def enter_temporal(s, n):
        state_swap.wait(s)
        state = r.state_dst[s].reshape(rows, width)
        r.state1[s] = state
        r.gathered[held(n), line.z, line.c] = norm(state, 1)

    def enter_spatial(s, n):
        grad_swap.wait(s)
        grad = r.grad_dst[s].reshape(rows, width)
        r.grad1[s] = grad
        r.gathered[held(n), line.z, line.c] = grad.astype(BF16)

    def compute_spatial(s, n):
        left = r.s_mixed[s].reshape(count, columns)
        r.part[s] = mm(left, r.s_wout[...]).astype(BF16).reshape(chips, 2, rows, width)

    def compute_temporal(s, n):
        a = r.gathered[held(n)].reshape(count, width)
        q = mm(a, r.t_wqkv[0]).astype(BF16)
        k = mm(a, r.t_wqkv[1]).astype(BF16)
        v = mm(a, r.t_wqkv[2]).astype(BF16)
        r.t_proj[0, s] = q
        r.t_proj[1, s] = k
        r.t_proj[2, s] = v
        mixed = attend(q, k, v, r.mask[...] > 0.0)
        r.t_mixed[s] = mixed
        r.part[s] = mm(mixed, r.t_wout[...]).astype(BF16).reshape(chips, 2, rows, width)

    def compute_mlp(s, n):
        a = r.gathered[held(n)].reshape(count, width)
        g = r.g_all[s].reshape(count, width)
        pre = mm(a, r.up[...]) + r.up_bias[...]
        t = jnp.tanh(GELU_C * (pre + 0.044715 * (pre * pre * pre)))
        act = (0.5 * pre * (1.0 + t)).astype(BF16)
        r.act[s] = act
        slope = 0.5 * (1.0 + t)
        slope = slope + 0.5 * pre * (1.0 - t * t) * (GELU_C * (1.0 + 0.134145 * (pre * pre)))
        dpre = (mm_nt(g, r.down[...]) * slope).astype(BF16)
        r.dpre[s] = dpre
        r.up_bias_grad[:, :hidden] += row_sum(dpre.astype(F32))
        r.part[s] = mm_nt(dpre, r.up[...]).astype(BF16).reshape(chips, 2, rows, width)

    def compute_back(s, n):
        grad = r.gathered[held(n)].reshape(count, width)
        dm = mm_nt(grad, r.t_wout[...]).astype(BF16)
        mask = r.mask[...] > 0.0
        dq, dk, dv = attend_back(r.t_proj[0, s], r.t_proj[1, s], r.t_proj[2, s], mask, dm)
        r.t_dproj[0, s] = dq
        r.t_dproj[1, s] = dk
        r.t_dproj[2, s] = dv
        da = mm_nt(dq, r.t_wqkv[0]) + mm_nt(dk, r.t_wqkv[1]) + mm_nt(dv, r.t_wqkv[2])
        r.part[s] = da.astype(BF16).reshape(chips, 2, rows, width)

    def gathered_last(n):
        grad = r.gathered[held(n)].reshape(count, width)
        moved = mm_nt(grad, r.s_wout[...]).astype(BF16)
        r.s_dmixed[n % streams] = moved.reshape(heads, rows, columns)

    def compute_last(s, n):
        y = mm(r.act[s], r.down[...])
        r.part[s] = y.astype(BF16).reshape(chips, 2, rows, width)

    def owner_spatial(s, n):
        state = r.state0[s] + r.total[...] + r.bias[0:1, :]
        r.state_src[s] = state.reshape(r.state_src.shape[1:])
        state_swap.start(s)

        @pl.when(s == streams - 1)
        def _():
            g_swap.start(chips - 1)

    def owner_temporal(s, n):
        state = r.state1[s] + r.total[...] + r.bias[1:2, :]
        r.state2[s] = state
        r.gathered[n, line.z, line.c] = norm(state, 2)

    def owner_mlp(s, n):
        grad = r.g_all[s, line.z, line.c].astype(F32)
        back, gain_grad, shift_grad = norm_back(r.state2[s], r.total[...], r.gain[2:3, :])
        dh = grad + back
        r.grad2[s] = dh
        r.gathered[n, line.z, line.c] = dh.astype(BF16)
        r.small[0:1] += gain_grad
        r.small[1:2] += shift_grad
        r.small[2:3] += row_sum(grad)
        r.small[3:4] += row_sum(dh)

    def owner_back(s, n):
        back, gain_grad, shift_grad = norm_back(r.state1[s], r.total[...], r.gain[1:2, :])
        dh = r.grad2[s] + back
        r.grad_src[s] = dh.reshape(r.grad_src.shape[1:])
        grad_swap.start(s)
        r.small[4:5] += gain_grad
        r.small[5:6] += shift_grad
        r.small[6:7] += row_sum(dh)

    def owner_last(s, n):
        r.y[s] = (r.state2[s] + r.total[...] + r.bias[2:3, :]).astype(BF16)

    def by_phase(bodies):
        def run(n, low=0, high=4):
            for i, one in enumerate(bodies):
                if one is not None and low <= i <= high:

                    @pl.when(n // streams == i)
                    def _():
                        one(n % streams, n)

        return run

    def down_chunk(i):
        cols = pl.ds(pl.multiple_of(i * 128, 128), 128)
        left = r.act[:, :, cols].reshape(all_tokens, 128)
        right = r.g_all[...].reshape(all_tokens, width)
        down_part[cols] = mm_tn(left, right).astype(BF16)

    def up_chunk(i):
        cols = pl.ds(pl.multiple_of(i * 256, 256), 256)
        left = r.gathered[streams : 2 * streams, :, :, :, cols].reshape(all_tokens, 256)
        right = r.dpre[...].reshape(all_tokens, hidden)
        up_part[cols] = mm_tn(left, right).astype(BF16)

    def t_out_chunk(i):
        left = r.t_mixed[...].reshape(all_tokens, columns)
        right = r.gathered[2 * streams : 3 * streams].reshape(all_tokens, width)
        t_out_part[...] = mm_tn(left, right).astype(BF16)

    def t_qkv_chunk(i):
        start = i * 256
        cols = pl.ds(pl.multiple_of(start, 256), 256)
        left = r.gathered[0:streams, :, :, :, cols].reshape(all_tokens, 256)
        for j in range(3):
            column_grads(start, left, r.t_dproj[j], t_parts[j])

    def s_cols_chunk(_):
        def from_streams(i, carry):
            rows_of = pl.ds(pl.multiple_of(i * s_rows, s_rows), s_rows)
            moved = mm(r.from_streams[...], r.s_dmixed[:, i].reshape(tokens, columns)).astype(BF16)
            r.s_cols[:, rows_of] = moved.reshape(steps, s_rows, columns)
            return carry

        lax.fori_loop(0, heads, from_streams, 0)

    def s_back_chunk(s):
        dq, dk, dv = attend_back(r.s_proj[0, s], r.s_proj[1, s], r.s_proj[2, s], None, r.s_cols[s])
        r.s_dproj[0, s] = dq
        r.s_dproj[1, s] = dk
        r.s_dproj[2, s] = dv
        da = mm_nt(dq, r.s_wqkv[0]) + mm_nt(dk, r.s_wqkv[1]) + mm_nt(dv, r.s_wqkv[2])
        last_part[s] = da.astype(BF16).reshape(last_part.shape[1:])
        for zb in range(chips):
            last_sums.across(s, zb).start()
        if early:

            @pl.when(s == 1)
            def _():
                drain_all(t_line, (sums,), streams)

            @pl.when(s > 0)
            def _():
                last_sums.hops(s - 1)

    def s_out_chunk(_):
        left = r.s_mixed[...].reshape(all_tokens, columns)
        right = r.gathered[3 * streams : 4 * streams].reshape(all_tokens, width)
        s_out_part[...] = mm_tn(left, right).astype(BF16)
        s_out_sums[0].send(0)

    def bias_chunk(_):
        r.bias_src[...] = jnp.broadcast_to(r.up_bias_grad[...], r.bias_src.shape)
        bias_swap.start(0)

    def g_in_chunk(i):
        @pl.when(i % 2 == 0)
        def _():
            g_swap.wait(i // 2)

        g_in(i)

    n_down, n_up = hidden // 128, width // 256
    turn_of = times.after
    slots = [i for i in range(times.every) if i % 2 == 1][:3]
    per_slot = 3
    per_turn = per_slot * len(slots)
    mlp_turn, back_turn = turn_of(3 * streams - 1), turn_of(4 * streams - 1)
    last_turn = turn_of(5 * streams - 1)
    chunks = (
        (2 * streams - 1 - heads // per_turn, 0, heads, g_in_chunk),
        (mlp_turn, 0, n_down, down_chunk),
        (mlp_turn, n_down, n_up, up_chunk),
        (mlp_turn, n_down + n_up, 1, bias_chunk),
        (back_turn, 0, 1, t_out_chunk),
        (back_turn, 1, width // 256, t_qkv_chunk),
        (last_turn, 0, 1, s_out_chunk),
        (last_turn, 1, 1, s_cols_chunk),
        (last_turn, 2, steps, s_back_chunk),
    )
    turns = max(times.turns, last_turn + -(-(steps + 2) // per_turn))
    early = times.y_owner(5 * streams - 1) < last_turn * times.every + slots[1]

    def begin_of(turn, number):
        return (turn + number // per_turn) * times.every + times.every - 1

    begin = begin_of(mlp_turn, n_down + n_up) * SLOT_US
    plan, free = stage_times(mlp_sums, [begin] * 2, MLP_US, bits, 0.0, FRAME_US, CHUNK_US)
    begin = begin_of(back_turn, 1 + width // 256) * SLOT_US
    plan += stage_times(t_sums, [begin] * 2, ATTENTION_US, bits, free, FRAME_US, WHOLE_US)[0]
    plan = [(t, i, step) for i, (t, _, step) in enumerate(plan)]
    plan.sort(key=lambda entry: entry[:2])
    end = turns * times.every * SLOT_US
    late = [entry for entry in plan if entry[0] >= end]

    def beside(m, i):
        if i in slots:
            for turn, first, number, chunk in chunks:
                which = per_turn * (m - turn) + per_slot * slots.index(i) - first
                here = jnp.clip(number - which, 0, per_slot)

                @pl.when((which > -per_slot) & (which < number))
                def _():
                    def one(j, carry):
                        @pl.when(which + j >= 0)
                        def _():
                            chunk(which + j)

                        return carry

                    lax.fori_loop(0, here, one, 0)

        for t, _, step in plan:
            moment = int(t / SLOT_US)
            if t < end and moment % times.every == i:

                @pl.when(m == moment // times.every)
                def _():
                    run_step(step)

    enter = by_phase((None, enter_temporal, None, None, enter_spatial))
    compute = by_phase(
        (compute_spatial, compute_temporal, compute_mlp, compute_back, compute_last)
    )
    owner = by_phase((owner_spatial, owner_temporal, owner_mlp, owner_back, owner_last))
    pipeline(
        t_line, times, turns, gather, sums, enter, compute, gathered_last, owner, r.total, beside
    )
    if not early:
        drain_all(t_line, (sums,), streams)

    y = mm(r.from_parts[...], r.y[...].reshape(tokens, width)).astype(BF16)
    r.y_src[0] = y.astype(r.y_src.dtype).reshape(r.y_src.shape[1:])
    y_swap.start(0)

    r.sums0[...] = jnp.zeros_like(r.sums0)

    def small_part(s):
        state = r.x[s].astype(F32) + added(s)
        da = last_part[s].reshape(patches, width).astype(F32)
        back, gain_grad, shift_grad = norm_back(state, da, r.gain[0:1, :])
        r.sums0[0:1] += gain_grad
        r.sums0[1:2] += shift_grad
        r.sums0[8 : 8 + entries] += jnp.where(table_row == r.ids[s], row_sum(back), 0.0)

    room = r.every_src.shape[0]
    filled = 9 + entries

    def small_value(own_grad):
        for s in range(steps):
            here = row_sum(own_grad[s * s_rows : (s + 1) * s_rows])
            r.sums0[8 : 8 + entries] += jnp.where(table_row == r.ids[s], here, 0.0)
        rows_of = [
            r.sums0[0:1], r.small[4:5], r.small[0:1],
            r.sums0[1:2], r.small[5:6], r.small[1:2],
            r.small[6:7], r.small[3:4], r.small[2:3],
            r.sums0[8 : 8 + entries], jnp.zeros((room - filled, width), F32),
        ]
        return jnp.concatenate(rows_of, axis=0)

    first = steps - 1 if early else 0
    begin = LAST_GRADS * STEP_US + 2.5
    last_plan = [(max(int((t - end) / STEP_US), 0) + first + 1, i, step) for t, i, step in late]
    begins = [begin] * len(s_sums) + [begin - 4.0]
    s_plan, _ = stage_times(
        s_sums + [s_out_sums], begins, ATTENTION_US, bits, 0.0, LAST_FRAME_US, WHOLE_US
    )
    last_plan += [
        (int(np.ceil(t / STEP_US)), len(plan) + i, step)
        for t, i, step in s_plan
        if step[0] == "end" or step[2] > 0
    ]
    last_plan.sort(key=lambda entry: entry[:2])
    bound = steps * (chips - 1) + (chips - 2) * LAG + 1
    bound = max(bound, LAST_SMALL[-1] + 1)

    def body(t, carry):
        last_sums.hops(t)

        @pl.when(t == LAST_GRADS)
        def _():
            for j in range(3):
                for i in range(width // 256):
                    left = r.normed0[:, :, i * 256 : (i + 1) * 256].reshape(all_tokens, 256)
                    column_grads(i * 256, left, r.s_dproj[j], s_parts[j])
            for one in s_q_sums + s_k_sums + s_v_sums:
                one.send(0)

        @pl.when((t > LAST_GRADS) & (t <= LAST_GRADS + steps // 2))
        def _():
            def one(i, carry):
                small_part((t - LAST_GRADS - 1) * 2 + i)
                return carry

            lax.fori_loop(0, 2, one, 0)

        @pl.when(t == LAST_SMALL[0])
        def _():
            grad = r.grad1[...].reshape(tokens, width)
            own_grad = moved_exactly(r.from_streams[...], grad)
            r.state0[...] = own_grad.reshape(r.state0.shape)
            every.over_pair(small_value(own_grad))

        steps_of = (every.over_line, every.over_frames, every.over_back)
        for moment, step in zip(LAST_SMALL[1:], steps_of):

            @pl.when(t == moment)
            def _():
                step()

        for moment, _, step in last_plan:
            if moment < bound:

                @pl.when(t == max(moment, first))
                def _():
                    run_step(step)

        return carry

    lax.fori_loop(first, bound, body, 0)
    for s in range(steps):
        last_sums.finish(s, last_total.at[s])
    own_grad = r.state0[...].reshape(tokens, width)
    for s in range(steps):
        state = r.x[s, own_rows].astype(F32) + added(s)
        back, _, _ = norm_back(state, last_total[s], r.gain[0:1, :])
        r.grad_res[pl.ds(s * s_rows, s_rows)] = own_grad[s * s_rows : (s + 1) * s_rows] + back
    y_swap.wait(0)
    r.y_res[...] = mm(r.from_peers[...], r.y_dst[0].reshape(tokens, width).astype(BF16)).astype(BF16)
    r.small_res[...] = every.result()
    bias_swap.wait(0)
    up_bias = r.bias_dst[0, 0]
    for i in range(1, frames):
        up_bias = up_bias + r.bias_dst[0, i]
    r.up_bias_res[...] = up_bias
    for name in ("grad_res", "y_res", "small_res", "up_bias_res") + MLP_RESULTS:
        store(name)
    for moment, _, step in last_plan:
        if moment >= bound:
            run_step(step)
    for name in T_RESULTS + S_RESULTS:
        store(name)
    drain_all(line, (last_sums,), steps)
    drain_all(t_line, (gather,), 4 * streams)
    for one in stored:
        one.wait()


def finish(names, parts, *refs):
    sources = dict(zip(names, refs))
    results = dict(zip(parts, refs[len(names) :]))
    held = refs[len(names) + len(parts) :]
    sems_in, sems_out = held[-2:]
    local = dict(zip(names, held))
    made = dict(zip(parts, held[len(names) :]))
    loads = {
        name: pltpu.make_async_copy(sources[name], local[name], sems_in.at[i])
        for i, name in enumerate(names)
    }
    for load in loads.values():
        load.start()
    loaded, stores = set(), []
    for i, (name, given) in enumerate(parts.items()):
        for j, (source, low, high, columns) in enumerate(given):
            if source not in loaded:
                loads[source].wait()
                loaded.add(source)
            value = local[source][low:high, :columns].astype(made[name].dtype)
            if len(given) > 1:
                made[name][j] = value
            else:
                made[name][...] = value
        stores.append(pltpu.make_async_copy(made[name], results[name], sems_out.at[i]))
        stores[-1].start()
    for store in stores:
        store.wait()


def results(found, entries):
    width, hidden = found["up_grad"].shape

    def whole(name):
        rows, columns = found[name].shape
        return [(name, 0, rows, columns)]

    parts = {
        "down": whole("down_grad"),
        "up": whole("up_grad"),
        "t_qkv": whole("t_q") + whole("t_k") + whole("t_v"),
        "t_out": whole("t_out"),
        "grad": whole("grad_res"),
        "y": whole("y_res"),
        "gain": [("small_res", 0, 3, width)],
        "shift": [("small_res", 3, 6, width)],
        "bias": [("small_res", 6, 9, width)],
        "table": [("small_res", 9, 9 + entries, width)],
        "up_bias": [("up_bias_res", 0, 1, hidden)],
        "s_out": whole("s_out"),
        "s_qkv": whole("s_q") + whole("s_k") + whole("s_v"),
    }
    shapes = []
    for name, given in parts.items():
        _, low, high, columns = given[0]
        lead = (len(given),) if len(given) > 1 else ()
        kind = BF16 if name == "y" else F32
        shapes.append(jax.ShapeDtypeStruct(lead + (high - low, columns), kind))
    names = tuple(found)
    made = pl.pallas_call(
        lambda *refs: finish(names, parts, *refs),
        name="finish",
        out_shape=shapes,
        in_specs=[pl.BlockSpec(memory_space=pltpu.HBM)] * len(names),
        out_specs=[pl.BlockSpec(memory_space=pltpu.HBM)] * len(shapes),
        scratch_shapes=[pltpu.VMEM(v.shape, v.dtype) for v in found.values()]
        + [pltpu.VMEM(v.shape, v.dtype) for v in shapes]
        + [pltpu.SemaphoreType.DMA((len(names),)), pltpu.SemaphoreType.DMA((len(shapes),))],
        compiler_params=pltpu.CompilerParams(vmem_limit_bytes=VMEM_LIMIT),
    )(*found.values())
    return dict(zip(parts, made))


def orders(frames_local, frames, places, streams):
    tokens = frames_local * frames * places
    index = np.arange(tokens).reshape(frames_local, frames, streams, places // streams)
    to_streams = index.transpose(2, 1, 0, 3).reshape(-1)
    to_peers = index.transpose(1, 0, 2, 3).reshape(-1)
    index = np.arange(tokens).reshape(frames * frames_local, streams, places // streams)
    to_parts = index.transpose(1, 0, 2).reshape(-1)
    eye = np.eye(tokens, dtype=np.float32)
    there = [eye[order] for order in (to_streams, to_peers, to_parts)]
    back = [m.T for m in there]
    names = ("to_streams", "to_peers", "to_parts", "from_streams", "from_peers", "from_parts")
    return {name: jnp.asarray(m, BF16) for name, m in zip(names, there + back)}


def on_device(
    block_input,
    action_ids,
    segment_ids,
    action_table,
    norm_gain,
    norm_shift,
    spatial_qkv,
    spatial_out,
    temporal_qkv,
    temporal_out,
    out_bias,
    up_weight,
    up_bias,
    down_weight,
    cotangent,
):
    frames, heads = lax.axis_size("frames"), lax.axis_size("heads")
    chips = heads // 2
    steps, patches, width = block_input.shape
    rows = patches // heads
    tokens = steps * rows
    total_frames = segment_ids.shape[0]
    places = rows // frames
    streams = min(4, places)
    t_rows = tokens // streams
    columns = spatial_out.shape[0]
    hidden = up_weight.shape[1]
    entries = action_table.shape[0]
    count = heads * t_rows
    room = -(-(10 + entries) // 16) * 16
    args = dict(
        ids=action_ids,
        segments=segment_ids,
        x=block_input,
        cotangent=cotangent,
        table=action_table,
        gain=norm_gain,
        shift=norm_shift,
        bias=out_bias,
        s_wqkv=spatial_qkv.transpose(1, 0, 2),
        s_wout=spatial_out,
        t_wqkv=temporal_qkv.transpose(1, 0, 2),
        t_wout=temporal_out,
        up=up_weight,
        up_bias=up_bias.reshape(1, hidden),
        down=down_weight,
        **orders(steps, frames, places, streams),
    )
    qkv, out = (width, columns), (columns, width)
    down, up = (hidden, width), (width, hidden)
    outs = dict(
        t_q=(qkv, BF16),
        t_k=(qkv, BF16),
        t_v=(qkv, BF16),
        t_out=(out, BF16),
        s_q=(qkv, BF16),
        s_k=(qkv, BF16),
        s_v=(qkv, BF16),
        s_out=(out, BF16),
        up_grad=(up, BF16),
        down_grad=(down, BF16),
        y_res=((tokens, width), BF16),
        grad_res=((tokens, width), F32),
        small_res=((room, width), F32),
        up_bias_res=((8, width), F32),
    )
    s_all = (steps, chips, 2, rows, width)
    t_all = (streams, chips, 2, t_rows, width)
    s_one, t_one = (steps, chips, rows, width), (streams, chips, t_rows, width)
    owned = (streams, t_rows, width)
    swapped = (streams, frames, t_rows // frames, width)
    whole = (1, frames, tokens // frames, width)
    g_part = (1, frames, chips, 2, tokens // frames, width)
    g_into = (chips, frames, 2, tokens // frames, width)

    def kind_of(shape):
        return BF16 if shape[-2] % 16 == 0 else F32

    cols = dict(
        s_cols=(steps, patches, columns),
        s_proj=(3, steps, patches, columns),
        s_dproj=(3, steps, patches, columns),
        s_mixed=(streams, heads, t_rows, columns),
        s_dmixed=(streams, heads, t_rows, columns),
        t_proj=(3, streams, count, columns),
        t_dproj=(3, streams, count, columns),
        t_mixed=(streams, count, columns),
        act=(streams, count, hidden),
        dpre=(streams, count, hidden),
        normed0=(steps, patches, width),
        gathered=(4 * streams,) + t_all[1:],
        g_all=t_all,
        part=t_all,
        sib=t_one,
        rise=t_one,
        fall=t_one,
        out=t_one,
        **({} if s_all == t_all else dict(last_part=s_all, last_out=s_one)),
        last_sib=s_one,
        last_rise=s_one,
        last_fall=s_one,
        y=owned,
    )
    floats = dict(
        state0=owned,
        state1=owned,
        state2=owned,
        grad1=owned,
        grad2=owned,
        total=(t_rows, width),
        **({} if (steps, rows) == (streams, t_rows) else dict(last_total=(steps, rows, width))),
        mask=(count, count),
        small=(8, width),
        sums0=(8 + entries, width),
        up_bias_grad=(1, width),
        state_src=swapped,
        state_dst=swapped,
        grad_src=swapped,
        grad_dst=swapped,
    )
    scratch = {name: pltpu.VMEM(shape, BF16) for name, shape in cols.items()}
    scratch |= {name: pltpu.VMEM(shape, F32) for name, shape in floats.items()}
    scratch["g_dst"] = pltpu.VMEM(g_into, kind_of(g_into))
    if g_part[1:] != t_all:
        scratch["g_src"] = pltpu.VMEM(g_part, kind_of(g_part))
    scratch |= {name: pltpu.VMEM(whole, kind_of(whole)) for name in ("y_src", "y_dst")}
    every_shape = (room, width)
    scratch |= dict(
        every_src=pltpu.VMEM(every_shape, BF16),
        every_sib=pltpu.VMEM(every_shape, BF16),
        every_line=pltpu.VMEM((chips, room, width // chips), BF16),
        every_frames=pltpu.VMEM((frames, room, width // chips), BF16),
        every_full=pltpu.VMEM(every_shape, BF16),
        every_sems=[pltpu.SemaphoreType.DMA((2 * chips + frames,))] * 2,
        bias_src=pltpu.VMEM((8, width), F32),
        bias_dst=pltpu.VMEM((1, frames, 8, width), F32),
        bias_sems=[pltpu.SemaphoreType.DMA((1, frames))] * 2,
        sum_sems=[pltpu.SemaphoreType.DMA((streams, chips))] * 5,
        last_sems=[pltpu.SemaphoreType.DMA((steps, chips))] * 5,
        gather_sems=[pltpu.SemaphoreType.DMA((4 * streams, chips))] * 5,
        state_sems=[pltpu.SemaphoreType.DMA((streams, frames))] * 2,
        grad_sems=[pltpu.SemaphoreType.DMA((streams, frames))] * 2,
        g_sems=[pltpu.SemaphoreType.DMA((chips, frames))] * 2,
        y_sems=[pltpu.SemaphoreType.DMA((1, frames))] * 2,
        reduce=[
            x
            for shape, dim, pieces in ((down, 0, 2), (up, 0, 2))
            + 2 * (((qkv, 0, 1),) * 3 + ((out, 1, 1),))
            for x in frame_sum_scratch(frames, shape, dim, pieces)
        ],
    )
    held = {k: v for k, v in args.items() if k not in ("ids", "segments")}
    scratch |= {name: pltpu.VMEM(v.shape, v.dtype) for name, v in held.items()}
    scratch |= {name: pltpu.VMEM(shape, kind) for name, (shape, kind) in outs.items()}
    scratch["fetch_sems"] = pltpu.SemaphoreType.DMA((len(held),))
    scratch["store_sems"] = pltpu.SemaphoreType.DMA((len(outs),))
    fetched, results_of, names = tuple(args), tuple(outs), tuple(scratch)
    parts = pl.pallas_call(
        lambda *refs: block(fetched, results_of, names, *refs),
        name="block",
        out_shape=[jax.ShapeDtypeStruct(shape, kind) for shape, kind in outs.values()],
        in_specs=[
            pl.BlockSpec(memory_space=pltpu.HBM if name in held else pltpu.SMEM)
            for name in args
        ],
        out_specs=[pl.BlockSpec(memory_space=pltpu.HBM)] * len(outs),
        scratch_shapes=list(scratch.values()),
        compiler_params=pltpu.CompilerParams(
            collective_id=0, has_side_effects=True, vmem_limit_bytes=VMEM_LIMIT
        ),
    )(*args.values())
    made = results(dict(zip(outs, parts)), entries)
    s_blocks = (steps, rows, width)
    return (
        made["y"].reshape(s_blocks),
        made["grad"].reshape(s_blocks),
        made["table"],
        made["gain"],
        made["shift"],
        made["s_qkv"].transpose(1, 0, 2),
        made["s_out"],
        made["t_qkv"].transpose(1, 0, 2),
        made["t_out"],
        made["bias"],
        made["up"],
        made["up_bias"].reshape(hidden),
        made["down"],
    )


def solution(mesh):
    return jax.shard_map(
        on_device,
        mesh=mesh,
        in_specs=(
            P("frames", None, None),
            P("frames"),
            P(),
            P(),
            P(),
            P(),
            P(None, None, "heads"),
            P("heads", None),
            P(None, None, "heads"),
            P("heads", None),
            P(),
            P(None, "heads"),
            P("heads"),
            P("heads", None),
            P("frames", None, None),
        ),
        out_specs=(
            P("frames", "heads", None),
            P("frames", "heads", None),
            P(),
            P(),
            P(),
            P(None, None, "heads"),
            P("heads", None),
            P(None, None, "heads"),
            P("heads", None),
            P(),
            P(None, "heads"),
            P("heads"),
            P("heads", None),
        ),
        check_vma=False,
    )
```

```python
import jax
import jax.numpy as jnp
import numpy as np
from jax import lax
from jax.experimental import pallas as pl
from jax.experimental.pallas import tpu as pltpu
from jax.sharding import PartitionSpec as P

HD = 64
SCALE = HD**-0.5
EPS = 1e-05
MASKED = -1000000000.0
F32 = jnp.float32
BF16 = jnp.bfloat16
MESH = pl.DeviceIdType.MESH
MLP_RESULTS = ("down_grad", "up_grad")
T_RESULTS = ("t_q", "t_k", "t_v", "t_out")
S_RESULTS = ("s_q", "s_k", "s_v", "s_out")
VMEM_LIMIT = 62 * 1024 * 1024
GELU_C = float(np.sqrt(2.0 / np.pi))
LAG = 2
SLOT_US, STEP_US, FRAME_US, MLP_US, ATTENTION_US, LAST_FRAME_US = 1.15, 1.45, 4.5, 5.8, 2.9, 3.6
CHUNK_US, WHOLE_US = 1.45, 100.0
ADJUST = {(1, 'hop', (0, 3)): -1.2, (4, 'owner', 0): 0.3}
LAST_GRADS = 3
LAST_SMALL = (5, 6, 9, 12)
HOP_US, SIBLING_US, COMPUTE_US, LINK_US, OWNER_US, SWAP_US = 3.4, 1.0, 2.0, 1.45, 1.0, 4.0


def mm(a, b):
    return lax.dot_general(a, b, (((1,), (0,)), ((), ())), preferred_element_type=F32)


def mm_nt(a, b):
    return lax.dot_general(a, b, (((1,), (1,)), ((), ())), preferred_element_type=F32)


def mm_tn(a, b):
    return lax.dot_general(a, b, (((0,), (0,)), ((), ())), preferred_element_type=F32)


def norm_stats(value):
    centered = value - jnp.mean(value, axis=-1, keepdims=True)
    inv = lax.rsqrt(jnp.mean(centered * centered, axis=-1, keepdims=True) + EPS)
    return centered * inv, inv


def norm_back(value, grad, gain):
    normed, inv = norm_stats(value)
    e = grad * gain
    first = jnp.mean(e, axis=-1, keepdims=True)
    second = jnp.mean(e * normed, axis=-1, keepdims=True)
    gain_grad = jnp.sum(grad * normed, axis=0, keepdims=True)
    shift_grad = jnp.sum(grad, axis=0, keepdims=True)
    return (e - first - normed * second) * inv, gain_grad, shift_grad


def head_lanes(shape, head):
    lane = lax.broadcasted_iota(jnp.int32, shape, 1)
    return (lane >= head * HD) & (lane < (head + 1) * HD)


def softmax_of(q, k, mask):
    scores = mm_nt(q, k) * SCALE
    if mask is not None:
        scores = jnp.where(mask, scores, MASKED)
    raised = jnp.exp(scores - jnp.max(scores, axis=-1, keepdims=True))
    return raised / jnp.sum(raised, axis=-1, keepdims=True)


def attend(q, k, v, mask):
    heads = q.shape[1] // HD
    mixed = None
    for head in range(heads):
        lanes = head_lanes(q.shape, head)
        probs = softmax_of(jnp.where(lanes, q, jnp.zeros_like(q)), k, mask).astype(BF16)
        out = mm(probs, v)
        mixed = out if mixed is None else jnp.where(lanes, out, mixed)
    return mixed.astype(BF16)


def attend_back(q, k, v, mask, grad):
    heads = q.shape[1] // HD
    dq = dk = dv = None
    for head in range(heads):
        lanes = head_lanes(q.shape, head)
        qh = jnp.where(lanes, q, jnp.zeros_like(q))
        gh = jnp.where(lanes, grad, jnp.zeros_like(grad))
        probs = softmax_of(qh, k, mask)
        dvh = mm_tn(probs.astype(BF16), gh)
        dp = mm_nt(gh, v)
        ds = (probs * (dp - jnp.sum(dp * probs, axis=-1, keepdims=True))).astype(BF16)
        dqh = mm(ds, k) * SCALE
        dkh = mm_tn(ds, qh) * SCALE
        if head == 0:
            dq, dk, dv = dqh, dkh, dvh
        else:
            dq = jnp.where(lanes, dqh, dq)
            dk = dk + dkh
            dv = dv + dvh
    return dq.astype(BF16), dk.astype(BF16), dv.astype(BF16)


class Line:
    def __init__(self, steps):
        self.frames = lax.axis_size("frames")
        self.heads = lax.axis_size("heads")
        self.chips = self.heads // 2
        self.f = lax.axis_index("frames")
        self.h = lax.axis_index("heads")
        self.z = self.h // 2
        self.c = self.h % 2
        self.steps = steps

    def at(self, z):
        return (self.f, jnp.clip(z, 0, self.chips - 1) * 2 + self.c)

    def sibling(self):
        return (self.f, self.z * 2 + 1 - self.c)

    def barrier(self, over_frames, whole_line=False):
        sem = pltpu.get_barrier_semaphore()

        def greet(device):
            pl.semaphore_signal(sem, inc=1, device_id=device, device_id_type=MESH)

        greet(self.sibling())
        count = 1
        if over_frames:
            for k in range(1, self.frames):
                greet(((self.f + k) % self.frames, self.h))
            count += self.frames - 1
        if whole_line:
            for k in range(1, self.chips):
                greet(self.at((self.z + k) % self.chips))
            count += self.chips - 1
        else:

            @pl.when(self.z > 0)
            def _():
                greet(self.at(self.z - 1))

            @pl.when(self.z < self.chips - 1)
            def _():
                greet(self.at(self.z + 1))

            count = count + (self.z > 0).astype(jnp.int32)
            count = count + (self.z < self.chips - 1).astype(jnp.int32)
        pl.semaphore_wait(sem, count)

    def copy(self, src, dst, send, recv, device):
        return pltpu.make_async_remote_copy(
            src_ref=src,
            dst_ref=dst,
            send_sem=send,
            recv_sem=recv,
            device_id=device,
            device_id_type=MESH,
        )


class Gather:
    def __init__(self, line, buf, sems):
        self.line, self.buf = line, buf
        self.got, self.got_sib, self.sent_up, self.sent_down, self.sent_sib = sems

    def up(self, s, zb):
        ln = self.line
        ref = self.buf.at[s, zb, ln.c]
        return ln.copy(ref, ref, self.sent_up.at[s, zb], self.got.at[s, zb], ln.at(ln.z + 1))

    def down(self, s, zb):
        ln = self.line
        ref = self.buf.at[s, zb, ln.c]
        return ln.copy(ref, ref, self.sent_down.at[s, zb], self.got.at[s, zb], ln.at(ln.z - 1))

    def across(self, s, zb):
        ln = self.line
        ref = self.buf.at[s, zb, ln.c]
        return ln.copy(ref, ref, self.sent_sib.at[s, zb], self.got_sib.at[s, zb], ln.sibling())

    def wait_across(self, s, zb):
        ln = self.line
        ref = self.buf.at[s, zb, 1 - ln.c]
        ln.copy(
            ref, ref, self.sent_sib.at[s, zb], self.got_sib.at[s, zb], ln.sibling()
        ).wait_recv()

    def send(self, s):
        ln = self.line

        @pl.when(ln.z < ln.chips - 1)
        def _():
            self.up(s, ln.z).start()

        @pl.when(ln.z > 0)
        def _():
            self.down(s, ln.z).start()

        self.across(s, ln.z).start()

    def start(self, own):
        ln = self.line
        for s in range(ln.steps):
            self.buf[s, ln.z, ln.c] = own[s]
            self.send(s)

    def arrive(self, distance, s):
        ln = self.line
        below, above = ln.z - distance, ln.z + distance

        @pl.when((distance > 0) & (below >= 0))
        def _():
            self.up(s, below).wait_recv()

            @pl.when(ln.z < ln.chips - 1)
            def _():
                self.up(s, below).start()

            self.across(s, below).start()

        @pl.when((distance > 0) & (above < ln.chips))
        def _():
            self.down(s, above).wait_recv()

            @pl.when(ln.z > 0)
            def _():
                self.down(s, above).start()

            self.across(s, above).start()

    def drain(self, s, zb):
        ln = self.line

        @pl.when((zb <= ln.z) & (ln.z < ln.chips - 1))
        def _():
            self.up(s, zb).wait_send()

        @pl.when((zb >= ln.z) & (ln.z > 0))
        def _():
            self.down(s, zb).wait_send()

        self.across(s, zb).wait_send()


class ChainSum:
    def __init__(self, line, bufs, sems):
        self.line = line
        self.part, self.sib, self.rise, self.fall, self.out = bufs
        self.sent_sib, self.got_sib, self.got_up, self.got_down, self.sent = sems

    def across(self, s, zb):
        ln = self.line
        return ln.copy(
            self.part.at[s, zb, 1 - ln.c],
            self.sib.at[s, zb],
            self.sent_sib.at[s, zb],
            self.got_sib.at[s, zb],
            ln.sibling(),
        )

    def up(self, s, o):
        ln = self.line
        return ln.copy(
            self.out.at[s, o],
            self.rise.at[s, o],
            self.sent.at[s, o],
            self.got_up.at[s, o],
            ln.at(ln.z + 1),
        )

    def down(self, s, o):
        ln = self.line
        return ln.copy(
            self.out.at[s, o],
            self.fall.at[s, o],
            self.sent.at[s, o],
            self.got_down.at[s, o],
            ln.at(ln.z - 1),
        )

    def mine(self, s, o):
        return self.part[s, o, self.line.c].astype(F32) + self.sib[s, o].astype(F32)

    def hop_up(self, s, o):
        ln = self.line
        self.across(s, o).wait_recv()

        @pl.when(ln.z == 0)
        def _():
            self.out[s, o] = self.mine(s, o).astype(BF16)

        @pl.when(ln.z > 0)
        def _():
            self.up(s, o).wait_recv()
            self.out[s, o] = (self.mine(s, o) + self.rise[s, o].astype(F32)).astype(BF16)

        self.up(s, o).start()

    def hop_down(self, s, o):
        ln = self.line
        self.across(s, o).wait_recv()

        @pl.when(ln.z == ln.chips - 1)
        def _():
            self.out[s, o] = self.mine(s, o).astype(BF16)

        @pl.when(ln.z < ln.chips - 1)
        def _():
            self.down(s, o).wait_recv()
            self.out[s, o] = (self.mine(s, o) + self.fall[s, o].astype(F32)).astype(BF16)

        self.down(s, o).start()

    def hops(self, t, part=None, fits=True):
        ln = self.line
        last = ln.chips - 1
        for upward in (True, False):
            place = ln.z if upward else last - ln.z
            q = t - place * LAG
            if part is None:
                turn = jnp.maximum(q, 0) // ln.steps
                s = jnp.maximum(q, 0) % ln.steps
            else:
                turn, s = jnp.maximum(q, 0), part
            far = jnp.clip(last - turn, 0, last)
            ok = (q >= 0) & (turn < last) & (far > place) & fits
            o = far if upward else last - far

            @pl.when(ok)
            def _():
                if upward:
                    self.hop_up(s, o)
                else:
                    self.hop_down(s, o)

    def finish(self, s, total):
        ln = self.line
        self.across(s, ln.z).wait_recv()
        total[...] = self.mine(s, ln.z)

        @pl.when(ln.z > 0)
        def _():
            self.up(s, ln.z).wait_recv()
            total[...] += self.rise[s, ln.z].astype(F32)

        @pl.when(ln.z < ln.chips - 1)
        def _():
            self.down(s, ln.z).wait_recv()
            total[...] += self.fall[s, ln.z].astype(F32)

    def drain(self, s, zb):
        ln = self.line
        self.across(s, zb).wait_send()

        @pl.when(zb != ln.z)
        def _():
            self.up(s, zb).wait_send()


def drain_all(line, things, parts):
    def body(i, carry):
        for thing in things:
            thing.drain(i // line.chips, i % line.chips)
        return carry

    lax.fori_loop(0, parts * line.chips, body, 0)


class Swap:
    def __init__(self, line, src_at, dst, sems):
        self.line, self.src_at, self.dst = line, src_at, dst
        self.sent, self.got = sems

    def copy(self, part, k):
        ln = self.line
        to = (ln.f + k) % ln.frames
        return ln.copy(
            self.src_at(part, to),
            self.dst.at[part, ln.f],
            self.sent.at[part, k],
            self.got.at[part, k],
            (to, ln.h),
        )

    def start(self, part):
        ln = self.line
        for k in range(1, ln.frames):
            self.copy(part, k).start()
        self.dst[part, ln.f] = self.src_at(part, ln.f)[...]

    def wait(self, part):
        for k in range(1, self.line.frames):
            self.copy(part, k).wait()


class FrameSum:
    def __init__(self, line, part, full, dim, reverse, recv_bufs, sems):
        self.line, self.part, self.full, self.dim = line, part, full, dim
        self.recv_bufs = recv_bufs
        self.sent, self.got, self.sent_back, self.got_back = sems
        bits = range(line.frames.bit_length() - 1)
        self.bits = list(reversed(bits)) if reverse else list(bits)
        self.spans = []
        start, size = 0, part.shape[dim]
        for bit in self.bits:
            size //= 2
            side = (line.f // (1 << bit)) % 2
            peer = (line.f + (1 - 2 * side) * (1 << bit), line.h)
            keep, give = start + side * size, start + (1 - side) * size
            self.spans.append((keep, give, size, peer))
            start = keep

    def view(self, ref, start, size, step):
        if self.dim == 0:
            return ref.at[pl.ds(pl.multiple_of(start, step), size)]
        return ref.at[:, pl.ds(pl.multiple_of(start, step), size)]

    def out(self, i, chunk=0, chunks=1):
        _, give, size, peer = self.spans[i]
        step = size // chunks
        src = self.view(self.part, give + chunk * step, step, step)
        dst = self.view(self.recv_bufs[i], chunk * step, step, step)
        return self.line.copy(src, dst, self.sent.at[i], self.got.at[i], peer)

    def back(self, i, chunk=0, chunks=1):
        keep, _, size, peer = self.spans[i]
        step = size // chunks
        ref = self.view(self.full, keep + chunk * step, step, step)
        return self.line.copy(ref, ref, self.sent_back.at[i], self.got_back.at[i], peer)

    def back_in(self, i):
        _, give, size, peer = self.spans[i]
        ref = self.view(self.full, give, size, size)
        return self.line.copy(ref, ref, self.sent_back.at[i], self.got_back.at[i], peer)

    def send(self, k, chunk=0, chunks=1):
        n = len(self.bits)
        if k < n:
            self.out(k, chunk, chunks).start()
        else:
            self.back(2 * n - 1 - k, chunk, chunks).start()

    def end(self, k):
        n = len(self.bits)
        if k < n:
            keep, _, size, _ = self.spans[k]
            self.out(k).wait()
            ref = self.view(self.part, keep, size, size)
            to = self.view(self.full, keep, size, size) if k == n - 1 else ref
            to[...] = (ref[...].astype(F32) + self.recv_bufs[k][...].astype(F32)).astype(BF16)
        else:
            i = 2 * n - 1 - k
            self.back(i).wait_send()
            self.back_in(i).wait_recv()


def frame_sum_scratch(frames, shape, dim, pieces):
    bits = frames.bit_length() - 1
    scratch = [pltpu.VMEM(shape, BF16)]
    for _ in range(pieces):
        for i in range(bits):
            part = list(shape)
            part[dim] = (shape[dim] // pieces) >> (i + 1)
            scratch.append(pltpu.VMEM(tuple(part), BF16))
        scratch += [pltpu.SemaphoreType.DMA((bits,))] * 4
    return scratch


def frame_sums(line, arrays, scratch):
    bits = line.frames.bit_length() - 1
    out = []
    for full, dim, reverse, pieces in arrays:
        part, scratch = scratch[0], scratch[1:]
        sums = []
        for i in range(pieces):
            mine, scratch = scratch[: bits + 4], scratch[bits + 4 :]
            size = full.shape[dim] // pieces
            at = (slice(None),) * dim + (pl.ds(i * size, size),)
            views = (part.at[at], full.at[at]) if pieces > 1 else (part, full)
            sums.append(FrameSum(line, *views, dim, reverse, mine[:bits], mine[bits:]))
        out.append((part, sums))
    return out


def stage_times(sums, begins, first, bits, free, latency, chunk_us):
    ready = list(begins)
    plan = []
    for k in range(2 * bits):
        for i, group in enumerate(sums):
            length = first / 2 ** (k if k < bits else 2 * bits - 1 - k)
            chunks = 1 << max(int(np.log2(length / chunk_us) + 0.5), 0)
            start = max(free, ready[i])
            for j in range(chunks):
                plan.append((start + j * length / chunks, len(plan), ("send", group, k, j, chunks)))
            free = start + length
            ready[i] = free + latency
            plan.append((ready[i], len(plan), ("end", group, k, 0, 0)))
    return plan, free


def run_step(step):
    what, group, k, chunk, chunks = step
    for one in group:
        if what == "send":
            one.send(k, chunk, chunks)
        else:
            one.end(k)


class Everyone:
    def __init__(self, line, refs, sems):
        self.line = line
        self.src, self.dst_sib, self.dst_line, self.dst_frames, self.full = refs
        self.sent, self.got = sems
        self.share = self.src.shape[1] // line.chips

    def cols(self, z):
        return pl.ds(pl.multiple_of(z * self.share, self.share), self.share)

    def pair_copy(self):
        ln = self.line
        return ln.copy(self.src, self.dst_sib, self.sent.at[0], self.got.at[0], ln.sibling())

    def line_copies(self):
        ln, copies = self.line, []
        for k in range(1, ln.chips):
            to = (ln.z + k) % ln.chips
            src, dst = self.dst_sib.at[:, self.cols(to)], self.dst_line.at[ln.z]
            copies.append(ln.copy(src, dst, self.sent.at[k], self.got.at[k], ln.at(to)))
        return copies

    def frame_copies(self):
        ln, copies = self.line, []
        for k in range(1, ln.frames):
            to, i = ((ln.f + k) % ln.frames, ln.h), ln.chips + k
            src, dst = self.dst_line.at[ln.z], self.dst_frames.at[ln.f]
            copies.append(ln.copy(src, dst, self.sent.at[i], self.got.at[i], to))
        return copies

    def back_copies(self):
        ln, copies = self.line, []
        for k in range(1, ln.chips):
            to, i = ln.at((ln.z + k) % ln.chips), ln.chips + ln.frames + k
            ref = self.full.at[:, self.cols(ln.z)]
            copies.append(ln.copy(ref, ref, self.sent.at[i], self.got.at[i], to))
        return copies

    def over_pair(self, value):
        self.src[...] = value.astype(BF16)
        self.pair_copy().start()

    def over_line(self):
        self.pair_copy().wait()
        pair = self.src[...].astype(F32) + self.dst_sib[...].astype(F32)
        self.dst_sib[...] = pair.astype(BF16)
        for copy in self.line_copies():
            copy.start()

    def over_frames(self):
        ln = self.line
        for copy in self.line_copies():
            copy.wait()
        total = self.dst_sib[:, self.cols(ln.z)].astype(F32)
        for k in range(1, ln.chips):
            total = total + self.dst_line[(ln.z + k) % ln.chips].astype(F32)
        self.dst_line[ln.z] = total.astype(BF16)
        for copy in self.frame_copies():
            copy.start()
        self.dst_frames[ln.f] = self.dst_line[ln.z]

    def over_back(self):
        for copy in self.frame_copies():
            copy.wait()
        total = self.dst_frames[0].astype(F32)
        for i in range(1, self.line.frames):
            total = total + self.dst_frames[i].astype(F32)
        self.full[:, self.cols(self.line.z)] = total.astype(BF16)
        for copy in self.back_copies():
            copy.start()

    def result(self):
        for copy in self.back_copies():
            copy.wait()
        return self.full[...].astype(F32)


class Timetable:
    PHASES = 5

    def __init__(self, chips, streams):
        self.chips, self.streams = chips, streams
        last = chips - 1
        arrivals = [(d * HOP_US, "arrive", d) for d in range(chips)]
        gathered = last * HOP_US + SIBLING_US
        first = self.sum_steps(0.0)
        middle = self.sum_steps(gathered)
        self.turn = max((middle[-1][0] + OWNER_US) / streams, chips * LINK_US)
        period = self.turn * streams
        second = max(HOP_US, SIBLING_US + COMPUTE_US + SIBLING_US)
        y = self.sum_steps(second - COMPUTE_US - SIBLING_US)
        leads = [0.0, first[-1][0] + OWNER_US + SWAP_US - period]
        leads.append(leads[1] + max(middle[-1][0] + OWNER_US + SWAP_US - period, 0.0))
        groups = (
            (0, 0, leads[0], first),
            (1, 3, leads[1], arrivals + middle),
            (4, 4, leads[2], arrivals + [(gathered, "gathered", 0)] + y),
        )
        self.every = 6
        self.order = []
        for i in range(self.every):
            at = (i + 0.5) * self.turn / self.every
            self.order.append((at, 0.0, "beside", i, 0, 0, 0))
        self.computed = {}
        self.turns = 0
        for low, high, lead, steps in groups:
            for t, what, which in steps:
                t += lead + ADJUST.get((low, what, which), 0.0)
                behind = int(np.floor(t / self.turn))
                at = t - behind * self.turn
                self.order.append((at, -t, what, which, behind, low, high))
                if what == ("gathered" if low == 4 else "compute"):
                    self.computed |= {phase: behind for phase in range(low, high + 1)}
                self.turns = max(self.turns, (high + 1) * streams + behind)
        self.order.sort(key=lambda step: step[:2])

    def sum_steps(self, compute):
        last = self.chips - 1
        steps = [(compute, "compute", 0)]
        start = compute + COMPUTE_US + SIBLING_US
        hops = {}
        for place in range(last):
            t = start
            for far in range(last, place, -1):
                if place:
                    t = max(t, hops[place - 1, far] + HOP_US)
                hops[place, far] = t
                steps.append((t, "hop", (place, far)))
                t += LINK_US
        owner = max(hops[far - 1, far] for far in range(1, self.chips)) + HOP_US
        return steps + [(owner, "owner", 0)]

    def y_owner(self, item):
        t = [t for t in self.order if t[2] == "owner" and t[5] == 4][0]
        return (item + t[4]) * self.every + int(t[0] / self.turn * self.every + 0.5)

    def after(self, item):
        return item + self.computed[item // self.streams] + 1


def pipeline(line, times, turns, gather, sums, enter, compute, gathered, owner, total, beside):
    last, streams = line.chips - 1, times.streams

    def body(m, carry):
        for _, _, what, which, behind, low, high in times.order:
            if what == "beside":
                beside(m, which)
                continue
            n = m - behind
            fits = (n >= low * streams) & (n < (high + 1) * streams)
            n = jnp.clip(n, low * streams, (high + 1) * streams - 1)
            s = n % streams
            held = n - streams
            if what == "hop":
                place, far = which

                @pl.when(fits & (line.z == place))
                def _():
                    sums.hop_up(s, far)

                @pl.when(fits & (line.z == last - place))
                def _():
                    sums.hop_down(s, last - far)

                continue

            @pl.when(fits)
            def _():
                if what == "arrive":
                    if which == 0:
                        enter(n)
                        gather.send(held)
                    else:
                        gather.arrive(which, held)
                elif what == "compute":
                    if low == 4:
                        gather.wait_across(held, line.z)
                    for zb in range(line.chips):
                        if 1 <= low <= 3:
                            gather.wait_across(held, zb)
                        if low:
                            sums.drain(s, zb)
                    compute(n, low, high)
                    for zb in range(line.chips):
                        sums.across(s, zb).start()
                elif what == "gathered":
                    for zb in range(line.chips):

                        @pl.when(line.z != zb)
                        def _():
                            gather.wait_across(held, zb)

                    gathered(n)
                else:
                    sums.finish(s, total)
                    owner(n, low, high)

        return carry

    lax.fori_loop(0, turns, body, 0)


def frame_mask(segments, places, rows):
    frames = segments.shape[0]
    bits, place_bits = frames.bit_length() - 1, places.bit_length() - 1

    def ids_along(axis, shape):
        index = lax.broadcasted_iota(jnp.int32, shape, axis)
        frame = lax.shift_right_logical(index, place_bits) & (frames - 1)
        segment = jnp.zeros(shape, jnp.int32)
        for i in range(frames):
            segment = jnp.where(frame == i, segments[i], segment)
        block = lax.shift_right_logical(index, place_bits + bits)
        return block * places + (index & (places - 1)), frame, segment

    place_q, frame_q, segment_q = ids_along(0, (rows, 1))
    place_k, frame_k, segment_k = ids_along(1, (1, rows))
    return (place_q == place_k) & (frame_k <= frame_q) & (segment_q == segment_k)


def column_grads(start, left, right, out):
    rows = pl.ds(pl.multiple_of(start, 256), 256)
    out[rows] = mm_tn(left, right.reshape(left.shape[0], right.shape[-1])).astype(BF16)


def row_sum(value):
    return jnp.sum(value, axis=0, keepdims=True)


def moved_exactly(order, value):
    out = None
    for _ in range(3):
        term = value.astype(BF16)
        value = value - term.astype(F32)
        out = mm(order, term) if out is None else out + mm(order, term)
    return out


class Refs:
    def __init__(self, names, refs):
        for name, ref in zip(names, refs, strict=True):
            setattr(self, name, ref)


def block(fetched, results, names, *refs):
    ends = len(fetched), len(fetched) + len(results)
    r = Refs(names, refs[ends[1] :])
    r.fetched = dict(zip(fetched, refs))
    r.stored = dict(zip(results, refs[ends[0] :]))
    r.ids, r.segments = r.fetched.pop("ids"), r.fetched.pop("segments")
    steps, patches, width = r.x.shape
    streams, rows, _ = r.y.shape
    heads = 2 * r.g_all.shape[1]
    line, t_line = Line(steps), Line(streams)
    chips, frames = line.chips, line.frames
    s_rows = patches // heads
    tokens = steps * s_rows
    columns, hidden = r.s_wout.shape[0], r.up.shape[1]
    entries = r.table.shape[0]
    count = heads * rows
    all_tokens = heads * tokens
    times = Timetable(chips, streams)
    sums = ChainSum(t_line, (r.part, r.sib, r.rise, r.fall, r.out), r.sum_sems)
    gather = Gather(t_line, r.gathered, r.gather_sems)
    last_part = getattr(r, "last_part", r.g_all)
    last_out = getattr(r, "last_out", r.out)
    last_total = getattr(r, "last_total", r.grad2)
    last_sums = ChainSum(
        line, (last_part, r.last_sib, r.last_rise, r.last_fall, last_out), r.last_sems
    )
    shared = not hasattr(r, "g_src")

    def g_src_at(part, to):
        return r.gathered.at[3 * streams + to, part] if shared else r.g_src.at[0, to, part]

    g_swap = Swap(line, g_src_at, r.g_dst, r.g_sems)
    state_swap = Swap(line, lambda s, to: r.state_src.at[s, to], r.state_dst, r.state_sems)
    grad_swap = Swap(line, lambda s, to: r.grad_src.at[s, to], r.grad_dst, r.grad_sems)
    y_swap = Swap(line, lambda s, to: r.y_src.at[s, to], r.y_dst, r.y_sems)
    every = Everyone(
        line,
        (r.every_src, r.every_sib, r.every_line, r.every_frames, r.every_full),
        r.every_sems,
    )
    (
        (down_part, down_sums), (up_part, up_sums),
        (t_q_part, t_q_sums), (t_k_part, t_k_sums), (t_v_part, t_v_sums), (t_out_part, t_out_sums),
        (s_q_part, s_q_sums), (s_k_part, s_k_sums), (s_v_part, s_v_sums), (s_out_part, s_out_sums),
    ) = frame_sums(
        line,
        [
            (r.down_grad, 0, False, 2), (r.up_grad, 0, True, 2),
            (r.t_q, 0, False, 1), (r.t_k, 0, True, 1), (r.t_v, 0, False, 1), (r.t_out, 1, True, 1),
            (r.s_q, 0, False, 1), (r.s_k, 0, True, 1), (r.s_v, 0, False, 1), (r.s_out, 1, True, 1),
        ],
        r.reduce,
    )
    t_parts = t_q_part, t_k_part, t_v_part
    s_parts = s_q_part, s_k_part, s_v_part
    mlp_sums = list(zip(down_sums, up_sums))
    t_sums = [t_q_sums + t_k_sums, t_v_sums + t_out_sums]
    s_sums = [s_q_sums + s_k_sums, s_v_sums]
    bits = len(down_sums[0].bits)
    bias_swap = Swap(line, lambda _, to: r.bias_src, r.bias_dst, r.bias_sems)
    fetches = [
        pltpu.make_async_copy(r.fetched[name], getattr(r, name), r.fetch_sems.at[i])
        for i, name in enumerate(r.fetched)
    ]
    for fetch in fetches:
        fetch.start()
    line.barrier(True, True)
    for fetch in fetches:
        fetch.wait()
    stored = []

    def store(name):
        i = list(r.stored).index(name)
        stored.append(
            pltpu.make_async_copy(getattr(r, name), r.stored[name], r.store_sems.at[i])
        )
        stored[-1].start()

    def g_out(i, carry):
        rows_of = pl.ds(pl.multiple_of(i * s_rows, s_rows), s_rows)
        moved = mm(r.to_peers[...], r.cotangent[:, rows_of].reshape(tokens, width))
        moved = moved.astype(BF16).astype(r.g_dst.dtype).reshape(frames, tokens // frames, width)
        if shared:
            r.gathered[3 * streams : 4 * streams, i // 2, i % 2] = moved
        else:
            r.g_src[0, :, i // 2, i % 2] = moved
        return carry

    lax.fori_loop(0, heads, g_out, 0)
    for part in range(chips - 2):
        g_swap.start(part)

    def g_in(i):
        moved = r.g_dst[i // 2, :, i % 2].reshape(tokens, width).astype(BF16)
        moved = mm(r.to_parts[...], moved).astype(BF16)
        r.g_all[:, i // 2, i % 2] = moved.reshape(streams, rows, width)

    table_row = lax.broadcasted_iota(jnp.int32, (entries, width), 0)

    def added(s):
        return row_sum(jnp.where(table_row == r.ids[s], r.table[...].astype(F32), 0.0))

    def norm(value, i):
        scaled = norm_stats(value)[0] * r.gain[i : i + 1, :]
        return (scaled + r.shift[i : i + 1, :]).astype(BF16)

    def attention(s, carry):
        normed = norm(r.x[s].astype(F32) + added(s), 0)
        r.normed0[s] = normed
        q = mm(normed, r.s_wqkv[0]).astype(BF16)
        k = mm(normed, r.s_wqkv[1]).astype(BF16)
        v = mm(normed, r.s_wqkv[2]).astype(BF16)
        r.s_proj[0, s] = q
        r.s_proj[1, s] = k
        r.s_proj[2, s] = v
        r.s_cols[s] = attend(q, k, v, None)
        return carry

    lax.fori_loop(0, steps, attention, 0)

    def to_streams(i, carry):
        rows_of = pl.ds(pl.multiple_of(i * s_rows, s_rows), s_rows)
        moved = mm(r.to_streams[...], r.s_cols[:, rows_of].reshape(tokens, columns)).astype(BF16)
        r.s_mixed[:, i] = moved.reshape(streams, rows, columns)
        return carry

    lax.fori_loop(0, heads, to_streams, 0)
    own_rows = pl.ds(pl.multiple_of(line.h * s_rows, s_rows), s_rows)
    own = mm(r.to_streams[...], r.x[:, own_rows].reshape(tokens, width))
    row = lax.broadcasted_iota(jnp.int32, (tokens, 1), 0)
    frame = lax.shift_right_logical(row, (rows // (frames * steps)).bit_length() - 1) & (steps - 1)
    entry = jnp.zeros_like(row)
    for s in range(steps):
        entry = jnp.where(frame == s, r.ids[s], entry)
    picker = (entry == lax.broadcasted_iota(jnp.int32, (tokens, entries), 1)).astype(BF16)
    own = own + mm(picker, r.table[...])
    r.state0[...] = own.reshape(streams, rows, width)
    r.mask[...] = frame_mask(r.segments, rows // (frames * steps), count).astype(F32)
    r.up_bias_grad[...] = jnp.zeros_like(r.up_bias_grad)
    r.small[...] = jnp.zeros_like(r.small)

    def held(n):
        return n - streams

    def enter_temporal(s, n):
        state_swap.wait(s)
        state = r.state_dst[s].reshape(rows, width)
        r.state1[s] = state
        r.gathered[held(n), line.z, line.c] = norm(state, 1)

    def enter_spatial(s, n):
        grad_swap.wait(s)
        grad = r.grad_dst[s].reshape(rows, width)
        r.grad1[s] = grad
        r.gathered[held(n), line.z, line.c] = grad.astype(BF16)

    def compute_spatial(s, n):
        left = r.s_mixed[s].reshape(count, columns)
        r.part[s] = mm(left, r.s_wout[...]).astype(BF16).reshape(chips, 2, rows, width)

    def compute_temporal(s, n):
        a = r.gathered[held(n)].reshape(count, width)
        q = mm(a, r.t_wqkv[0]).astype(BF16)
        k = mm(a, r.t_wqkv[1]).astype(BF16)
        v = mm(a, r.t_wqkv[2]).astype(BF16)
        r.t_proj[0, s] = q
        r.t_proj[1, s] = k
        r.t_proj[2, s] = v
        mixed = attend(q, k, v, r.mask[...] > 0.0)
        r.t_mixed[s] = mixed
        r.part[s] = mm(mixed, r.t_wout[...]).astype(BF16).reshape(chips, 2, rows, width)

    def compute_mlp(s, n):
        a = r.gathered[held(n)].reshape(count, width)
        g = r.g_all[s].reshape(count, width)
        pre = mm(a, r.up[...]) + r.up_bias[...]
        t = jnp.tanh(GELU_C * (pre + 0.044715 * (pre * pre * pre)))
        act = (0.5 * pre * (1.0 + t)).astype(BF16)
        r.act[s] = act
        slope = 0.5 * (1.0 + t)
        slope = slope + 0.5 * pre * (1.0 - t * t) * (GELU_C * (1.0 + 0.134145 * (pre * pre)))
        dpre = (mm_nt(g, r.down[...]) * slope).astype(BF16)
        r.dpre[s] = dpre
        r.up_bias_grad[:, :hidden] += row_sum(dpre.astype(F32))
        r.part[s] = mm_nt(dpre, r.up[...]).astype(BF16).reshape(chips, 2, rows, width)

    def compute_back(s, n):
        grad = r.gathered[held(n)].reshape(count, width)
        dm = mm_nt(grad, r.t_wout[...]).astype(BF16)
        mask = r.mask[...] > 0.0
        dq, dk, dv = attend_back(r.t_proj[0, s], r.t_proj[1, s], r.t_proj[2, s], mask, dm)
        r.t_dproj[0, s] = dq
        r.t_dproj[1, s] = dk
        r.t_dproj[2, s] = dv
        da = mm_nt(dq, r.t_wqkv[0]) + mm_nt(dk, r.t_wqkv[1]) + mm_nt(dv, r.t_wqkv[2])
        r.part[s] = da.astype(BF16).reshape(chips, 2, rows, width)

    def gathered_last(n):
        grad = r.gathered[held(n)].reshape(count, width)
        moved = mm_nt(grad, r.s_wout[...]).astype(BF16)
        r.s_dmixed[n % streams] = moved.reshape(heads, rows, columns)

    def compute_last(s, n):
        y = mm(r.act[s], r.down[...])
        r.part[s] = y.astype(BF16).reshape(chips, 2, rows, width)

    def owner_spatial(s, n):
        state = r.state0[s] + r.total[...] + r.bias[0:1, :]
        r.state_src[s] = state.reshape(r.state_src.shape[1:])
        state_swap.start(s)

        for part, after in ((chips - 2, streams // 2 - 1), (chips - 1, streams - 1)):

            @pl.when(s == after)
            def _():
                g_swap.start(part)

    def owner_temporal(s, n):
        state = r.state1[s] + r.total[...] + r.bias[1:2, :]
        r.state2[s] = state
        r.gathered[n, line.z, line.c] = norm(state, 2)

    def owner_mlp(s, n):
        grad = r.g_all[s, line.z, line.c].astype(F32)
        back, gain_grad, shift_grad = norm_back(r.state2[s], r.total[...], r.gain[2:3, :])
        dh = grad + back
        r.grad2[s] = dh
        r.gathered[n, line.z, line.c] = dh.astype(BF16)
        r.small[0:1] += gain_grad
        r.small[1:2] += shift_grad
        r.small[2:3] += row_sum(grad)
        r.small[3:4] += row_sum(dh)

    def owner_back(s, n):
        back, gain_grad, shift_grad = norm_back(r.state1[s], r.total[...], r.gain[1:2, :])
        dh = r.grad2[s] + back
        r.grad_src[s] = dh.reshape(r.grad_src.shape[1:])
        grad_swap.start(s)
        r.small[4:5] += gain_grad
        r.small[5:6] += shift_grad
        r.small[6:7] += row_sum(dh)

    def owner_last(s, n):
        r.y[s] = (r.state2[s] + r.total[...] + r.bias[2:3, :]).astype(BF16)

    def by_phase(bodies):
        def run(n, low=0, high=4):
            for i, one in enumerate(bodies):
                if one is not None and low <= i <= high:

                    @pl.when(n // streams == i)
                    def _():
                        one(n % streams, n)

        return run

    def down_chunk(i):
        cols = pl.ds(pl.multiple_of(i * 128, 128), 128)
        left = r.act[:, :, cols].reshape(all_tokens, 128)
        right = r.g_all[...].reshape(all_tokens, width)
        down_part[cols] = mm_tn(left, right).astype(BF16)

    def up_chunk(i):
        cols = pl.ds(pl.multiple_of(i * 256, 256), 256)
        left = r.gathered[streams : 2 * streams, :, :, :, cols].reshape(all_tokens, 256)
        right = r.dpre[...].reshape(all_tokens, hidden)
        up_part[cols] = mm_tn(left, right).astype(BF16)

    def t_out_chunk(i):
        left = r.t_mixed[...].reshape(all_tokens, columns)
        right = r.gathered[2 * streams : 3 * streams].reshape(all_tokens, width)
        t_out_part[...] = mm_tn(left, right).astype(BF16)

    def t_qkv_chunk(i):
        start = i * 256
        cols = pl.ds(pl.multiple_of(start, 256), 256)
        left = r.gathered[0:streams, :, :, :, cols].reshape(all_tokens, 256)
        for j in range(3):
            column_grads(start, left, r.t_dproj[j], t_parts[j])

    def s_cols_chunk(_):
        def from_streams(i, carry):
            rows_of = pl.ds(pl.multiple_of(i * s_rows, s_rows), s_rows)
            moved = mm(r.from_streams[...], r.s_dmixed[:, i].reshape(tokens, columns)).astype(BF16)
            r.s_cols[:, rows_of] = moved.reshape(steps, s_rows, columns)
            return carry

        lax.fori_loop(0, heads, from_streams, 0)

    def s_back_chunk(s):
        dq, dk, dv = attend_back(r.s_proj[0, s], r.s_proj[1, s], r.s_proj[2, s], None, r.s_cols[s])
        r.s_dproj[0, s] = dq
        r.s_dproj[1, s] = dk
        r.s_dproj[2, s] = dv
        da = mm_nt(dq, r.s_wqkv[0]) + mm_nt(dk, r.s_wqkv[1]) + mm_nt(dv, r.s_wqkv[2])
        last_part[s] = da.astype(BF16).reshape(last_part.shape[1:])
        for zb in range(chips):
            last_sums.across(s, zb).start()
        if early:

            @pl.when(s == 1)
            def _():
                drain_all(t_line, (sums,), streams)

            @pl.when(s > 0)
            def _():
                last_sums.hops(s - 1)

    def s_out_chunk(_):
        left = r.s_mixed[...].reshape(all_tokens, columns)
        right = r.gathered[3 * streams : 4 * streams].reshape(all_tokens, width)
        s_out_part[...] = mm_tn(left, right).astype(BF16)
        s_out_sums[0].send(0)

    def bias_chunk(_):
        r.bias_src[...] = jnp.broadcast_to(r.up_bias_grad[...], r.bias_src.shape)
        bias_swap.start(0)

    def g_in_chunk(i):
        @pl.when(i % 2 == 0)
        def _():
            g_swap.wait(i // 2)

        g_in(i)

    n_down, n_up = hidden // 128, width // 256
    turn_of = times.after
    slots = [i for i in range(times.every) if i % 2 == 1][:3]
    per_slot = 3
    per_turn = per_slot * len(slots)
    mlp_turn, back_turn = turn_of(3 * streams - 1), turn_of(4 * streams - 1)
    last_turn = turn_of(5 * streams - 1)
    chunks = (
        (2 * streams - 1 - heads // per_turn, 0, heads, g_in_chunk),
        (mlp_turn, 0, n_down, down_chunk),
        (mlp_turn, n_down, n_up, up_chunk),
        (mlp_turn, n_down + n_up, 1, bias_chunk),
        (back_turn, 0, 1, t_out_chunk),
        (back_turn, 1, width // 256, t_qkv_chunk),
        (last_turn, 0, 1, s_out_chunk),
        (last_turn, 1, 1, s_cols_chunk),
        (last_turn, 2, steps, s_back_chunk),
    )
    turns = max(times.turns, last_turn + -(-(steps + 2) // per_turn))
    early = times.y_owner(5 * streams - 1) < last_turn * times.every + slots[1]

    def begin_of(turn, number):
        return (turn + number // per_turn) * times.every + times.every - 1

    begin = begin_of(mlp_turn, n_down + n_up) * SLOT_US
    plan, free = stage_times(mlp_sums, [begin] * 2, MLP_US, bits, 0.0, FRAME_US, CHUNK_US)
    begin = begin_of(back_turn, 1 + width // 256) * SLOT_US
    plan += stage_times(t_sums, [begin] * 2, ATTENTION_US, bits, free, FRAME_US, WHOLE_US)[0]
    plan = [(t, i, step) for i, (t, _, step) in enumerate(plan)]
    plan.sort(key=lambda entry: entry[:2])
    end = turns * times.every * SLOT_US
    late = [entry for entry in plan if entry[0] >= end]

    def beside(m, i):
        if i in slots:
            for turn, first, number, chunk in chunks:
                which = per_turn * (m - turn) + per_slot * slots.index(i) - first
                here = jnp.clip(number - which, 0, per_slot)

                @pl.when((which > -per_slot) & (which < number))
                def _():
                    def one(j, carry):
                        @pl.when(which + j >= 0)
                        def _():
                            chunk(which + j)

                        return carry

                    lax.fori_loop(0, here, one, 0)

        for t, _, step in plan:
            moment = int(t / SLOT_US)
            if t < end and moment % times.every == i:

                @pl.when(m == moment // times.every)
                def _():
                    run_step(step)

    enter = by_phase((None, enter_temporal, None, None, enter_spatial))
    compute = by_phase(
        (compute_spatial, compute_temporal, compute_mlp, compute_back, compute_last)
    )
    owner = by_phase((owner_spatial, owner_temporal, owner_mlp, owner_back, owner_last))
    pipeline(
        t_line, times, turns, gather, sums, enter, compute, gathered_last, owner, r.total, beside
    )
    if not early:
        drain_all(t_line, (sums,), streams)

    y = mm(r.from_parts[...], r.y[...].reshape(tokens, width)).astype(BF16)
    r.y_src[0] = y.astype(r.y_src.dtype).reshape(r.y_src.shape[1:])
    y_swap.start(0)

    r.sums0[...] = jnp.zeros_like(r.sums0)

    def small_part(s):
        state = r.x[s].astype(F32) + added(s)
        da = last_part[s].reshape(patches, width).astype(F32)
        back, gain_grad, shift_grad = norm_back(state, da, r.gain[0:1, :])
        r.sums0[0:1] += gain_grad
        r.sums0[1:2] += shift_grad
        r.sums0[8 : 8 + entries] += jnp.where(table_row == r.ids[s], row_sum(back), 0.0)

    room = r.every_src.shape[0]
    filled = 9 + entries

    def small_value(own_grad):
        for s in range(steps):
            here = row_sum(own_grad[s * s_rows : (s + 1) * s_rows])
            r.sums0[8 : 8 + entries] += jnp.where(table_row == r.ids[s], here, 0.0)
        rows_of = [
            r.sums0[0:1], r.small[4:5], r.small[0:1],
            r.sums0[1:2], r.small[5:6], r.small[1:2],
            r.small[6:7], r.small[3:4], r.small[2:3],
            r.sums0[8 : 8 + entries], jnp.zeros((room - filled, width), F32),
        ]
        return jnp.concatenate(rows_of, axis=0)

    first = steps - 1 if early else 0
    begin = LAST_GRADS * STEP_US + 2.5
    last_plan = [(max(int((t - end) / STEP_US), 0) + first + 1, i, step) for t, i, step in late]
    begins = [begin] * len(s_sums) + [begin - 4.0]
    s_plan, _ = stage_times(
        s_sums + [s_out_sums], begins, ATTENTION_US, bits, 0.0, LAST_FRAME_US, WHOLE_US
    )
    last_plan += [
        (int(np.ceil(t / STEP_US)), len(plan) + i, step)
        for t, i, step in s_plan
        if step[0] == "end" or step[2] > 0
    ]
    last_plan.sort(key=lambda entry: entry[:2])
    bound = steps * (chips - 1) + (chips - 2) * LAG + 1
    bound = max(bound, LAST_SMALL[-1] + 1)

    def body(t, carry):
        last_sums.hops(t)

        @pl.when(t == LAST_GRADS)
        def _():
            for j in range(3):
                for i in range(width // 256):
                    left = r.normed0[:, :, i * 256 : (i + 1) * 256].reshape(all_tokens, 256)
                    column_grads(i * 256, left, r.s_dproj[j], s_parts[j])
            for one in s_q_sums + s_k_sums + s_v_sums:
                one.send(0)

        @pl.when((t > LAST_GRADS) & (t <= LAST_GRADS + steps // 2))
        def _():
            def one(i, carry):
                small_part((t - LAST_GRADS - 1) * 2 + i)
                return carry

            lax.fori_loop(0, 2, one, 0)

        @pl.when(t == LAST_SMALL[0])
        def _():
            grad = r.grad1[...].reshape(tokens, width)
            own_grad = moved_exactly(r.from_streams[...], grad)
            r.state0[...] = own_grad.reshape(r.state0.shape)
            every.over_pair(small_value(own_grad))

        steps_of = (every.over_line, every.over_frames, every.over_back)
        for moment, step in zip(LAST_SMALL[1:], steps_of):

            @pl.when(t == moment)
            def _():
                step()

        for moment, _, step in last_plan:
            if moment < bound:

                @pl.when(t == max(moment, first))
                def _():
                    run_step(step)

        return carry

    lax.fori_loop(first, bound, body, 0)
    for s in range(steps):
        last_sums.finish(s, last_total.at[s])
    own_grad = r.state0[...].reshape(tokens, width)
    for s in range(steps):
        state = r.x[s, own_rows].astype(F32) + added(s)
        back, _, _ = norm_back(state, last_total[s], r.gain[0:1, :])
        r.grad_res[pl.ds(s * s_rows, s_rows)] = own_grad[s * s_rows : (s + 1) * s_rows] + back
    y_swap.wait(0)
    r.y_res[...] = mm(r.from_peers[...], r.y_dst[0].reshape(tokens, width).astype(BF16)).astype(BF16)
    r.small_res[...] = every.result()
    bias_swap.wait(0)
    up_bias = r.bias_dst[0, 0]
    for i in range(1, frames):
        up_bias = up_bias + r.bias_dst[0, i]
    r.up_bias_res[...] = up_bias
    for name in ("grad_res", "y_res", "small_res", "up_bias_res") + MLP_RESULTS:
        store(name)
    for moment, _, step in last_plan:
        if moment >= bound:
            run_step(step)
    for name in T_RESULTS + S_RESULTS:
        store(name)
    drain_all(line, (last_sums,), steps)
    drain_all(t_line, (gather,), 4 * streams)
    for one in stored:
        one.wait()


def finish(names, parts, *refs):
    sources = dict(zip(names, refs))
    results = dict(zip(parts, refs[len(names) :]))
    held = refs[len(names) + len(parts) :]
    sems_in, sems_out = held[-2:]
    local = dict(zip(names, held))
    made = dict(zip(parts, held[len(names) :]))
    loads = {
        name: pltpu.make_async_copy(sources[name], local[name], sems_in.at[i])
        for i, name in enumerate(names)
    }
    for load in loads.values():
        load.start()
    loaded, stores = set(), []
    for i, (name, given) in enumerate(parts.items()):
        for j, (source, low, high, columns) in enumerate(given):
            if source not in loaded:
                loads[source].wait()
                loaded.add(source)
            value = local[source][low:high, :columns].astype(made[name].dtype)
            if len(given) > 1:
                made[name][j] = value
            else:
                made[name][...] = value
        stores.append(pltpu.make_async_copy(made[name], results[name], sems_out.at[i]))
        stores[-1].start()
    for store in stores:
        store.wait()


def results(found, entries):
    width, hidden = found["up_grad"].shape

    def whole(name):
        rows, columns = found[name].shape
        return [(name, 0, rows, columns)]

    parts = {
        "t_out": whole("t_out"),
        "t_qkv": whole("t_q") + whole("t_k") + whole("t_v"),
        "down": whole("down_grad"),
        "up": whole("up_grad"),
        "grad": whole("grad_res"),
        "y": whole("y_res"),
        "gain": [("small_res", 0, 3, width)],
        "shift": [("small_res", 3, 6, width)],
        "bias": [("small_res", 6, 9, width)],
        "table": [("small_res", 9, 9 + entries, width)],
        "up_bias": [("up_bias_res", 0, 1, hidden)],
        "s_out": whole("s_out"),
        "s_qkv": whole("s_q") + whole("s_k") + whole("s_v"),
    }
    shapes = []
    for name, given in parts.items():
        _, low, high, columns = given[0]
        lead = (len(given),) if len(given) > 1 else ()
        kind = BF16 if name == "y" else F32
        shapes.append(jax.ShapeDtypeStruct(lead + (high - low, columns), kind))
    order = [name for given in parts.values() for name, _, _, _ in given]
    found = {name: found[name] for name in dict.fromkeys(order)}
    names = tuple(found)
    made = pl.pallas_call(
        lambda *refs: finish(names, parts, *refs),
        name="finish",
        out_shape=shapes,
        in_specs=[pl.BlockSpec(memory_space=pltpu.HBM)] * len(names),
        out_specs=[pl.BlockSpec(memory_space=pltpu.HBM)] * len(shapes),
        scratch_shapes=[pltpu.VMEM(v.shape, v.dtype) for v in found.values()]
        + [pltpu.VMEM(v.shape, v.dtype) for v in shapes]
        + [pltpu.SemaphoreType.DMA((len(names),)), pltpu.SemaphoreType.DMA((len(shapes),))],
        compiler_params=pltpu.CompilerParams(vmem_limit_bytes=VMEM_LIMIT),
    )(*found.values())
    return dict(zip(parts, made))


def orders(frames_local, frames, places, streams):
    tokens = frames_local * frames * places
    index = np.arange(tokens).reshape(frames_local, frames, streams, places // streams)
    to_streams = index.transpose(2, 1, 0, 3).reshape(-1)
    to_peers = index.transpose(1, 0, 2, 3).reshape(-1)
    index = np.arange(tokens).reshape(frames * frames_local, streams, places // streams)
    to_parts = index.transpose(1, 0, 2).reshape(-1)
    eye = np.eye(tokens, dtype=np.float32)
    there = [eye[order] for order in (to_streams, to_peers, to_parts)]
    back = [m.T for m in there]
    names = ("to_streams", "to_peers", "to_parts", "from_streams", "from_peers", "from_parts")
    return {name: jnp.asarray(m, BF16) for name, m in zip(names, there + back)}


def on_device(
    block_input,
    action_ids,
    segment_ids,
    action_table,
    norm_gain,
    norm_shift,
    spatial_qkv,
    spatial_out,
    temporal_qkv,
    temporal_out,
    out_bias,
    up_weight,
    up_bias,
    down_weight,
    cotangent,
):
    frames, heads = lax.axis_size("frames"), lax.axis_size("heads")
    chips = heads // 2
    steps, patches, width = block_input.shape
    rows = patches // heads
    tokens = steps * rows
    total_frames = segment_ids.shape[0]
    places = rows // frames
    streams = min(4, places)
    t_rows = tokens // streams
    columns = spatial_out.shape[0]
    hidden = up_weight.shape[1]
    entries = action_table.shape[0]
    count = heads * t_rows
    room = -(-(10 + entries) // 16) * 16
    args = dict(
        ids=action_ids,
        segments=segment_ids,
        x=block_input,
        cotangent=cotangent,
        table=action_table,
        gain=norm_gain,
        shift=norm_shift,
        bias=out_bias,
        s_wqkv=spatial_qkv.transpose(1, 0, 2),
        s_wout=spatial_out,
        t_wqkv=temporal_qkv.transpose(1, 0, 2),
        t_wout=temporal_out,
        up=up_weight,
        up_bias=up_bias.reshape(1, hidden),
        down=down_weight,
        **orders(steps, frames, places, streams),
    )
    qkv, out = (width, columns), (columns, width)
    down, up = (hidden, width), (width, hidden)
    outs = dict(
        t_q=(qkv, BF16),
        t_k=(qkv, BF16),
        t_v=(qkv, BF16),
        t_out=(out, BF16),
        s_q=(qkv, BF16),
        s_k=(qkv, BF16),
        s_v=(qkv, BF16),
        s_out=(out, BF16),
        up_grad=(up, BF16),
        down_grad=(down, BF16),
        y_res=((tokens, width), BF16),
        grad_res=((tokens, width), F32),
        small_res=((room, width), F32),
        up_bias_res=((8, width), F32),
    )
    s_all = (steps, chips, 2, rows, width)
    t_all = (streams, chips, 2, t_rows, width)
    s_one, t_one = (steps, chips, rows, width), (streams, chips, t_rows, width)
    owned = (streams, t_rows, width)
    swapped = (streams, frames, t_rows // frames, width)
    whole = (1, frames, tokens // frames, width)
    g_part = (1, frames, chips, 2, tokens // frames, width)
    g_into = (chips, frames, 2, tokens // frames, width)

    def kind_of(shape):
        return BF16 if shape[-2] % 16 == 0 else F32

    cols = dict(
        s_cols=(steps, patches, columns),
        s_proj=(3, steps, patches, columns),
        s_dproj=(3, steps, patches, columns),
        s_mixed=(streams, heads, t_rows, columns),
        s_dmixed=(streams, heads, t_rows, columns),
        t_proj=(3, streams, count, columns),
        t_dproj=(3, streams, count, columns),
        t_mixed=(streams, count, columns),
        act=(streams, count, hidden),
        dpre=(streams, count, hidden),
        normed0=(steps, patches, width),
        gathered=(4 * streams,) + t_all[1:],
        g_all=t_all,
        part=t_all,
        sib=t_one,
        rise=t_one,
        fall=t_one,
        out=t_one,
        **({} if s_all == t_all else dict(last_part=s_all, last_out=s_one)),
        last_sib=s_one,
        last_rise=s_one,
        last_fall=s_one,
        y=owned,
    )
    floats = dict(
        state0=owned,
        state1=owned,
        state2=owned,
        grad1=owned,
        grad2=owned,
        total=(t_rows, width),
        **({} if (steps, rows) == (streams, t_rows) else dict(last_total=(steps, rows, width))),
        mask=(count, count),
        small=(8, width),
        sums0=(8 + entries, width),
        up_bias_grad=(1, width),
        state_src=swapped,
        state_dst=swapped,
        grad_src=swapped,
        grad_dst=swapped,
    )
    scratch = {name: pltpu.VMEM(shape, BF16) for name, shape in cols.items()}
    scratch |= {name: pltpu.VMEM(shape, F32) for name, shape in floats.items()}
    scratch["g_dst"] = pltpu.VMEM(g_into, kind_of(g_into))
    if g_part[1:] != t_all:
        scratch["g_src"] = pltpu.VMEM(g_part, kind_of(g_part))
    scratch |= {name: pltpu.VMEM(whole, kind_of(whole)) for name in ("y_src", "y_dst")}
    every_shape = (room, width)
    scratch |= dict(
        every_src=pltpu.VMEM(every_shape, BF16),
        every_sib=pltpu.VMEM(every_shape, BF16),
        every_line=pltpu.VMEM((chips, room, width // chips), BF16),
        every_frames=pltpu.VMEM((frames, room, width // chips), BF16),
        every_full=pltpu.VMEM(every_shape, BF16),
        every_sems=[pltpu.SemaphoreType.DMA((2 * chips + frames,))] * 2,
        bias_src=pltpu.VMEM((8, width), F32),
        bias_dst=pltpu.VMEM((1, frames, 8, width), F32),
        bias_sems=[pltpu.SemaphoreType.DMA((1, frames))] * 2,
        sum_sems=[pltpu.SemaphoreType.DMA((streams, chips))] * 5,
        last_sems=[pltpu.SemaphoreType.DMA((steps, chips))] * 5,
        gather_sems=[pltpu.SemaphoreType.DMA((4 * streams, chips))] * 5,
        state_sems=[pltpu.SemaphoreType.DMA((streams, frames))] * 2,
        grad_sems=[pltpu.SemaphoreType.DMA((streams, frames))] * 2,
        g_sems=[pltpu.SemaphoreType.DMA((chips, frames))] * 2,
        y_sems=[pltpu.SemaphoreType.DMA((1, frames))] * 2,
        reduce=[
            x
            for shape, dim, pieces in ((down, 0, 2), (up, 0, 2))
            + 2 * (((qkv, 0, 1),) * 3 + ((out, 1, 1),))
            for x in frame_sum_scratch(frames, shape, dim, pieces)
        ],
    )
    held = {k: v for k, v in args.items() if k not in ("ids", "segments")}
    scratch |= {name: pltpu.VMEM(v.shape, v.dtype) for name, v in held.items()}
    scratch |= {name: pltpu.VMEM(shape, kind) for name, (shape, kind) in outs.items()}
    scratch["fetch_sems"] = pltpu.SemaphoreType.DMA((len(held),))
    scratch["store_sems"] = pltpu.SemaphoreType.DMA((len(outs),))
    fetched, results_of, names = tuple(args), tuple(outs), tuple(scratch)
    parts = pl.pallas_call(
        lambda *refs: block(fetched, results_of, names, *refs),
        name="block",
        out_shape=[jax.ShapeDtypeStruct(shape, kind) for shape, kind in outs.values()],
        in_specs=[
            pl.BlockSpec(memory_space=pltpu.HBM if name in held else pltpu.SMEM)
            for name in args
        ],
        out_specs=[pl.BlockSpec(memory_space=pltpu.HBM)] * len(outs),
        scratch_shapes=list(scratch.values()),
        compiler_params=pltpu.CompilerParams(
            collective_id=0, has_side_effects=True, vmem_limit_bytes=VMEM_LIMIT
        ),
    )(*args.values())
    made = results(dict(zip(outs, parts)), entries)
    s_blocks = (steps, rows, width)
    return (
        made["y"].reshape(s_blocks),
        made["grad"].reshape(s_blocks),
        made["table"],
        made["gain"],
        made["shift"],
        made["s_qkv"].transpose(1, 0, 2),
        made["s_out"],
        made["t_qkv"].transpose(1, 0, 2),
        made["t_out"],
        made["bias"],
        made["up"],
        made["up_bias"].reshape(hidden),
        made["down"],
    )


def solution(mesh):
    return jax.shard_map(
        on_device,
        mesh=mesh,
        in_specs=(
            P("frames", None, None),
            P("frames"),
            P(),
            P(),
            P(),
            P(),
            P(None, None, "heads"),
            P("heads", None),
            P(None, None, "heads"),
            P("heads", None),
            P(),
            P(None, "heads"),
            P("heads"),
            P("heads", None),
            P("frames", None, None),
        ),
        out_specs=(
            P("frames", "heads", None),
            P("frames", "heads", None),
            P(),
            P(),
            P(),
            P(None, None, "heads"),
            P("heads", None),
            P(None, None, "heads"),
            P("heads", None),
            P(),
            P(None, "heads"),
            P("heads"),
            P("heads", None),
        ),
        check_vma=False,
    )
```

```python
import jax
import jax.numpy as jnp
import numpy as np
from jax import lax
from jax.experimental import pallas as pl
from jax.experimental.pallas import tpu as pltpu
from jax.sharding import PartitionSpec as P

HD = 64
SCALE = HD**-0.5
EPS = 1e-05
MASKED = -1000000000.0
F32 = jnp.float32
BF16 = jnp.bfloat16
MESH = pl.DeviceIdType.MESH
MLP_RESULTS = ("down_grad", "up_grad")
T_RESULTS = ("t_q", "t_k", "t_v", "t_out")
S_RESULTS = ("s_q", "s_k", "s_v", "s_out")
VMEM_LIMIT = 62 * 1024 * 1024
GELU_C = float(np.sqrt(2.0 / np.pi))
LAG = 2
SLOT_US, STEP_US, FRAME_US, MLP_US, ATTENTION_US, LAST_FRAME_US = 1.15, 1.45, 4.5, 6.4, 3.2, 3.6
CHUNK_US, WHOLE_US = 1.45, 100.0
ADJUST = {(1, 'hop', (0, 3)): -1.2, (4, 'owner', 0): 0.3}
LAST_GRADS = 3
LAST_SMALL = (5, 6, 9, 12)
HOP_US, SIBLING_US, COMPUTE_US, LINK_US, OWNER_US, SWAP_US = 3.4, 1.0, 2.0, 1.45, 1.0, 4.0


def mm(a, b):
    return lax.dot_general(a, b, (((1,), (0,)), ((), ())), preferred_element_type=F32)


def mm_nt(a, b):
    return lax.dot_general(a, b, (((1,), (1,)), ((), ())), preferred_element_type=F32)


def mm_tn(a, b):
    return lax.dot_general(a, b, (((0,), (0,)), ((), ())), preferred_element_type=F32)


def norm_stats(value):
    centered = value - jnp.mean(value, axis=-1, keepdims=True)
    inv = lax.rsqrt(jnp.mean(centered * centered, axis=-1, keepdims=True) + EPS)
    return centered * inv, inv


def norm_back(value, grad, gain):
    normed, inv = norm_stats(value)
    e = grad * gain
    first = jnp.mean(e, axis=-1, keepdims=True)
    second = jnp.mean(e * normed, axis=-1, keepdims=True)
    gain_grad = jnp.sum(grad * normed, axis=0, keepdims=True)
    shift_grad = jnp.sum(grad, axis=0, keepdims=True)
    return (e - first - normed * second) * inv, gain_grad, shift_grad


def head_lanes(shape, head):
    lane = lax.broadcasted_iota(jnp.int32, shape, 1)
    return (lane >= head * HD) & (lane < (head + 1) * HD)


def softmax_of(q, k, mask):
    scores = mm_nt(q, k) * SCALE
    if mask is not None:
        scores = jnp.where(mask, scores, MASKED)
    raised = jnp.exp(scores - jnp.max(scores, axis=-1, keepdims=True))
    return raised / jnp.sum(raised, axis=-1, keepdims=True)


def attend(q, k, v, mask):
    heads = q.shape[1] // HD
    mixed = None
    for head in range(heads):
        lanes = head_lanes(q.shape, head)
        probs = softmax_of(jnp.where(lanes, q, jnp.zeros_like(q)), k, mask).astype(BF16)
        out = mm(probs, v)
        mixed = out if mixed is None else jnp.where(lanes, out, mixed)
    return mixed.astype(BF16)


def attend_back(q, k, v, mask, grad):
    heads = q.shape[1] // HD
    dq = dk = dv = None
    for head in range(heads):
        lanes = head_lanes(q.shape, head)
        qh = jnp.where(lanes, q, jnp.zeros_like(q))
        gh = jnp.where(lanes, grad, jnp.zeros_like(grad))
        probs = softmax_of(qh, k, mask)
        dvh = mm_tn(probs.astype(BF16), gh)
        dp = mm_nt(gh, v)
        ds = (probs * (dp - jnp.sum(dp * probs, axis=-1, keepdims=True))).astype(BF16)
        dqh = mm(ds, k) * SCALE
        dkh = mm_tn(ds, qh) * SCALE
        if head == 0:
            dq, dk, dv = dqh, dkh, dvh
        else:
            dq = jnp.where(lanes, dqh, dq)
            dk = dk + dkh
            dv = dv + dvh
    return dq.astype(BF16), dk.astype(BF16), dv.astype(BF16)


class Line:
    def __init__(self, steps):
        self.frames = lax.axis_size("frames")
        self.heads = lax.axis_size("heads")
        self.chips = self.heads // 2
        self.f = lax.axis_index("frames")
        self.h = lax.axis_index("heads")
        self.z = self.h // 2
        self.c = self.h % 2
        self.steps = steps

    def at(self, z):
        return (self.f, jnp.clip(z, 0, self.chips - 1) * 2 + self.c)

    def sibling(self):
        return (self.f, self.z * 2 + 1 - self.c)

    def barrier(self, over_frames, whole_line=False):
        sem = pltpu.get_barrier_semaphore()

        def greet(device):
            pl.semaphore_signal(sem, inc=1, device_id=device, device_id_type=MESH)

        greet(self.sibling())
        count = 1
        if over_frames:
            for k in range(1, self.frames):
                greet(((self.f + k) % self.frames, self.h))
            count += self.frames - 1
        if whole_line:
            for k in range(1, self.chips):
                greet(self.at((self.z + k) % self.chips))
            count += self.chips - 1
        else:

            @pl.when(self.z > 0)
            def _():
                greet(self.at(self.z - 1))

            @pl.when(self.z < self.chips - 1)
            def _():
                greet(self.at(self.z + 1))

            count = count + (self.z > 0).astype(jnp.int32)
            count = count + (self.z < self.chips - 1).astype(jnp.int32)
        pl.semaphore_wait(sem, count)

    def copy(self, src, dst, send, recv, device):
        return pltpu.make_async_remote_copy(
            src_ref=src,
            dst_ref=dst,
            send_sem=send,
            recv_sem=recv,
            device_id=device,
            device_id_type=MESH,
        )


class Gather:
    def __init__(self, line, buf, sems):
        self.line, self.buf = line, buf
        self.got, self.got_sib, self.sent_up, self.sent_down, self.sent_sib = sems

    def up(self, s, zb):
        ln = self.line
        ref = self.buf.at[s, zb, ln.c]
        return ln.copy(ref, ref, self.sent_up.at[s, zb], self.got.at[s, zb], ln.at(ln.z + 1))

    def down(self, s, zb):
        ln = self.line
        ref = self.buf.at[s, zb, ln.c]
        return ln.copy(ref, ref, self.sent_down.at[s, zb], self.got.at[s, zb], ln.at(ln.z - 1))

    def across(self, s, zb):
        ln = self.line
        ref = self.buf.at[s, zb, ln.c]
        return ln.copy(ref, ref, self.sent_sib.at[s, zb], self.got_sib.at[s, zb], ln.sibling())

    def wait_across(self, s, zb):
        ln = self.line
        ref = self.buf.at[s, zb, 1 - ln.c]
        ln.copy(
            ref, ref, self.sent_sib.at[s, zb], self.got_sib.at[s, zb], ln.sibling()
        ).wait_recv()

    def send(self, s):
        ln = self.line

        @pl.when(ln.z < ln.chips - 1)
        def _():
            self.up(s, ln.z).start()

        @pl.when(ln.z > 0)
        def _():
            self.down(s, ln.z).start()

        self.across(s, ln.z).start()

    def start(self, own):
        ln = self.line
        for s in range(ln.steps):
            self.buf[s, ln.z, ln.c] = own[s]
            self.send(s)

    def arrive(self, distance, s):
        ln = self.line
        below, above = ln.z - distance, ln.z + distance

        @pl.when((distance > 0) & (below >= 0))
        def _():
            self.up(s, below).wait_recv()

            @pl.when(ln.z < ln.chips - 1)
            def _():
                self.up(s, below).start()

            self.across(s, below).start()

        @pl.when((distance > 0) & (above < ln.chips))
        def _():
            self.down(s, above).wait_recv()

            @pl.when(ln.z > 0)
            def _():
                self.down(s, above).start()

            self.across(s, above).start()

    def drain(self, s, zb):
        ln = self.line

        @pl.when((zb <= ln.z) & (ln.z < ln.chips - 1))
        def _():
            self.up(s, zb).wait_send()

        @pl.when((zb >= ln.z) & (ln.z > 0))
        def _():
            self.down(s, zb).wait_send()

        self.across(s, zb).wait_send()


class ChainSum:
    def __init__(self, line, bufs, sems):
        self.line = line
        self.part, self.sib, self.rise, self.fall, self.out = bufs
        self.sent_sib, self.got_sib, self.got_up, self.got_down, self.sent = sems

    def across(self, s, zb):
        ln = self.line
        return ln.copy(
            self.part.at[s, zb, 1 - ln.c],
            self.sib.at[s, zb],
            self.sent_sib.at[s, zb],
            self.got_sib.at[s, zb],
            ln.sibling(),
        )

    def up(self, s, o):
        ln = self.line
        return ln.copy(
            self.out.at[s, o],
            self.rise.at[s, o],
            self.sent.at[s, o],
            self.got_up.at[s, o],
            ln.at(ln.z + 1),
        )

    def down(self, s, o):
        ln = self.line
        return ln.copy(
            self.out.at[s, o],
            self.fall.at[s, o],
            self.sent.at[s, o],
            self.got_down.at[s, o],
            ln.at(ln.z - 1),
        )

    def mine(self, s, o):
        return self.part[s, o, self.line.c].astype(F32) + self.sib[s, o].astype(F32)

    def hop_up(self, s, o):
        ln = self.line
        self.across(s, o).wait_recv()

        @pl.when(ln.z == 0)
        def _():
            self.out[s, o] = self.mine(s, o).astype(BF16)

        @pl.when(ln.z > 0)
        def _():
            self.up(s, o).wait_recv()
            self.out[s, o] = (self.mine(s, o) + self.rise[s, o].astype(F32)).astype(BF16)

        self.up(s, o).start()

    def hop_down(self, s, o):
        ln = self.line
        self.across(s, o).wait_recv()

        @pl.when(ln.z == ln.chips - 1)
        def _():
            self.out[s, o] = self.mine(s, o).astype(BF16)

        @pl.when(ln.z < ln.chips - 1)
        def _():
            self.down(s, o).wait_recv()
            self.out[s, o] = (self.mine(s, o) + self.fall[s, o].astype(F32)).astype(BF16)

        self.down(s, o).start()

    def hops(self, t, part=None, fits=True):
        ln = self.line
        last = ln.chips - 1
        for upward in (True, False):
            place = ln.z if upward else last - ln.z
            q = t - place * LAG
            if part is None:
                turn = jnp.maximum(q, 0) // ln.steps
                s = jnp.maximum(q, 0) % ln.steps
            else:
                turn, s = jnp.maximum(q, 0), part
            far = jnp.clip(last - turn, 0, last)
            ok = (q >= 0) & (turn < last) & (far > place) & fits
            o = far if upward else last - far

            @pl.when(ok)
            def _():
                if upward:
                    self.hop_up(s, o)
                else:
                    self.hop_down(s, o)

    def finish(self, s, total):
        ln = self.line
        self.across(s, ln.z).wait_recv()
        total[...] = self.mine(s, ln.z)

        @pl.when(ln.z > 0)
        def _():
            self.up(s, ln.z).wait_recv()
            total[...] += self.rise[s, ln.z].astype(F32)

        @pl.when(ln.z < ln.chips - 1)
        def _():
            self.down(s, ln.z).wait_recv()
            total[...] += self.fall[s, ln.z].astype(F32)

    def drain(self, s, zb):
        ln = self.line
        self.across(s, zb).wait_send()

        @pl.when(zb != ln.z)
        def _():
            self.up(s, zb).wait_send()


def drain_all(line, things, parts):
    def body(i, carry):
        for thing in things:
            thing.drain(i // line.chips, i % line.chips)
        return carry

    lax.fori_loop(0, parts * line.chips, body, 0)


class Swap:
    def __init__(self, line, src_at, dst, sems):
        self.line, self.src_at, self.dst = line, src_at, dst
        self.sent, self.got = sems

    def copy(self, part, k):
        ln = self.line
        to = (ln.f + k) % ln.frames
        return ln.copy(
            self.src_at(part, to),
            self.dst.at[part, ln.f],
            self.sent.at[part, k],
            self.got.at[part, k],
            (to, ln.h),
        )

    def start(self, part):
        ln = self.line
        for k in range(1, ln.frames):
            self.copy(part, k).start()
        self.dst[part, ln.f] = self.src_at(part, ln.f)[...]

    def wait(self, part):
        for k in range(1, self.line.frames):
            self.copy(part, k).wait()


class FrameSum:
    def __init__(self, line, part, full, dim, reverse, recv_bufs, sems):
        self.line, self.part, self.full, self.dim = line, part, full, dim
        self.recv_bufs = recv_bufs
        self.sent, self.got, self.sent_back, self.got_back = sems
        bits = range(line.frames.bit_length() - 1)
        self.bits = list(reversed(bits)) if reverse else list(bits)
        self.spans = []
        start, size = 0, part.shape[dim]
        for bit in self.bits:
            size //= 2
            side = (line.f // (1 << bit)) % 2
            peer = (line.f + (1 - 2 * side) * (1 << bit), line.h)
            keep, give = start + side * size, start + (1 - side) * size
            self.spans.append((keep, give, size, peer))
            start = keep

    def view(self, ref, start, size, step):
        if self.dim == 0:
            return ref.at[pl.ds(pl.multiple_of(start, step), size)]
        return ref.at[:, pl.ds(pl.multiple_of(start, step), size)]

    def out(self, i, chunk=0, chunks=1):
        _, give, size, peer = self.spans[i]
        step = size // chunks
        src = self.view(self.part, give + chunk * step, step, step)
        dst = self.view(self.recv_bufs[i], chunk * step, step, step)
        return self.line.copy(src, dst, self.sent.at[i], self.got.at[i], peer)

    def back(self, i, chunk=0, chunks=1):
        keep, _, size, peer = self.spans[i]
        step = size // chunks
        ref = self.view(self.full, keep + chunk * step, step, step)
        return self.line.copy(ref, ref, self.sent_back.at[i], self.got_back.at[i], peer)

    def back_in(self, i):
        _, give, size, peer = self.spans[i]
        ref = self.view(self.full, give, size, size)
        return self.line.copy(ref, ref, self.sent_back.at[i], self.got_back.at[i], peer)

    def send(self, k, chunk=0, chunks=1):
        n = len(self.bits)
        if k < n:
            self.out(k, chunk, chunks).start()
        else:
            self.back(2 * n - 1 - k, chunk, chunks).start()

    def end(self, k):
        n = len(self.bits)
        if k < n:
            keep, _, size, _ = self.spans[k]
            self.out(k).wait()
            ref = self.view(self.part, keep, size, size)
            to = self.view(self.full, keep, size, size) if k == n - 1 else ref
            to[...] = (ref[...].astype(F32) + self.recv_bufs[k][...].astype(F32)).astype(BF16)
        else:
            i = 2 * n - 1 - k
            self.back(i).wait_send()
            self.back_in(i).wait_recv()


def frame_sum_scratch(frames, shape, dim, pieces):
    bits = frames.bit_length() - 1
    scratch = [pltpu.VMEM(shape, BF16)]
    for _ in range(pieces):
        for i in range(bits):
            part = list(shape)
            part[dim] = (shape[dim] // pieces) >> (i + 1)
            scratch.append(pltpu.VMEM(tuple(part), BF16))
        scratch += [pltpu.SemaphoreType.DMA((bits,))] * 4
    return scratch


def frame_sums(line, arrays, scratch):
    bits = line.frames.bit_length() - 1
    out = []
    for full, dim, reverse, pieces in arrays:
        part, scratch = scratch[0], scratch[1:]
        sums = []
        for i in range(pieces):
            mine, scratch = scratch[: bits + 4], scratch[bits + 4 :]
            size = full.shape[dim] // pieces
            at = (slice(None),) * dim + (pl.ds(i * size, size),)
            views = (part.at[at], full.at[at]) if pieces > 1 else (part, full)
            sums.append(FrameSum(line, *views, dim, reverse, mine[:bits], mine[bits:]))
        out.append((part, sums))
    return out


def stage_times(sums, begins, first, bits, free, latency, chunk_us):
    ready = list(begins)
    plan = []
    for k in range(2 * bits):
        for i, group in enumerate(sums):
            length = first / 2 ** (k if k < bits else 2 * bits - 1 - k)
            chunks = 1 << max(int(np.log2(length / chunk_us) + 0.5), 0)
            start = max(free, ready[i])
            for j in range(chunks):
                plan.append((start + j * length / chunks, len(plan), ("send", group, k, j, chunks)))
            free = start + length
            ready[i] = free + latency
            plan.append((ready[i], len(plan), ("end", group, k, 0, 0)))
    return plan, free


def run_step(step):
    what, group, k, chunk, chunks = step
    for one in group:
        if what == "send":
            one.send(k, chunk, chunks)
        else:
            one.end(k)


class Everyone:
    def __init__(self, line, refs, sems):
        self.line = line
        self.src, self.dst_sib, self.dst_line, self.dst_frames, self.full = refs
        self.sent, self.got = sems
        self.share = self.src.shape[1] // line.chips

    def cols(self, z):
        return pl.ds(pl.multiple_of(z * self.share, self.share), self.share)

    def pair_copy(self):
        ln = self.line
        return ln.copy(self.src, self.dst_sib, self.sent.at[0], self.got.at[0], ln.sibling())

    def line_copies(self):
        ln, copies = self.line, []
        for k in range(1, ln.chips):
            to = (ln.z + k) % ln.chips
            src, dst = self.dst_sib.at[:, self.cols(to)], self.dst_line.at[ln.z]
            copies.append(ln.copy(src, dst, self.sent.at[k], self.got.at[k], ln.at(to)))
        return copies

    def frame_copies(self):
        ln, copies = self.line, []
        for k in range(1, ln.frames):
            to, i = ((ln.f + k) % ln.frames, ln.h), ln.chips + k
            src, dst = self.dst_line.at[ln.z], self.dst_frames.at[ln.f]
            copies.append(ln.copy(src, dst, self.sent.at[i], self.got.at[i], to))
        return copies

    def back_copies(self):
        ln, copies = self.line, []
        for k in range(1, ln.chips):
            to, i = ln.at((ln.z + k) % ln.chips), ln.chips + ln.frames + k
            ref = self.full.at[:, self.cols(ln.z)]
            copies.append(ln.copy(ref, ref, self.sent.at[i], self.got.at[i], to))
        return copies

    def over_pair(self, value):
        self.src[...] = value.astype(BF16)
        self.pair_copy().start()

    def over_line(self):
        self.pair_copy().wait()
        pair = self.src[...].astype(F32) + self.dst_sib[...].astype(F32)
        self.dst_sib[...] = pair.astype(BF16)
        for copy in self.line_copies():
            copy.start()

    def over_frames(self):
        ln = self.line
        for copy in self.line_copies():
            copy.wait()
        total = self.dst_sib[:, self.cols(ln.z)].astype(F32)
        for k in range(1, ln.chips):
            total = total + self.dst_line[(ln.z + k) % ln.chips].astype(F32)
        self.dst_line[ln.z] = total.astype(BF16)
        for copy in self.frame_copies():
            copy.start()
        self.dst_frames[ln.f] = self.dst_line[ln.z]

    def over_back(self):
        for copy in self.frame_copies():
            copy.wait()
        total = self.dst_frames[0].astype(F32)
        for i in range(1, self.line.frames):
            total = total + self.dst_frames[i].astype(F32)
        self.full[:, self.cols(self.line.z)] = total.astype(BF16)
        for copy in self.back_copies():
            copy.start()

    def result(self):
        for copy in self.back_copies():
            copy.wait()
        return self.full[...].astype(F32)


class Timetable:
    PHASES = 5

    def __init__(self, chips, streams):
        self.chips, self.streams = chips, streams
        last = chips - 1
        arrivals = [(d * HOP_US, "arrive", d) for d in range(chips)]
        gathered = last * HOP_US + SIBLING_US
        first = self.sum_steps(0.0)
        middle = self.sum_steps(gathered)
        self.turn = max((middle[-1][0] + OWNER_US) / streams, chips * LINK_US)
        period = self.turn * streams
        second = max(HOP_US, SIBLING_US + COMPUTE_US + SIBLING_US)
        y = self.sum_steps(second - COMPUTE_US - SIBLING_US)
        leads = [0.0, first[-1][0] + OWNER_US + SWAP_US - period]
        leads.append(leads[1] + max(middle[-1][0] + OWNER_US + SWAP_US - period, 0.0))
        groups = (
            (0, 0, leads[0], first),
            (1, 3, leads[1], arrivals + middle),
            (4, 4, leads[2], arrivals + [(gathered, "gathered", 0)] + y),
        )
        self.every = 6
        self.order = []
        for i in range(self.every):
            at = (i + 0.5) * self.turn / self.every
            self.order.append((at, 0.0, "beside", i, 0, 0, 0))
        self.computed = {}
        self.turns = 0
        for low, high, lead, steps in groups:
            for t, what, which in steps:
                t += lead + ADJUST.get((low, what, which), 0.0)
                behind = int(np.floor(t / self.turn))
                at = t - behind * self.turn
                self.order.append((at, -t, what, which, behind, low, high))
                if what == ("gathered" if low == 4 else "compute"):
                    self.computed |= {phase: behind for phase in range(low, high + 1)}
                self.turns = max(self.turns, (high + 1) * streams + behind)
        self.order.sort(key=lambda step: step[:2])

    def sum_steps(self, compute):
        last = self.chips - 1
        steps = [(compute, "compute", 0)]
        start = compute + COMPUTE_US + SIBLING_US
        hops = {}
        for place in range(last):
            t = start
            for far in range(last, place, -1):
                if place:
                    t = max(t, hops[place - 1, far] + HOP_US)
                hops[place, far] = t
                steps.append((t, "hop", (place, far)))
                t += LINK_US
        owner = max(hops[far - 1, far] for far in range(1, self.chips)) + HOP_US
        return steps + [(owner, "owner", 0)]

    def y_owner(self, item):
        t = [t for t in self.order if t[2] == "owner" and t[5] == 4][0]
        return (item + t[4]) * self.every + int(t[0] / self.turn * self.every + 0.5)

    def after(self, item):
        return item + self.computed[item // self.streams] + 1


def pipeline(line, times, turns, gather, sums, enter, compute, gathered, owner, total, beside):
    last, streams = line.chips - 1, times.streams

    def body(m, carry):
        for _, _, what, which, behind, low, high in times.order:
            if what == "beside":
                beside(m, which)
                continue
            n = m - behind
            fits = (n >= low * streams) & (n < (high + 1) * streams)
            n = jnp.clip(n, low * streams, (high + 1) * streams - 1)
            s = n % streams
            held = n - streams
            if what == "hop":
                place, far = which

                @pl.when(fits & (line.z == place))
                def _():
                    sums.hop_up(s, far)

                @pl.when(fits & (line.z == last - place))
                def _():
                    sums.hop_down(s, last - far)

                continue

            @pl.when(fits)
            def _():
                if what == "arrive":
                    if which == 0:
                        enter(n)
                        gather.send(held)
                    else:
                        gather.arrive(which, held)
                elif what == "compute":
                    if low == 4:
                        gather.wait_across(held, line.z)
                    for zb in range(line.chips):
                        if 1 <= low <= 3:
                            gather.wait_across(held, zb)
                        if low:
                            sums.drain(s, zb)
                    compute(n, low, high)
                    for zb in range(line.chips):
                        sums.across(s, zb).start()
                elif what == "gathered":
                    for zb in range(line.chips):

                        @pl.when(line.z != zb)
                        def _():
                            gather.wait_across(held, zb)

                    gathered(n)
                else:
                    sums.finish(s, total)
                    owner(n, low, high)

        return carry

    lax.fori_loop(0, turns, body, 0)


def frame_mask(segments, places, rows):
    frames = segments.shape[0]
    bits, place_bits = frames.bit_length() - 1, places.bit_length() - 1

    def ids_along(axis, shape):
        index = lax.broadcasted_iota(jnp.int32, shape, axis)
        frame = lax.shift_right_logical(index, place_bits) & (frames - 1)
        segment = jnp.zeros(shape, jnp.int32)
        for i in range(frames):
            segment = jnp.where(frame == i, segments[i], segment)
        block = lax.shift_right_logical(index, place_bits + bits)
        return block * places + (index & (places - 1)), frame, segment

    place_q, frame_q, segment_q = ids_along(0, (rows, 1))
    place_k, frame_k, segment_k = ids_along(1, (1, rows))
    return (place_q == place_k) & (frame_k <= frame_q) & (segment_q == segment_k)


def column_grads(start, left, right, out):
    rows = pl.ds(pl.multiple_of(start, 256), 256)
    out[rows] = mm_tn(left, right.reshape(left.shape[0], right.shape[-1])).astype(BF16)


def row_sum(value):
    return jnp.sum(value, axis=0, keepdims=True)


def moved_exactly(order, value):
    out = None
    for _ in range(3):
        term = value.astype(BF16)
        value = value - term.astype(F32)
        out = mm(order, term) if out is None else out + mm(order, term)
    return out


class Refs:
    def __init__(self, names, refs):
        for name, ref in zip(names, refs, strict=True):
            setattr(self, name, ref)


def block(fetched, results, names, *refs):
    ends = len(fetched), len(fetched) + len(results)
    r = Refs(names, refs[ends[1] :])
    r.fetched = dict(zip(fetched, refs))
    r.stored = dict(zip(results, refs[ends[0] :]))
    r.ids, r.segments = r.fetched.pop("ids"), r.fetched.pop("segments")
    steps, patches, width = r.x.shape
    streams, rows, _ = r.y.shape
    heads = 2 * r.g_all.shape[1]
    line, t_line = Line(steps), Line(streams)
    chips, frames = line.chips, line.frames
    s_rows = patches // heads
    tokens = steps * s_rows
    columns, hidden = r.s_wout.shape[0], r.up.shape[1]
    entries = r.table.shape[0]
    count = heads * rows
    all_tokens = heads * tokens
    times = Timetable(chips, streams)
    sums = ChainSum(t_line, (r.part, r.sib, r.rise, r.fall, r.out), r.sum_sems)
    gather = Gather(t_line, r.gathered, r.gather_sems)
    last_part = getattr(r, "last_part", r.g_all)
    last_out = getattr(r, "last_out", r.out)
    last_total = getattr(r, "last_total", r.grad2)
    last_sums = ChainSum(
        line, (last_part, r.last_sib, r.last_rise, r.last_fall, last_out), r.last_sems
    )
    shared = not hasattr(r, "g_src")

    def g_src_at(part, to):
        return r.gathered.at[3 * streams + to, part] if shared else r.g_src.at[0, to, part]

    g_swap = Swap(line, g_src_at, r.g_dst, r.g_sems)
    state_swap = Swap(line, lambda s, to: r.state_src.at[s, to], r.state_dst, r.state_sems)
    grad_swap = Swap(line, lambda s, to: r.grad_src.at[s, to], r.grad_dst, r.grad_sems)
    y_swap = Swap(line, lambda s, to: r.y_src.at[s, to], r.y_dst, r.y_sems)
    every = Everyone(
        line,
        (r.every_src, r.every_sib, r.every_line, r.every_frames, r.every_full),
        r.every_sems,
    )
    (
        (down_part, down_sums), (up_part, up_sums),
        (t_q_part, t_q_sums), (t_k_part, t_k_sums), (t_v_part, t_v_sums), (t_out_part, t_out_sums),
        (s_q_part, s_q_sums), (s_k_part, s_k_sums), (s_v_part, s_v_sums), (s_out_part, s_out_sums),
    ) = frame_sums(
        line,
        [
            (r.down_grad, 0, False, 2), (r.up_grad, 0, True, 2),
            (r.t_q, 0, False, 1), (r.t_k, 0, True, 1), (r.t_v, 0, False, 1), (r.t_out, 1, True, 1),
            (r.s_q, 0, False, 1), (r.s_k, 0, True, 1), (r.s_v, 0, False, 1), (r.s_out, 1, True, 1),
        ],
        r.reduce,
    )
    t_parts = t_q_part, t_k_part, t_v_part
    s_parts = s_q_part, s_k_part, s_v_part
    mlp_sums = list(zip(down_sums, up_sums))
    t_sums = [t_q_sums + t_k_sums, t_v_sums + t_out_sums]
    s_sums = [s_q_sums + s_k_sums, s_v_sums]
    bits = len(down_sums[0].bits)
    bias_swap = Swap(line, lambda _, to: r.bias_src, r.bias_dst, r.bias_sems)
    fetches = [
        pltpu.make_async_copy(r.fetched[name], getattr(r, name), r.fetch_sems.at[i])
        for i, name in enumerate(r.fetched)
    ]
    for fetch in fetches:
        fetch.start()
    line.barrier(True, True)
    for fetch in fetches:
        fetch.wait()
    stored = []

    def store(name):
        i = list(r.stored).index(name)
        stored.append(
            pltpu.make_async_copy(getattr(r, name), r.stored[name], r.store_sems.at[i])
        )
        stored[-1].start()

    def g_out(i, carry):
        rows_of = pl.ds(pl.multiple_of(i * s_rows, s_rows), s_rows)
        moved = mm(r.to_peers[...], r.cotangent[:, rows_of].reshape(tokens, width))
        moved = moved.astype(BF16).astype(r.g_dst.dtype).reshape(frames, tokens // frames, width)
        if shared:
            r.gathered[3 * streams : 4 * streams, i // 2, i % 2] = moved
        else:
            r.g_src[0, :, i // 2, i % 2] = moved
        return carry

    lax.fori_loop(0, heads, g_out, 0)
    for part in range(chips - 2):
        g_swap.start(part)

    def g_in(i):
        moved = r.g_dst[i // 2, :, i % 2].reshape(tokens, width).astype(BF16)
        moved = mm(r.to_parts[...], moved).astype(BF16)
        r.g_all[:, i // 2, i % 2] = moved.reshape(streams, rows, width)

    table_row = lax.broadcasted_iota(jnp.int32, (entries, width), 0)

    def added(s):
        return row_sum(jnp.where(table_row == r.ids[s], r.table[...].astype(F32), 0.0))

    def norm(value, i):
        scaled = norm_stats(value)[0] * r.gain[i : i + 1, :]
        return (scaled + r.shift[i : i + 1, :]).astype(BF16)

    def attention(s, carry):
        normed = norm(r.x[s].astype(F32) + added(s), 0)
        r.normed0[s] = normed
        q = mm(normed, r.s_wqkv[0]).astype(BF16)
        k = mm(normed, r.s_wqkv[1]).astype(BF16)
        v = mm(normed, r.s_wqkv[2]).astype(BF16)
        r.s_proj[0, s] = q
        r.s_proj[1, s] = k
        r.s_proj[2, s] = v
        r.s_cols[s] = attend(q, k, v, None)
        return carry

    lax.fori_loop(0, steps, attention, 0)

    def to_streams(i, carry):
        rows_of = pl.ds(pl.multiple_of(i * s_rows, s_rows), s_rows)
        moved = mm(r.to_streams[...], r.s_cols[:, rows_of].reshape(tokens, columns)).astype(BF16)
        r.s_mixed[:, i] = moved.reshape(streams, rows, columns)
        return carry

    lax.fori_loop(0, heads, to_streams, 0)
    own_rows = pl.ds(pl.multiple_of(line.h * s_rows, s_rows), s_rows)
    own = mm(r.to_streams[...], r.x[:, own_rows].reshape(tokens, width))
    row = lax.broadcasted_iota(jnp.int32, (tokens, 1), 0)
    frame = lax.shift_right_logical(row, (rows // (frames * steps)).bit_length() - 1) & (steps - 1)
    entry = jnp.zeros_like(row)
    for s in range(steps):
        entry = jnp.where(frame == s, r.ids[s], entry)
    picker = (entry == lax.broadcasted_iota(jnp.int32, (tokens, entries), 1)).astype(BF16)
    own = own + mm(picker, r.table[...])
    r.state0[...] = own.reshape(streams, rows, width)
    r.mask[...] = frame_mask(r.segments, rows // (frames * steps), count).astype(F32)
    r.up_bias_grad[...] = jnp.zeros_like(r.up_bias_grad)
    r.small[...] = jnp.zeros_like(r.small)

    def held(n):
        return n - streams

    def enter_temporal(s, n):
        state_swap.wait(s)
        state = r.state_dst[s].reshape(rows, width)
        r.state1[s] = state
        r.gathered[held(n), line.z, line.c] = norm(state, 1)

    def enter_spatial(s, n):
        grad_swap.wait(s)
        grad = r.grad_dst[s].reshape(rows, width)
        r.grad1[s] = grad
        r.gathered[held(n), line.z, line.c] = grad.astype(BF16)

    def compute_spatial(s, n):
        left = r.s_mixed[s].reshape(count, columns)
        r.part[s] = mm(left, r.s_wout[...]).astype(BF16).reshape(chips, 2, rows, width)

    def compute_temporal(s, n):
        a = r.gathered[held(n)].reshape(count, width)
        q = mm(a, r.t_wqkv[0]).astype(BF16)
        k = mm(a, r.t_wqkv[1]).astype(BF16)
        v = mm(a, r.t_wqkv[2]).astype(BF16)
        r.t_proj[0, s] = q
        r.t_proj[1, s] = k
        r.t_proj[2, s] = v
        mixed = attend(q, k, v, r.mask[...] > 0.0)
        r.t_mixed[s] = mixed
        r.part[s] = mm(mixed, r.t_wout[...]).astype(BF16).reshape(chips, 2, rows, width)

    def compute_mlp(s, n):
        a = r.gathered[held(n)].reshape(count, width)
        g = r.g_all[s].reshape(count, width)
        pre = mm(a, r.up[...]) + r.up_bias[...]
        t = jnp.tanh(GELU_C * (pre + 0.044715 * (pre * pre * pre)))
        act = (0.5 * pre * (1.0 + t)).astype(BF16)
        r.act[s] = act
        slope = 0.5 * (1.0 + t)
        slope = slope + 0.5 * pre * (1.0 - t * t) * (GELU_C * (1.0 + 0.134145 * (pre * pre)))
        dpre = (mm_nt(g, r.down[...]) * slope).astype(BF16)
        r.dpre[s] = dpre
        r.up_bias_grad[:, :hidden] += row_sum(dpre.astype(F32))
        r.part[s] = mm_nt(dpre, r.up[...]).astype(BF16).reshape(chips, 2, rows, width)

    def compute_back(s, n):
        grad = r.gathered[held(n)].reshape(count, width)
        dm = mm_nt(grad, r.t_wout[...]).astype(BF16)
        mask = r.mask[...] > 0.0
        dq, dk, dv = attend_back(r.t_proj[0, s], r.t_proj[1, s], r.t_proj[2, s], mask, dm)
        r.t_dproj[0, s] = dq
        r.t_dproj[1, s] = dk
        r.t_dproj[2, s] = dv
        da = mm_nt(dq, r.t_wqkv[0]) + mm_nt(dk, r.t_wqkv[1]) + mm_nt(dv, r.t_wqkv[2])
        r.part[s] = da.astype(BF16).reshape(chips, 2, rows, width)

    def gathered_last(n):
        grad = r.gathered[held(n)].reshape(count, width)
        moved = mm_nt(grad, r.s_wout[...]).astype(BF16)
        r.s_dmixed[n % streams] = moved.reshape(heads, rows, columns)

    def compute_last(s, n):
        y = mm(r.act[s], r.down[...])
        r.part[s] = y.astype(BF16).reshape(chips, 2, rows, width)

    def owner_spatial(s, n):
        state = r.state0[s] + r.total[...] + r.bias[0:1, :]
        r.state_src[s] = state.reshape(r.state_src.shape[1:])
        state_swap.start(s)

        for part, after in ((chips - 2, streams // 2 - 1), (chips - 1, streams - 1)):

            @pl.when(s == after)
            def _():
                g_swap.start(part)

    def owner_temporal(s, n):
        state = r.state1[s] + r.total[...] + r.bias[1:2, :]
        r.state2[s] = state
        r.gathered[n, line.z, line.c] = norm(state, 2)

    def owner_mlp(s, n):
        grad = r.g_all[s, line.z, line.c].astype(F32)
        back, gain_grad, shift_grad = norm_back(r.state2[s], r.total[...], r.gain[2:3, :])
        dh = grad + back
        r.grad2[s] = dh
        r.gathered[n, line.z, line.c] = dh.astype(BF16)
        r.small[0:1] += gain_grad
        r.small[1:2] += shift_grad
        r.small[2:3] += row_sum(grad)
        r.small[3:4] += row_sum(dh)

    def owner_back(s, n):
        back, gain_grad, shift_grad = norm_back(r.state1[s], r.total[...], r.gain[1:2, :])
        dh = r.grad2[s] + back
        r.grad_src[s] = dh.reshape(r.grad_src.shape[1:])
        grad_swap.start(s)
        r.small[4:5] += gain_grad
        r.small[5:6] += shift_grad
        r.small[6:7] += row_sum(dh)

    def owner_last(s, n):
        r.y[s] = (r.state2[s] + r.total[...] + r.bias[2:3, :]).astype(BF16)

    def by_phase(bodies):
        def run(n, low=0, high=4):
            for i, one in enumerate(bodies):
                if one is not None and low <= i <= high:

                    @pl.when(n // streams == i)
                    def _():
                        one(n % streams, n)

        return run

    def down_chunk(i):
        cols = pl.ds(pl.multiple_of(i * 128, 128), 128)
        left = r.act[:, :, cols].reshape(all_tokens, 128)
        right = r.g_all[...].reshape(all_tokens, width)
        down_part[cols] = mm_tn(left, right).astype(BF16)

    def up_chunk(i):
        cols = pl.ds(pl.multiple_of(i * 256, 256), 256)
        left = r.gathered[streams : 2 * streams, :, :, :, cols].reshape(all_tokens, 256)
        right = r.dpre[...].reshape(all_tokens, hidden)
        up_part[cols] = mm_tn(left, right).astype(BF16)

    def t_out_chunk(i):
        left = r.t_mixed[...].reshape(all_tokens, columns)
        right = r.gathered[2 * streams : 3 * streams].reshape(all_tokens, width)
        t_out_part[...] = mm_tn(left, right).astype(BF16)

    def t_qkv_chunk(i):
        start = i * 256
        cols = pl.ds(pl.multiple_of(start, 256), 256)
        left = r.gathered[0:streams, :, :, :, cols].reshape(all_tokens, 256)
        for j in range(3):
            column_grads(start, left, r.t_dproj[j], t_parts[j])

    def s_cols_chunk(_):
        def from_streams(i, carry):
            rows_of = pl.ds(pl.multiple_of(i * s_rows, s_rows), s_rows)
            moved = mm(r.from_streams[...], r.s_dmixed[:, i].reshape(tokens, columns)).astype(BF16)
            r.s_cols[:, rows_of] = moved.reshape(steps, s_rows, columns)
            return carry

        lax.fori_loop(0, heads, from_streams, 0)

    def s_back_chunk(s):
        dq, dk, dv = attend_back(r.s_proj[0, s], r.s_proj[1, s], r.s_proj[2, s], None, r.s_cols[s])
        r.s_dproj[0, s] = dq
        r.s_dproj[1, s] = dk
        r.s_dproj[2, s] = dv
        da = mm_nt(dq, r.s_wqkv[0]) + mm_nt(dk, r.s_wqkv[1]) + mm_nt(dv, r.s_wqkv[2])
        last_part[s] = da.astype(BF16).reshape(last_part.shape[1:])
        for zb in range(chips):
            last_sums.across(s, zb).start()
        if early:

            @pl.when(s == 1)
            def _():
                drain_all(t_line, (sums,), streams)

            @pl.when(s > 0)
            def _():
                last_sums.hops(s - 1)

    def s_out_chunk(_):
        left = r.s_mixed[...].reshape(all_tokens, columns)
        right = r.gathered[3 * streams : 4 * streams].reshape(all_tokens, width)
        s_out_part[...] = mm_tn(left, right).astype(BF16)
        s_out_sums[0].send(0)

    def bias_chunk(_):
        r.bias_src[...] = jnp.broadcast_to(r.up_bias_grad[...], r.bias_src.shape)
        bias_swap.start(0)

    def g_in_chunk(i):
        @pl.when(i % 2 == 0)
        def _():
            g_swap.wait(i // 2)

        g_in(i)

    n_down, n_up = hidden // 128, width // 256
    turn_of = times.after
    slots = [i for i in range(times.every) if i % 2 == 1][:3]
    per_slot = 3
    per_turn = per_slot * len(slots)
    mlp_turn, back_turn = turn_of(3 * streams - 1), turn_of(4 * streams - 1)
    last_turn = turn_of(5 * streams - 1)
    chunks = (
        (2 * streams - 1 - heads // per_turn, 0, heads, g_in_chunk),
        (mlp_turn, 0, n_down, down_chunk),
        (mlp_turn, n_down, n_up, up_chunk),
        (mlp_turn, n_down + n_up, 1, bias_chunk),
        (back_turn, 0, 1, t_out_chunk),
        (back_turn, 1, width // 256, t_qkv_chunk),
        (last_turn, 0, 1, s_out_chunk),
        (last_turn, 1, 1, s_cols_chunk),
        (last_turn, 2, steps, s_back_chunk),
    )
    turns = max(times.turns, last_turn + -(-(steps + 2) // per_turn))
    early = times.y_owner(5 * streams - 1) < last_turn * times.every + slots[1]

    def begin_of(turn, number):
        return (turn + number // per_turn) * times.every + times.every - 1

    begin = begin_of(mlp_turn, n_down + n_up) * SLOT_US
    plan, free = stage_times(mlp_sums, [begin] * 2, MLP_US, bits, 0.0, FRAME_US, CHUNK_US)
    begin = begin_of(back_turn, 1 + width // 256) * SLOT_US
    plan += stage_times(t_sums, [begin] * 2, ATTENTION_US, bits, free, FRAME_US, WHOLE_US)[0]
    plan = [(t, i, step) for i, (t, _, step) in enumerate(plan)]
    plan.sort(key=lambda entry: entry[:2])
    end = turns * times.every * SLOT_US
    late = [entry for entry in plan if entry[0] >= end]

    def beside(m, i):
        if i in slots:
            for turn, first, number, chunk in chunks:
                which = per_turn * (m - turn) + per_slot * slots.index(i) - first
                here = jnp.clip(number - which, 0, per_slot)

                @pl.when((which > -per_slot) & (which < number))
                def _():
                    def one(j, carry):
                        @pl.when(which + j >= 0)
                        def _():
                            chunk(which + j)

                        return carry

                    lax.fori_loop(0, here, one, 0)

        for t, _, step in plan:
            moment = int(t / SLOT_US)
            if t < end and moment % times.every == i:

                @pl.when(m == moment // times.every)
                def _():
                    run_step(step)

    enter = by_phase((None, enter_temporal, None, None, enter_spatial))
    compute = by_phase(
        (compute_spatial, compute_temporal, compute_mlp, compute_back, compute_last)
    )
    owner = by_phase((owner_spatial, owner_temporal, owner_mlp, owner_back, owner_last))
    pipeline(
        t_line, times, turns, gather, sums, enter, compute, gathered_last, owner, r.total, beside
    )
    if not early:
        drain_all(t_line, (sums,), streams)

    y = mm(r.from_parts[...], r.y[...].reshape(tokens, width)).astype(BF16)
    r.y_src[0] = y.astype(r.y_src.dtype).reshape(r.y_src.shape[1:])
    y_swap.start(0)

    r.sums0[...] = jnp.zeros_like(r.sums0)

    def small_part(s):
        state = r.x[s].astype(F32) + added(s)
        da = last_part[s].reshape(patches, width).astype(F32)
        back, gain_grad, shift_grad = norm_back(state, da, r.gain[0:1, :])
        r.sums0[0:1] += gain_grad
        r.sums0[1:2] += shift_grad
        r.sums0[8 : 8 + entries] += jnp.where(table_row == r.ids[s], row_sum(back), 0.0)

    room = r.every_src.shape[0]
    filled = 9 + entries

    def small_value(own_grad):
        for s in range(steps):
            here = row_sum(own_grad[s * s_rows : (s + 1) * s_rows])
            r.sums0[8 : 8 + entries] += jnp.where(table_row == r.ids[s], here, 0.0)
        rows_of = [
            r.sums0[0:1], r.small[4:5], r.small[0:1],
            r.sums0[1:2], r.small[5:6], r.small[1:2],
            r.small[6:7], r.small[3:4], r.small[2:3],
            r.sums0[8 : 8 + entries], jnp.zeros((room - filled, width), F32),
        ]
        return jnp.concatenate(rows_of, axis=0)

    first = steps - 1 if early else 0
    begin = LAST_GRADS * STEP_US + 2.5
    last_plan = [(max(int((t - end) / STEP_US), 0) + first + 1, i, step) for t, i, step in late]
    begins = [begin] * len(s_sums) + [begin - 4.0]
    s_plan, _ = stage_times(
        s_sums + [s_out_sums], begins, ATTENTION_US, bits, 0.0, LAST_FRAME_US, WHOLE_US
    )
    last_plan += [
        (int(np.ceil(t / STEP_US)), len(plan) + i, step)
        for t, i, step in s_plan
        if step[0] == "end" or step[2] > 0
    ]
    last_plan.sort(key=lambda entry: entry[:2])
    bound = steps * (chips - 1) + (chips - 2) * LAG + 1
    bound = max(bound, LAST_SMALL[-1] + 1)

    def body(t, carry):
        last_sums.hops(t)

        @pl.when(t == LAST_GRADS)
        def _():
            for j in range(3):
                for i in range(width // 256):
                    left = r.normed0[:, :, i * 256 : (i + 1) * 256].reshape(all_tokens, 256)
                    column_grads(i * 256, left, r.s_dproj[j], s_parts[j])
            for one in s_q_sums + s_k_sums + s_v_sums:
                one.send(0)

        @pl.when((t > LAST_GRADS) & (t <= LAST_GRADS + steps // 2))
        def _():
            def one(i, carry):
                small_part((t - LAST_GRADS - 1) * 2 + i)
                return carry

            lax.fori_loop(0, 2, one, 0)

        @pl.when(t == LAST_SMALL[0])
        def _():
            grad = r.grad1[...].reshape(tokens, width)
            own_grad = moved_exactly(r.from_streams[...], grad)
            r.state0[...] = own_grad.reshape(r.state0.shape)
            every.over_pair(small_value(own_grad))

        steps_of = (every.over_line, every.over_frames, every.over_back)
        for moment, step in zip(LAST_SMALL[1:], steps_of):

            @pl.when(t == moment)
            def _():
                step()

        for moment, _, step in last_plan:
            if moment < bound:

                @pl.when(t == max(moment, first))
                def _():
                    run_step(step)

        return carry

    lax.fori_loop(first, bound, body, 0)
    for s in range(steps):
        last_sums.finish(s, last_total.at[s])
    own_grad = r.state0[...].reshape(tokens, width)
    for s in range(steps):
        state = r.x[s, own_rows].astype(F32) + added(s)
        back, _, _ = norm_back(state, last_total[s], r.gain[0:1, :])
        r.grad_res[pl.ds(s * s_rows, s_rows)] = own_grad[s * s_rows : (s + 1) * s_rows] + back
    y_swap.wait(0)
    r.y_res[...] = mm(r.from_peers[...], r.y_dst[0].reshape(tokens, width).astype(BF16)).astype(BF16)
    r.small_res[...] = every.result()
    bias_swap.wait(0)
    up_bias = r.bias_dst[0, 0]
    for i in range(1, frames):
        up_bias = up_bias + r.bias_dst[0, i]
    r.up_bias_res[...] = up_bias
    for name in ("grad_res", "y_res", "small_res", "up_bias_res") + MLP_RESULTS:
        store(name)
    for moment, _, step in last_plan:
        if moment >= bound:
            run_step(step)
    for name in T_RESULTS + S_RESULTS:
        store(name)
    drain_all(line, (last_sums,), steps)
    drain_all(t_line, (gather,), 4 * streams)
    for one in stored:
        one.wait()


def finish(names, parts, *refs):
    sources = dict(zip(names, refs))
    results = dict(zip(parts, refs[len(names) :]))
    held = refs[len(names) + len(parts) :]
    sems_in, sems_out = held[-2:]
    local = dict(zip(names, held))
    made = dict(zip(parts, held[len(names) :]))
    loads = {
        name: pltpu.make_async_copy(sources[name], local[name], sems_in.at[i])
        for i, name in enumerate(names)
    }
    for load in loads.values():
        load.start()
    loaded, stores = set(), []
    for i, (name, given) in enumerate(parts.items()):
        for j, (source, low, high, columns) in enumerate(given):
            if source not in loaded:
                loads[source].wait()
                loaded.add(source)
            value = local[source][low:high, :columns].astype(made[name].dtype)
            if len(given) > 1:
                made[name][j] = value
            else:
                made[name][...] = value
        stores.append(pltpu.make_async_copy(made[name], results[name], sems_out.at[i]))
        stores[-1].start()
    for store in stores:
        store.wait()


def results(found, entries):
    width, hidden = found["up_grad"].shape

    def whole(name):
        rows, columns = found[name].shape
        return [(name, 0, rows, columns)]

    parts = {
        "t_out": whole("t_out"),
        "t_qkv": whole("t_q") + whole("t_k") + whole("t_v"),
        "down": whole("down_grad"),
        "up": whole("up_grad"),
        "grad": whole("grad_res"),
        "y": whole("y_res"),
        "gain": [("small_res", 0, 3, width)],
        "shift": [("small_res", 3, 6, width)],
        "bias": [("small_res", 6, 9, width)],
        "table": [("small_res", 9, 9 + entries, width)],
        "up_bias": [("up_bias_res", 0, 1, hidden)],
        "s_out": whole("s_out"),
        "s_qkv": whole("s_q") + whole("s_k") + whole("s_v"),
    }
    shapes = []
    for name, given in parts.items():
        _, low, high, columns = given[0]
        lead = (len(given),) if len(given) > 1 else ()
        kind = BF16 if name == "y" else F32
        shapes.append(jax.ShapeDtypeStruct(lead + (high - low, columns), kind))
    order = [name for given in parts.values() for name, _, _, _ in given]
    found = {name: found[name] for name in dict.fromkeys(order)}
    names = tuple(found)
    made = pl.pallas_call(
        lambda *refs: finish(names, parts, *refs),
        name="finish",
        out_shape=shapes,
        in_specs=[pl.BlockSpec(memory_space=pltpu.HBM)] * len(names),
        out_specs=[pl.BlockSpec(memory_space=pltpu.HBM)] * len(shapes),
        scratch_shapes=[pltpu.VMEM(v.shape, v.dtype) for v in found.values()]
        + [pltpu.VMEM(v.shape, v.dtype) for v in shapes]
        + [pltpu.SemaphoreType.DMA((len(names),)), pltpu.SemaphoreType.DMA((len(shapes),))],
        compiler_params=pltpu.CompilerParams(vmem_limit_bytes=VMEM_LIMIT),
    )(*found.values())
    return dict(zip(parts, made))


def orders(frames_local, frames, places, streams):
    tokens = frames_local * frames * places
    index = np.arange(tokens).reshape(frames_local, frames, streams, places // streams)
    to_streams = index.transpose(2, 1, 0, 3).reshape(-1)
    to_peers = index.transpose(1, 0, 2, 3).reshape(-1)
    index = np.arange(tokens).reshape(frames * frames_local, streams, places // streams)
    to_parts = index.transpose(1, 0, 2).reshape(-1)
    eye = np.eye(tokens, dtype=np.float32)
    there = [eye[order] for order in (to_streams, to_peers, to_parts)]
    back = [m.T for m in there]
    names = ("to_streams", "to_peers", "to_parts", "from_streams", "from_peers", "from_parts")
    return {name: jnp.asarray(m, BF16) for name, m in zip(names, there + back)}


def on_device(
    block_input,
    action_ids,
    segment_ids,
    action_table,
    norm_gain,
    norm_shift,
    spatial_qkv,
    spatial_out,
    temporal_qkv,
    temporal_out,
    out_bias,
    up_weight,
    up_bias,
    down_weight,
    cotangent,
):
    frames, heads = lax.axis_size("frames"), lax.axis_size("heads")
    chips = heads // 2
    steps, patches, width = block_input.shape
    rows = patches // heads
    tokens = steps * rows
    total_frames = segment_ids.shape[0]
    places = rows // frames
    streams = min(4, places)
    t_rows = tokens // streams
    columns = spatial_out.shape[0]
    hidden = up_weight.shape[1]
    entries = action_table.shape[0]
    count = heads * t_rows
    room = -(-(10 + entries) // 16) * 16
    args = dict(
        ids=action_ids,
        segments=segment_ids,
        x=block_input,
        cotangent=cotangent,
        table=action_table,
        gain=norm_gain,
        shift=norm_shift,
        bias=out_bias,
        s_wqkv=spatial_qkv.transpose(1, 0, 2),
        s_wout=spatial_out,
        t_wqkv=temporal_qkv.transpose(1, 0, 2),
        t_wout=temporal_out,
        up=up_weight,
        up_bias=up_bias.reshape(1, hidden),
        down=down_weight,
        **orders(steps, frames, places, streams),
    )
    qkv, out = (width, columns), (columns, width)
    down, up = (hidden, width), (width, hidden)
    outs = dict(
        t_q=(qkv, BF16),
        t_k=(qkv, BF16),
        t_v=(qkv, BF16),
        t_out=(out, BF16),
        s_q=(qkv, BF16),
        s_k=(qkv, BF16),
        s_v=(qkv, BF16),
        s_out=(out, BF16),
        up_grad=(up, BF16),
        down_grad=(down, BF16),
        y_res=((tokens, width), BF16),
        grad_res=((tokens, width), F32),
        small_res=((room, width), F32),
        up_bias_res=((8, width), F32),
    )
    s_all = (steps, chips, 2, rows, width)
    t_all = (streams, chips, 2, t_rows, width)
    s_one, t_one = (steps, chips, rows, width), (streams, chips, t_rows, width)
    owned = (streams, t_rows, width)
    swapped = (streams, frames, t_rows // frames, width)
    whole = (1, frames, tokens // frames, width)
    g_part = (1, frames, chips, 2, tokens // frames, width)
    g_into = (chips, frames, 2, tokens // frames, width)

    def kind_of(shape):
        return BF16 if shape[-2] % 16 == 0 else F32

    cols = dict(
        s_cols=(steps, patches, columns),
        s_proj=(3, steps, patches, columns),
        s_dproj=(3, steps, patches, columns),
        s_mixed=(streams, heads, t_rows, columns),
        s_dmixed=(streams, heads, t_rows, columns),
        t_proj=(3, streams, count, columns),
        t_dproj=(3, streams, count, columns),
        t_mixed=(streams, count, columns),
        act=(streams, count, hidden),
        dpre=(streams, count, hidden),
        normed0=(steps, patches, width),
        gathered=(4 * streams,) + t_all[1:],
        g_all=t_all,
        part=t_all,
        sib=t_one,
        rise=t_one,
        fall=t_one,
        out=t_one,
        **({} if s_all == t_all else dict(last_part=s_all, last_out=s_one)),
        last_sib=s_one,
        last_rise=s_one,
        last_fall=s_one,
        y=owned,
    )
    floats = dict(
        state0=owned,
        state1=owned,
        state2=owned,
        grad1=owned,
        grad2=owned,
        total=(t_rows, width),
        **({} if (steps, rows) == (streams, t_rows) else dict(last_total=(steps, rows, width))),
        mask=(count, count),
        small=(8, width),
        sums0=(8 + entries, width),
        up_bias_grad=(1, width),
        state_src=swapped,
        state_dst=swapped,
        grad_src=swapped,
        grad_dst=swapped,
    )
    scratch = {name: pltpu.VMEM(shape, BF16) for name, shape in cols.items()}
    scratch |= {name: pltpu.VMEM(shape, F32) for name, shape in floats.items()}
    scratch["g_dst"] = pltpu.VMEM(g_into, kind_of(g_into))
    if g_part[1:] != t_all:
        scratch["g_src"] = pltpu.VMEM(g_part, kind_of(g_part))
    scratch |= {name: pltpu.VMEM(whole, kind_of(whole)) for name in ("y_src", "y_dst")}
    every_shape = (room, width)
    scratch |= dict(
        every_src=pltpu.VMEM(every_shape, BF16),
        every_sib=pltpu.VMEM(every_shape, BF16),
        every_line=pltpu.VMEM((chips, room, width // chips), BF16),
        every_frames=pltpu.VMEM((frames, room, width // chips), BF16),
        every_full=pltpu.VMEM(every_shape, BF16),
        every_sems=[pltpu.SemaphoreType.DMA((2 * chips + frames,))] * 2,
        bias_src=pltpu.VMEM((8, width), F32),
        bias_dst=pltpu.VMEM((1, frames, 8, width), F32),
        bias_sems=[pltpu.SemaphoreType.DMA((1, frames))] * 2,
        sum_sems=[pltpu.SemaphoreType.DMA((streams, chips))] * 5,
        last_sems=[pltpu.SemaphoreType.DMA((steps, chips))] * 5,
        gather_sems=[pltpu.SemaphoreType.DMA((4 * streams, chips))] * 5,
        state_sems=[pltpu.SemaphoreType.DMA((streams, frames))] * 2,
        grad_sems=[pltpu.SemaphoreType.DMA((streams, frames))] * 2,
        g_sems=[pltpu.SemaphoreType.DMA((chips, frames))] * 2,
        y_sems=[pltpu.SemaphoreType.DMA((1, frames))] * 2,
        reduce=[
            x
            for shape, dim, pieces in ((down, 0, 2), (up, 0, 2))
            + 2 * (((qkv, 0, 1),) * 3 + ((out, 1, 1),))
            for x in frame_sum_scratch(frames, shape, dim, pieces)
        ],
    )
    held = {k: v for k, v in args.items() if k not in ("ids", "segments")}
    scratch |= {name: pltpu.VMEM(v.shape, v.dtype) for name, v in held.items()}
    scratch |= {name: pltpu.VMEM(shape, kind) for name, (shape, kind) in outs.items()}
    scratch["fetch_sems"] = pltpu.SemaphoreType.DMA((len(held),))
    scratch["store_sems"] = pltpu.SemaphoreType.DMA((len(outs),))
    fetched, results_of, names = tuple(args), tuple(outs), tuple(scratch)
    parts = pl.pallas_call(
        lambda *refs: block(fetched, results_of, names, *refs),
        name="block",
        out_shape=[jax.ShapeDtypeStruct(shape, kind) for shape, kind in outs.values()],
        in_specs=[
            pl.BlockSpec(memory_space=pltpu.HBM if name in held else pltpu.SMEM)
            for name in args
        ],
        out_specs=[pl.BlockSpec(memory_space=pltpu.HBM)] * len(outs),
        scratch_shapes=list(scratch.values()),
        compiler_params=pltpu.CompilerParams(
            collective_id=0, has_side_effects=True, vmem_limit_bytes=VMEM_LIMIT
        ),
    )(*args.values())
    made = results(dict(zip(outs, parts)), entries)
    s_blocks = (steps, rows, width)
    return (
        made["y"].reshape(s_blocks),
        made["grad"].reshape(s_blocks),
        made["table"],
        made["gain"],
        made["shift"],
        made["s_qkv"].transpose(1, 0, 2),
        made["s_out"],
        made["t_qkv"].transpose(1, 0, 2),
        made["t_out"],
        made["bias"],
        made["up"],
        made["up_bias"].reshape(hidden),
        made["down"],
    )


def solution(mesh):
    return jax.shard_map(
        on_device,
        mesh=mesh,
        in_specs=(
            P("frames", None, None),
            P("frames"),
            P(),
            P(),
            P(),
            P(),
            P(None, None, "heads"),
            P("heads", None),
            P(None, None, "heads"),
            P("heads", None),
            P(),
            P(None, "heads"),
            P("heads"),
            P("heads", None),
            P("frames", None, None),
        ),
        out_specs=(
            P("frames", "heads", None),
            P("frames", "heads", None),
            P(),
            P(),
            P(),
            P(None, None, "heads"),
            P("heads", None),
            P(None, None, "heads"),
            P("heads", None),
            P(),
            P(None, "heads"),
            P("heads"),
            P("heads", None),
        ),
        check_vma=False,
    )
```
